32 devices in a mesh: rep: 4 (over y, core), shard: 8 (over z, x).
Axes of the slice: x: 2, y: 2, z: 4, core: 2. Of those that a mesh axis runs over, the one named last changes fastest.
Arguments:
- inputs: bfloat16 [32768, 768], P(('rep', 'shard')), may hold values from -6 to 6
- cotangent: bfloat16 [32768, 768], P(('rep', 'shard')), may hold values from -6 to 6
- segment: int32 [32768], P(('rep', 'shard')), may hold values from 0 to 12, as said below
- parent: int32 [32, 13], P(('rep', 'shard')), may hold values from 0 to 4, as said below
- clusters: int32 [12, 32768], P(None, ('rep', 'shard')), may hold values from 0 to 7, as said below
- qkv_weight: bfloat16 [2, 768, 2304], P(None, 'shard'), may hold values from -0.21875 to 0.21875
- qv_bias: bfloat16 [2, 1536], P(None, 'shard'), may hold values from -2 to 2
- out_weight: bfloat16 [2, 768, 768], P(None, 'shard'), may hold values from -1.75 to 1.75
- out_bias: bfloat16 [2, 768], P(None, 'shard'), may hold values from -2 to 2
- attn_gain: bfloat16 [2, 768], P(None, 'shard'), may hold values from 0.5 to 1.5
- attn_shift: bfloat16 [2, 768], P(None, 'shard'), may hold values from -2 to 2
- ffin_weight: bfloat16 [2, 768, 3072], P(None, 'shard'), may hold values from -0.21875 to 0.21875
- ffin_bias: bfloat16 [2, 3072], P(None, 'shard'), may hold values from -2 to 2
- ffout_weight: bfloat16 [2, 3072, 768], P(None, 'shard'), may hold values from -0.109375 to 0.109375
- ffout_bias: bfloat16 [2, 768], P(None, 'shard'), may hold values from -2 to 2
- ffn_gain: bfloat16 [2, 768], P(None, 'shard'), may hold values from 0.5 to 1.5
- ffn_shift: bfloat16 [2, 768], P(None, 'shard'), may hold values from -2 to 2
Outputs:
- out: bfloat16 [32768, 768], P(('rep', 'shard'))
- grad_input: float32 [32768, 768], P(('rep', 'shard'))
- qkv_weight_grad: float32 [2, 768, 2304], P(None, 'shard')
- qv_bias_grad: float32 [2, 1536], P(None, 'shard')
- out_weight_grad: float32 [2, 768, 768], P(None, 'shard')
- out_bias_grad: float32 [2, 768], P(None, 'shard')
- attn_gain_grad: float32 [2, 768], P(None, 'shard')
- attn_shift_grad: float32 [2, 768], P(None, 'shard')
- ffin_weight_grad: float32 [2, 768, 3072], P(None, 'shard')
- ffin_bias_grad: float32 [2, 3072], P(None, 'shard')
- ffout_weight_grad: float32 [2, 3072, 768], P(None, 'shard')
- ffout_bias_grad: float32 [2, 768], P(None, 'shard')
- ffn_gain_grad: float32 [2, 768], P(None, 'shard')
- ffn_shift_grad: float32 [2, 768], P(None, 'shard')
The draws below stay inside these ranges and needn't reach their ends.
Inputs may be any that keep to these rules, and one draw needn't show every extreme that they name: In each tree the first 512 tokens have segment 0; each of segments 1 to 4 covers 64 consecutive tokens and each of segments 5 to 12 covers 32 consecutive tokens after the trunk, the order of these twelve blocks differing between trees. For every tree, segments 0 to 4 have parent 0 and each of segments 1 to 4 is the parent of exactly two of segments 5 to 12. For every head and tree, each of the 8 clusters holds exactly 128 tokens.
All inputs are finite; a program needn't handle non-finite values.
Results may differ from the reference program's by a relative error of at most 0.02.
Values may be sent and summed in bfloat16 or wider, within the bound.
A program may use at most 320 MiB of HBM per device.

```python
import jax
import jax.numpy as jnp
from jax import lax

D = 768
HEADS = 12
HEAD_DIM = 64
FF = 3072
LAYERS = 2
TRUNK = 512
BRANCH = 64
LEAF = 32
CLUSTER = 128
TREE_LEN = 1024
TREES = 32
TOKENS = 32768


def draw_segment(key, part):
    keys_all = jax.random.split(key, TREES)

    def one_tree(tree_key):
        order = jax.random.permutation(tree_key, 12).astype(jnp.int32) + 1
        block_sizes = jnp.where(order <= 4, BRANCH, LEAF).astype(jnp.int32)
        block_ends = jnp.cumsum(block_sizes).astype(jnp.int32)
        place = jnp.arange(TREE_LEN - TRUNK, dtype=jnp.int32)
        block_index = jnp.sum((place[:, None] >= block_ends[None, :]).astype(jnp.int32), axis=1)
        rest = order[block_index]
        return jnp.concatenate([jnp.zeros((TRUNK,), jnp.int32), rest]).astype(jnp.int32)
    return jax.vmap(one_tree)(keys_all).reshape(TREES * TREE_LEN)


def draw_parent(key, part):
    keys_all = jax.random.split(key, TREES)

    def one_tree(tree_key):
        order = jax.random.permutation(tree_key, 8).astype(jnp.int32)
        leaves = 1 + order // 2
        return jnp.concatenate([jnp.zeros((5,), jnp.int32), leaves]).astype(jnp.int32)
    return jax.vmap(one_tree)(keys_all)


def draw_clusters(key, part):
    keys_all = jax.random.split(key, HEADS * TREES)

    def one_tree(tree_key):
        return (jax.random.permutation(tree_key, TREE_LEN).astype(jnp.int32) // CLUSTER).astype(jnp.int32)
    return jax.vmap(one_tree)(keys_all).reshape(HEADS, TREES * TREE_LEN)


def level_of(stream_key, dims, cuts, smallest, largest):
    gain = 1.0
    for position, shards_of in cuts:
        steps = jax.random.uniform(jax.random.fold_in(jax.random.fold_in(stream_key, 6), position), (shards_of,), jnp.float32, smallest / len(cuts), largest / len(cuts))
        gain = gain * jnp.repeat(jnp.exp(steps), dims[position] // shards_of).reshape((-1,) + (1,) * (len(dims) - 1 - position))
    return gain


def noise(key, shape, deviation, reach, cuts=(), held_as=jnp.bfloat16):
    drawn = jax.random.normal(key, shape, jnp.float32) * deviation
    if len(cuts) > 0:
        drawn = level_of(key, shape, cuts, -0.22, 0.18) * drawn
    return jnp.clip(drawn, min=-reach, max=reach).astype(held_as)


def setup_inputs(seed: int = 0) -> dict:
    keys = jax.random.split(jax.random.key(seed), 18)
    inputs = noise(keys[0], (TOKENS, D), 1.0, 6.0, ((0, 32),))
    cotangent = noise(keys[1], (TOKENS, D), 1.0, 6.0, ((0, 32),))
    segment = draw_segment(jax.random.fold_in(keys[17], 71), 0)
    parent = draw_parent(jax.random.fold_in(keys[17], 71), 0)
    clusters = draw_clusters(jax.random.fold_in(keys[17], 71), 0)
    qkv_weight = noise(keys[5], (LAYERS, D, 3 * D), D ** -0.5, 0.21875, ((1, 8),))
    qv_bias = noise(keys[6], (LAYERS, 2 * D), 0.3, 2.0, ((1, 8),))
    out_weight = noise(keys[7], (LAYERS, D, D), (2 * D // CLUSTER) ** -0.5, 1.75, ((1, 8),))
    out_bias = noise(keys[8], (LAYERS, D), 0.3, 2.0, ((1, 8),))
    attn_gain = jnp.clip(1.0 + 0.1 * jax.random.normal(keys[9], (LAYERS, D), jnp.float32), 0.5, 1.5).astype(jnp.bfloat16)
    attn_shift = noise(keys[10], (LAYERS, D), 0.3, 2.0, ((1, 8),))
    ffin_weight = noise(keys[11], (LAYERS, D, FF), D ** -0.5, 0.21875, ((1, 8),))
    ffin_bias = noise(keys[12], (LAYERS, FF), 0.3, 2.0, ((1, 8),))
    ffout_weight = noise(keys[13], (LAYERS, FF, D), FF ** -0.5, 0.109375, ((1, 8),))
    ffout_bias = noise(keys[14], (LAYERS, D), 0.3, 2.0, ((1, 8),))
    ffn_gain = jnp.clip(1.0 + 0.1 * jax.random.normal(keys[15], (LAYERS, D), jnp.float32), 0.5, 1.5).astype(jnp.bfloat16)
    ffn_shift = noise(keys[16], (LAYERS, D), 0.3, 2.0, ((1, 8),))
    return {"inputs": inputs, "cotangent": cotangent, "segment": segment, "parent": parent, "clusters": clusters, "qkv_weight": qkv_weight, "qv_bias": qv_bias, "out_weight": out_weight, "out_bias": out_bias, "attn_gain": attn_gain, "attn_shift": attn_shift, "ffin_weight": ffin_weight, "ffin_bias": ffin_bias, "ffout_weight": ffout_weight, "ffout_bias": ffout_bias, "ffn_gain": ffn_gain, "ffn_shift": ffn_shift}


@jax.custom_vjp
def low(v):
    return lax.optimization_barrier(v.astype(jnp.bfloat16)).astype(jnp.float32)

@jax.custom_vjp
def low_back(v):
    return v

def low_keep(v):
    return (low(v), None)

def low_pass(kept, grad):
    return (grad,)

def back_keep(v):
    return (v, None)

def back_low(kept, grad):
    return (low(grad),)
low.defvjp(low_keep, low_pass)
low_back.defvjp(back_keep, back_low)
norm_eps = 1e-06

def matmul_high(left_side, right_side):
    return jnp.dot(left_side, right_side, precision=lax.Precision.HIGHEST, preferred_element_type=jnp.float32)

def layer_norm(values, norm_gain, norm_shift):
    average = lax.optimization_barrier(jnp.mean(values, axis=-1, keepdims=True))
    centred = values - average
    variance = lax.optimization_barrier(jnp.mean(centred * centred, axis=-1, keepdims=True))
    return centred * lax.rsqrt(variance + norm_eps) * norm_gain + norm_shift

def lookup(index, table):
    return table[index]

def head_attend(head_inputs):
    query_rows, key_rows, value_rows, segments, parents, grands, cluster_ids = head_inputs
    on_path = (segments[None, :] == segments[:, None]) | (segments[None, :] == parents[:, None]) | (segments[None, :] == grands[:, None])
    allowed = on_path & (cluster_ids[:, None] == cluster_ids[None, :])
    scaling = query_rows.shape[-1] ** (-0.5)
    scores = low_back(matmul_high(query_rows, key_rows.T) * scaling)
    masked = jnp.where(allowed, scores, -1e+30)
    maxima = lax.optimization_barrier(jnp.max(masked, axis=1, keepdims=True))
    numerator = jnp.exp(masked - maxima)
    softmax_rows = numerator / lax.optimization_barrier(jnp.sum(numerator, axis=1, keepdims=True))
    return low(low_back(matmul_high(low(softmax_rows), value_rows)))

def layer_apply(layer_in, weights, path_info):
    qkv_weight, qv_bias, out_weight, out_bias, attn_gain, attn_shift, ffin_weight, ffin_bias, ffout_weight, ffout_bias, ffn_gain, ffn_shift = weights
    row_count = layer_in.shape[0]
    tree_count = row_count // TREE_LEN
    full_bias = jnp.concatenate([qv_bias[:D], jnp.zeros_like(qv_bias[:D]), qv_bias[D:]])
    projected = low(low_back(matmul_high(low(layer_in), qkv_weight) + full_bias))
    heads_all = projected.reshape(tree_count, TREE_LEN, 3, HEADS, HEAD_DIM).transpose(2, 0, 3, 1, 4)
    heads_all = heads_all.reshape(3, tree_count * HEADS, TREE_LEN, HEAD_DIM)
    context_heads = lax.map(jax.checkpoint(head_attend), (heads_all[0], heads_all[1], heads_all[2]) + path_info)
    context = context_heads.reshape(tree_count, HEADS, TREE_LEN, HEAD_DIM).transpose(0, 2, 1, 3).reshape(row_count, D)
    attn_sum = layer_in + low_back(matmul_high(context, out_weight) + out_bias)
    hidden_one = layer_norm(attn_sum, attn_gain, attn_shift)
    pre_act = low_back(matmul_high(low(hidden_one), ffin_weight) + ffin_bias)
    activated = low(jax.nn.gelu(pre_act, approximate=False))
    ffn_sum = hidden_one + low_back(matmul_high(activated, ffout_weight) + ffout_bias)
    return layer_norm(ffn_sum, ffn_gain, ffn_shift)

def reference(inputs, cotangent, segment, parent, clusters, qkv_weight, qv_bias, out_weight, out_bias, attn_gain, attn_shift, ffin_weight, ffin_bias, ffout_weight, ffout_bias, ffn_gain, ffn_shift):
    tree_count = parent.shape[0]
    group = 1
    while group * 2 * TREE_LEN <= 4096 and tree_count % (group * 2) == 0:
        group = group * 2
    step_count = tree_count // group
    segments = segment.reshape(tree_count, TREE_LEN)
    parents = jax.vmap(lookup)(segments, parent)
    grands = jax.vmap(lookup)(parents, parent)
    cluster_ids = clusters.reshape(HEADS, tree_count, TREE_LEN).transpose(1, 0, 2)
    float_params = (qkv_weight.astype(jnp.float32), qv_bias.astype(jnp.float32), out_weight.astype(jnp.float32), out_bias.astype(jnp.float32), attn_gain.astype(jnp.float32), attn_shift.astype(jnp.float32), ffin_weight.astype(jnp.float32), ffin_bias.astype(jnp.float32), ffout_weight.astype(jnp.float32), ffout_bias.astype(jnp.float32), ffn_gain.astype(jnp.float32), ffn_shift.astype(jnp.float32))

    def forward(layer_in, params):

        def one_group(group_inputs):
            group_rows, group_segs, group_parents, group_grands, group_clusters = group_inputs
            path_info = (jnp.repeat(group_segs, HEADS, axis=0), jnp.repeat(group_parents, HEADS, axis=0), jnp.repeat(group_grands, HEADS, axis=0), group_clusters.reshape(group * HEADS, TREE_LEN))
            hidden = group_rows
            for layer_index in range(LAYERS):
                weights = tuple((param[layer_index] for param in params))
                hidden = layer_apply(hidden, weights, path_info)
            return hidden
        outputs = lax.map(jax.checkpoint(one_group), (layer_in.reshape(step_count, group * TREE_LEN, D), segments.reshape(step_count, group, TREE_LEN), parents.reshape(step_count, group, TREE_LEN), grands.reshape(step_count, group, TREE_LEN), cluster_ids.reshape(step_count, group, HEADS, TREE_LEN)))
        return outputs.reshape(step_count * group * TREE_LEN, D)
    result, pull = jax.vjp(forward, inputs.astype(jnp.float32), float_params)
    grad_input, grads = pull(cotangent.astype(jnp.float32))
    return (result.astype(jnp.bfloat16), grad_input, grads[0], grads[1], grads[2], grads[3], grads[4], grads[5], grads[6], grads[7], grads[8], grads[9], grads[10], grads[11])
```

```python
import functools

import jax
import jax.numpy as jnp
from jax import lax
from jax.experimental import pallas as pl
from jax.experimental.pallas import tpu as pltpu
from jax.sharding import PartitionSpec as P

D = 768
HEADS = 12
HEAD_DIM = 64
LAYERS = 2
CLUSTER = 128
TREE_LEN = 1024


norm_eps = 1e-06


def layer_norm(values, norm_gain, norm_shift):
    average = jnp.mean(values, axis=-1, keepdims=True)
    centred = values - average
    variance = jnp.mean(centred * centred, axis=-1, keepdims=True)
    return centred * lax.rsqrt(variance + norm_eps) * norm_gain + norm_shift


def gelu_exact(values):
    return jax.nn.gelu(values, approximate=False)


def dot_first(left_side, right_side):
    return lax.dot_general(
        left_side, right_side, (((0,), (0,)), ((), ())), preferred_element_type=jnp.float32
    )


def dot_last(left_side, right_side):
    return lax.dot_general(
        left_side, right_side, (((1,), (1,)), ((), ())), preferred_element_type=jnp.float32
    )


def lookup_small(index, table):
    match = index[:, None] == jnp.arange(table.shape[0], dtype=jnp.int32)[None, :]
    return jnp.sum(jnp.where(match, table[None, :], 0), axis=1)


PAIRS = HEADS // 2
LANES = 2 * HEAD_DIM
KERNEL_VMEM = 60 * 2**20


def slot_ranks(cluster_ids):
    length = cluster_ids.shape[-1]
    count = length // CLUSTER
    order = jnp.arange(count, dtype=jnp.int32)
    member = cluster_ids[..., None, :] == order[:, None]
    upto = jnp.arange(length, dtype=jnp.int32)
    triangle = (upto[:, None] <= upto[None, :]).astype(jnp.bfloat16)
    ranks = jnp.dot(
        member.astype(jnp.bfloat16), triangle, preferred_element_type=jnp.float32
    ).astype(jnp.int32)
    return jnp.sum(jnp.where(member, ranks - 1 + CLUSTER * order[:, None], 0), axis=-2)


def one_hot_rows(slot_row):
    length = slot_row.shape[-1]
    rows = lax.broadcasted_iota(jnp.int32, (length, length), 0)
    return jnp.where(rows == slot_row, 1.0, 0.0).astype(jnp.bfloat16)


def first_lanes(length):
    return lax.broadcasted_iota(jnp.int32, (length, LANES), 1) < HEAD_DIM


def contract_last(left_side, right_side):
    return lax.dot_general(
        left_side, right_side, (((1,), (1,)), ((), ())), preferred_element_type=jnp.float32
    )


def contract_first(left_side, right_side):
    return lax.dot_general(
        left_side, right_side, (((0,), (0,)), ((), ())), preferred_element_type=jnp.float32
    )


def cluster_blocks(values):
    return [values[at : at + CLUSTER] for at in range(0, values.shape[0], CLUSTER)]


def mask_kernel(slot_ref, ids_ref, bias_ref):
    for head in range(2):
        table = one_hot_rows(slot_ref[0, 0, head : head + 1, :])
        ids = jnp.dot(table, ids_ref[0], preferred_element_type=jnp.float32)
        turned = ids.T
        for at in range(0, TREE_LEN, CLUSTER):
            segs = turned[0:1, at : at + CLUSTER]
            block = ids[at : at + CLUSTER]
            allowed = (
                (segs == block[:, 0:1]) | (segs == block[:, 1:2]) | (segs == block[:, 2:3])
            )
            bias_ref[0, head, at : at + CLUSTER, :] = jnp.where(allowed, 0.0, -1e30).astype(
                jnp.bfloat16
            )


def attend_kernel(slot_ref, query_ref, key_ref, value_ref, bias_ref, ctx_ref, qk_ref, val_ref, p_ref):
    low = first_lanes(TREE_LEN)
    query = query_ref[...] * jnp.bfloat16(HEAD_DIM**-0.5)
    key = key_ref[...]
    value = value_ref[...]
    packed = (
        jnp.where(low, query, pltpu.roll(key, HEAD_DIM, 1)),
        jnp.where(low, pltpu.roll(query, HEAD_DIM, 1), key),
    )
    context = []
    for head in range(2):
        table = one_hot_rows(slot_ref[0, 0, head : head + 1, :])
        joined = jnp.concatenate([packed[head], value], axis=1)
        slots = jnp.dot(table, joined, preferred_element_type=jnp.float32).astype(jnp.bfloat16)
        both, values = slots[:, :LANES], slots[:, LANES:]
        qk_ref[0, head] = both
        val_ref[0, head] = values
        queries = jnp.where(low, both, jnp.bfloat16(0))
        keys = pltpu.roll(both, HEAD_DIM, 1)
        scores = jnp.concatenate(
            [contract_last(q, k) for q, k in zip(cluster_blocks(queries), cluster_blocks(keys))],
            axis=0,
        )
        scores = scores + bias_ref[0, head].astype(jnp.float32)
        numerator = jnp.exp(scores - jnp.max(scores, axis=1, keepdims=True))
        total = jnp.sum(numerator, axis=1, keepdims=True)
        soft = (numerator * (1.0 / total)).astype(jnp.bfloat16)
        p_ref[0, head] = soft
        out = jnp.concatenate(
            [
                jnp.dot(p, v, preferred_element_type=jnp.float32)
                for p, v in zip(cluster_blocks(soft), cluster_blocks(values))
            ],
            axis=0,
        ).astype(jnp.bfloat16)
        context.append(contract_first(table, out))
    ctx_ref[...] = jnp.where(low, context[0], context[1]).astype(jnp.bfloat16)


def attend_back_kernel(slot_ref, grad_ref, qk_ref, val_ref, p_ref, out_ref):
    low = first_lanes(TREE_LEN)
    grads = grad_ref[...]
    placed = []
    for head in range(2):
        table = one_hot_rows(slot_ref[0, 0, head : head + 1, :])
        slots = jnp.dot(table, grads, preferred_element_type=jnp.float32)
        slots = jnp.where(low == (head == 0), slots, 0.0).astype(jnp.bfloat16)
        both, values, soft = qk_ref[0, head], val_ref[0, head], p_ref[0, head]
        grad_soft = jnp.concatenate(
            [contract_last(g, v) for g, v in zip(cluster_blocks(slots), cluster_blocks(values))],
            axis=0,
        )
        grad_value = jnp.concatenate(
            [contract_first(p, g) for p, g in zip(cluster_blocks(soft), cluster_blocks(slots))],
            axis=0,
        ).astype(jnp.bfloat16)
        weights = soft.astype(jnp.float32)
        delta = jnp.sum(weights * grad_soft, axis=1, keepdims=True)
        grad_scores = (weights * (grad_soft - delta)).astype(jnp.bfloat16)
        pairs = list(zip(cluster_blocks(grad_scores), cluster_blocks(both)))
        by_key = jnp.concatenate([contract_first(s, b) for s, b in pairs], axis=0)
        by_query = jnp.concatenate(
            [jnp.dot(s, b, preferred_element_type=jnp.float32) for s, b in pairs], axis=0
        )
        mixed = jnp.where(low, by_key, by_query * HEAD_DIM**-0.5).astype(jnp.bfloat16)
        joined = jnp.concatenate([mixed, grad_value], axis=1)
        placed.append(contract_first(table, joined))
    first, second = placed
    out_ref[0] = jnp.where(
        low, pltpu.roll(first[:, :LANES], HEAD_DIM, 1), second[:, :LANES]
    ).astype(jnp.bfloat16)
    out_ref[1] = jnp.where(
        low, first[:, :LANES], pltpu.roll(second[:, :LANES], HEAD_DIM, 1)
    ).astype(jnp.bfloat16)
    out_ref[2] = jnp.where(low, first[:, LANES:], second[:, LANES:]).astype(jnp.bfloat16)


def slot_spec():
    return pl.BlockSpec((1, 1, 2, TREE_LEN), lambda tree, pair: (tree, pair, 0, 0))


def head_spec():
    return pl.BlockSpec((1, 2, TREE_LEN, LANES), lambda tree, pair: (tree, pair, 0, 0))


def column_spec(offset):
    return pl.BlockSpec((TREE_LEN, LANES), lambda tree, pair: (tree, offset + pair))


def kernel_params():
    return pltpu.CompilerParams(vmem_limit_bytes=KERNEL_VMEM)


def mask_bias(slots, ids):
    trees = slots.shape[0]
    return pl.pallas_call(
        mask_kernel,
        grid=(trees, PAIRS),
        in_specs=[
            slot_spec(),
            pl.BlockSpec((1, TREE_LEN, LANES), lambda tree, pair: (tree, 0, 0)),
        ],
        out_specs=head_spec(),
        out_shape=jax.ShapeDtypeStruct((trees, HEADS, TREE_LEN, LANES), jnp.bfloat16),
        compiler_params=kernel_params(),
        cost_estimate=pl.CostEstimate(
            flops=trees * 12_000_000_000, bytes_accessed=trees * 4_000_000, transcendentals=0
        ),
    )(slots, ids)


def attend(projected, slots, bias):
    trees = slots.shape[0]
    stored = jax.ShapeDtypeStruct((trees, HEADS, TREE_LEN, LANES), jnp.bfloat16)
    return pl.pallas_call(
        attend_kernel,
        grid=(trees, PAIRS),
        in_specs=[
            slot_spec(),
            column_spec(0),
            column_spec(PAIRS),
            column_spec(2 * PAIRS),
            head_spec(),
        ],
        out_specs=[column_spec(0), head_spec(), head_spec(), head_spec()],
        out_shape=[
            jax.ShapeDtypeStruct((trees * TREE_LEN, D), jnp.bfloat16),
            stored,
            stored,
            stored,
        ],
        compiler_params=kernel_params(),
        cost_estimate=pl.CostEstimate(
            flops=trees * 30_000_000_000, bytes_accessed=trees * 20_000_000, transcendentals=0
        ),
    )(slots, projected, projected, projected, bias)


def attend_back(grad_context, slots, kept):
    trees = slots.shape[0]
    return pl.pallas_call(
        attend_back_kernel,
        grid=(trees, PAIRS),
        in_specs=[slot_spec(), column_spec(0), head_spec(), head_spec(), head_spec()],
        out_specs=pl.BlockSpec((3, TREE_LEN, LANES), lambda tree, pair: (0, tree, pair)),
        out_shape=jax.ShapeDtypeStruct((3, trees * TREE_LEN, D), jnp.bfloat16),
        compiler_params=kernel_params(),
        cost_estimate=pl.CostEstimate(
            flops=trees * 40_000_000_000, bytes_accessed=trees * 20_000_000, transcendentals=0
        ),
    )(slots, grad_context, *kept)


def layer_forward(layer_in, weights, path_info):
    (
        qkv_weight,
        qv_bias,
        out_weight,
        out_bias,
        attn_gain,
        attn_shift,
        ffin_weight,
        ffin_bias,
        ffout_weight,
        ffout_bias,
        ffn_gain,
        ffn_shift,
    ) = weights
    layer_low = layer_in.astype(jnp.bfloat16)
    bias_float = qv_bias.astype(jnp.float32)
    full_bias = jnp.concatenate([bias_float[:D], jnp.zeros((D,), jnp.float32), bias_float[D:]])
    projected = (
        jnp.dot(layer_low, qkv_weight, preferred_element_type=jnp.float32) + full_bias
    ).astype(jnp.bfloat16)
    slots, bias = path_info
    context, *kept_heads = attend(projected, slots, bias)
    attn_sum = (
        layer_in
        + jnp.dot(context, out_weight, preferred_element_type=jnp.float32)
        + out_bias.astype(jnp.float32)
    )
    hidden_one = layer_norm(attn_sum, attn_gain.astype(jnp.float32), attn_shift.astype(jnp.float32))
    hidden_low = hidden_one.astype(jnp.bfloat16)
    pre_act = jnp.dot(
        hidden_low, ffin_weight, preferred_element_type=jnp.float32
    ) + ffin_bias.astype(jnp.float32)
    act_low = gelu_exact(pre_act).astype(jnp.bfloat16)
    ffn_sum = (
        hidden_one
        + jnp.dot(act_low, ffout_weight, preferred_element_type=jnp.float32)
        + ffout_bias.astype(jnp.float32)
    )
    result = layer_norm(ffn_sum, ffn_gain.astype(jnp.float32), ffn_shift.astype(jnp.float32))
    saved = (
        layer_low,
        kept_heads,
        context,
        attn_sum,
        hidden_low,
        pre_act,
        act_low,
        ffn_sum,
    )
    return (result, saved)


def layer_backward(grad_out, weights, saved, path_info, reduce):
    (
        qkv_weight,
        qv_bias,
        out_weight,
        out_bias,
        attn_gain,
        attn_shift,
        ffin_weight,
        ffin_bias,
        ffout_weight,
        ffout_bias,
        ffn_gain,
        ffn_shift,
    ) = weights
    (
        layer_low,
        kept_heads,
        context,
        attn_sum,
        hidden_low,
        pre_act,
        act_low,
        ffn_sum,
    ) = saved
    ignored, norm_pull = jax.vjp(
        layer_norm, ffn_sum, ffn_gain.astype(jnp.float32), ffn_shift.astype(jnp.float32)
    )
    grad_ffn_sum, grad_ffn_gain, grad_ffn_shift = norm_pull(grad_out)
    grad_down = grad_ffn_sum.astype(jnp.bfloat16)
    grad_ffout_weight = reduce(act_low, grad_down[None], False)
    grad_ffout_bias = jnp.sum(grad_down.astype(jnp.float32), axis=0)
    grad_act = dot_last(grad_down, ffout_weight)
    ignored, gelu_pull = jax.vjp(gelu_exact, pre_act)
    grad_pre = gelu_pull(grad_act)[0].astype(jnp.bfloat16)
    grad_ffin_weight = reduce(hidden_low, grad_pre[None], True)
    grad_ffin_bias = jnp.sum(grad_pre.astype(jnp.float32), axis=0)
    grad_hidden = grad_ffn_sum + dot_last(grad_pre, ffin_weight)
    ignored, first_pull = jax.vjp(
        layer_norm, attn_sum, attn_gain.astype(jnp.float32), attn_shift.astype(jnp.float32)
    )
    grad_attn_sum, grad_attn_gain, grad_attn_shift = first_pull(grad_hidden)
    grad_attn_low = grad_attn_sum.astype(jnp.bfloat16)
    grad_out_weight = reduce(context, grad_attn_low[None], False)
    grad_out_bias = jnp.sum(grad_attn_low.astype(jnp.float32), axis=0)
    grad_context = dot_last(grad_attn_low, out_weight).astype(jnp.bfloat16)
    grad_proj = attend_back(grad_context, path_info[0], kept_heads)
    grad_qkv_weight = reduce(layer_low, grad_proj, True)
    column_sums = jnp.sum(grad_proj.astype(jnp.float32), axis=1)
    grad_qv_bias = jnp.concatenate([column_sums[0], column_sums[2]])
    grad_in = grad_attn_sum
    for part in range(3):
        grad_in = grad_in + dot_last(grad_proj[part], qkv_weight[:, part * D : (part + 1) * D])
    grads = (
        grad_qkv_weight,
        grad_qv_bias,
        grad_out_weight,
        grad_out_bias,
        grad_attn_gain,
        grad_attn_shift,
        grad_ffin_weight,
        grad_ffin_bias,
        grad_ffout_weight,
        grad_ffout_bias,
        grad_ffn_gain,
        grad_ffn_shift,
    )
    return (grad_in, grads)


MATRICES = (0, 2, 6, 8)
VECTORS = (1, 3, 4, 5, 7, 9, 10, 11)
AXES = ("rep", "shard")
CHIPS_Z, CHIPS_X, CHIPS_Y, CORES = 4, 2, 2, 2


class Place:
    def __init__(self):
        rep = lax.axis_index("rep")
        shard = lax.axis_index("shard")
        self.y, self.core = rep // CORES, rep % CORES
        self.z, self.x = shard // CHIPS_X, shard % CHIPS_X


def hop(value, dz=0, dx=0, dy=0, dc=0):
    pairs = []
    for y in range(CHIPS_Y):
        for c in range(CORES):
            for z in range(CHIPS_Z):
                for x in range(CHIPS_X):
                    source = ((y * CORES + c) * CHIPS_Z + z) * CHIPS_X + x
                    y2, c2 = (y + dy) % CHIPS_Y, (c + dc) % CORES
                    z2, x2 = (z + dz) % CHIPS_Z, (x + dx) % CHIPS_X
                    pairs.append((source, ((y2 * CORES + c2) * CHIPS_Z + z2) * CHIPS_X + x2))
    return lax.ppermute(value, AXES, pairs)


def pick(array, index, axis):
    return lax.dynamic_index_in_dim(array, index, axis, keepdims=False)


def ordered(first, own, other, axis):
    return jnp.where(
        first, jnp.concatenate([own, other], axis), jnp.concatenate([other, own], axis)
    )


def place_kernel(split_y, half, count, *refs):
    pieces, out, sems = refs[:count], refs[count], refs[count + 1]
    rep = lax.axis_index("rep")
    shard = lax.axis_index("shard")
    y, core = rep // CORES, rep % CORES
    z, x = shard // CHIPS_X, shard % CHIPS_X
    copies = []
    for number, piece in enumerate(pieces):
        dc = number % CORES
        dx = number // CORES % CHIPS_X
        dy = number // (CORES * CHIPS_X)
        column = pl.multiple_of((core + dc) % CORES * half, 128)
        for dz in range(CHIPS_Z):
            owner = (z + CHIPS_Z - dz) % CHIPS_Z * CHIPS_X + (x + dx) % CHIPS_X
            row = (y + dy) % CHIPS_Y if split_y else 0
            copies.append(
                pltpu.make_async_copy(
                    piece.at[dz],
                    out.at[owner, row, :, pl.ds(column, half)],
                    sems.at[number * CHIPS_Z + dz],
                )
            )
    for copy in copies:
        copy.start()
    for copy in copies:
        copy.wait()


def gather_start(block):
    return [block] + [hop(block, dz=k) for k in range(1, CHIPS_Z)]


def gather_finish(parts, split_y):
    _, rows, half = parts[0].shape[0], parts[0].shape[0], parts[0].shape[1]
    stack = jnp.stack(parts)
    pieces = [stack, hop(stack, dx=1)]
    if split_y:
        pieces = pieces + [hop(piece, dy=1) for piece in pieces]
    pieces = [item for piece in pieces for item in (piece, hop(piece, dc=1))]
    splits = CHIPS_Y if split_y else 1
    count = len(pieces)
    whole = pl.pallas_call(
        lambda *refs: place_kernel(split_y, half, count, *refs),
        in_specs=[pl.BlockSpec(memory_space=pl.ANY)] * count,
        out_specs=pl.BlockSpec(memory_space=pl.ANY),
        out_shape=jax.ShapeDtypeStruct(
            (CHIPS_Z * CHIPS_X, splits, rows, 2 * half), jnp.bfloat16
        ),
        scratch_shapes=[pltpu.SemaphoreType.DMA((count * CHIPS_Z,))],
        cost_estimate=pl.CostEstimate(
            flops=0, bytes_accessed=4 * CHIPS_Z * count * rows * half, transcendentals=0
        ),
    )(*pieces)
    return whole.reshape(CHIPS_Z * CHIPS_X * splits * rows, 2 * half)


def gather_vectors(vectors, place):
    sizes = [vector.shape[1] for vector in vectors]
    own = jnp.concatenate(vectors, axis=1)
    layers, width = own.shape
    count = CHIPS_Z * CHIPS_X
    rounds = [
        hop(own, dz=dz, dx=dx) if dz or dx else own
        for dz in range(CHIPS_Z)
        for dx in range(CHIPS_X)
    ]
    stack = jnp.stack(rounds).astype(jnp.float32)
    wanted = jnp.arange(count, dtype=jnp.int32)
    behind = (place.z - wanted // CHIPS_X) % CHIPS_Z * CHIPS_X + (
        place.x - wanted % CHIPS_X
    ) % CHIPS_X
    turn = (behind[:, None] == wanted[None, :]).astype(jnp.float32)
    stack = jnp.sum(turn[:, :, None, None] * stack[None], axis=1)
    out, at = [], 0
    for size in sizes:
        out.append(
            stack[:, :, at : at + size].transpose(1, 0, 2).reshape(layers, count * size)
        )
        at += size
    return out


def gather_all(weights, place):
    vectors = gather_vectors([weights[number] for number in VECTORS], place)
    gathered = [[None] * 12 for _ in range(LAYERS)]
    previous = None
    for layer in range(LAYERS):
        for number in MATRICES:
            shard = weights[number][layer]
            rows, columns = shard.shape
            split_y = number in (6, 8)
            tall = rows // CHIPS_Y if split_y else rows
            block = lax.dynamic_slice(
                shard,
                (place.y * tall if split_y else 0, place.core * (columns // 2)),
                (tall, columns // 2),
            )
            if previous is not None:
                block, *_ = lax.optimization_barrier((block, *previous))
            parts = gather_start(block)
            previous = parts[1:]
            gathered[layer][number] = gather_finish(parts, split_y)
        for number, vector in zip(VECTORS, vectors):
            gathered[layer][number] = vector[layer]
    return gathered


def low_sum(*terms):
    total = terms[0].astype(jnp.float32)
    for term in terms[1:]:
        total = total + term.astype(jnp.float32)
    return total


def reduce_matrix(left, right, place, y_first):
    parts, _, columns = right.shape
    half = columns // 2
    depth = left.shape[1]

    def product(core):
        cut = lax.dynamic_slice_in_dim(right, core * half, half, axis=2)
        grads = [dot_first(left, cut[part]).astype(jnp.bfloat16) for part in range(parts)]
        return [
            grad.reshape(CHIPS_Z, CHIPS_X, CHIPS_Y, depth // 16, half) for grad in grads
        ]

    away = product(1 - place.core)
    arrived = [hop(part, dc=1) for part in away]
    kept = product(place.core)
    total = jnp.stack([low_sum(mine, other) for mine, other in zip(kept, arrived)], axis=0)

    def swap(values, index, axis, **step):
        sent = pick(values, 1 - index, axis).astype(jnp.bfloat16)
        return low_sum(pick(values, index, axis), hop(sent, **step))

    if y_first:
        total = swap(total, place.y, 3, dy=1)
    total = swap(total, place.x, 2, dx=1)
    landed = []
    for k in range(1, CHIPS_Z):
        sent = pick(total, (place.z + k) % CHIPS_Z, 1).astype(jnp.bfloat16)
        landed.append(hop(sent, dz=k))
    total = low_sum(pick(total, place.z, 1), *landed).astype(jnp.bfloat16)
    if y_first:
        rows = total[:, None]
        rows = ordered(place.y == 0, rows, hop(rows, dy=1), 1)
    else:
        rows = low_sum(total, hop(total, dy=1)).astype(jnp.bfloat16)
    rows = rows.reshape(parts, depth // 8, half)
    rows = ordered(place.core == 0, rows, hop(rows, dc=1), 2).astype(jnp.float32)
    return rows.transpose(1, 0, 2).reshape(depth // 8, parts * columns)


def reduce_vectors(vectors, place):
    sizes = [vector.shape[0] for vector in vectors]
    total = jnp.concatenate(vectors)
    for step in (dict(dc=1), dict(dy=1), dict(dx=1), dict(dz=2)):
        total = total + hop(total, **step)
    up, down = hop(total, dz=1), hop(total, dz=3)
    total = total + jnp.where(place.z % 2 == 0, down, up)
    count = CHIPS_Z * CHIPS_X
    shard = place.z * CHIPS_X + place.x
    out, at = [], 0
    for size in sizes:
        share = size // count
        out.append(lax.dynamic_slice_in_dim(total, at + shard * share, share))
        at += size
    return out


def local(
    fast,
    inputs,
    cotangent,
    segment,
    parent,
    clusters,
    qkv_weight,
    qv_bias,
    out_weight,
    out_bias,
    attn_gain,
    attn_shift,
    ffin_weight,
    ffin_bias,
    ffout_weight,
    ffout_bias,
    ffn_gain,
    ffn_shift,
):
    tree_count = parent.shape[0]
    segments = segment.reshape(tree_count, TREE_LEN)
    parents = jax.vmap(lookup_small)(segments, parent)
    grands = jax.vmap(lookup_small)(parents, parent)
    cluster_ids = clusters.reshape(HEADS, tree_count, TREE_LEN).transpose(1, 0, 2)
    slots = slot_ranks(cluster_ids).reshape(tree_count, PAIRS, 2, TREE_LEN)
    ids = jnp.stack([segments, parents, grands], axis=-1).astype(jnp.bfloat16)
    ids = jnp.pad(ids, ((0, 0), (0, 0), (0, LANES - 3)))
    path_info = (slots, mask_bias(slots, ids))
    weights = (
        qkv_weight,
        qv_bias,
        out_weight,
        out_bias,
        attn_gain,
        attn_shift,
        ffin_weight,
        ffin_bias,
        ffout_weight,
        ffout_bias,
        ffn_gain,
        ffn_shift,
    )
    if fast:
        place = Place()
        gathered = gather_all(weights, place)

        def reduce(left, right, y_first):
            return reduce_matrix(left, right, place, y_first)

    else:
        gathered = [
            [lax.all_gather(weight[layer], "shard", axis=0, tiled=True) for weight in weights]
            for layer in range(LAYERS)
        ]

        def reduce(left, right, y_first):
            grads = jnp.concatenate([dot_first(left, part) for part in right], axis=1)
            grads = lax.psum_scatter(grads, "shard", scatter_dimension=0, tiled=True)
            return lax.psum(grads.astype(jnp.bfloat16), "rep").astype(jnp.float32)

    hidden = inputs.astype(jnp.float32)
    kept_saved = []
    for layer_index in range(LAYERS):
        hidden, saved = layer_forward(hidden, gathered[layer_index], path_info)
        kept_saved.append(saved)
    result = hidden.astype(jnp.bfloat16)
    grad_rows = cotangent.astype(jnp.float32)
    per_layer = [None] * LAYERS
    for layer_index in reversed(range(LAYERS)):
        grad_rows, grads = layer_backward(
            grad_rows, gathered[layer_index], kept_saved[layer_index], path_info, reduce
        )
        per_layer[layer_index] = list(grads)
    order = [(layer, number) for layer in reversed(range(LAYERS)) for number in VECTORS]
    early = [item for item in order if item != (0, 1)]
    for items in (early, [(0, 1)]):
        vectors = [per_layer[layer][number] for layer, number in items]
        if fast:
            vectors = reduce_vectors(vectors, place)
        else:
            vectors = [
                lax.psum(lax.psum_scatter(vector, "shard", tiled=True), "rep")
                for vector in vectors
            ]
        for (layer, number), vector in zip(items, vectors):
            per_layer[layer][number] = vector
    stacked = tuple(
        (
            jnp.stack([per_layer[layer_index][member] for layer_index in range(LAYERS)])
            for member in range(12)
        )
    )
    return (
        result,
        grad_rows,
        stacked[0],
        stacked[1],
        stacked[2],
        stacked[3],
        stacked[4],
        stacked[5],
        stacked[6],
        stacked[7],
        stacked[8],
        stacked[9],
        stacked[10],
        stacked[11],
    )


def solution(mesh):
    in_specs = (
        P(("rep", "shard"), None),
        P(("rep", "shard"), None),
        P(("rep", "shard")),
        P(("rep", "shard"), None),
        P(None, ("rep", "shard")),
        P(None, "shard", None),
        P(None, "shard"),
        P(None, "shard", None),
        P(None, "shard"),
        P(None, "shard"),
        P(None, "shard"),
        P(None, "shard", None),
        P(None, "shard"),
        P(None, "shard", None),
        P(None, "shard"),
        P(None, "shard"),
        P(None, "shard"),
    )
    out_specs = (
        P(("rep", "shard"), None),
        P(("rep", "shard"), None),
        P(None, "shard", None),
        P(None, "shard"),
        P(None, "shard", None),
        P(None, "shard"),
        P(None, "shard"),
        P(None, "shard"),
        P(None, "shard", None),
        P(None, "shard"),
        P(None, "shard", None),
        P(None, "shard"),
        P(None, "shard"),
        P(None, "shard"),
    )
    fast = mesh.shape["rep"] == CHIPS_Y * CORES and mesh.shape["shard"] == CHIPS_Z * CHIPS_X
    return jax.shard_map(
        functools.partial(local, fast),
        mesh=mesh,
        in_specs=in_specs,
        out_specs=out_specs,
        check_vma=False,
    )
```

```python
import functools

import jax
import jax.numpy as jnp
from jax import lax
from jax.experimental import pallas as pl
from jax.experimental.pallas import tpu as pltpu
from jax.sharding import PartitionSpec as P

D = 768
HEADS = 12
HEAD_DIM = 64
LAYERS = 2
CLUSTER = 128
TREE_LEN = 1024


norm_eps = 1e-06


def layer_norm(values, norm_gain, norm_shift):
    average = jnp.mean(values, axis=-1, keepdims=True)
    centred = values - average
    variance = jnp.mean(centred * centred, axis=-1, keepdims=True)
    return centred * lax.rsqrt(variance + norm_eps) * norm_gain + norm_shift


def gelu_exact(values):
    return jax.nn.gelu(values, approximate=False)


def dot_first(left_side, right_side):
    return lax.dot_general(
        left_side, right_side, (((0,), (0,)), ((), ())), preferred_element_type=jnp.float32
    )


def dot_last(left_side, right_side):
    return lax.dot_general(
        left_side, right_side, (((1,), (1,)), ((), ())), preferred_element_type=jnp.float32
    )


def lookup_small(index, table):
    match = index[:, None] == jnp.arange(table.shape[0], dtype=jnp.int32)[None, :]
    return jnp.sum(jnp.where(match, table[None, :], 0), axis=1)


PAIRS = HEADS // 2
LANES = 2 * HEAD_DIM
KERNEL_VMEM = 60 * 2**20


def slot_ranks(cluster_ids):
    length = cluster_ids.shape[-1]
    count = length // CLUSTER
    order = jnp.arange(count, dtype=jnp.int32)
    member = cluster_ids[..., None, :] == order[:, None]
    upto = jnp.arange(length, dtype=jnp.int32)
    triangle = (upto[:, None] <= upto[None, :]).astype(jnp.bfloat16)
    ranks = jnp.dot(
        member.astype(jnp.bfloat16), triangle, preferred_element_type=jnp.float32
    ).astype(jnp.int32)
    return jnp.sum(jnp.where(member, ranks - 1 + CLUSTER * order[:, None], 0), axis=-2)


def one_hot_rows(slot_row):
    length = slot_row.shape[-1]
    rows = lax.broadcasted_iota(jnp.int32, (length, length), 0)
    return jnp.where(rows == slot_row, 1.0, 0.0).astype(jnp.bfloat16)


def first_lanes(length):
    return lax.broadcasted_iota(jnp.int32, (length, LANES), 1) < HEAD_DIM


def contract_last(left_side, right_side):
    return lax.dot_general(
        left_side, right_side, (((1,), (1,)), ((), ())), preferred_element_type=jnp.float32
    )


def contract_first(left_side, right_side):
    return lax.dot_general(
        left_side, right_side, (((0,), (0,)), ((), ())), preferred_element_type=jnp.float32
    )


def cluster_blocks(values):
    return [values[at : at + CLUSTER] for at in range(0, values.shape[0], CLUSTER)]


def mask_kernel(slot_ref, ids_ref, bias_ref):
    for head in range(2):
        table = one_hot_rows(slot_ref[0, 0, head : head + 1, :])
        ids = jnp.dot(table, ids_ref[0], preferred_element_type=jnp.float32)
        turned = ids.T
        for at in range(0, TREE_LEN, CLUSTER):
            segs = turned[0:1, at : at + CLUSTER]
            block = ids[at : at + CLUSTER]
            allowed = (
                (segs == block[:, 0:1]) | (segs == block[:, 1:2]) | (segs == block[:, 2:3])
            )
            bias_ref[0, head, at : at + CLUSTER, :] = jnp.where(allowed, 0.0, -1e30).astype(
                jnp.bfloat16
            )


def attend_kernel(slot_ref, query_ref, key_ref, value_ref, bias_ref, ctx_ref, qk_ref, val_ref, p_ref):
    low = first_lanes(TREE_LEN)
    query = query_ref[...] * jnp.bfloat16(HEAD_DIM**-0.5)
    key = key_ref[...]
    value = value_ref[...]
    packed = (
        jnp.where(low, query, pltpu.roll(key, HEAD_DIM, 1)),
        jnp.where(low, pltpu.roll(query, HEAD_DIM, 1), key),
    )
    context = []
    for head in range(2):
        table = one_hot_rows(slot_ref[0, 0, head : head + 1, :])
        joined = jnp.concatenate([packed[head], value], axis=1)
        slots = jnp.dot(table, joined, preferred_element_type=jnp.float32).astype(jnp.bfloat16)
        both, values = slots[:, :LANES], slots[:, LANES:]
        qk_ref[0, head] = both
        val_ref[0, head] = values
        queries = jnp.where(low, both, jnp.bfloat16(0))
        keys = pltpu.roll(both, HEAD_DIM, 1)
        scores = jnp.concatenate(
            [contract_last(q, k) for q, k in zip(cluster_blocks(queries), cluster_blocks(keys))],
            axis=0,
        )
        scores = scores + bias_ref[0, head].astype(jnp.float32)
        numerator = jnp.exp(scores - jnp.max(scores, axis=1, keepdims=True))
        total = jnp.sum(numerator, axis=1, keepdims=True)
        soft = (numerator * (1.0 / total)).astype(jnp.bfloat16)
        p_ref[0, head] = soft
        out = jnp.concatenate(
            [
                jnp.dot(p, v, preferred_element_type=jnp.float32)
                for p, v in zip(cluster_blocks(soft), cluster_blocks(values))
            ],
            axis=0,
        ).astype(jnp.bfloat16)
        context.append(contract_first(table, out))
    ctx_ref[...] = jnp.where(low, context[0], context[1]).astype(jnp.bfloat16)


def attend_back_kernel(slot_ref, grad_ref, qk_ref, val_ref, p_ref, out_ref):
    low = first_lanes(TREE_LEN)
    grads = grad_ref[...]
    placed = []
    for head in range(2):
        table = one_hot_rows(slot_ref[0, 0, head : head + 1, :])
        slots = jnp.dot(table, grads, preferred_element_type=jnp.float32)
        slots = jnp.where(low == (head == 0), slots, 0.0).astype(jnp.bfloat16)
        both, values, soft = qk_ref[0, head], val_ref[0, head], p_ref[0, head]
        grad_soft = jnp.concatenate(
            [contract_last(g, v) for g, v in zip(cluster_blocks(slots), cluster_blocks(values))],
            axis=0,
        )
        grad_value = jnp.concatenate(
            [contract_first(p, g) for p, g in zip(cluster_blocks(soft), cluster_blocks(slots))],
            axis=0,
        ).astype(jnp.bfloat16)
        weights = soft.astype(jnp.float32)
        delta = jnp.sum(weights * grad_soft, axis=1, keepdims=True)
        grad_scores = (weights * (grad_soft - delta)).astype(jnp.bfloat16)
        pairs = list(zip(cluster_blocks(grad_scores), cluster_blocks(both)))
        by_key = jnp.concatenate([contract_first(s, b) for s, b in pairs], axis=0)
        by_query = jnp.concatenate(
            [jnp.dot(s, b, preferred_element_type=jnp.float32) for s, b in pairs], axis=0
        )
        mixed = jnp.where(low, by_key, by_query * HEAD_DIM**-0.5).astype(jnp.bfloat16)
        joined = jnp.concatenate([mixed, grad_value], axis=1)
        placed.append(contract_first(table, joined))
    first, second = placed
    out_ref[0] = jnp.where(
        low, pltpu.roll(first[:, :LANES], HEAD_DIM, 1), second[:, :LANES]
    ).astype(jnp.bfloat16)
    out_ref[1] = jnp.where(
        low, first[:, :LANES], pltpu.roll(second[:, :LANES], HEAD_DIM, 1)
    ).astype(jnp.bfloat16)
    out_ref[2] = jnp.where(low, first[:, LANES:], second[:, LANES:]).astype(jnp.bfloat16)


def slot_spec():
    return pl.BlockSpec((1, 1, 2, TREE_LEN), lambda tree, pair: (tree, pair, 0, 0))


def head_spec():
    return pl.BlockSpec((1, 2, TREE_LEN, LANES), lambda tree, pair: (tree, pair, 0, 0))


def column_spec(offset):
    return pl.BlockSpec((TREE_LEN, LANES), lambda tree, pair: (tree, offset + pair))


def kernel_params():
    return pltpu.CompilerParams(vmem_limit_bytes=KERNEL_VMEM)


def mask_bias(slots, ids):
    trees = slots.shape[0]
    return pl.pallas_call(
        mask_kernel,
        grid=(trees, PAIRS),
        in_specs=[
            slot_spec(),
            pl.BlockSpec((1, TREE_LEN, LANES), lambda tree, pair: (tree, 0, 0)),
        ],
        out_specs=head_spec(),
        out_shape=jax.ShapeDtypeStruct((trees, HEADS, TREE_LEN, LANES), jnp.bfloat16),
        compiler_params=kernel_params(),
        cost_estimate=pl.CostEstimate(
            flops=trees * 12_000_000_000, bytes_accessed=trees * 4_000_000, transcendentals=0
        ),
    )(slots, ids)


def attend(projected, slots, bias):
    trees = slots.shape[0]
    stored = jax.ShapeDtypeStruct((trees, HEADS, TREE_LEN, LANES), jnp.bfloat16)
    return pl.pallas_call(
        attend_kernel,
        grid=(trees, PAIRS),
        in_specs=[
            slot_spec(),
            column_spec(0),
            column_spec(PAIRS),
            column_spec(2 * PAIRS),
            head_spec(),
        ],
        out_specs=[column_spec(0), head_spec(), head_spec(), head_spec()],
        out_shape=[
            jax.ShapeDtypeStruct((trees * TREE_LEN, D), jnp.bfloat16),
            stored,
            stored,
            stored,
        ],
        compiler_params=kernel_params(),
        cost_estimate=pl.CostEstimate(
            flops=trees * 30_000_000_000, bytes_accessed=trees * 20_000_000, transcendentals=0
        ),
    )(slots, projected, projected, projected, bias)


def attend_back(grad_context, slots, kept):
    trees = slots.shape[0]
    return pl.pallas_call(
        attend_back_kernel,
        grid=(trees, PAIRS),
        in_specs=[slot_spec(), column_spec(0), head_spec(), head_spec(), head_spec()],
        out_specs=pl.BlockSpec((3, TREE_LEN, LANES), lambda tree, pair: (0, tree, pair)),
        out_shape=jax.ShapeDtypeStruct((3, trees * TREE_LEN, D), jnp.bfloat16),
        compiler_params=kernel_params(),
        cost_estimate=pl.CostEstimate(
            flops=trees * 40_000_000_000, bytes_accessed=trees * 20_000_000, transcendentals=0
        ),
    )(slots, grad_context, *kept)


def layer_forward(layer_in, get, path_info, tick):
    qv_bias, out_bias, attn_gain, attn_shift, ffin_bias, ffout_bias, ffn_gain, ffn_shift = (
        get(number) for number in VECTORS
    )
    layer_low = layer_in.astype(jnp.bfloat16)
    bias_float = qv_bias.astype(jnp.float32)
    full_bias = jnp.concatenate([bias_float[:D], jnp.zeros((D,), jnp.float32), bias_float[D:]])
    projected = (
        jnp.dot(layer_low, get(0), preferred_element_type=jnp.float32) + full_bias
    ).astype(jnp.bfloat16)
    projected = tick("projected", projected)
    slots, bias = path_info
    context, *kept_heads = attend(projected, slots, bias)
    context = tick("context", context)
    attn_sum = (
        layer_in
        + jnp.dot(context, get(2), preferred_element_type=jnp.float32)
        + out_bias.astype(jnp.float32)
    )
    hidden_one = layer_norm(attn_sum, attn_gain.astype(jnp.float32), attn_shift.astype(jnp.float32))
    hidden_low = hidden_one.astype(jnp.bfloat16)
    hidden_low = tick("hidden", hidden_low)
    pre_act = jnp.dot(
        hidden_low, get(6), preferred_element_type=jnp.float32
    ) + ffin_bias.astype(jnp.float32)
    act_low = gelu_exact(pre_act).astype(jnp.bfloat16)
    act_low = tick("act", act_low)
    ffn_sum = (
        hidden_one
        + jnp.dot(act_low, get(8), preferred_element_type=jnp.float32)
        + ffout_bias.astype(jnp.float32)
    )
    result = layer_norm(ffn_sum, ffn_gain.astype(jnp.float32), ffn_shift.astype(jnp.float32))
    result = tick("result", result)
    saved = (
        layer_low,
        kept_heads,
        context,
        attn_sum,
        hidden_low,
        pre_act,
        act_low,
        ffn_sum,
    )
    return (result, saved)


def layer_backward(grad_out, weights, saved, path_info, reduce, tick):
    (
        qkv_weight,
        qv_bias,
        out_weight,
        out_bias,
        attn_gain,
        attn_shift,
        ffin_weight,
        ffin_bias,
        ffout_weight,
        ffout_bias,
        ffn_gain,
        ffn_shift,
    ) = weights
    (
        layer_low,
        kept_heads,
        context,
        attn_sum,
        hidden_low,
        pre_act,
        act_low,
        ffn_sum,
    ) = saved
    ignored, norm_pull = jax.vjp(
        layer_norm, ffn_sum, ffn_gain.astype(jnp.float32), ffn_shift.astype(jnp.float32)
    )
    grad_ffn_sum, grad_ffn_gain, grad_ffn_shift = norm_pull(grad_out)
    grad_down = grad_ffn_sum.astype(jnp.bfloat16)
    grad_down = tick("down", grad_down)
    grad_ffout_weight = reduce(8, act_low, grad_down[None])
    grad_ffout_bias = jnp.sum(grad_down.astype(jnp.float32), axis=0)
    grad_act = dot_last(grad_down, ffout_weight)
    ignored, gelu_pull = jax.vjp(gelu_exact, pre_act)
    grad_pre = gelu_pull(grad_act)[0].astype(jnp.bfloat16)
    grad_pre = tick("pre", grad_pre)
    grad_ffin_weight = reduce(6, hidden_low, grad_pre[None])
    grad_ffin_bias = jnp.sum(grad_pre.astype(jnp.float32), axis=0)
    grad_hidden = grad_ffn_sum + dot_last(grad_pre, ffin_weight)
    ignored, first_pull = jax.vjp(
        layer_norm, attn_sum, attn_gain.astype(jnp.float32), attn_shift.astype(jnp.float32)
    )
    grad_attn_sum, grad_attn_gain, grad_attn_shift = first_pull(grad_hidden)
    grad_attn_low = grad_attn_sum.astype(jnp.bfloat16)
    grad_attn_low = tick("attn", grad_attn_low)
    grad_out_weight = reduce(2, context, grad_attn_low[None])
    grad_out_bias = jnp.sum(grad_attn_low.astype(jnp.float32), axis=0)
    grad_context = dot_last(grad_attn_low, out_weight).astype(jnp.bfloat16)
    grad_context = tick("context", grad_context)
    grad_proj = attend_back(grad_context, path_info[0], kept_heads)
    grad_proj = tick("proj", grad_proj)
    grad_qkv_weight = reduce(0, layer_low, grad_proj)
    column_sums = jnp.sum(grad_proj.astype(jnp.float32), axis=1)
    grad_qv_bias = jnp.concatenate([column_sums[0], column_sums[2]])
    grad_in = grad_attn_sum
    for part in range(3):
        grad_in = grad_in + dot_last(grad_proj[part], qkv_weight[:, part * D : (part + 1) * D])
    grads = (
        grad_qkv_weight,
        grad_qv_bias,
        grad_out_weight,
        grad_out_bias,
        grad_attn_gain,
        grad_attn_shift,
        grad_ffin_weight,
        grad_ffin_bias,
        grad_ffout_weight,
        grad_ffout_bias,
        grad_ffn_gain,
        grad_ffn_shift,
    )
    return (grad_in, grads)


MATRICES = (0, 2, 6, 8)
VECTORS = (1, 3, 4, 5, 7, 9, 10, 11)
AXES = ("rep", "shard")
CHIPS_Z, CHIPS_X, CHIPS_Y, CORES = 4, 2, 2, 2


FORWARD = {
    "begin": ((), ((0, 0),)),
    "slots": (((0, 0),), ((0, 2), (0, 6))),
    "mask": (((0, 0),), ()),
    "ready": (((0, 0), (0, 2), (0, 6)), ((0, 8),)),
    (0, "projected"): (((0, 2), (0, 6), (0, 8)), ((1, 0),)),
    (0, "context"): (((0, 2), (0, 6), (0, 8), (1, 0)), ((1, 2), (1, 6))),
    (0, "hidden"): (((0, 6),), ()),
    (0, "act"): (((0, 8), (1, 0), (1, 2), (1, 6)), ((1, 8),)),
    (0, "result"): (((1, 0), (1, 2)), ()),
    (1, "projected"): (((1, 2), (1, 6), (1, 8)), ()),
    (1, "context"): (((1, 6), (1, 8)), ()),
    (1, "hidden"): (((1, 6), (1, 8)), ()),
    (1, "act"): (((1, 8),), ()),
}


class Place:
    def __init__(self):
        rep = lax.axis_index("rep")
        shard = lax.axis_index("shard")
        self.y, self.core = rep // CORES, rep % CORES
        self.z, self.x = shard // CHIPS_X, shard % CHIPS_X

    def vector(self):
        return jnp.stack([self.z, self.x, self.y, self.core]).astype(jnp.int32)


def hop(value, dz=0, dx=0, dy=0, dc=0):
    pairs = []
    for y in range(CHIPS_Y):
        for c in range(CORES):
            for z in range(CHIPS_Z):
                for x in range(CHIPS_X):
                    source = ((y * CORES + c) * CHIPS_Z + z) * CHIPS_X + x
                    y2, c2 = (y + dy) % CHIPS_Y, (c + dc) % CORES
                    z2, x2 = (z + dz) % CHIPS_Z, (x + dx) % CHIPS_X
                    pairs.append((source, ((y2 * CORES + c2) * CHIPS_Z + z2) * CHIPS_X + x2))
    return lax.ppermute(value, AXES, pairs)


def pick(array, index, axis):
    return lax.dynamic_index_in_dim(array, index, axis, keepdims=False)


def ordered(first, own, other, axis):
    return jnp.where(
        first, jnp.concatenate([own, other], axis), jnp.concatenate([other, own], axis)
    )


def place_kernel(split_y, half, at_ref, *refs):
    pieces, out_ref = refs[:-1], refs[-1]
    for number, piece in enumerate(pieces):
        core = (at_ref[3] + number % CORES) % CORES
        x = (at_ref[1] + number // CORES % CHIPS_X) % CHIPS_X
        row = (at_ref[2] + number // (CORES * CHIPS_X)) % CHIPS_Y if split_y else 0
        out_ref[x, row, :, pl.ds(pl.multiple_of(core * half, 128), half)] = piece[0]


def place_pieces(pieces, split_y, place):
    _, rows, half = pieces[0].shape
    splits = CHIPS_Y if split_y else 1
    whole = pl.pallas_call(
        functools.partial(place_kernel, split_y, half),
        grid_spec=pltpu.PrefetchScalarGridSpec(
            num_scalar_prefetch=1,
            grid=(CHIPS_Z,),
            in_specs=[pl.BlockSpec((1, rows, half), lambda k, at: (k, 0, 0))] * len(pieces),
            out_specs=pl.BlockSpec(
                (CHIPS_X, splits, rows, 2 * half),
                lambda k, at: (lax.rem(at[0] + CHIPS_Z - k, CHIPS_Z), 0, 0, 0),
            ),
        ),
        out_shape=jax.ShapeDtypeStruct(
            (CHIPS_Z * CHIPS_X, splits, rows, 2 * half), jnp.bfloat16
        ),
        compiler_params=kernel_params(),
        cost_estimate=pl.CostEstimate(
            flops=0,
            bytes_accessed=4 * CHIPS_Z * len(pieces) * rows * half,
            transcendentals=0,
        ),
    )(place.vector(), *pieces)
    return whole.reshape(CHIPS_Z * CHIPS_X * splits * rows, 2 * half)


def gather_chain(block, split_y, place):
    parts = yield [hop(block, dz=k) for k in range(1, CHIPS_Z)]
    stack = jnp.stack([block, *parts])
    (across,) = yield [hop(stack, dx=1)]
    pieces = [stack, across]
    if split_y:
        pieces = pieces + (yield [hop(piece, dy=1) for piece in pieces])
    others = yield [hop(piece, dc=1) for piece in pieces]
    return place_pieces(
        [item for pair in zip(pieces, others) for item in pair], split_y, place
    )


class Flow:
    def __init__(self):
        self.running, self.done = {}, {}

    def start(self, name, chain):
        self.running[name] = (chain, next(chain))

    def advance(self, name, arrived):
        chain, _ = self.running.pop(name)
        try:
            self.running[name] = (chain, chain.send(list(arrived)))
        except StopIteration as end:
            self.done[name] = end.value

    def tick(self, main, *names):
        names = [name for name in names if name in self.running]
        pending = [self.running[name][1] for name in names]
        main, pending = lax.optimization_barrier((main, pending))
        for name, arrived in zip(names, pending):
            self.advance(name, arrived)
        return main

    def finish(self, name):
        while name in self.running:
            self.advance(name, self.running[name][1])
        return self.done[name]


def gather_vectors(vectors, place):
    sizes = [vector.shape[1] for vector in vectors]
    own = jnp.concatenate(vectors, axis=1)
    layers, width = own.shape
    count = CHIPS_Z * CHIPS_X
    rounds = [
        hop(own, dz=dz, dx=dx) if dz or dx else own
        for dz in range(CHIPS_Z)
        for dx in range(CHIPS_X)
    ]
    stack = jnp.stack(rounds).astype(jnp.float32)
    wanted = jnp.arange(count, dtype=jnp.int32)
    behind = (place.z - wanted // CHIPS_X) % CHIPS_Z * CHIPS_X + (
        place.x - wanted % CHIPS_X
    ) % CHIPS_X
    turn = (behind[:, None] == wanted[None, :]).astype(jnp.float32)
    stack = jnp.sum(turn[:, :, None, None] * stack[None], axis=1)
    out, at = [], 0
    for size in sizes:
        out.append(
            stack[:, :, at : at + size].transpose(1, 0, 2).reshape(layers, count * size)
        )
        at += size
    return out


def gather_block(weights, layer, number, place):
    shard = weights[number][layer]
    rows, columns = shard.shape
    split_y = number in (6, 8)
    tall = rows // CHIPS_Y if split_y else rows
    start = (place.y * tall if split_y else 0, place.core * (columns // 2))
    return lax.dynamic_slice(shard, start, (tall, columns // 2)), split_y


def low_sum(*terms):
    total = terms[0].astype(jnp.float32)
    for term in terms[1:]:
        total = total + term.astype(jnp.float32)
    return total


def reduce_chain(left, right, place, y_first):
    parts, _, columns = right.shape
    half = columns // 2
    depth = left.shape[1]

    def product(core):
        cut = lax.dynamic_slice_in_dim(right, core * half, half, axis=2)
        grads = [dot_first(left, cut[part]).astype(jnp.bfloat16) for part in range(parts)]
        return [
            grad.reshape(CHIPS_Z, CHIPS_X, CHIPS_Y, depth // 16, half) for grad in grads
        ]

    away = product(1 - place.core)
    hops = [hop(part, dc=1) for part in away]
    kept = product(place.core)
    arrived = yield hops
    total = jnp.stack([low_sum(mine, other) for mine, other in zip(kept, arrived)], axis=0)

    def swap(values, index, axis, step):
        sent = pick(values, 1 - index, axis).astype(jnp.bfloat16)
        (other,) = yield [hop(sent, **step)]
        return low_sum(pick(values, index, axis), other)

    if y_first:
        total = yield from swap(total, place.y, 3, dict(dy=1))
    total = yield from swap(total, place.x, 2, dict(dx=1))
    landed = yield [
        hop(pick(total, (place.z + k) % CHIPS_Z, 1).astype(jnp.bfloat16), dz=k)
        for k in range(1, CHIPS_Z)
    ]
    total = low_sum(pick(total, place.z, 1), *landed).astype(jnp.bfloat16)
    (other,) = yield [hop(total, dy=1)]
    if y_first:
        rows = ordered(place.y == 0, total[:, None], other[:, None], 1)
    else:
        rows = low_sum(total, other).astype(jnp.bfloat16)
    rows = rows.reshape(parts, depth // 8, half)
    (other,) = yield [hop(rows, dc=1)]
    rows = ordered(place.core == 0, rows, other, 2).astype(jnp.float32)
    return rows.transpose(1, 0, 2).reshape(depth // 8, parts * columns)


def reduce_vectors(vectors, place):
    sizes = [vector.shape[0] for vector in vectors]
    total = jnp.concatenate(vectors)
    for step in (dict(dc=1), dict(dy=1), dict(dx=1), dict(dz=2)):
        (other,) = yield [hop(total, **step)]
        total = total + other
    up, down = yield [hop(total, dz=1), hop(total, dz=3)]
    total = total + jnp.where(place.z % 2 == 0, down, up)
    count = CHIPS_Z * CHIPS_X
    shard = place.z * CHIPS_X + place.x
    out, at = [], 0
    for size in sizes:
        share = size // count
        out.append(lax.dynamic_slice_in_dim(total, at + shard * share, share))
        at += size
    return out


def local(
    fast,
    inputs,
    cotangent,
    segment,
    parent,
    clusters,
    qkv_weight,
    qv_bias,
    out_weight,
    out_bias,
    attn_gain,
    attn_shift,
    ffin_weight,
    ffin_bias,
    ffout_weight,
    ffout_bias,
    ffn_gain,
    ffn_shift,
):
    tree_count = parent.shape[0]
    segments = segment.reshape(tree_count, TREE_LEN)
    parents = jax.vmap(lookup_small)(segments, parent)
    grands = jax.vmap(lookup_small)(parents, parent)
    cluster_ids = clusters.reshape(HEADS, tree_count, TREE_LEN).transpose(1, 0, 2)
    slots = slot_ranks(cluster_ids).reshape(tree_count, PAIRS, 2, TREE_LEN)
    ids = jnp.stack([segments, parents, grands], axis=-1).astype(jnp.bfloat16)
    ids = jnp.pad(ids, ((0, 0), (0, 0), (0, LANES - 3)))
    weights = (
        qkv_weight,
        qv_bias,
        out_weight,
        out_bias,
        attn_gain,
        attn_shift,
        ffin_weight,
        ffin_bias,
        ffout_weight,
        ffout_bias,
        ffn_gain,
        ffn_shift,
    )
    flow = Flow()
    if fast:
        place = Place()
        vectors = gather_vectors([weights[number] for number in VECTORS], place)

        def begin(layer, number):
            flow.start((layer, number), gather_chain(*gather_block(weights, layer, number, place), place))

        def get(layer, number):
            if number in VECTORS:
                return vectors[VECTORS.index(number)][layer]
            return flow.finish((layer, number))

        def step(point, main):
            advanced, started = FORWARD.get(point, ((), ()))
            main = flow.tick(main, *advanced)
            for name in started:
                begin(*name)
            return main

        def reduce(layer, number, left, right):
            flow.start(
                ("grad", layer, number), reduce_chain(left, right, place, number in (0, 6))
            )

        def back_step(point, main):
            return flow.tick(main, *[name for name in flow.running if name[0] == "grad"])

    else:

        def get(layer, number):
            return lax.all_gather(weights[number][layer], "shard", axis=0, tiled=True)

        def step(point, main):
            return main

        def reduce(layer, number, left, right):
            grads = jnp.concatenate([dot_first(left, part) for part in right], axis=1)
            grads = lax.psum_scatter(grads, "shard", scatter_dimension=0, tiled=True)
            grads = lax.psum(grads.astype(jnp.bfloat16), "rep").astype(jnp.float32)
            flow.done[("grad", layer, number)] = grads

        back_step = step

    step("begin", ())
    slots = step("slots", slots)
    path_info = (slots, step("mask", mask_bias(slots, ids)))
    hidden = step("ready", inputs.astype(jnp.float32))
    kept_saved = []
    for layer_index in range(LAYERS):
        hidden, saved = layer_forward(
            hidden,
            functools.partial(get, layer_index),
            path_info,
            lambda point, main: step((layer_index, point), main),
        )
        kept_saved.append(saved)
    result = hidden.astype(jnp.bfloat16)
    grad_rows = cotangent.astype(jnp.float32)
    per_layer = [None] * LAYERS
    vector_items = [(1, number) for number in VECTORS] + [(0, number) for number in VECTORS[1:]]
    for layer_index in reversed(range(LAYERS)):
        grad_rows, grads = layer_backward(
            grad_rows,
            [get(layer_index, number) for number in range(12)],
            kept_saved[layer_index],
            path_info,
            functools.partial(reduce, layer_index),
            lambda point, main: back_step((layer_index, point), main),
        )
        per_layer[layer_index] = list(grads)
        grad_rows = back_step((layer_index, "end"), grad_rows)
    for tag, items in (("early", vector_items), ("late", [(0, 1)])):
        vectors_in = [per_layer[layer][number] for layer, number in items]
        if fast:
            flow.start(tag, reduce_vectors(vectors_in, place))
            vectors_out = flow.finish(tag)
        else:
            vectors_out = [
                lax.psum(lax.psum_scatter(vector, "shard", tiled=True), "rep")
                for vector in vectors_in
            ]
        for (layer, number), vector in zip(items, vectors_out):
            per_layer[layer][number] = vector
    for layer_index in range(LAYERS):
        for number in MATRICES:
            per_layer[layer_index][number] = flow.finish(("grad", layer_index, number))
    stacked = tuple(
        (
            jnp.stack([per_layer[layer_index][member] for layer_index in range(LAYERS)])
            for member in range(12)
        )
    )
    return (
        result,
        grad_rows,
        stacked[0],
        stacked[1],
        stacked[2],
        stacked[3],
        stacked[4],
        stacked[5],
        stacked[6],
        stacked[7],
        stacked[8],
        stacked[9],
        stacked[10],
        stacked[11],
    )


def solution(mesh):
    in_specs = (
        P(("rep", "shard"), None),
        P(("rep", "shard"), None),
        P(("rep", "shard")),
        P(("rep", "shard"), None),
        P(None, ("rep", "shard")),
        P(None, "shard", None),
        P(None, "shard"),
        P(None, "shard", None),
        P(None, "shard"),
        P(None, "shard"),
        P(None, "shard"),
        P(None, "shard", None),
        P(None, "shard"),
        P(None, "shard", None),
        P(None, "shard"),
        P(None, "shard"),
        P(None, "shard"),
    )
    out_specs = (
        P(("rep", "shard"), None),
        P(("rep", "shard"), None),
        P(None, "shard", None),
        P(None, "shard"),
        P(None, "shard", None),
        P(None, "shard"),
        P(None, "shard"),
        P(None, "shard"),
        P(None, "shard", None),
        P(None, "shard"),
        P(None, "shard", None),
        P(None, "shard"),
        P(None, "shard"),
        P(None, "shard"),
    )
    fast = mesh.shape["rep"] == CHIPS_Y * CORES and mesh.shape["shard"] == CHIPS_Z * CHIPS_X
    return jax.shard_map(
        functools.partial(local, fast),
        mesh=mesh,
        in_specs=in_specs,
        out_specs=out_specs,
        check_vma=False,
    )
```

```python
import functools

import jax
import jax.numpy as jnp
from jax import lax
from jax.experimental import pallas as pl
from jax.experimental.pallas import tpu as pltpu
from jax.sharding import PartitionSpec as P

D = 768
HEADS = 12
HEAD_DIM = 64
LAYERS = 2
CLUSTER = 128
TREE_LEN = 1024
SEGMENTS = 13
PAIRS = HEADS // 2
LANES = 2 * HEAD_DIM
KERNEL_VMEM = 60 * 2**20
ROW_TILE = 256
FEED_TILE = 768
DEPTH_TILE = 384
INV_ROOT = (2.0 * 3.141592653589793) ** -0.5
MATRICES = (0, 2, 6, 8)
VECTORS = (1, 3, 4, 5, 7, 9, 10, 11)
AXES = ("rep", "shard")
CHIPS_Z, CHIPS_X, CHIPS_Y, CORES = 4, 2, 2, 2
norm_eps = 1e-06


def one_hot_rows(slot_row):
    length = slot_row.shape[-1]
    rows = lax.broadcasted_iota(jnp.int32, (length, length), 0)
    return jnp.where(rows == slot_row, 1.0, 0.0).astype(jnp.bfloat16)


def first_lanes(length):
    return lax.broadcasted_iota(jnp.int32, (length, LANES), 1) < HEAD_DIM


def contract_last(left_side, right_side):
    return lax.dot_general(
        left_side, right_side, (((1,), (1,)), ((), ())), preferred_element_type=jnp.float32
    )


def contract_first(left_side, right_side):
    return lax.dot_general(
        left_side, right_side, (((0,), (0,)), ((), ())), preferred_element_type=jnp.float32
    )


def cluster_blocks(values):
    return [values[at : at + CLUSTER] for at in range(0, values.shape[0], CLUSTER)]


def attend_kernel(slot_ref, query_ref, key_ref, value_ref, bias_ref, ctx_ref, qk_ref, val_ref, p_ref):
    low = first_lanes(TREE_LEN)
    query = query_ref[...] * jnp.bfloat16(HEAD_DIM**-0.5)
    key = key_ref[...]
    value = value_ref[...]
    packed = (
        jnp.where(low, query, pltpu.roll(key, HEAD_DIM, 1)),
        jnp.where(low, pltpu.roll(query, HEAD_DIM, 1), key),
    )
    context = []
    for head in range(2):
        table = one_hot_rows(slot_ref[0, 0, head : head + 1, :])
        joined = jnp.concatenate([packed[head], value], axis=1)
        slots = jnp.dot(table, joined, preferred_element_type=jnp.float32).astype(jnp.bfloat16)
        both, values = slots[:, :LANES], slots[:, LANES:]
        qk_ref[0, head] = both
        val_ref[0, head] = values
        queries = jnp.where(low, both, jnp.bfloat16(0))
        keys = pltpu.roll(both, HEAD_DIM, 1)
        scores = jnp.concatenate(
            [contract_last(q, k) for q, k in zip(cluster_blocks(queries), cluster_blocks(keys))],
            axis=0,
        )
        scores = scores + bias_ref[0, head].astype(jnp.float32)
        numerator = jnp.exp(scores - jnp.max(scores, axis=1, keepdims=True))
        total = jnp.sum(numerator, axis=1, keepdims=True)
        soft = (numerator * (1.0 / total)).astype(jnp.bfloat16)
        p_ref[0, head] = soft
        out = jnp.concatenate(
            [
                jnp.dot(p, v, preferred_element_type=jnp.float32)
                for p, v in zip(cluster_blocks(soft), cluster_blocks(values))
            ],
            axis=0,
        ).astype(jnp.bfloat16)
        context.append(contract_first(table, out))
    ctx_ref[...] = jnp.where(low, context[0], context[1]).astype(jnp.bfloat16)


def attend_back_kernel(slot_ref, grad_ref, qk_ref, val_ref, p_ref, out_ref, sums_ref):
    low = first_lanes(TREE_LEN)
    grads = grad_ref[...]
    placed = []
    for head in range(2):
        table = one_hot_rows(slot_ref[0, 0, head : head + 1, :])
        slots = jnp.dot(table, grads, preferred_element_type=jnp.float32)
        slots = jnp.where(low == (head == 0), slots, 0.0).astype(jnp.bfloat16)
        both, values, soft = qk_ref[0, head], val_ref[0, head], p_ref[0, head]
        grad_soft = jnp.concatenate(
            [contract_last(g, v) for g, v in zip(cluster_blocks(slots), cluster_blocks(values))],
            axis=0,
        )
        grad_value = jnp.concatenate(
            [contract_first(p, g) for p, g in zip(cluster_blocks(soft), cluster_blocks(slots))],
            axis=0,
        ).astype(jnp.bfloat16)
        weights = soft.astype(jnp.float32)
        delta = jnp.sum(weights * grad_soft, axis=1, keepdims=True)
        grad_scores = (weights * (grad_soft - delta)).astype(jnp.bfloat16)
        pairs = list(zip(cluster_blocks(grad_scores), cluster_blocks(both)))
        by_key = jnp.concatenate([contract_first(s, b) for s, b in pairs], axis=0)
        by_query = jnp.concatenate(
            [jnp.dot(s, b, preferred_element_type=jnp.float32) for s, b in pairs], axis=0
        )
        mixed = jnp.where(low, by_key, by_query * HEAD_DIM**-0.5).astype(jnp.bfloat16)
        joined = jnp.concatenate([mixed, grad_value], axis=1)
        placed.append(contract_first(table, joined))
    first, second = placed
    queries = jnp.where(low, pltpu.roll(first[:, :LANES], HEAD_DIM, 1), second[:, :LANES])
    keys = jnp.where(low, first[:, :LANES], pltpu.roll(second[:, :LANES], HEAD_DIM, 1))
    values = jnp.where(low, first[:, LANES:], second[:, LANES:])
    sums = []
    for part, grad in enumerate((queries, keys, values)):
        rounded = grad.astype(jnp.bfloat16)
        out_ref[part] = rounded
        sums.append(rows_sum(rounded.astype(jnp.float32)))
    sums_ref[0, 0] = jnp.concatenate(sums + [jnp.zeros((5, LANES), jnp.float32)], axis=0)


def slot_spec():
    return pl.BlockSpec((1, 1, 2, TREE_LEN), lambda tree, pair: (tree, pair, 0, 0))


def head_spec():
    return pl.BlockSpec((1, 2, TREE_LEN, LANES), lambda tree, pair: (tree, pair, 0, 0))


def column_spec(offset):
    return pl.BlockSpec((TREE_LEN, LANES), lambda tree, pair: (tree, offset + pair))


def kernel_params():
    return pltpu.CompilerParams(vmem_limit_bytes=KERNEL_VMEM)


def attend(projected, slots, bias):
    trees = slots.shape[0]
    stored = jax.ShapeDtypeStruct((trees, HEADS, TREE_LEN, LANES), jnp.bfloat16)
    return pl.pallas_call(
        attend_kernel,
        grid=(trees, PAIRS),
        in_specs=[
            slot_spec(),
            column_spec(0),
            column_spec(PAIRS),
            column_spec(2 * PAIRS),
            head_spec(),
        ],
        out_specs=[column_spec(0), head_spec(), head_spec(), head_spec()],
        out_shape=[
            jax.ShapeDtypeStruct((trees * TREE_LEN, D), jnp.bfloat16),
            stored,
            stored,
            stored,
        ],
        compiler_params=kernel_params(),
        cost_estimate=pl.CostEstimate(
            flops=trees * 30_000_000_000, bytes_accessed=trees * 20_000_000, transcendentals=0
        ),
    )(slots, projected, projected, projected, bias)


def attend_back(grad_context, slots, kept):
    trees = slots.shape[0]
    return pl.pallas_call(
        attend_back_kernel,
        grid=(trees, PAIRS),
        in_specs=[slot_spec(), column_spec(0), head_spec(), head_spec(), head_spec()],
        out_specs=[
            pl.BlockSpec((3, TREE_LEN, LANES), lambda tree, pair: (0, tree, pair)),
            pl.BlockSpec((1, 1, 8, LANES), lambda tree, pair: (tree, pair, 0, 0)),
        ],
        out_shape=[
            jax.ShapeDtypeStruct((3, trees * TREE_LEN, D), jnp.bfloat16),
            jax.ShapeDtypeStruct((trees, PAIRS, 8, LANES), jnp.float32),
        ],
        compiler_params=kernel_params(),
        cost_estimate=pl.CostEstimate(
            flops=trees * 40_000_000_000, bytes_accessed=trees * 20_000_000, transcendentals=0
        ),
    )(slots, grad_context, *kept)


def erf_parts(values):
    size = jnp.abs(values)
    turn = 1.0 / (1.0 + (0.3275911 * 0.5**0.5) * size)
    bell = jnp.exp(-0.5 * values * values)
    series = 1.061405429 * 0.5
    for factor in (-1.453152027, 1.421413741, -0.284496736, 0.254829592):
        series = series * turn + factor * 0.5
    tail = series * turn * bell
    return jnp.where(values < 0.0, tail, 1.0 - tail), bell


def norm_parts(values):
    centred = values - jnp.mean(values, axis=-1, keepdims=True)
    scale = lax.rsqrt(jnp.mean(centred * centred, axis=-1, keepdims=True) + norm_eps)
    return centred * scale, scale


def norm_back(grad, normal, scale, gain):
    inner = grad * gain
    mean = jnp.mean(inner, axis=-1, keepdims=True)
    along = jnp.mean(inner * normal, axis=-1, keepdims=True)
    return scale * (inner - mean - normal * along)


def spread(column):
    return jnp.broadcast_to(column, (column.shape[0], 128))


def rows_sum(values):
    return jnp.sum(values, axis=0, keepdims=True)


def project_kernel(rows_ref, weight_ref, bias_ref, out_ref):
    product = jnp.dot(rows_ref[...], weight_ref[...], preferred_element_type=jnp.float32)
    out_ref[...] = (product + bias_ref[...]).astype(jnp.bfloat16)


def feed_kernel(
    context_ref,
    rows_ref,
    out_weight_ref,
    ffin_weight_ref,
    ffout_weight_ref,
    out_bias_ref,
    attn_gain_ref,
    attn_shift_ref,
    ffin_bias_ref,
    ffout_bias_ref,
    ffn_gain_ref,
    ffn_shift_ref,
    hidden_ref,
    act_ref,
    slope_ref,
    attn_normal_ref,
    attn_scale_ref,
    ffn_normal_ref,
    ffn_scale_ref,
    result_ref,
    result_low_ref,
):
    product = jnp.dot(context_ref[...], out_weight_ref[...], preferred_element_type=jnp.float32)
    attn_sum = rows_ref[...].astype(jnp.float32) + product + out_bias_ref[...]
    normal, scale = norm_parts(attn_sum)
    attn_normal_ref[...] = normal
    attn_scale_ref[...] = spread(scale)
    hidden = normal * attn_gain_ref[...] + attn_shift_ref[...]
    hidden_low = hidden.astype(jnp.bfloat16)
    hidden_ref[...] = hidden_low
    total = hidden + ffout_bias_ref[...]
    width = ffin_weight_ref.shape[1]
    for at in range(0, width, FEED_TILE):
        part = slice(at, at + FEED_TILE)
        pre = (
            jnp.dot(hidden_low, ffin_weight_ref[:, part], preferred_element_type=jnp.float32)
            + ffin_bias_ref[:, part]
        )
        below, bell = erf_parts(pre)
        act = (pre * below).astype(jnp.bfloat16)
        act_ref[:, part] = act
        slope_ref[:, part] = (below + pre * bell * INV_ROOT).astype(jnp.bfloat16)
        total = total + jnp.dot(
            act, ffout_weight_ref[part, :], preferred_element_type=jnp.float32
        )
    normal, scale = norm_parts(total)
    ffn_normal_ref[...] = normal
    ffn_scale_ref[...] = spread(scale)
    result = normal * ffn_gain_ref[...] + ffn_shift_ref[...]
    result_ref[...] = result
    result_low_ref[...] = result.astype(jnp.bfloat16)


def feed_back_kernel(with_proj, *refs):
    if with_proj:
        above_ref, proj_ref, qkv_weight_ref, *refs = refs
        grad = above_ref[...]
        for part in range(3):
            grad = grad + contract_last(
                proj_ref[part], qkv_weight_ref[:, part * D : (part + 1) * D]
            )
    else:
        above_ref, *refs = refs
        grad = above_ref[...].astype(jnp.float32)
    (
        ffn_normal_ref,
        ffn_scale_ref,
        slope_ref,
        attn_normal_ref,
        attn_scale_ref,
        out_weight_ref,
        ffin_weight_ref,
        ffout_weight_ref,
        attn_gain_ref,
        ffn_gain_ref,
        down_ref,
        pre_ref,
        attn_ref,
        attn_low_ref,
        context_ref,
        sums_ref,
        ffin_sum_ref,
    ) = refs

    @pl.when(pl.program_id(0) == 0)
    def _():
        sums_ref[...] = jnp.zeros_like(sums_ref)
        ffin_sum_ref[...] = jnp.zeros_like(ffin_sum_ref)

    normal = ffn_normal_ref[...]
    sums_ref[0:1] += rows_sum(grad * normal)
    sums_ref[1:2] += rows_sum(grad)
    grad_sum = norm_back(grad, normal, ffn_scale_ref[:, 0:1], ffn_gain_ref[...])
    down = grad_sum.astype(jnp.bfloat16)
    down_ref[...] = down
    sums_ref[2:3] += rows_sum(down.astype(jnp.float32))
    total = grad_sum
    width = ffin_weight_ref.shape[1]
    for at in range(0, width, FEED_TILE):
        part = slice(at, at + FEED_TILE)
        grad_act = contract_last(down, ffout_weight_ref[part, :])
        pre = (grad_act * slope_ref[:, part].astype(jnp.float32)).astype(jnp.bfloat16)
        pre_ref[:, part] = pre
        ffin_sum_ref[:, part] += rows_sum(pre.astype(jnp.float32))
        total = total + contract_last(pre, ffin_weight_ref[:, part])
    normal = attn_normal_ref[...]
    sums_ref[3:4] += rows_sum(total * normal)
    sums_ref[4:5] += rows_sum(total)
    attn = norm_back(total, normal, attn_scale_ref[:, 0:1], attn_gain_ref[...])
    attn_ref[...] = attn
    low = attn.astype(jnp.bfloat16)
    attn_low_ref[...] = low
    sums_ref[5:6] += rows_sum(low.astype(jnp.float32))
    context_ref[...] = contract_last(low, out_weight_ref[...]).astype(jnp.bfloat16)


def input_grad_kernel(above_ref, proj_ref, weight_ref, out_ref):
    grad = above_ref[...]
    for part in range(3):
        grad = grad + contract_last(proj_ref[part], weight_ref[:, part * D : (part + 1) * D])
    out_ref[...] = grad


def prep_kernel(parent_ref, segment_ref, cluster_ref, slot_ref, bias_ref):
    tree = pl.program_id(0)
    segs = segment_ref[0]
    length = segs.shape[1]

    def parent_of(values):
        found = jnp.zeros_like(values)
        for number in range(SEGMENTS):
            found = jnp.where(values == number, parent_ref[tree, number], found)
        return found

    parents = parent_of(segs)
    grands = parent_of(parents)
    ids = jnp.concatenate([segs, parents, grands, jnp.zeros((5, length), jnp.int32)], axis=0)
    ids = jnp.concatenate([ids, jnp.zeros((8, length), jnp.int32)], axis=0)
    ids = ids.astype(jnp.float32).astype(jnp.bfloat16)
    count = length // CLUSTER
    order = lax.broadcasted_iota(jnp.int32, (count, length), 0)
    lanes = lax.broadcasted_iota(jnp.int32, (count, length), 1)
    for head in range(2):
        member = order == cluster_ref[0, 0, head : head + 1, :]
        ranks = member.astype(jnp.int32)
        step = 1
        while step < length:
            ranks = ranks + jnp.where(lanes >= step, pltpu.roll(ranks, step, 1), 0)
            step *= 2
        slot = jnp.sum(
            jnp.where(member, ranks - 1 + CLUSTER * order, 0), axis=0, keepdims=True
        )
        slot_ref[0, 0, head : head + 1, :] = slot
        table = one_hot_rows(slot)
        rows = contract_last(ids, table)
        columns = jnp.concatenate([rows] * (128 // rows.shape[0]), axis=0).T
        for at in range(0, length, CLUSTER):
            here = rows[0:1, at : at + CLUSTER]
            block = columns[at : at + CLUSTER]
            allowed = (
                (here == block[:, 0:1]) | (here == block[:, 1:2]) | (here == block[:, 2:3])
            )
            bias_ref[0, head, at : at + CLUSTER, :] = jnp.where(allowed, 0.0, -1e30).astype(
                jnp.bfloat16
            )


def row_spec(width, rows=ROW_TILE):
    return pl.BlockSpec((rows, width), lambda i: (i, 0))


def whole_spec(shape):
    return pl.BlockSpec(
        shape, lambda i: (0,) * len(shape), pipeline_mode=pl.Buffered(1)
    )


def part_spec(rows=ROW_TILE):
    return pl.BlockSpec((3, rows, D), lambda i: (0, i, 0))


def cost(flops, *arrays):
    moved = sum(array.size * array.dtype.itemsize for array in arrays)
    return pl.CostEstimate(flops=int(flops), bytes_accessed=moved, transcendentals=0)


def shape_of(rows, width, kind=jnp.bfloat16):
    return jax.ShapeDtypeStruct((rows, width), kind)


def project(rows, weight, bias):
    count, width = rows.shape[0], weight.shape[1]
    return pl.pallas_call(
        project_kernel,
        grid=(count // ROW_TILE,),
        in_specs=[row_spec(D), whole_spec(weight.shape), whole_spec((1, width))],
        out_specs=row_spec(width),
        out_shape=shape_of(count, width),
        compiler_params=kernel_params(),
        cost_estimate=cost(2.4 * count * D * width, rows, weight),
    )(rows, weight, bias[None])


def feed(context, rows, weights, vectors):
    count = context.shape[0]
    width = weights[1].shape[1]
    f32 = jnp.float32
    vectors = [vector[None] for vector in vectors]
    return pl.pallas_call(
        feed_kernel,
        grid=(count // ROW_TILE,),
        in_specs=[row_spec(D), row_spec(D)]
        + [whole_spec(weight.shape) for weight in weights]
        + [whole_spec(vector.shape) for vector in vectors],
        out_specs=[
            row_spec(D),
            row_spec(width),
            row_spec(width),
            row_spec(D),
            row_spec(128),
            row_spec(D),
            row_spec(128),
            row_spec(D),
            row_spec(D),
        ],
        out_shape=[
            shape_of(count, D),
            shape_of(count, width),
            shape_of(count, width),
            shape_of(count, D, f32),
            shape_of(count, 128, f32),
            shape_of(count, D, f32),
            shape_of(count, 128, f32),
            shape_of(count, D, f32),
            shape_of(count, D),
        ],
        compiler_params=kernel_params(),
        cost_estimate=cost(5 * count * D * (2 * width + D), context, *weights),
    )(context, rows, *weights, *vectors)


def feed_back(above, proj, qkv_weight, saved, weights, gains):
    count = above.shape[0]
    width = weights[1].shape[1]
    f32 = jnp.float32
    gains = [gain[None] for gain in gains]
    lead, lead_specs = [above], [row_spec(D)]
    if proj is not None:
        lead += [proj, qkv_weight]
        lead_specs += [part_spec(), whole_spec(qkv_weight.shape)]
    return pl.pallas_call(
        functools.partial(feed_back_kernel, proj is not None),
        grid=(count // ROW_TILE,),
        in_specs=lead_specs
        + [row_spec(D), row_spec(128), row_spec(width), row_spec(D), row_spec(128)]
        + [whole_spec(weight.shape) for weight in weights]
        + [whole_spec(gain.shape) for gain in gains],
        out_specs=[
            row_spec(D),
            row_spec(width),
            row_spec(D),
            row_spec(D),
            row_spec(D),
            pl.BlockSpec((8, D), lambda i: (0, 0)),
            pl.BlockSpec((1, width), lambda i: (0, 0)),
        ],
        out_shape=[
            shape_of(count, D),
            shape_of(count, width),
            shape_of(count, D, f32),
            shape_of(count, D),
            shape_of(count, D),
            shape_of(8, D, f32),
            shape_of(1, width, f32),
        ],
        compiler_params=kernel_params(),
        cost_estimate=cost(5 * count * D * (2 * width + D), above, *weights),
    )(*lead, *saved, *weights, *gains)


def input_grad(above, proj, qkv_weight):
    count = above.shape[0]
    return pl.pallas_call(
        input_grad_kernel,
        grid=(count // ROW_TILE,),
        in_specs=[row_spec(D), part_spec(), whole_spec(qkv_weight.shape)],
        out_specs=row_spec(D),
        out_shape=shape_of(count, D, jnp.float32),
        compiler_params=kernel_params(),
        cost_estimate=cost(2.4 * count * D * 3 * D, above, proj, qkv_weight),
    )(above, proj, qkv_weight)


def prepare(segment, parent, clusters):
    trees = parent.shape[0]
    segment = segment.reshape(trees, 1, TREE_LEN)
    clusters = clusters.reshape(PAIRS, 2, trees, TREE_LEN).transpose(2, 0, 1, 3)
    return pl.pallas_call(
        prep_kernel,
        grid=(trees, PAIRS),
        in_specs=[
            pl.BlockSpec(memory_space=pltpu.SMEM),
            pl.BlockSpec((1, 1, TREE_LEN), lambda tree, pair: (tree, 0, 0)),
            slot_spec(),
        ],
        out_specs=[slot_spec(), head_spec()],
        out_shape=[
            jax.ShapeDtypeStruct((trees, PAIRS, 2, TREE_LEN), jnp.int32),
            jax.ShapeDtypeStruct((trees, HEADS, TREE_LEN, LANES), jnp.bfloat16),
        ],
        compiler_params=kernel_params(),
        cost_estimate=pl.CostEstimate(
            flops=trees * 20_000_000_000, bytes_accessed=trees * 4_000_000, transcendentals=0
        ),
    )(parent, segment, clusters)


def weight_grad_kernel(at_ref, left_ref, right_ref, out_ref):
    for part in range(right_ref.shape[0]):
        out_ref[part] = contract_first(left_ref[...], right_ref[part]).astype(jnp.bfloat16)


def weight_grad(left, right, at, other):
    count, depth = left.shape
    parts, _, width = right.shape
    half = width // CORES
    flip = 1 if other else 0
    return pl.pallas_call(
        weight_grad_kernel,
        grid_spec=pltpu.PrefetchScalarGridSpec(
            num_scalar_prefetch=1,
            grid=(depth // DEPTH_TILE,),
            in_specs=[
                pl.BlockSpec((count, DEPTH_TILE), lambda i, at: (0, i)),
                pl.BlockSpec(
                    (parts, count, half), lambda i, at: (0, 0, lax.rem(at[3] + flip, CORES))
                ),
            ],
            out_specs=pl.BlockSpec((parts, DEPTH_TILE, half), lambda i, at: (0, i, 0)),
        ),
        out_shape=jax.ShapeDtypeStruct((parts, depth, half), jnp.bfloat16),
        compiler_params=kernel_params(),
        cost_estimate=cost(3 * count * depth * parts * half, left, right),
    )(at, left, right)


def combine_kernel(groups, at_ref, *refs):
    total = sum(groups)
    ins, outs = refs[:total], refs[total:]
    first = 0
    for count, out_ref in zip(groups, outs):
        value = None
        for ref in ins[first : first + count]:
            term = ref[...].astype(jnp.float32).reshape(out_ref.shape)
            value = term if value is None else value + term
        out_ref[...] = value.astype(out_ref.dtype)
        first += count


def combine(at, steps, groups, blocks):
    terms = [term for group in groups for term in group]
    return pl.pallas_call(
        functools.partial(combine_kernel, [len(group) for group in groups]),
        grid_spec=pltpu.PrefetchScalarGridSpec(
            num_scalar_prefetch=1,
            grid=(steps,),
            in_specs=[pl.BlockSpec(block, index) for _, block, index in terms],
            out_specs=[pl.BlockSpec(block, index) for _, block, index in blocks],
        ),
        out_shape=[jax.ShapeDtypeStruct(shape, jnp.bfloat16) for shape, _, _ in blocks],
        compiler_params=kernel_params(),
        cost_estimate=pl.CostEstimate(
            flops=0, bytes_accessed=2_000_000, transcendentals=0
        ),
    )(at, *[array for array, _, _ in terms])


FORWARD = {
    "begin": ((), ((0, 0),)),
    "prepared": (((0, 0),), ((0, 2), (0, 6), (0, 8))),
    "ready": (((0, 0),), ()),
    (0, "projected"): (((0, 6), (0, 2), (0, 8)), ()),
    (0, "context"): (((0, 6), (0, 2), (0, 8)), ((1, 0), (1, 6))),
    (0, "feed"): (((0, 6), (1, 0), (1, 6)), ((1, 2), (1, 8))),
    (0, "result"): (((1, 0), (1, 6), (1, 2), (1, 8)), ()),
    (1, "projected"): (((1, 2), (1, 8)), ()),
    (1, "context"): (((1, 6), (1, 8)), ()),
}


class Place:
    def __init__(self):
        rep = lax.axis_index("rep")
        shard = lax.axis_index("shard")
        self.y, self.core = rep // CORES, rep % CORES
        self.z, self.x = shard // CHIPS_X, shard % CHIPS_X
        self.at = jnp.stack([self.z, self.x, self.y, self.core]).astype(jnp.int32)


def hop(value, dz=0, dx=0, dy=0, dc=0):
    pairs = []
    for y in range(CHIPS_Y):
        for c in range(CORES):
            for z in range(CHIPS_Z):
                for x in range(CHIPS_X):
                    source = ((y * CORES + c) * CHIPS_Z + z) * CHIPS_X + x
                    y2, c2 = (y + dy) % CHIPS_Y, (c + dc) % CORES
                    z2, x2 = (z + dz) % CHIPS_Z, (x + dx) % CHIPS_X
                    pairs.append((source, ((y2 * CORES + c2) * CHIPS_Z + z2) * CHIPS_X + x2))
    return lax.ppermute(value, AXES, pairs)


def place_kernel(split_y, half, at_ref, *refs):
    pieces, out_ref = refs[:-1], refs[-1]
    for number, piece in enumerate(pieces):
        core = (at_ref[3] + number % CORES) % CORES
        x = (at_ref[1] + number // CORES % CHIPS_X) % CHIPS_X
        row = (at_ref[2] + number // (CORES * CHIPS_X)) % CHIPS_Y if split_y else 0
        out_ref[x, row, :, pl.ds(pl.multiple_of(core * half, 128), half)] = piece[0]


def place_pieces(pieces, split_y, place):
    _, rows, half = pieces[0].shape
    splits = CHIPS_Y if split_y else 1
    whole = pl.pallas_call(
        functools.partial(place_kernel, split_y, half),
        grid_spec=pltpu.PrefetchScalarGridSpec(
            num_scalar_prefetch=1,
            grid=(CHIPS_Z,),
            in_specs=[pl.BlockSpec((1, rows, half), lambda k, at: (k, 0, 0))] * len(pieces),
            out_specs=pl.BlockSpec(
                (CHIPS_X, splits, rows, 2 * half),
                lambda k, at: (lax.rem(at[0] + CHIPS_Z - k, CHIPS_Z), 0, 0, 0),
            ),
        ),
        out_shape=jax.ShapeDtypeStruct(
            (CHIPS_Z * CHIPS_X, splits, rows, 2 * half), jnp.bfloat16
        ),
        compiler_params=kernel_params(),
        cost_estimate=pl.CostEstimate(
            flops=0,
            bytes_accessed=4 * CHIPS_Z * len(pieces) * rows * half,
            transcendentals=0,
        ),
    )(place.at, *pieces)
    return whole.reshape(CHIPS_Z * CHIPS_X * splits * rows, 2 * half)


def gather_chain(block, split_y, place):
    parts = yield [hop(block, dz=k) for k in range(1, CHIPS_Z)]
    stack = jnp.stack([block, *parts])
    (across,) = yield [hop(stack, dx=1)]
    pieces = [stack, across]
    if split_y:
        pieces = pieces + (yield [hop(piece, dy=1) for piece in pieces])
    others = yield [hop(piece, dc=1) for piece in pieces]
    return place_pieces(
        [item for pair in zip(pieces, others) for item in pair], split_y, place
    )


class Flow:
    def __init__(self):
        self.running, self.done = {}, {}

    def start(self, name, chain):
        self.running[name] = (chain, next(chain))

    def advance(self, name, arrived):
        chain, _ = self.running.pop(name)
        try:
            self.running[name] = (chain, chain.send(list(arrived)))
        except StopIteration as end:
            self.done[name] = end.value

    def tick(self, main, *names):
        names = [name for name in names if name in self.running]
        pending = [self.running[name][1] for name in names]
        main, pending = lax.optimization_barrier((main, pending))
        for name, arrived in zip(names, pending):
            self.advance(name, arrived)
        return main

    def finish(self, name):
        while name in self.running:
            self.advance(name, self.running[name][1])
        return self.done[name]


def gather_vectors(vectors, place):
    sizes = [vector.shape[1] for vector in vectors]
    own = jnp.concatenate(vectors, axis=1)
    layers, width = own.shape
    count = CHIPS_Z * CHIPS_X
    rounds = [
        hop(own, dz=dz, dx=dx) if dz or dx else own
        for dz in range(CHIPS_Z)
        for dx in range(CHIPS_X)
    ]
    stack = jnp.stack(rounds).astype(jnp.float32)
    wanted = jnp.arange(count, dtype=jnp.int32)
    behind = (place.z - wanted // CHIPS_X) % CHIPS_Z * CHIPS_X + (
        place.x - wanted % CHIPS_X
    ) % CHIPS_X
    turn = (behind[:, None] == wanted[None, :]).astype(jnp.float32)
    stack = jnp.sum(turn[:, :, None, None] * stack[None], axis=1)
    out, at = [], 0
    for size in sizes:
        out.append(
            stack[:, :, at : at + size].transpose(1, 0, 2).reshape(layers, count * size)
        )
        at += size
    return out


def gather_block(weights, layer, number, place):
    shard = weights[number][layer]
    rows, columns = shard.shape
    split_y = number == 6 or (number == 8 and layer > 0)
    tall = rows // CHIPS_Y if split_y else rows
    start = (place.y * tall if split_y else 0, place.core * (columns // 2))
    return lax.dynamic_slice(shard, start, (tall, columns // 2)), split_y


def reduce_chain(left, right, place, y_first):
    at = place.at
    parts, _, columns = right.shape
    half = columns // CORES
    rows = left.shape[1] // (CHIPS_Z * CHIPS_X * CHIPS_Y)
    grid = (parts, CHIPS_Z, CHIPS_X, CHIPS_Y, rows, half)
    away = weight_grad(left, right, at, True)
    sent = [hop(away.reshape(grid), dc=1)]
    kept = weight_grad(left, right, at, False).reshape(grid)
    (near,) = yield sent
    flip = lambda value: 1 - value
    if y_first:
        block = (parts, 1, CHIPS_X, 1, rows, half)
        index = lambda i, at: (0, i, 0, flip(at[2]), 0, 0)
        shape = (parts, CHIPS_Z, CHIPS_X, rows, half)
        (send,) = combine(
            at,
            CHIPS_Z,
            [[(kept, block, index), (near, block, index)]],
            [(shape, (parts, 1, CHIPS_X, rows, half), lambda i, at: (0, i, 0, 0, 0))],
        )
        (over,) = yield [hop(send, dy=1)]
        block = (parts, 1, 1, 1, rows, half)
        index = lambda i, at: (0, i, flip(at[1]), at[2], 0, 0)
        shape = (parts, CHIPS_Z, rows, half)
        (send,) = combine(
            at,
            CHIPS_Z,
            [
                [
                    (kept, block, index),
                    (near, block, index),
                    (over, block[:-3] + (rows, half), lambda i, at: (0, i, flip(at[1]), 0, 0)),
                ]
            ],
            [(shape, (parts, 1, rows, half), lambda i, at: (0, i, 0, 0))],
        )
        (across,) = yield [hop(send, dx=1)]

        def terms(k):
            turn = lambda at: lax.rem(at[0] + k, CHIPS_Z)
            index = lambda i, at: (0, turn(at), at[1], at[2], 0, 0)
            return [
                (kept, block, index),
                (near, block, index),
                (over, block[:-3] + (rows, half), lambda i, at: (0, turn(at), at[1], 0, 0)),
                (across, (parts, 1, rows, half), lambda i, at: (0, turn(at), 0, 0)),
            ]

        piece = (parts, rows, half)
    else:
        block = (parts, 1, 1, CHIPS_Y, rows, half)
        index = lambda i, at: (0, i, flip(at[1]), 0, 0, 0)
        shape = (parts, CHIPS_Z, CHIPS_Y, rows, half)
        (send,) = combine(
            at,
            CHIPS_Z,
            [[(kept, block, index), (near, block, index)]],
            [(shape, (parts, 1, CHIPS_Y, rows, half), lambda i, at: (0, i, 0, 0, 0))],
        )
        (across,) = yield [hop(send, dx=1)]

        def terms(k):
            turn = lambda at: lax.rem(at[0] + k, CHIPS_Z)
            index = lambda i, at: (0, turn(at), at[1], 0, 0, 0)
            return [
                (kept, block, index),
                (near, block, index),
                (across, (parts, 1, CHIPS_Y, rows, half), lambda i, at: (0, turn(at), 0, 0, 0)),
            ]

        piece = (parts, CHIPS_Y, rows, half)
    zeros = lambda i, at: (0,) * len(piece)
    whole = (piece, piece, zeros)
    own, *sends = combine(at, 1, [terms(k) for k in range(CHIPS_Z)], [whole] * CHIPS_Z)
    landed = yield [hop(send, dz=k) for k, send in zip(range(1, CHIPS_Z), sends)]
    (own,) = combine(at, 1, [[(term, piece, zeros) for term in (own, *landed)]], [whole])
    (other,) = yield [hop(own, dy=1)]
    if y_first:
        pieces = [own, other]
    else:
        pieces = combine(at, 1, [[(own, piece, zeros), (other, piece, zeros)]], [whole])
    others = yield [hop(item, dc=1) for item in pieces]
    return [*pieces, *others]


def join_kernel(at_ref, *refs):
    out_ref = refs[-1]
    half = refs[0].shape[-1]
    per_layer = (len(refs) - 1) // LAYERS
    for number, ref in enumerate(refs[:-1]):
        layer, place = divmod(number, per_layer)
        core = lax.rem(at_ref[3] + place // (per_layer // CORES), CORES)
        row = 0
        if per_layer > CORES:
            row = lax.rem(at_ref[2] + place % CHIPS_Y, CHIPS_Y) * ref.shape[1]
            row = pl.multiple_of(row, 16)
        for part in range(ref.shape[0]):
            column = pl.multiple_of((part * CORES + core) * half, 128)
            out_ref[layer, pl.ds(row, ref.shape[1]), pl.ds(column, half)] = ref[part].astype(
                jnp.float32
            )


def join(at, layers):
    pieces = []
    for layer in layers:
        for piece in layer:
            if piece.ndim == 4:
                piece = piece.reshape(piece.shape[0], -1, piece.shape[-1])
            pieces.append(piece)
    parts, rows, half = pieces[0].shape
    tall = rows * (len(pieces) // LAYERS // CORES)
    zeros = lambda i, at: (0, 0, 0)
    shape = (LAYERS, tall, parts * CORES * half)
    return pl.pallas_call(
        join_kernel,
        grid_spec=pltpu.PrefetchScalarGridSpec(
            num_scalar_prefetch=1,
            grid=(1,),
            in_specs=[pl.BlockSpec(piece.shape, zeros) for piece in pieces],
            out_specs=pl.BlockSpec(shape, zeros),
        ),
        out_shape=jax.ShapeDtypeStruct(shape, jnp.float32),
        compiler_params=kernel_params(),
        cost_estimate=pl.CostEstimate(flops=0, bytes_accessed=4_000_000, transcendentals=0),
    )(at, *pieces)


def reduce_total(total, place):
    for step in (dict(dc=1), dict(dy=1), dict(dx=1), dict(dz=2)):
        (other,) = yield [hop(total, **step)]
        total = total + other
    up, down = yield [hop(total, dz=1), hop(total, dz=3)]
    return total + jnp.where(place.z % 2 == 0, down, up)


def path_vectors(qv_bias):
    low = qv_bias.astype(jnp.float32)
    return jnp.concatenate([low[:D], jnp.zeros((D,), jnp.float32), low[D:]])


def local(
    fast,
    inputs,
    cotangent,
    segment,
    parent,
    clusters,
    *weights,
):
    flow = Flow()
    if fast:
        place = Place()
        vectors = gather_vectors([weights[number] for number in VECTORS], place)

        def begin(layer, number):
            flow.start(
                (layer, number), gather_chain(*gather_block(weights, layer, number, place), place)
            )

        def get(layer, number):
            if number in VECTORS:
                return vectors[VECTORS.index(number)][layer]
            return flow.finish((layer, number))

        def step(point, main):
            advanced, started = FORWARD.get(point, ((), ()))
            main = flow.tick(main, *advanced)
            for name in started:
                begin(*name)
            return main

        def reduce(layer, number, left, right):
            flow.start(
                ("grad", layer, number), reduce_chain(left, right, place, number in (0, 6))
            )

        def back_step(main, *only):
            return flow.tick(
                main,
                *[
                    name
                    for name in flow.running
                    if name[0] == "grad" and (not only or name[1:] in only)
                ],
            )

    else:

        def get(layer, number):
            whole = lax.all_gather(weights[number][layer], "shard", axis=0, tiled=True)
            return whole.astype(jnp.float32) if number in VECTORS else whole

        def step(point, main):
            return main

        def reduce(layer, number, left, right):
            grads = jnp.concatenate([contract_first(left, part) for part in right], axis=1)
            grads = lax.psum_scatter(grads, "shard", scatter_dimension=0, tiled=True)
            grads = lax.psum(grads.astype(jnp.bfloat16), "rep").astype(jnp.float32)
            flow.done[("grad", layer, number)] = grads

        def back_step(main, *only):
            return main

    step("begin", ())
    slots, bias = step("prepared", prepare(segment, parent, clusters))
    hidden, hidden_low = step("ready", (inputs, inputs))
    saved = []
    for layer in range(LAYERS):
        pull = functools.partial(get, layer)
        projected = project(hidden_low, pull(0), path_vectors(pull(1)))
        projected = step((layer, "projected"), projected)
        context, *heads = attend(projected, slots, bias)
        context = step((layer, "context"), context)
        context = step((layer, "feed"), context)
        entered = hidden_low
        middle, act, slope, *norms, hidden, hidden_low = feed(
            context,
            hidden,
            [pull(2), pull(6), pull(8)],
            [pull(number) for number in (3, 4, 5, 7, 9, 10, 11)],
        )
        hidden_low = step((layer, "result"), hidden_low)
        saved.append((entered, heads, context, middle, act, slope, norms))
    result = hidden_low
    above, proj = cotangent, None
    sums = [None] * LAYERS
    for layer in reversed(range(LAYERS)):
        entered, heads, context, middle, act, slope, norms = saved[layer]
        pull = functools.partial(get, layer)
        down, grad_pre, grad_attn, attn_low, grad_context, row_sums, ffin_sum = feed_back(
            above,
            proj,
            None if proj is None else get(layer + 1, 0),
            [norms[2], norms[3], slope, norms[0], norms[1]],
            [pull(2), pull(6), pull(8)],
            [pull(4), pull(10)],
        )
        down = back_step(down)
        reduce(layer, 8, act, down[None])
        reduce(layer, 6, middle, grad_pre[None])
        reduce(layer, 2, context, attn_low[None])
        grad_context = back_step(grad_context)
        proj, proj_sums = attend_back(grad_context, slots, heads)
        proj = back_step(proj)
        reduce(layer, 0, entered, proj)
        proj = back_step(proj, (layer, 0))
        above = grad_attn
        sums[layer] = (row_sums, ffin_sum, jnp.sum(proj_sums, axis=0))
    grad_input = input_grad(above, proj, get(0, 0))

    def qv_sum(layer):
        return jnp.concatenate([sums[layer][2][:, part].reshape(D) for part in (0, 2)])

    early = jnp.concatenate(
        [qv_sum(1)]
        + [piece for layer in range(LAYERS) for piece in (sums[layer][0][:6].reshape(-1), sums[layer][1][0])]
    )
    totals = {"early": early, "late": qv_sum(0)}
    count = lax.axis_size("shard")
    shard = lax.axis_index("shard")
    for name, total in totals.items():
        if fast:
            flow.start(name, reduce_total(total, place))
            totals[name] = flow.finish(name)
        else:
            totals[name] = lax.psum(total, AXES)
    early, late = totals["early"], totals["late"]
    ff = sums[0][1].shape[1]
    rest = early[2 * D :].reshape(LAYERS, 6 * D + ff)

    def share(stacked):
        width = stacked.shape[1] // count
        return lax.dynamic_slice_in_dim(stacked, shard * width, width, axis=1)

    grads = {1: share(jnp.stack([late, early[: 2 * D]])), 7: share(rest[:, 6 * D :])}
    for number, row in ((10, 0), (11, 1), (9, 2), (4, 3), (5, 4), (3, 5)):
        grads[number] = share(rest[:, row * D : (row + 1) * D])
    for number in (8, 6, 2, 0):
        done = [flow.finish(("grad", layer, number)) for layer in range(LAYERS)]
        grads[number] = join(place.at, done) if fast else jnp.stack(done)
    return (result, grad_input, *[grads[number] for number in range(12)])


def solution(mesh):
    in_specs = (
        P(("rep", "shard"), None),
        P(("rep", "shard"), None),
        P(("rep", "shard")),
        P(("rep", "shard"), None),
        P(None, ("rep", "shard")),
        P(None, "shard", None),
        P(None, "shard"),
        P(None, "shard", None),
        P(None, "shard"),
        P(None, "shard"),
        P(None, "shard"),
        P(None, "shard", None),
        P(None, "shard"),
        P(None, "shard", None),
        P(None, "shard"),
        P(None, "shard"),
        P(None, "shard"),
    )
    out_specs = (
        P(("rep", "shard"), None),
        P(("rep", "shard"), None),
        P(None, "shard", None),
        P(None, "shard"),
        P(None, "shard", None),
        P(None, "shard"),
        P(None, "shard"),
        P(None, "shard"),
        P(None, "shard", None),
        P(None, "shard"),
        P(None, "shard", None),
        P(None, "shard"),
        P(None, "shard"),
        P(None, "shard"),
    )
    fast = mesh.shape["rep"] == CHIPS_Y * CORES and mesh.shape["shard"] == CHIPS_Z * CHIPS_X
    return jax.shard_map(
        functools.partial(local, fast),
        mesh=mesh,
        in_specs=in_specs,
        out_specs=out_specs,
        check_vma=False,
    )
```

```python
import functools

import jax
import jax.numpy as jnp
from jax import lax
from jax.experimental import pallas as pl
from jax.experimental.pallas import tpu as pltpu
from jax.sharding import PartitionSpec as P

D = 768
HEADS = 12
HEAD_DIM = 64
LAYERS = 2
CLUSTER = 128
TREE_LEN = 1024
SEGMENTS = 13
PAIRS = HEADS // 2
LANES = 2 * HEAD_DIM
KERNEL_VMEM = 60 * 2**20
ROW_TILE = 256
FEED_TILE = 768
DEPTH_TILE = 384
INV_ROOT = (2.0 * 3.141592653589793) ** -0.5
MATRICES = (0, 2, 6, 8)
VECTORS = (1, 3, 4, 5, 7, 9, 10, 11)
AXES = ("rep", "shard")
CHIPS_Z, CHIPS_X, CHIPS_Y, CORES = 4, 2, 2, 2
norm_eps = 1e-06


def one_hot_rows(slot_row):
    length = slot_row.shape[-1]
    rows = lax.broadcasted_iota(jnp.int32, (length, length), 0)
    return jnp.where(rows == slot_row, 1.0, 0.0).astype(jnp.bfloat16)


def first_lanes(length):
    return lax.broadcasted_iota(jnp.int32, (length, LANES), 1) < HEAD_DIM


def contract_last(left_side, right_side):
    return lax.dot_general(
        left_side, right_side, (((1,), (1,)), ((), ())), preferred_element_type=jnp.float32
    )


def contract_first(left_side, right_side):
    return lax.dot_general(
        left_side, right_side, (((0,), (0,)), ((), ())), preferred_element_type=jnp.float32
    )


def cluster_blocks(values):
    return [values[at : at + CLUSTER] for at in range(0, values.shape[0], CLUSTER)]


def attend_kernel(slot_ref, query_ref, key_ref, value_ref, bias_ref, *refs):
    ctx_ref, qk_ref, val_ref, p_ref = refs[-4:]
    low = first_lanes(TREE_LEN)
    query = query_ref[...] * jnp.bfloat16(HEAD_DIM**-0.5)
    key = key_ref[...]
    value = value_ref[...]
    packed = (
        jnp.where(low, query, pltpu.roll(key, HEAD_DIM, 1)),
        jnp.where(low, pltpu.roll(query, HEAD_DIM, 1), key),
    )
    context = []
    for head in range(2):
        table = one_hot_rows(slot_ref[0, 0, head : head + 1, :])
        joined = jnp.concatenate([packed[head], value], axis=1)
        slots = jnp.dot(table, joined, preferred_element_type=jnp.float32).astype(jnp.bfloat16)
        both, values = slots[:, :LANES], slots[:, LANES:]
        qk_ref[0, head] = both
        val_ref[0, head] = values
        queries = jnp.where(low, both, jnp.bfloat16(0))
        keys = pltpu.roll(both, HEAD_DIM, 1)
        scores = jnp.concatenate(
            [contract_last(q, k) for q, k in zip(cluster_blocks(queries), cluster_blocks(keys))],
            axis=0,
        )
        scores = scores + bias_ref[0, head].astype(jnp.float32)
        numerator = jnp.exp(scores - jnp.max(scores, axis=1, keepdims=True))
        total = jnp.sum(numerator, axis=1, keepdims=True)
        soft = (numerator * (1.0 / total)).astype(jnp.bfloat16)
        p_ref[0, head] = soft
        out = jnp.concatenate(
            [
                jnp.dot(p, v, preferred_element_type=jnp.float32)
                for p, v in zip(cluster_blocks(soft), cluster_blocks(values))
            ],
            axis=0,
        ).astype(jnp.bfloat16)
        context.append(contract_first(table, out))
    ctx_ref[...] = jnp.where(low, context[0], context[1]).astype(jnp.bfloat16)


def attend_back_kernel(at_ref, slot_ref, grad_ref, qk_ref, val_ref, p_ref, out_ref, sums_ref):
    low = first_lanes(TREE_LEN)
    grads = grad_ref[...]
    placed = []
    for head in range(2):
        table = one_hot_rows(slot_ref[0, 0, head : head + 1, :])
        slots = jnp.dot(table, grads, preferred_element_type=jnp.float32)
        slots = jnp.where(low == (head == 0), slots, 0.0).astype(jnp.bfloat16)
        both, values, soft = qk_ref[0, head], val_ref[0, head], p_ref[0, head]
        grad_soft = jnp.concatenate(
            [contract_last(g, v) for g, v in zip(cluster_blocks(slots), cluster_blocks(values))],
            axis=0,
        )
        grad_value = jnp.concatenate(
            [contract_first(p, g) for p, g in zip(cluster_blocks(soft), cluster_blocks(slots))],
            axis=0,
        ).astype(jnp.bfloat16)
        weights = soft.astype(jnp.float32)
        delta = jnp.sum(weights * grad_soft, axis=1, keepdims=True)
        grad_scores = (weights * (grad_soft - delta)).astype(jnp.bfloat16)
        pairs = list(zip(cluster_blocks(grad_scores), cluster_blocks(both)))
        by_key = jnp.concatenate([contract_first(s, b) for s, b in pairs], axis=0)
        by_query = jnp.concatenate(
            [jnp.dot(s, b, preferred_element_type=jnp.float32) for s, b in pairs], axis=0
        )
        mixed = jnp.where(low, by_key, by_query * HEAD_DIM**-0.5).astype(jnp.bfloat16)
        joined = jnp.concatenate([mixed, grad_value], axis=1)
        placed.append(contract_first(table, joined))
    first, second = placed
    queries = jnp.where(low, pltpu.roll(first[:, :LANES], HEAD_DIM, 1), second[:, :LANES])
    keys = jnp.where(low, first[:, :LANES], pltpu.roll(second[:, :LANES], HEAD_DIM, 1))
    values = jnp.where(low, first[:, LANES:], second[:, LANES:])
    sums = []
    for part, grad in enumerate((queries, keys, values)):
        rounded = grad.astype(jnp.bfloat16)
        out_ref[part] = rounded
        sums.append(rows_sum(rounded.astype(jnp.float32)))
    sums_ref[0, 0] = jnp.concatenate(sums + [jnp.zeros((5, LANES), jnp.float32)], axis=0)


def slot_spec(start=0):
    return pl.BlockSpec((1, 1, 2, TREE_LEN), lambda tree, pair: (tree, start + pair, 0, 0))


def head_spec(start=0):
    return pl.BlockSpec((1, 2, TREE_LEN, LANES), lambda tree, pair: (tree, start + pair, 0, 0))


def column_spec(offset):
    return pl.BlockSpec((TREE_LEN, LANES), lambda tree, pair: (tree, offset + pair))


def kernel_params():
    return pltpu.CompilerParams(vmem_limit_bytes=KERNEL_VMEM)


def attend(projected, slots, bias, half, before):
    trees = slots.shape[0]
    start = half * (PAIRS // 2)
    stored = jax.ShapeDtypeStruct((trees, HEADS, TREE_LEN, LANES), jnp.bfloat16)
    return pl.pallas_call(
        attend_kernel,
        grid=(trees, PAIRS // 2),
        in_specs=[
            slot_spec(start),
            column_spec(start),
            column_spec(PAIRS + start),
            column_spec(2 * PAIRS + start),
            head_spec(start),
        ]
        + [pl.BlockSpec(memory_space=pl.ANY)] * len(before),
        out_specs=[column_spec(start), head_spec(start), head_spec(start), head_spec(start)],
        out_shape=[
            jax.ShapeDtypeStruct((trees * TREE_LEN, D), jnp.bfloat16),
            stored,
            stored,
            stored,
        ],
        input_output_aliases={5 + place: place for place in range(len(before))},
        compiler_params=kernel_params(),
        cost_estimate=pl.CostEstimate(
            flops=trees * 15_000_000_000, bytes_accessed=trees * 10_000_000, transcendentals=0
        ),
    )(slots, projected, projected, projected, bias, *before)


def attend_back(grad_context, slots, kept, at, other):
    trees = slots.shape[0]
    count = PAIRS // CORES
    flip = 1 if other else 0

    def pair_of(pair, at):
        return lax.rem(at[3] + flip, CORES) * count + pair

    head = pl.BlockSpec(
        (1, 2, TREE_LEN, LANES), lambda tree, pair, at: (tree, pair_of(pair, at), 0, 0)
    )
    return pl.pallas_call(
        attend_back_kernel,
        grid_spec=pltpu.PrefetchScalarGridSpec(
            num_scalar_prefetch=1,
            grid=(trees, count),
            in_specs=[
                pl.BlockSpec(
                    (1, 1, 2, TREE_LEN), lambda tree, pair, at: (tree, pair_of(pair, at), 0, 0)
                ),
                pl.BlockSpec((TREE_LEN, LANES), lambda tree, pair, at: (tree, pair_of(pair, at))),
                head,
                head,
                head,
            ],
            out_specs=[
                pl.BlockSpec((3, TREE_LEN, LANES), lambda tree, pair, at: (0, tree, pair)),
                pl.BlockSpec((1, 1, 8, LANES), lambda tree, pair, at: (tree, pair, 0, 0)),
            ],
        ),
        out_shape=[
            jax.ShapeDtypeStruct((3, trees * TREE_LEN, D // CORES), jnp.bfloat16),
            jax.ShapeDtypeStruct((trees, count, 8, LANES), jnp.float32),
        ],
        compiler_params=kernel_params(),
        cost_estimate=pl.CostEstimate(
            flops=trees * 17_000_000_000, bytes_accessed=trees * 10_000_000, transcendentals=0
        ),
    )(at, slots, grad_context, *kept)


def erf_parts(values):
    size = jnp.abs(values)
    turn = 1.0 / (1.0 + (0.3275911 * 0.5**0.5) * size)
    bell = jnp.exp(-0.5 * values * values)
    series = 1.061405429 * 0.5
    for factor in (-1.453152027, 1.421413741, -0.284496736, 0.254829592):
        series = series * turn + factor * 0.5
    tail = series * turn * bell
    return jnp.where(values < 0.0, tail, 1.0 - tail), bell


def norm_parts(values):
    centred = values - jnp.mean(values, axis=-1, keepdims=True)
    scale = lax.rsqrt(jnp.mean(centred * centred, axis=-1, keepdims=True) + norm_eps)
    return centred * scale, scale


def norm_back(grad, normal, scale, gain):
    inner = grad * gain
    mean = jnp.mean(inner, axis=-1, keepdims=True)
    along = jnp.mean(inner * normal, axis=-1, keepdims=True)
    return scale * (inner - mean - normal * along)


def spread(column):
    return jnp.broadcast_to(column, (column.shape[0], 128))


def rows_sum(values):
    return jnp.sum(values, axis=0, keepdims=True)


def project_kernel(rows_ref, weight_ref, bias_ref, out_ref):
    product = jnp.dot(rows_ref[...], weight_ref[...], preferred_element_type=jnp.float32)
    out_ref[...] = (product + bias_ref[...]).astype(jnp.bfloat16)


def feed_kernel(
    context_ref,
    rows_ref,
    out_weight_ref,
    ffin_weight_ref,
    ffout_weight_ref,
    out_bias_ref,
    attn_gain_ref,
    attn_shift_ref,
    ffin_bias_ref,
    ffout_bias_ref,
    ffn_gain_ref,
    ffn_shift_ref,
    hidden_ref,
    act_ref,
    slope_ref,
    attn_normal_ref,
    attn_scale_ref,
    ffn_normal_ref,
    ffn_scale_ref,
    result_ref,
    result_low_ref,
):
    product = jnp.dot(context_ref[...], out_weight_ref[...], preferred_element_type=jnp.float32)
    attn_sum = rows_ref[...].astype(jnp.float32) + product + out_bias_ref[...]
    normal, scale = norm_parts(attn_sum)
    attn_normal_ref[...] = normal
    attn_scale_ref[...] = spread(scale)
    hidden = normal * attn_gain_ref[...] + attn_shift_ref[...]
    hidden_low = hidden.astype(jnp.bfloat16)
    hidden_ref[...] = hidden_low
    total = hidden + ffout_bias_ref[...]
    width = ffin_weight_ref.shape[1]
    for at in range(0, width, FEED_TILE):
        part = slice(at, at + FEED_TILE)
        pre = (
            jnp.dot(hidden_low, ffin_weight_ref[:, part], preferred_element_type=jnp.float32)
            + ffin_bias_ref[:, part]
        )
        below, bell = erf_parts(pre)
        act = (pre * below).astype(jnp.bfloat16)
        act_ref[:, part] = act
        slope_ref[:, part] = (below + pre * bell * INV_ROOT).astype(jnp.bfloat16)
        total = total + jnp.dot(
            act, ffout_weight_ref[part, :], preferred_element_type=jnp.float32
        )
    normal, scale = norm_parts(total)
    ffn_normal_ref[...] = normal
    ffn_scale_ref[...] = spread(scale)
    result = normal * ffn_gain_ref[...] + ffn_shift_ref[...]
    result_ref[...] = result
    result_low_ref[...] = result.astype(jnp.bfloat16)


def add_projected(grad, at_ref, own_ref, away_ref, weight_ref):
    half = own_ref.shape[2]
    for flip, ref in enumerate((own_ref, away_ref)):
        core = lax.rem(at_ref[3] + flip, CORES)
        for part in range(3):
            column = pl.multiple_of((part * CORES + core) * half, 128)
            grad = grad + contract_last(ref[part], weight_ref[:, pl.ds(column, half)])
    return grad


def feed_back_kernel(with_proj, *refs):
    if with_proj:
        above_ref, at_ref, own_ref, away_ref, qkv_weight_ref, *refs = refs
        grad = add_projected(above_ref[...], at_ref, own_ref, away_ref, qkv_weight_ref)
    else:
        above_ref, *refs = refs
        grad = above_ref[...].astype(jnp.float32)
    (
        ffn_normal_ref,
        ffn_scale_ref,
        slope_ref,
        attn_normal_ref,
        attn_scale_ref,
        out_weight_ref,
        ffin_weight_ref,
        ffout_weight_ref,
        attn_gain_ref,
        ffn_gain_ref,
        down_ref,
        pre_ref,
        attn_ref,
        attn_low_ref,
        context_ref,
        sums_ref,
        ffin_sum_ref,
    ) = refs

    @pl.when(pl.program_id(0) == 0)
    def _():
        sums_ref[...] = jnp.zeros_like(sums_ref)
        ffin_sum_ref[...] = jnp.zeros_like(ffin_sum_ref)

    normal = ffn_normal_ref[...]
    sums_ref[0:1] += rows_sum(grad * normal)
    sums_ref[1:2] += rows_sum(grad)
    grad_sum = norm_back(grad, normal, ffn_scale_ref[:, 0:1], ffn_gain_ref[...])
    down = grad_sum.astype(jnp.bfloat16)
    down_ref[...] = down
    sums_ref[2:3] += rows_sum(down.astype(jnp.float32))
    total = grad_sum
    width = ffin_weight_ref.shape[1]
    for at in range(0, width, FEED_TILE):
        part = slice(at, at + FEED_TILE)
        grad_act = contract_last(down, ffout_weight_ref[part, :])
        pre = (grad_act * slope_ref[:, part].astype(jnp.float32)).astype(jnp.bfloat16)
        pre_ref[:, part] = pre
        ffin_sum_ref[:, part] += rows_sum(pre.astype(jnp.float32))
        total = total + contract_last(pre, ffin_weight_ref[:, part])
    normal = attn_normal_ref[...]
    sums_ref[3:4] += rows_sum(total * normal)
    sums_ref[4:5] += rows_sum(total)
    attn = norm_back(total, normal, attn_scale_ref[:, 0:1], attn_gain_ref[...])
    attn_ref[...] = attn
    low = attn.astype(jnp.bfloat16)
    attn_low_ref[...] = low
    sums_ref[5:6] += rows_sum(low.astype(jnp.float32))
    context_ref[...] = contract_last(low, out_weight_ref[...]).astype(jnp.bfloat16)


def input_grad_kernel(above_ref, at_ref, own_ref, away_ref, weight_ref, out_ref):
    out_ref[...] = add_projected(above_ref[...], at_ref, own_ref, away_ref, weight_ref)


def prep_kernel(parent_ref, segment_ref, cluster_ref, slot_ref, bias_ref):
    tree = pl.program_id(0)
    segs = segment_ref[0]
    length = segs.shape[1]

    def parent_of(values):
        found = jnp.zeros_like(values)
        for number in range(SEGMENTS):
            found = jnp.where(values == number, parent_ref[tree, number], found)
        return found

    parents = parent_of(segs)
    grands = parent_of(parents)
    ids = jnp.concatenate([segs, parents, grands, jnp.zeros((5, length), jnp.int32)], axis=0)
    ids = jnp.concatenate([ids, jnp.zeros((8, length), jnp.int32)], axis=0)
    ids = ids.astype(jnp.float32).astype(jnp.bfloat16)
    count = length // CLUSTER
    order = lax.broadcasted_iota(jnp.int32, (count, length), 0)
    lanes = lax.broadcasted_iota(jnp.int32, (count, length), 1)
    for head in range(2):
        member = order == cluster_ref[0, 0, head : head + 1, :]
        ranks = member.astype(jnp.int32)
        step = 1
        while step < length:
            ranks = ranks + jnp.where(lanes >= step, pltpu.roll(ranks, step, 1), 0)
            step *= 2
        slot = jnp.sum(
            jnp.where(member, ranks - 1 + CLUSTER * order, 0), axis=0, keepdims=True
        )
        slot_ref[0, 0, head : head + 1, :] = slot
        table = one_hot_rows(slot)
        rows = contract_last(ids, table)
        columns = jnp.concatenate([rows] * (128 // rows.shape[0]), axis=0).T
        for at in range(0, length, CLUSTER):
            here = rows[0:1, at : at + CLUSTER]
            block = columns[at : at + CLUSTER]
            allowed = (
                (here == block[:, 0:1]) | (here == block[:, 1:2]) | (here == block[:, 2:3])
            )
            bias_ref[0, head, at : at + CLUSTER, :] = jnp.where(allowed, 0.0, -1e30).astype(
                jnp.bfloat16
            )


def row_spec(width, rows=ROW_TILE):
    return pl.BlockSpec((rows, width), lambda i: (i, 0))


def whole_spec(shape):
    return pl.BlockSpec(
        shape, lambda i: (0,) * len(shape), pipeline_mode=pl.Buffered(1)
    )


def part_spec(rows=ROW_TILE):
    return pl.BlockSpec((3, rows, D // CORES), lambda i: (0, i, 0))


def cost(flops, *arrays):
    moved = sum(array.size * array.dtype.itemsize for array in arrays)
    return pl.CostEstimate(flops=int(flops), bytes_accessed=moved, transcendentals=0)


def shape_of(rows, width, kind=jnp.bfloat16):
    return jax.ShapeDtypeStruct((rows, width), kind)


def project(rows, weight, bias):
    count, width = rows.shape[0], weight.shape[1]
    return pl.pallas_call(
        project_kernel,
        grid=(count // ROW_TILE,),
        in_specs=[row_spec(D), whole_spec(weight.shape), whole_spec((1, width))],
        out_specs=row_spec(width),
        out_shape=shape_of(count, width),
        compiler_params=kernel_params(),
        cost_estimate=cost(2.4 * count * D * width, rows, weight),
    )(rows, weight, bias[None])


def feed(context, rows, weights, vectors):
    count = context.shape[0]
    width = weights[1].shape[1]
    f32 = jnp.float32
    vectors = [vector[None] for vector in vectors]
    return pl.pallas_call(
        feed_kernel,
        grid=(count // ROW_TILE,),
        in_specs=[row_spec(D), row_spec(D)]
        + [whole_spec(weight.shape) for weight in weights]
        + [whole_spec(vector.shape) for vector in vectors],
        out_specs=[
            row_spec(D),
            row_spec(width),
            row_spec(width),
            row_spec(D),
            row_spec(128),
            row_spec(D),
            row_spec(128),
            row_spec(D),
            row_spec(D),
        ],
        out_shape=[
            shape_of(count, D),
            shape_of(count, width),
            shape_of(count, width),
            shape_of(count, D, f32),
            shape_of(count, 128, f32),
            shape_of(count, D, f32),
            shape_of(count, 128, f32),
            shape_of(count, D, f32),
            shape_of(count, D),
        ],
        compiler_params=kernel_params(),
        cost_estimate=cost(5 * count * D * (2 * width + D), context, *weights),
    )(context, rows, *weights, *vectors)


def feed_back(above, proj, qkv_weight, at, saved, weights, gains):
    count = above.shape[0]
    width = weights[1].shape[1]
    f32 = jnp.float32
    gains = [gain[None] for gain in gains]
    lead, lead_specs = [above], [row_spec(D)]
    if proj is not None:
        lead += [at, *proj, qkv_weight]
        lead_specs += [
            pl.BlockSpec(memory_space=pltpu.SMEM),
            part_spec(),
            part_spec(),
            whole_spec(qkv_weight.shape),
        ]
    return pl.pallas_call(
        functools.partial(feed_back_kernel, proj is not None),
        grid=(count // ROW_TILE,),
        in_specs=lead_specs
        + [row_spec(D), row_spec(128), row_spec(width), row_spec(D), row_spec(128)]
        + [whole_spec(weight.shape) for weight in weights]
        + [whole_spec(gain.shape) for gain in gains],
        out_specs=[
            row_spec(D),
            row_spec(width),
            row_spec(D),
            row_spec(D),
            row_spec(D),
            pl.BlockSpec((8, D), lambda i: (0, 0)),
            pl.BlockSpec((1, width), lambda i: (0, 0)),
        ],
        out_shape=[
            shape_of(count, D),
            shape_of(count, width),
            shape_of(count, D, f32),
            shape_of(count, D),
            shape_of(count, D),
            shape_of(8, D, f32),
            shape_of(1, width, f32),
        ],
        compiler_params=kernel_params(),
        cost_estimate=cost(5 * count * D * (2 * width + D), above, *weights),
    )(*lead, *saved, *weights, *gains)


def input_grad(above, proj, qkv_weight, at):
    count = above.shape[0]
    return pl.pallas_call(
        input_grad_kernel,
        grid=(count // ROW_TILE,),
        in_specs=[
            row_spec(D),
            pl.BlockSpec(memory_space=pltpu.SMEM),
            part_spec(),
            part_spec(),
            whole_spec(qkv_weight.shape),
        ],
        out_specs=row_spec(D),
        out_shape=shape_of(count, D, jnp.float32),
        compiler_params=kernel_params(),
        cost_estimate=cost(2.4 * count * D * 3 * D, above, qkv_weight),
    )(above, at, *proj, qkv_weight)


def prepare(segment, parent, clusters):
    trees = parent.shape[0]
    segment = segment.reshape(trees, 1, TREE_LEN)
    clusters = clusters.reshape(PAIRS, 2, trees, TREE_LEN).transpose(2, 0, 1, 3)
    return pl.pallas_call(
        prep_kernel,
        grid=(trees, PAIRS),
        in_specs=[
            pl.BlockSpec(memory_space=pltpu.SMEM),
            pl.BlockSpec((1, 1, TREE_LEN), lambda tree, pair: (tree, 0, 0)),
            slot_spec(),
        ],
        out_specs=[slot_spec(), head_spec()],
        out_shape=[
            jax.ShapeDtypeStruct((trees, PAIRS, 2, TREE_LEN), jnp.int32),
            jax.ShapeDtypeStruct((trees, HEADS, TREE_LEN, LANES), jnp.bfloat16),
        ],
        compiler_params=kernel_params(),
        cost_estimate=pl.CostEstimate(
            flops=trees * 20_000_000_000, bytes_accessed=trees * 4_000_000, transcendentals=0
        ),
    )(parent, segment, clusters)


def weight_grad_kernel(split_y, at_ref, left_ref, right_ref, *refs):
    product = contract_first(
        left_ref[...].reshape(left_ref.shape[-2:]), right_ref[...].reshape(right_ref.shape[-2:])
    )
    if split_y is None:
        (out_ref,) = refs
        out_ref[...] = product.astype(jnp.bfloat16).reshape(out_ref.shape)
        return
    near_ref, send_ref, keep_ref, sum_ref = refs
    total = product + near_ref[...].astype(jnp.float32).reshape(product.shape)
    sum_ref[...] = total.astype(jnp.bfloat16).reshape(sum_ref.shape)
    if split_y:
        send_ref[0] = sum_ref[:, :, 1 - at_ref[2]]
        keep_ref[0] = sum_ref[:, :, at_ref[2]]
    else:
        send_ref[0] = sum_ref[:, 1 - at_ref[1]]
        keep_ref[0] = sum_ref[:, at_ref[1]]


class Grad:
    def __init__(self, left, own, away, cut, tiles, half):
        self.left, self.rights = left, (own, away)
        self.cut, self.tiles, self.half = cut, tiles, half
        self.depth = left.shape[1]
        self.parts = 1 if self.depth > D else tiles
        self.rows = self.depth // (CHIPS_Z * CHIPS_X)

    def product(self, at, other, split_y=None, near=None):
        flip = 1 if other else 0
        left, right = self.left, self.rights[flip]
        count = left.shape[0]
        tall = self.depth > D
        core = lambda at: lax.rem(at[3] + flip, CORES)
        in_specs = [
            pl.BlockSpec((count, D), (lambda i, at: (0, i)) if tall else (lambda i, at: (0, 0)))
        ]
        if not self.cut:
            in_specs.append(pl.BlockSpec((1, count, self.half), lambda i, at: (i, 0, 0)))
        elif tall:
            in_specs.append(pl.BlockSpec((count, self.half), lambda i, at: (0, core(at))))
        else:
            in_specs.append(
                pl.BlockSpec((count, self.half), lambda i, at: (0, core(at) * self.tiles + i))
            )
        zs = D // (self.rows * CHIPS_X)
        place = (lambda i: (0, i)) if tall else (lambda i: (i, 0))
        whole = (self.parts, CHIPS_Z, CHIPS_X, self.rows, self.half)
        block = (1, zs, CHIPS_X, self.rows, self.half)
        full = pl.BlockSpec(block, lambda i, at: (*place(i), 0, 0, 0))
        args, scratch = [left, right], []
        if split_y is None:
            out_specs, shapes = full, jax.ShapeDtypeStruct(whole, jnp.bfloat16)
        else:
            in_specs.append(full)
            args.append(near)
            if split_y:
                short = self.rows // CHIPS_Y
                kept = (CHIPS_X, short, self.half)
                scratch = [pltpu.VMEM((zs, CHIPS_X, CHIPS_Y, short, self.half), jnp.bfloat16)]
            else:
                kept = (self.rows, self.half)
                scratch = [pltpu.VMEM((zs, CHIPS_X, self.rows, self.half), jnp.bfloat16)]
            rest = (0,) * len(kept)
            out_specs = [pl.BlockSpec((1, zs, *kept), lambda i, at: (*place(i), *rest))] * 2
            shapes = [jax.ShapeDtypeStruct((self.parts, CHIPS_Z, *kept), jnp.bfloat16)] * 2
        return pl.pallas_call(
            functools.partial(weight_grad_kernel, split_y),
            grid_spec=pltpu.PrefetchScalarGridSpec(
                num_scalar_prefetch=1,
                grid=(self.tiles,),
                in_specs=in_specs,
                out_specs=out_specs,
                scratch_shapes=scratch,
            ),
            out_shape=shapes,
            compiler_params=kernel_params(),
            cost_estimate=cost(4 * count * D * self.tiles * self.half, left, right),
        )(at, *args)


def combine_kernel(groups, at_ref, *refs):
    total = sum(groups)
    ins, outs = refs[:total], refs[total:]
    first = 0
    for count, out_ref in zip(groups, outs):
        value = None
        for ref in ins[first : first + count]:
            term = ref[...].astype(jnp.float32).reshape(out_ref.shape)
            value = term if value is None else value + term
        out_ref[...] = value.astype(out_ref.dtype)
        first += count


def combine(at, steps, groups, blocks):
    terms = [term for group in groups for term in group]
    return pl.pallas_call(
        functools.partial(combine_kernel, [len(group) for group in groups]),
        grid_spec=pltpu.PrefetchScalarGridSpec(
            num_scalar_prefetch=1,
            grid=(steps,),
            in_specs=[pl.BlockSpec(block, index) for _, block, index in terms],
            out_specs=[pl.BlockSpec(block, index) for _, block, index in blocks],
        ),
        out_shape=[jax.ShapeDtypeStruct(shape, jnp.bfloat16) for shape, _, _ in blocks],
        compiler_params=kernel_params(),
        cost_estimate=pl.CostEstimate(
            flops=0, bytes_accessed=2_000_000, transcendentals=0
        ),
    )(at, *[array for array, _, _ in terms])


FORWARD = {
    "begin": ((), ((0, 0),)),
    "prepared": (((0, 0),), ((0, 2), (0, 6), (0, 8))),
    "ready": (((0, 0),), ()),
    (0, "projected"): (((0, 6), (0, 2)), ()),
    (0, "half"): (((0, 6), (0, 2), (0, 8)), ((1, 0),)),
    (0, "context"): (((0, 6), (0, 8), (1, 0)), ((1, 6), (1, 2))),
    (0, "placed"): (((1, 0), (1, 6), (1, 2)), ((1, 8),)),
    (0, "result"): (((1, 6), (1, 2), (1, 8)), ()),
    (1, "half"): (((1, 6), (1, 8)), ()),
}


class Place:
    def __init__(self):
        rep = lax.axis_index("rep")
        shard = lax.axis_index("shard")
        self.y, self.core = rep // CORES, rep % CORES
        self.z, self.x = shard // CHIPS_X, shard % CHIPS_X
        self.at = jnp.stack([self.z, self.x, self.y, self.core]).astype(jnp.int32)


def hop(value, dz=0, dx=0, dy=0, dc=0):
    pairs = []
    for y in range(CHIPS_Y):
        for c in range(CORES):
            for z in range(CHIPS_Z):
                for x in range(CHIPS_X):
                    source = ((y * CORES + c) * CHIPS_Z + z) * CHIPS_X + x
                    y2, c2 = (y + dy) % CHIPS_Y, (c + dc) % CORES
                    z2, x2 = (z + dz) % CHIPS_Z, (x + dx) % CHIPS_X
                    pairs.append((source, ((y2 * CORES + c2) * CHIPS_Z + z2) * CHIPS_X + x2))
    return lax.ppermute(value, AXES, pairs)


def place_kernel(split_y, half, at_ref, *refs):
    pieces, out_ref = refs[:-1], refs[-1]
    rows = out_ref.shape[2]
    for number, piece in enumerate(pieces):
        core = (at_ref[3] + number % CORES) % CORES
        x = (at_ref[1] + number // CORES % CHIPS_X) % CHIPS_X
        row = (at_ref[2] + number // (CORES * CHIPS_X)) % CHIPS_Y if split_y else 0
        column = pl.multiple_of(core * half, 128)
        out_ref[x, row, :, pl.ds(column, half)] = piece[0, 0:rows]


def place_pieces(pieces, rows, split_y, place):
    _, held, half = pieces[0].shape
    splits = CHIPS_Y if split_y else 1
    whole = pl.pallas_call(
        functools.partial(place_kernel, split_y, half),
        grid_spec=pltpu.PrefetchScalarGridSpec(
            num_scalar_prefetch=1,
            grid=(CHIPS_Z,),
            in_specs=[pl.BlockSpec((1, held, half), lambda k, at: (k, 0, 0))] * len(pieces),
            out_specs=pl.BlockSpec(
                (CHIPS_X, splits, rows, 2 * half),
                lambda k, at: (lax.rem(at[0] + CHIPS_Z - k, CHIPS_Z), 0, 0, 0),
            ),
        ),
        out_shape=jax.ShapeDtypeStruct(
            (CHIPS_Z * CHIPS_X, splits, rows, 2 * half), jnp.bfloat16
        ),
        compiler_params=kernel_params(),
        cost_estimate=pl.CostEstimate(
            flops=0,
            bytes_accessed=4 * CHIPS_Z * len(pieces) * rows * half,
            transcendentals=0,
        ),
    )(place.at, *pieces)
    return whole.reshape(CHIPS_Z * CHIPS_X * splits * rows, 2 * half)


def gather_chain(block, rows, split_y, place):
    parts = yield [hop(block, dz=k) for k in range(1, CHIPS_Z)]
    stack = jnp.stack([block, *parts])
    (across,) = yield [hop(stack, dx=1)]
    pieces = [stack, across]
    if split_y:
        pieces = pieces + (yield [hop(piece, dy=1) for piece in pieces])
    others = yield [hop(piece, dc=1) for piece in pieces]
    whole = place_pieces(
        [item for pair in zip(pieces, others) for item in pair], rows, split_y, place
    )
    return whole, jnp.stack([stack[:, rows:], across[:, rows:]], axis=1)


class Flow:
    def __init__(self):
        self.running, self.done = {}, {}

    def start(self, name, chain):
        self.running[name] = (chain, next(chain))

    def advance(self, name, arrived):
        chain, _ = self.running.pop(name)
        try:
            self.running[name] = (chain, chain.send(list(arrived)))
        except StopIteration as end:
            self.done[name] = end.value

    def tick(self, main, *names):
        names = [name for name in names if name in self.running]
        pending = [self.running[name][1] for name in names]
        main, pending = lax.optimization_barrier((main, pending))
        for name, arrived in zip(names, pending):
            self.advance(name, arrived)
        return main

    def finish(self, name):
        while name in self.running:
            self.advance(name, self.running[name][1])
        return self.done[name]


def spread_vectors(stack, sizes, place):
    count = CHIPS_Z * CHIPS_X
    stack = stack[:, :, :LAYERS].reshape(count, LAYERS, -1).astype(jnp.float32)
    wanted = jnp.arange(count, dtype=jnp.int32)
    behind = (place.z - wanted // CHIPS_X) % CHIPS_Z * CHIPS_X + (
        place.x - wanted % CHIPS_X
    ) % CHIPS_X
    turn = (behind[:, None] == wanted[None, :]).astype(jnp.float32)
    stack = jnp.sum(turn[:, :, None, None] * stack[None], axis=1)
    out, at = [], 0
    for size in sizes:
        out.append(
            stack[:, :, at : at + size].transpose(1, 0, 2).reshape(LAYERS, count * size)
        )
        at += size
    return out


def gather_block(weights, layer, number, place):
    shard = weights[number][layer]
    rows, columns = shard.shape
    split_y = number == 6
    tall = rows // CHIPS_Y if split_y else rows
    start = (place.y * tall if split_y else 0, place.core * (columns // 2))
    block = lax.dynamic_slice(shard, start, (tall, columns // 2))
    if (layer, number) == (0, 0):
        vectors = jnp.concatenate([weights[member] for member in VECTORS], axis=1)
        block = jnp.concatenate([block, jnp.pad(vectors, ((0, 16 - LAYERS), (0, 0)))])
    return block, tall, split_y


def reduce_chain(grad, place, y_first):
    at = place.at
    parts, half = grad.parts, grad.half
    away = grad.product(at, True)
    (near,) = yield [hop(away, dc=1)]
    send, keep = grad.product(at, False, y_first, near)
    flip = lambda value: 1 - value
    if y_first:
        rows = grad.rows // CHIPS_Y
        (over,) = yield [hop(send, dy=1)]
        block = (parts, 1, 1, rows, half)
        index = lambda i, at: (0, i, flip(at[1]), 0, 0)
        (send,) = combine(
            at,
            CHIPS_Z,
            [[(keep, block, index), (over, block, index)]],
            [
                (
                    (parts, CHIPS_Z, rows, half),
                    (parts, 1, rows, half),
                    lambda i, at: (0, i, 0, 0),
                )
            ],
        )
        (across,) = yield [hop(send, dx=1)]

        def terms(k):
            turn = lambda at: lax.rem(at[0] + k, CHIPS_Z)
            index = lambda i, at: (0, turn(at), at[1], 0, 0)
            return [
                (keep, block, index),
                (over, block, index),
                (across, (parts, 1, rows, half), lambda i, at: (0, turn(at), 0, 0)),
            ]

    else:
        rows = grad.rows
        (across,) = yield [hop(send, dx=1)]
        block = (parts, 1, rows, half)

        def terms(k):
            index = lambda i, at: (0, lax.rem(at[0] + k, CHIPS_Z), 0, 0)
            return [(keep, block, index), (across, block, index)]

    piece = (parts, rows, half)
    zeros = lambda i, at: (0, 0, 0)
    whole = (piece, piece, zeros)
    own, *sends = combine(at, 1, [terms(k) for k in range(CHIPS_Z)], [whole] * CHIPS_Z)
    landed = yield [hop(send, dz=k) for k, send in zip(range(1, CHIPS_Z), sends)]
    (own,) = combine(at, 1, [[(term, piece, zeros) for term in (own, *landed)]], [whole])
    if y_first:
        others = yield [hop(own, dy=1), hop(own, dc=1), hop(own, dy=1, dc=1)]
        return [own, *others]
    (other,) = yield [hop(own, dy=1)]
    (own,) = combine(at, 1, [[(own, piece, zeros), (other, piece, zeros)]], [whole])
    (other,) = yield [hop(own, dc=1)]
    return [own, other]


def join_kernel(parts_outer, at_ref, *refs):
    out_ref = refs[-1]
    half = refs[0].shape[-1]
    per_layer = (len(refs) - 1) // LAYERS
    for number, ref in enumerate(refs[:-1]):
        layer, place = divmod(number, per_layer)
        core = lax.rem(at_ref[3] + place // (per_layer // CORES), CORES)
        row = 0
        if per_layer > CORES:
            row = lax.rem(at_ref[2] + place % CHIPS_Y, CHIPS_Y) * ref.shape[1]
            row = pl.multiple_of(row, 16)
        for part in range(ref.shape[0]):
            column = part * CORES + core if parts_outer else core * ref.shape[0] + part
            column = pl.multiple_of(column * half, 128)
            out_ref[layer, pl.ds(row, ref.shape[1]), pl.ds(column, half)] = ref[part].astype(
                jnp.float32
            )


def join(at, layers, parts_outer):
    pieces = [piece for layer in layers for piece in layer]
    parts, rows, half = pieces[0].shape
    tall = rows * (len(pieces) // LAYERS // CORES)
    zeros = lambda i, at: (0, 0, 0)
    shape = (LAYERS, tall, parts * CORES * half)
    return pl.pallas_call(
        functools.partial(join_kernel, parts_outer),
        grid_spec=pltpu.PrefetchScalarGridSpec(
            num_scalar_prefetch=1,
            grid=(1,),
            in_specs=[pl.BlockSpec(piece.shape, zeros) for piece in pieces],
            out_specs=pl.BlockSpec(shape, zeros),
        ),
        out_shape=jax.ShapeDtypeStruct(shape, jnp.float32),
        compiler_params=kernel_params(),
        cost_estimate=pl.CostEstimate(flops=0, bytes_accessed=4_000_000, transcendentals=0),
    )(at, *pieces)


def reduce_total(total, place):
    for step in (dict(dc=1), dict(dy=1), dict(dx=1), dict(dz=2)):
        (other,) = yield [hop(total, **step)]
        total = total + other
    up, down = yield [hop(total, dz=1), hop(total, dz=3)]
    return total + jnp.where(place.z % 2 == 0, down, up)


def qv_sum(halves):
    own, away, at = halves
    own, away = jnp.sum(own, axis=0), jnp.sum(away, axis=0)
    order = jnp.where(
        at[3] == 0, jnp.concatenate([own, away], axis=0), jnp.concatenate([away, own], axis=0)
    )
    return jnp.concatenate([order[:, part].reshape(D) for part in (0, 2)])


def path_vectors(qv_bias):
    low = qv_bias.astype(jnp.float32)
    return jnp.concatenate([low[:D], jnp.zeros((D,), jnp.float32), low[D:]])


def local(
    fast,
    inputs,
    cotangent,
    segment,
    parent,
    clusters,
    *weights,
):
    flow = Flow()
    if fast:
        place = Place()
        at = place.at
        sizes = [weights[number].shape[1] for number in VECTORS]
        spread_out = []

        def get(layer, number):
            if number not in VECTORS:
                return flow.finish((layer, number))[0]
            if not spread_out:
                spread_out.extend(spread_vectors(flow.finish((0, 0))[1], sizes, place))
            return spread_out[VECTORS.index(number)][layer]

        def step(point, main):
            advanced, started = FORWARD.get(point, ((), ()))
            main = flow.tick(main, *advanced)
            for name in started:
                flow.start(name, gather_chain(*gather_block(weights, *name, place), place))
            return main

        def reduce(layer, number, grad):
            flow.start(("grad", layer, number), reduce_chain(grad, place, number in (0, 6)))

        def back_step(main, *held):
            return flow.tick(main, *[name for name in flow.running if name not in held])

        def add_up(name, total):
            flow.start(name, reduce_total(total, place))

    else:
        at = jnp.zeros((4,), jnp.int32)

        def get(layer, number):
            whole = lax.all_gather(weights[number][layer], "shard", axis=0, tiled=True)
            return whole.astype(jnp.float32) if number in VECTORS else whole

        def step(point, main):
            return main

        def reduce(layer, number, grad):
            own, away = grad.rights
            if not grad.cut:
                own = jnp.concatenate([own, away], axis=2)
                own = own.transpose(1, 0, 2).reshape(own.shape[1], -1)
            total = contract_first(grad.left, own)
            total = lax.psum_scatter(total, "shard", scatter_dimension=0, tiled=True)
            total = lax.psum(total.astype(jnp.bfloat16), "rep").astype(jnp.float32)
            flow.done[("grad", layer, number)] = total

        def back_step(main, *held):
            return main

        def add_up(name, total):
            flow.done[name] = lax.psum(total, AXES)

    step("begin", ())
    slots, bias = step("prepared", prepare(segment, parent, clusters))
    hidden, hidden_low = step("ready", (inputs, inputs))
    saved = []
    for layer in range(LAYERS):
        pull = functools.partial(get, layer)
        projected = project(hidden_low, pull(0), path_vectors(pull(1)))
        projected = step((layer, "projected"), projected)
        first = attend(projected, slots, bias, 0, ())
        first = step((layer, "half"), first)
        context, *heads = attend(projected, slots, bias, 1, first)
        context = step((layer, "context"), context)
        context, *wide = step((layer, "placed"), (context, pull(2), pull(6), pull(8)))
        entered = hidden_low
        middle, act, slope, *norms, hidden, hidden_low = feed(
            context,
            hidden,
            wide,
            [pull(number) for number in (3, 4, 5, 7, 9, 10, 11)],
        )
        hidden_low = step((layer, "result"), hidden_low)
        saved.append((entered, heads, context, middle, act, slope, norms))
    result = hidden_low
    above, proj = cotangent, None
    sums = [None] * LAYERS
    for layer in reversed(range(LAYERS)):
        entered, heads, context, middle, act, slope, norms = saved[layer]
        pull = functools.partial(get, layer)
        down, grad_pre, grad_attn, attn_low, grad_context, row_sums, ffin_sum = feed_back(
            above,
            proj,
            None if proj is None else get(layer + 1, 0),
            at,
            [norms[2], norms[3], slope, norms[0], norms[1]],
            [pull(2), pull(6), pull(8)],
            [pull(4), pull(10)],
        )
        sums[layer] = [row_sums, ffin_sum, None]
        down = back_step(down)
        wide = grad_pre.shape[1] // CORES
        reduce(layer, 8, Grad(act, down, down, True, act.shape[1] // D, D // CORES))
        reduce(layer, 6, Grad(middle, grad_pre, grad_pre, True, wide // D, D))
        reduce(layer, 2, Grad(context, attn_low, attn_low, True, 1, D // CORES))
        if layer == 0:
            pieces = [qv_sum(sums[1][2])]
            for row_sums, ffin_sum, _ in sums:
                pieces += [row_sums[:6].reshape(-1), ffin_sum[0]]
            add_up("early", jnp.concatenate(pieces))
        grad_context = back_step(grad_context)
        away, away_sums = attend_back(grad_context, slots, heads, at, True)
        grad_context, away = back_step((grad_context, away))
        own, own_sums = attend_back(grad_context, slots, heads, at, False)
        proj = (own, away)
        reduce(layer, 0, Grad(entered, own, away, False, 3, D // CORES))
        sums[layer][2] = (own_sums, away_sums, at)
        proj = back_step(proj, ("grad", layer, 8))
        above = grad_attn
    add_up("late", qv_sum(sums[0][2]))
    grad_input = input_grad(above, proj, get(0, 0), at)
    grad_input = back_step(grad_input)
    while flow.running:
        grad_input = back_step(grad_input)
    early, late = flow.finish("early"), flow.finish("late")
    count = lax.axis_size("shard")
    shard = lax.axis_index("shard")
    ff = sums[0][1].shape[1]
    rest = early[2 * D :].reshape(LAYERS, 6 * D + ff)

    def share(stacked):
        width = stacked.shape[1] // count
        return lax.dynamic_slice_in_dim(stacked, shard * width, width, axis=1)

    grads = {1: share(jnp.stack([late, early[: 2 * D]])), 7: share(rest[:, 6 * D :])}
    for number, row in ((10, 0), (11, 1), (9, 2), (4, 3), (5, 4), (3, 5)):
        grads[number] = share(rest[:, row * D : (row + 1) * D])
    for number in (8, 6, 2, 0):
        done = [flow.finish(("grad", layer, number)) for layer in range(LAYERS)]
        grads[number] = join(at, done, number == 0) if fast else jnp.stack(done)
    return (result, grad_input, *[grads[number] for number in range(12)])


def solution(mesh):
    in_specs = (
        P(("rep", "shard"), None),
        P(("rep", "shard"), None),
        P(("rep", "shard")),
        P(("rep", "shard"), None),
        P(None, ("rep", "shard")),
        P(None, "shard", None),
        P(None, "shard"),
        P(None, "shard", None),
        P(None, "shard"),
        P(None, "shard"),
        P(None, "shard"),
        P(None, "shard", None),
        P(None, "shard"),
        P(None, "shard", None),
        P(None, "shard"),
        P(None, "shard"),
        P(None, "shard"),
    )
    out_specs = (
        P(("rep", "shard"), None),
        P(("rep", "shard"), None),
        P(None, "shard", None),
        P(None, "shard"),
        P(None, "shard", None),
        P(None, "shard"),
        P(None, "shard"),
        P(None, "shard"),
        P(None, "shard", None),
        P(None, "shard"),
        P(None, "shard", None),
        P(None, "shard"),
        P(None, "shard"),
        P(None, "shard"),
    )
    fast = mesh.shape["rep"] == CHIPS_Y * CORES and mesh.shape["shard"] == CHIPS_Z * CHIPS_X
    return jax.shard_map(
        functools.partial(local, fast),
        mesh=mesh,
        in_specs=in_specs,
        out_specs=out_specs,
        check_vma=False,
    )
```

```python
import functools

import jax
import jax.numpy as jnp
from jax import lax
from jax.experimental import pallas as pl
from jax.experimental.pallas import tpu as pltpu
from jax.sharding import PartitionSpec as P

D = 768
HEADS = 12
HEAD_DIM = 64
LAYERS = 2
CLUSTER = 128
TREE_LEN = 1024
SEGMENTS = 13
PAIRS = HEADS // 2
LANES = 2 * HEAD_DIM
KERNEL_VMEM = 60 * 2**20
ROW_TILE = 256
FEED_TILE = 768
DEPTH_TILE = 384
INV_ROOT = (2.0 * 3.141592653589793) ** -0.5
MATRICES = (0, 2, 6, 8)
VECTORS = (1, 3, 4, 5, 7, 9, 10, 11)
UNIT = 384
AXES = ("rep", "shard")
CHIPS_Z, CHIPS_X, CHIPS_Y, CORES = 4, 2, 2, 2
norm_eps = 1e-06


def one_hot_rows(slot_row):
    length = slot_row.shape[-1]
    rows = lax.broadcasted_iota(jnp.int32, (length, length), 0)
    return jnp.where(rows == slot_row, 1.0, 0.0).astype(jnp.bfloat16)


def first_lanes(length):
    return lax.broadcasted_iota(jnp.int32, (length, LANES), 1) < HEAD_DIM


def contract_last(left_side, right_side):
    return lax.dot_general(
        left_side, right_side, (((1,), (1,)), ((), ())), preferred_element_type=jnp.float32
    )


def contract_first(left_side, right_side):
    return lax.dot_general(
        left_side, right_side, (((0,), (0,)), ((), ())), preferred_element_type=jnp.float32
    )


def cluster_blocks(values):
    return [values[at : at + CLUSTER] for at in range(0, values.shape[0], CLUSTER)]


def attend_kernel(slot_ref, query_ref, key_ref, value_ref, bias_ref, *refs):
    ctx_ref, qk_ref, val_ref, p_ref = refs[-4:]
    low = first_lanes(TREE_LEN)
    query = query_ref[...] * jnp.bfloat16(HEAD_DIM**-0.5)
    key = key_ref[...]
    value = value_ref[...]
    packed = (
        jnp.where(low, query, pltpu.roll(key, HEAD_DIM, 1)),
        jnp.where(low, pltpu.roll(query, HEAD_DIM, 1), key),
    )
    context = []
    for head in range(2):
        table = one_hot_rows(slot_ref[0, 0, head : head + 1, :])
        joined = jnp.concatenate([packed[head], value], axis=1)
        slots = jnp.dot(table, joined, preferred_element_type=jnp.float32).astype(jnp.bfloat16)
        both, values = slots[:, :LANES], slots[:, LANES:]
        qk_ref[0, head] = both
        val_ref[0, head] = values
        queries = jnp.where(low, both, jnp.bfloat16(0))
        keys = pltpu.roll(both, HEAD_DIM, 1)
        scores = jnp.concatenate(
            [contract_last(q, k) for q, k in zip(cluster_blocks(queries), cluster_blocks(keys))],
            axis=0,
        )
        scores = scores + bias_ref[0, head].astype(jnp.float32)
        numerator = jnp.exp(scores - jnp.max(scores, axis=1, keepdims=True))
        total = jnp.sum(numerator, axis=1, keepdims=True)
        soft = (numerator * (1.0 / total)).astype(jnp.bfloat16)
        p_ref[0, head] = soft
        out = jnp.concatenate(
            [
                jnp.dot(p, v, preferred_element_type=jnp.float32)
                for p, v in zip(cluster_blocks(soft), cluster_blocks(values))
            ],
            axis=0,
        ).astype(jnp.bfloat16)
        context.append(contract_first(table, out))
    ctx_ref[...] = jnp.where(low, context[0], context[1]).astype(jnp.bfloat16)


def attend_back_kernel(at_ref, slot_ref, grad_ref, qk_ref, val_ref, p_ref, out_ref, sums_ref):
    low = first_lanes(TREE_LEN)
    grads = grad_ref[...]
    placed = []
    for head in range(2):
        table = one_hot_rows(slot_ref[0, 0, head : head + 1, :])
        slots = jnp.dot(table, grads, preferred_element_type=jnp.float32)
        slots = jnp.where(low == (head == 0), slots, 0.0).astype(jnp.bfloat16)
        both, values, soft = qk_ref[0, head], val_ref[0, head], p_ref[0, head]
        grad_soft = jnp.concatenate(
            [contract_last(g, v) for g, v in zip(cluster_blocks(slots), cluster_blocks(values))],
            axis=0,
        )
        grad_value = jnp.concatenate(
            [contract_first(p, g) for p, g in zip(cluster_blocks(soft), cluster_blocks(slots))],
            axis=0,
        ).astype(jnp.bfloat16)
        weights = soft.astype(jnp.float32)
        delta = jnp.sum(weights * grad_soft, axis=1, keepdims=True)
        grad_scores = (weights * (grad_soft - delta)).astype(jnp.bfloat16)
        pairs = list(zip(cluster_blocks(grad_scores), cluster_blocks(both)))
        by_key = jnp.concatenate([contract_first(s, b) for s, b in pairs], axis=0)
        by_query = jnp.concatenate(
            [jnp.dot(s, b, preferred_element_type=jnp.float32) for s, b in pairs], axis=0
        )
        mixed = jnp.where(low, by_key, by_query * HEAD_DIM**-0.5).astype(jnp.bfloat16)
        joined = jnp.concatenate([mixed, grad_value], axis=1)
        placed.append(contract_first(table, joined))
    first, second = placed
    queries = jnp.where(low, pltpu.roll(first[:, :LANES], HEAD_DIM, 1), second[:, :LANES])
    keys = jnp.where(low, first[:, :LANES], pltpu.roll(second[:, :LANES], HEAD_DIM, 1))
    values = jnp.where(low, first[:, LANES:], second[:, LANES:])
    sums = []
    for part, grad in enumerate((queries, keys, values)):
        rounded = grad.astype(jnp.bfloat16)
        out_ref[part] = rounded
        sums.append(rows_sum(rounded.astype(jnp.float32)))
    sums_ref[0, 0] = jnp.concatenate(sums + [jnp.zeros((5, LANES), jnp.float32)], axis=0)


def slot_spec(start=0):
    return pl.BlockSpec((1, 1, 2, TREE_LEN), lambda tree, pair: (tree, start + pair, 0, 0))


def head_spec(start=0):
    return pl.BlockSpec((1, 2, TREE_LEN, LANES), lambda tree, pair: (tree, start + pair, 0, 0))


def column_spec(offset):
    return pl.BlockSpec((TREE_LEN, LANES), lambda tree, pair: (tree, offset + pair))


def kernel_params():
    return pltpu.CompilerParams(vmem_limit_bytes=KERNEL_VMEM)


def attend(projected, slots, bias, half, before):
    trees = slots.shape[0]
    start = half * (PAIRS // 2)
    stored = jax.ShapeDtypeStruct((trees, HEADS, TREE_LEN, LANES), jnp.bfloat16)
    return pl.pallas_call(
        attend_kernel,
        grid=(trees, PAIRS // 2),
        in_specs=[
            slot_spec(start),
            column_spec(start),
            column_spec(PAIRS + start),
            column_spec(2 * PAIRS + start),
            head_spec(start),
        ]
        + [pl.BlockSpec(memory_space=pl.ANY)] * len(before),
        out_specs=[column_spec(start), head_spec(start), head_spec(start), head_spec(start)],
        out_shape=[
            jax.ShapeDtypeStruct((trees * TREE_LEN, D), jnp.bfloat16),
            stored,
            stored,
            stored,
        ],
        input_output_aliases={5 + place: place for place in range(len(before))},
        compiler_params=kernel_params(),
        cost_estimate=pl.CostEstimate(
            flops=trees * 15_000_000_000, bytes_accessed=trees * 10_000_000, transcendentals=0
        ),
    )(slots, projected, projected, projected, bias, *before)


def attend_back(grad_context, slots, kept, at, other):
    trees = slots.shape[0]
    count = PAIRS // CORES
    flip = 1 if other else 0

    def pair_of(pair, at):
        return lax.rem(at[3] + flip, CORES) * count + pair

    head = pl.BlockSpec(
        (1, 2, TREE_LEN, LANES), lambda tree, pair, at: (tree, pair_of(pair, at), 0, 0)
    )
    return pl.pallas_call(
        attend_back_kernel,
        grid_spec=pltpu.PrefetchScalarGridSpec(
            num_scalar_prefetch=1,
            grid=(trees, count),
            in_specs=[
                pl.BlockSpec(
                    (1, 1, 2, TREE_LEN), lambda tree, pair, at: (tree, pair_of(pair, at), 0, 0)
                ),
                pl.BlockSpec((TREE_LEN, LANES), lambda tree, pair, at: (tree, pair_of(pair, at))),
                head,
                head,
                head,
            ],
            out_specs=[
                pl.BlockSpec((3, TREE_LEN, LANES), lambda tree, pair, at: (0, tree, pair)),
                pl.BlockSpec((1, 1, 8, LANES), lambda tree, pair, at: (tree, pair, 0, 0)),
            ],
        ),
        out_shape=[
            jax.ShapeDtypeStruct((3, trees * TREE_LEN, D // CORES), jnp.bfloat16),
            jax.ShapeDtypeStruct((trees, count, 8, LANES), jnp.float32),
        ],
        compiler_params=kernel_params(),
        cost_estimate=pl.CostEstimate(
            flops=trees * 17_000_000_000, bytes_accessed=trees * 10_000_000, transcendentals=0
        ),
    )(at, slots, grad_context, *kept)


def erf_parts(values):
    size = jnp.abs(values)
    turn = 1.0 / (1.0 + (0.3275911 * 0.5**0.5) * size)
    bell = jnp.exp(-0.5 * values * values)
    series = 1.061405429 * 0.5
    for factor in (-1.453152027, 1.421413741, -0.284496736, 0.254829592):
        series = series * turn + factor * 0.5
    tail = series * turn * bell
    return jnp.where(values < 0.0, tail, 1.0 - tail), bell


def norm_parts(values):
    centred = values - jnp.mean(values, axis=-1, keepdims=True)
    scale = lax.rsqrt(jnp.mean(centred * centred, axis=-1, keepdims=True) + norm_eps)
    return centred * scale, scale


def norm_back(grad, normal, scale, gain):
    inner = grad * gain
    mean = jnp.mean(inner, axis=-1, keepdims=True)
    along = jnp.mean(inner * normal, axis=-1, keepdims=True)
    return scale * (inner - mean - normal * along)


def spread(column):
    return jnp.broadcast_to(column, (column.shape[0], 128))


def rows_sum(values):
    return jnp.sum(values, axis=0, keepdims=True)


def project_kernel(rows_ref, weight_ref, bias_ref, out_ref):
    product = jnp.dot(rows_ref[...], weight_ref[...], preferred_element_type=jnp.float32)
    out_ref[...] = (product + bias_ref[...]).astype(jnp.bfloat16)


def feed_kernel(
    context_ref,
    rows_ref,
    out_weight_ref,
    ffin_weight_ref,
    ffout_weight_ref,
    out_bias_ref,
    attn_gain_ref,
    attn_shift_ref,
    ffin_bias_ref,
    ffout_bias_ref,
    ffn_gain_ref,
    ffn_shift_ref,
    hidden_ref,
    act_ref,
    slope_ref,
    attn_normal_ref,
    attn_scale_ref,
    ffn_normal_ref,
    ffn_scale_ref,
    result_ref,
    result_low_ref,
):
    product = jnp.dot(context_ref[...], out_weight_ref[...], preferred_element_type=jnp.float32)
    attn_sum = rows_ref[...].astype(jnp.float32) + product + out_bias_ref[...]
    normal, scale = norm_parts(attn_sum)
    attn_normal_ref[...] = normal
    attn_scale_ref[...] = spread(scale)
    hidden = normal * attn_gain_ref[...] + attn_shift_ref[...]
    hidden_low = hidden.astype(jnp.bfloat16)
    hidden_ref[...] = hidden_low
    total = hidden + ffout_bias_ref[...]
    width = ffin_weight_ref.shape[1]
    for at in range(0, width, FEED_TILE):
        part = slice(at, at + FEED_TILE)
        pre = (
            jnp.dot(hidden_low, ffin_weight_ref[:, part], preferred_element_type=jnp.float32)
            + ffin_bias_ref[:, part]
        )
        below, bell = erf_parts(pre)
        act = (pre * below).astype(jnp.bfloat16)
        act_ref[:, part] = act
        slope_ref[:, part] = (below + pre * bell * INV_ROOT).astype(jnp.bfloat16)
        total = total + jnp.dot(
            act, ffout_weight_ref[part, :], preferred_element_type=jnp.float32
        )
    normal, scale = norm_parts(total)
    ffn_normal_ref[...] = normal
    ffn_scale_ref[...] = spread(scale)
    result = normal * ffn_gain_ref[...] + ffn_shift_ref[...]
    result_ref[...] = result
    result_low_ref[...] = result.astype(jnp.bfloat16)


def add_projected(grad, at_ref, own_ref, away_ref, weight_ref):
    half = own_ref.shape[2]
    for flip, ref in enumerate((own_ref, away_ref)):
        core = lax.rem(at_ref[3] + flip, CORES)
        for part in range(3):
            column = pl.multiple_of((part * CORES + core) * half, 128)
            grad = grad + contract_last(ref[part], weight_ref[:, pl.ds(column, half)])
    return grad


def feed_back_kernel(with_proj, *refs):
    if with_proj:
        above_ref, at_ref, own_ref, away_ref, qkv_weight_ref, *refs = refs
        grad = add_projected(above_ref[...], at_ref, own_ref, away_ref, qkv_weight_ref)
    else:
        above_ref, *refs = refs
        grad = above_ref[...].astype(jnp.float32)
    (
        ffn_normal_ref,
        ffn_scale_ref,
        slope_ref,
        attn_normal_ref,
        attn_scale_ref,
        out_weight_ref,
        ffin_weight_ref,
        ffout_weight_ref,
        attn_gain_ref,
        ffn_gain_ref,
        down_ref,
        pre_ref,
        attn_ref,
        attn_low_ref,
        context_ref,
        sums_ref,
        ffin_sum_ref,
    ) = refs

    @pl.when(pl.program_id(0) == 0)
    def _():
        sums_ref[...] = jnp.zeros_like(sums_ref)
        ffin_sum_ref[...] = jnp.zeros_like(ffin_sum_ref)

    normal = ffn_normal_ref[...]
    sums_ref[0:1] += rows_sum(grad * normal)
    sums_ref[1:2] += rows_sum(grad)
    grad_sum = norm_back(grad, normal, ffn_scale_ref[:, 0:1], ffn_gain_ref[...])
    down = grad_sum.astype(jnp.bfloat16)
    down_ref[...] = down
    sums_ref[2:3] += rows_sum(down.astype(jnp.float32))
    total = grad_sum
    width = ffin_weight_ref.shape[1]
    for at in range(0, width, FEED_TILE):
        part = slice(at, at + FEED_TILE)
        grad_act = contract_last(down, ffout_weight_ref[part, :])
        pre = (grad_act * slope_ref[:, part].astype(jnp.float32)).astype(jnp.bfloat16)
        pre_ref[:, part] = pre
        ffin_sum_ref[:, part] += rows_sum(pre.astype(jnp.float32))
        total = total + contract_last(pre, ffin_weight_ref[:, part])
    normal = attn_normal_ref[...]
    sums_ref[3:4] += rows_sum(total * normal)
    sums_ref[4:5] += rows_sum(total)
    attn = norm_back(total, normal, attn_scale_ref[:, 0:1], attn_gain_ref[...])
    attn_ref[...] = attn
    low = attn.astype(jnp.bfloat16)
    attn_low_ref[...] = low
    sums_ref[5:6] += rows_sum(low.astype(jnp.float32))
    context_ref[...] = contract_last(low, out_weight_ref[...]).astype(jnp.bfloat16)


def input_grad_kernel(above_ref, at_ref, own_ref, away_ref, weight_ref, out_ref):
    out_ref[...] = add_projected(above_ref[...], at_ref, own_ref, away_ref, weight_ref)


def prep_kernel(parent_ref, segment_ref, cluster_ref, slot_ref, bias_ref):
    tree = pl.program_id(0)
    segs = segment_ref[0]
    length = segs.shape[1]

    def parent_of(values):
        found = jnp.zeros_like(values)
        for number in range(SEGMENTS):
            found = jnp.where(values == number, parent_ref[tree, number], found)
        return found

    parents = parent_of(segs)
    grands = parent_of(parents)
    ids = jnp.concatenate([segs, parents, grands, jnp.zeros((5, length), jnp.int32)], axis=0)
    ids = jnp.concatenate([ids, jnp.zeros((8, length), jnp.int32)], axis=0)
    ids = ids.astype(jnp.float32).astype(jnp.bfloat16)
    count = length // CLUSTER
    order = lax.broadcasted_iota(jnp.int32, (count, length), 0)
    lanes = lax.broadcasted_iota(jnp.int32, (count, length), 1)
    for head in range(2):
        member = order == cluster_ref[0, 0, head : head + 1, :]
        ranks = member.astype(jnp.int32)
        step = 1
        while step < length:
            ranks = ranks + jnp.where(lanes >= step, pltpu.roll(ranks, step, 1), 0)
            step *= 2
        slot = jnp.sum(
            jnp.where(member, ranks - 1 + CLUSTER * order, 0), axis=0, keepdims=True
        )
        slot_ref[0, 0, head : head + 1, :] = slot
        table = one_hot_rows(slot)
        rows = contract_last(ids, table)
        columns = jnp.concatenate([rows] * (128 // rows.shape[0]), axis=0).T
        for at in range(0, length, CLUSTER):
            here = rows[0:1, at : at + CLUSTER]
            block = columns[at : at + CLUSTER]
            allowed = (
                (here == block[:, 0:1]) | (here == block[:, 1:2]) | (here == block[:, 2:3])
            )
            bias_ref[0, head, at : at + CLUSTER, :] = jnp.where(allowed, 0.0, -1e30).astype(
                jnp.bfloat16
            )


def row_spec(width, rows=ROW_TILE):
    return pl.BlockSpec((rows, width), lambda i: (i, 0))


def whole_spec(shape):
    return pl.BlockSpec(
        shape, lambda i: (0,) * len(shape), pipeline_mode=pl.Buffered(1)
    )


def part_spec(rows=ROW_TILE):
    return pl.BlockSpec((3, rows, D // CORES), lambda i: (0, i, 0))


def cost(flops, *arrays):
    moved = sum(array.size * array.dtype.itemsize for array in arrays)
    return pl.CostEstimate(flops=int(flops), bytes_accessed=moved, transcendentals=0)


def shape_of(rows, width, kind=jnp.bfloat16):
    return jax.ShapeDtypeStruct((rows, width), kind)


def project(rows, weight, bias):
    count, width = rows.shape[0], weight.shape[1]
    return pl.pallas_call(
        project_kernel,
        grid=(count // ROW_TILE,),
        in_specs=[row_spec(D), whole_spec(weight.shape), whole_spec((1, width))],
        out_specs=row_spec(width),
        out_shape=shape_of(count, width),
        compiler_params=kernel_params(),
        cost_estimate=cost(2.4 * count * D * width, rows, weight),
    )(rows, weight, bias[None])


def feed(context, rows, weights, vectors):
    count = context.shape[0]
    width = weights[1].shape[1]
    f32 = jnp.float32
    vectors = [vector[None] for vector in vectors]
    return pl.pallas_call(
        feed_kernel,
        grid=(count // ROW_TILE,),
        in_specs=[row_spec(D), row_spec(D)]
        + [whole_spec(weight.shape) for weight in weights]
        + [whole_spec(vector.shape) for vector in vectors],
        out_specs=[
            row_spec(D),
            row_spec(width),
            row_spec(width),
            row_spec(D),
            row_spec(128),
            row_spec(D),
            row_spec(128),
            row_spec(D),
            row_spec(D),
        ],
        out_shape=[
            shape_of(count, D),
            shape_of(count, width),
            shape_of(count, width),
            shape_of(count, D, f32),
            shape_of(count, 128, f32),
            shape_of(count, D, f32),
            shape_of(count, 128, f32),
            shape_of(count, D, f32),
            shape_of(count, D),
        ],
        compiler_params=kernel_params(),
        cost_estimate=cost(5 * count * D * (2 * width + D), context, *weights),
    )(context, rows, *weights, *vectors)


def feed_back(above, proj, qkv_weight, at, saved, weights, gains):
    count = above.shape[0]
    width = weights[1].shape[1]
    f32 = jnp.float32
    gains = [gain[None] for gain in gains]
    lead, lead_specs = [above], [row_spec(D)]
    if proj is not None:
        lead += [at, *proj, qkv_weight]
        lead_specs += [
            pl.BlockSpec(memory_space=pltpu.SMEM),
            part_spec(),
            part_spec(),
            whole_spec(qkv_weight.shape),
        ]
    return pl.pallas_call(
        functools.partial(feed_back_kernel, proj is not None),
        grid=(count // ROW_TILE,),
        in_specs=lead_specs
        + [row_spec(D), row_spec(128), row_spec(width), row_spec(D), row_spec(128)]
        + [whole_spec(weight.shape) for weight in weights]
        + [whole_spec(gain.shape) for gain in gains],
        out_specs=[
            row_spec(D),
            row_spec(width),
            row_spec(D),
            row_spec(D),
            row_spec(D),
            pl.BlockSpec((8, D), lambda i: (0, 0)),
            pl.BlockSpec((1, width), lambda i: (0, 0)),
        ],
        out_shape=[
            shape_of(count, D),
            shape_of(count, width),
            shape_of(count, D, f32),
            shape_of(count, D),
            shape_of(count, D),
            shape_of(8, D, f32),
            shape_of(1, width, f32),
        ],
        compiler_params=kernel_params(),
        cost_estimate=cost(5 * count * D * (2 * width + D), above, *weights),
    )(*lead, *saved, *weights, *gains)


def input_grad(above, proj, qkv_weight, at):
    count = above.shape[0]
    return pl.pallas_call(
        input_grad_kernel,
        grid=(count // ROW_TILE,),
        in_specs=[
            row_spec(D),
            pl.BlockSpec(memory_space=pltpu.SMEM),
            part_spec(),
            part_spec(),
            whole_spec(qkv_weight.shape),
        ],
        out_specs=row_spec(D),
        out_shape=shape_of(count, D, jnp.float32),
        compiler_params=kernel_params(),
        cost_estimate=cost(2.4 * count * D * 3 * D, above, qkv_weight),
    )(above, at, *proj, qkv_weight)


def prepare(segment, parent, clusters):
    trees = parent.shape[0]
    segment = segment.reshape(trees, 1, TREE_LEN)
    clusters = clusters.reshape(PAIRS, 2, trees, TREE_LEN).transpose(2, 0, 1, 3)
    return pl.pallas_call(
        prep_kernel,
        grid=(trees, PAIRS),
        in_specs=[
            pl.BlockSpec(memory_space=pltpu.SMEM),
            pl.BlockSpec((1, 1, TREE_LEN), lambda tree, pair: (tree, 0, 0)),
            slot_spec(),
        ],
        out_specs=[slot_spec(), head_spec()],
        out_shape=[
            jax.ShapeDtypeStruct((trees, PAIRS, 2, TREE_LEN), jnp.int32),
            jax.ShapeDtypeStruct((trees, HEADS, TREE_LEN, LANES), jnp.bfloat16),
        ],
        compiler_params=kernel_params(),
        cost_estimate=pl.CostEstimate(
            flops=trees * 20_000_000_000, bytes_accessed=trees * 4_000_000, transcendentals=0
        ),
    )(parent, segment, clusters)


def weight_grad_kernel(split_y, at_ref, left_ref, right_ref, *refs):
    product = contract_first(
        left_ref[...].reshape(left_ref.shape[-2:]), right_ref[...].reshape(right_ref.shape[-2:])
    )
    if split_y is None:
        (out_ref,) = refs
        out_ref[...] = product.astype(jnp.bfloat16).reshape(out_ref.shape)
        return
    near_ref, (send_ref, keep_ref, sum_ref) = refs[0], refs[-3:]
    total = product + near_ref[...].astype(jnp.float32).reshape(product.shape)
    sum_ref[...] = total.astype(jnp.bfloat16).reshape(sum_ref.shape)
    if split_y:
        send_ref[0] = sum_ref[:, :, 1 - at_ref[2]]
        keep_ref[0] = sum_ref[:, :, at_ref[2]]
    else:
        send_ref[...] = sum_ref[:, 1 - at_ref[1]]
        keep_ref[...] = sum_ref[:, at_ref[1]]


class Grad:
    def __init__(self, number, left, own, away, cut, tiles, half):
        self.number = number
        self.left, self.rights = left, (own, away)
        self.cut, self.tiles, self.half = cut, tiles, half
        self.depth = left.shape[1]
        self.parts = 1 if self.depth > D else tiles
        self.rows = self.depth // (CHIPS_Z * CHIPS_X)

    def product(self, at, other, split_y=None, near=None, start=0, total=0, before=()):
        flip = 1 if other else 0
        left, right = self.left, self.rights[flip]
        count = left.shape[0]
        tall = self.depth > D
        core = lambda at: lax.rem(at[3] + flip, CORES)
        in_specs = [
            pl.BlockSpec((count, D), (lambda i, at: (0, i)) if tall else (lambda i, at: (0, 0)))
        ]
        if not self.cut:
            in_specs.append(pl.BlockSpec((1, count, self.half), lambda i, at: (i, 0, 0)))
        elif tall:
            in_specs.append(pl.BlockSpec((count, self.half), lambda i, at: (0, core(at))))
        else:
            in_specs.append(
                pl.BlockSpec((count, self.half), lambda i, at: (0, core(at) * self.tiles + i))
            )
        zs = D // (self.rows * CHIPS_X)
        place = (lambda i: (0, i)) if tall else (lambda i: (i, 0))
        whole = (self.parts, CHIPS_Z, CHIPS_X, self.rows, self.half)
        block = (1, zs, CHIPS_X, self.rows, self.half)
        full = pl.BlockSpec(block, lambda i, at: (*place(i), 0, 0, 0))
        args, scratch = [left, right], []
        if split_y is None:
            out_specs, shapes = full, jax.ShapeDtypeStruct(whole, jnp.bfloat16)
        else:
            in_specs.append(full)
            args.append(near)
            in_specs += [pl.BlockSpec(memory_space=pl.ANY)] * len(before)
            args += before
            if split_y:
                short = self.rows // CHIPS_Y
                kept = (CHIPS_X, short, self.half)
                scratch = [pltpu.VMEM((zs, CHIPS_X, CHIPS_Y, short, self.half), jnp.bfloat16)]
                spec = pl.BlockSpec((1, zs, *kept), lambda i, at: (*place(i), 0, 0, 0))
                shape = (self.parts, CHIPS_Z, *kept)
            else:
                scratch = [pltpu.VMEM((zs, CHIPS_X, self.rows, self.half), jnp.bfloat16)]
                first = start // self.rows
                index = (lambda i, at: (i, first, 0)) if tall else (lambda i, at: (0, first + i, 0))
                spec = pl.BlockSpec((zs, self.rows, self.half), index)
                shape = (CHIPS_Z, total, self.half)
            out_specs, shapes = [spec] * 2, [jax.ShapeDtypeStruct(shape, jnp.bfloat16)] * 2
        return pl.pallas_call(
            functools.partial(weight_grad_kernel, split_y),
            grid_spec=pltpu.PrefetchScalarGridSpec(
                num_scalar_prefetch=1,
                grid=(self.tiles,),
                in_specs=in_specs,
                out_specs=out_specs,
                scratch_shapes=scratch,
            ),
            out_shape=shapes,
            input_output_aliases={4 + place: place for place in range(len(before))},
            compiler_params=kernel_params(),
            cost_estimate=cost(4 * count * D * self.tiles * self.half, left, right),
        )(at, *args)


def combine_kernel(groups, at_ref, *refs):
    total = sum(groups)
    ins, outs = refs[:total], refs[total:]
    first = 0
    for count, out_ref in zip(groups, outs):
        value = None
        for ref in ins[first : first + count]:
            term = ref[...].astype(jnp.float32).reshape(out_ref.shape)
            value = term if value is None else value + term
        out_ref[...] = value.astype(out_ref.dtype)
        first += count


def combine(at, steps, groups, blocks):
    terms = [term for group in groups for term in group]
    return pl.pallas_call(
        functools.partial(combine_kernel, [len(group) for group in groups]),
        grid_spec=pltpu.PrefetchScalarGridSpec(
            num_scalar_prefetch=1,
            grid=(steps,),
            in_specs=[pl.BlockSpec(block, index) for _, block, index in terms],
            out_specs=[pl.BlockSpec(block, index) for _, block, index in blocks],
        ),
        out_shape=[jax.ShapeDtypeStruct(shape, jnp.bfloat16) for shape, _, _ in blocks],
        compiler_params=kernel_params(),
        cost_estimate=pl.CostEstimate(
            flops=0, bytes_accessed=2_000_000, transcendentals=0
        ),
    )(at, *[array for array, _, _ in terms])


CHUNKS = {
    "first": (0, (0,), False),
    "rest": (0, (2, 6, 8), True),
    "next": (1, (0, 2), False),
    "last": (1, (6, 8), False),
}
FORWARD = {
    "begin": ((), ("first",)),
    "packed": (("first",), ("rest",)),
    "prepared": (("first",), ()),
    "ready": (("rest",), ("next",)),
    (0, "half"): (("rest", "next"), ("last",)),
    (0, "context"): (("next",), ()),
    (0, "waited"): (("rest",), ()),
    (0, "placed"): (("last",), ()),
    (1, "half"): (("last",), ()),
}


class Place:
    def __init__(self):
        rep = lax.axis_index("rep")
        shard = lax.axis_index("shard")
        self.y, self.core = rep // CORES, rep % CORES
        self.z, self.x = shard // CHIPS_X, shard % CHIPS_X
        self.at = jnp.stack([self.z, self.x, self.y, self.core]).astype(jnp.int32)


def hop(value, dz=0, dx=0, dy=0, dc=0):
    pairs = []
    for y in range(CHIPS_Y):
        for c in range(CORES):
            for z in range(CHIPS_Z):
                for x in range(CHIPS_X):
                    source = ((y * CORES + c) * CHIPS_Z + z) * CHIPS_X + x
                    y2, c2 = (y + dy) % CHIPS_Y, (c + dc) % CORES
                    z2, x2 = (z + dz) % CHIPS_Z, (x + dx) % CHIPS_X
                    pairs.append((source, ((y2 * CORES + c2) * CHIPS_Z + z2) * CHIPS_X + x2))
    return lax.ppermute(value, AXES, pairs)


def pack_kernel(plan, at_ref, *refs):
    ins, outs = refs[: len(MATRICES)], refs[len(MATRICES) :]
    for out_ref, (layer, numbers, split_y) in zip(outs, plan):
        start = 0
        for number in numbers:
            ref = ins[MATRICES.index(number)]
            rows, half = ref.shape[1], ref.shape[2] // CORES
            first = 0
            if split_y:
                rows = rows // CHIPS_Y
                first = pl.multiple_of(at_ref[2] * rows, 16)
            for at in range(0, half, UNIT):
                column = pl.multiple_of(at_ref[3] * half + at, 128)
                out_ref[start : start + rows] = ref[layer, pl.ds(first, rows), pl.ds(column, UNIT)]
                start += rows


def chunk_rows(weights, numbers, split_y):
    found = []
    for number in numbers:
        _, rows, columns = weights[number].shape
        found.append((columns // (CORES * UNIT), rows // (CHIPS_Y if split_y else 1)))
    return found


def pack(weights, names, place):
    plan = [CHUNKS[name] for name in names]
    shapes = []
    for _, numbers, split_y in plan:
        shapes.append((sum(u * r for u, r in chunk_rows(weights, numbers, split_y)), UNIT))
    matrices = [weights[number] for number in MATRICES]
    packed = pl.pallas_call(
        functools.partial(pack_kernel, plan),
        grid_spec=pltpu.PrefetchScalarGridSpec(
            num_scalar_prefetch=1,
            grid=(1,),
            in_specs=[pl.BlockSpec(matrix.shape, lambda i, at: (0, 0, 0)) for matrix in matrices],
            out_specs=[pl.BlockSpec(shape, lambda i, at: (0, 0)) for shape in shapes],
        ),
        out_shape=[jax.ShapeDtypeStruct(shape, jnp.bfloat16) for shape in shapes],
        compiler_params=kernel_params(),
        cost_estimate=cost(0, *matrices),
    )(place.at, *matrices)
    return dict(zip(names, packed))


def place_kernel(layout, split_y, count, at_ref, *refs):
    pieces, outs = refs[:count], refs[count:]
    for number, piece in enumerate(pieces):
        core = (at_ref[3] + number % CORES) % CORES
        x = (at_ref[1] + number // CORES % CHIPS_X) % CHIPS_X
        row = (at_ref[2] + number // (CORES * CHIPS_X)) % CHIPS_Y if split_y else 0
        start, unit = 0, piece.shape[2]
        for out_ref, (units, rows) in zip(outs, layout):
            for at in range(units):
                column = pl.multiple_of((core * units + at) * unit, 128)
                out_ref[x, row, :, pl.ds(column, unit)] = piece[0, start : start + rows]
                start += rows


def place_pieces(pieces, layout, split_y, place):
    _, held, unit = pieces[0].shape
    splits = CHIPS_Y if split_y else 1
    shapes = [(CHIPS_Z * CHIPS_X, splits, rows, CORES * units * unit) for units, rows in layout]
    wholes = pl.pallas_call(
        functools.partial(place_kernel, layout, split_y, len(pieces)),
        grid_spec=pltpu.PrefetchScalarGridSpec(
            num_scalar_prefetch=1,
            grid=(CHIPS_Z,),
            in_specs=[pl.BlockSpec((1, held, unit), lambda k, at: (k, 0, 0))] * len(pieces),
            out_specs=[
                pl.BlockSpec(
                    (CHIPS_X, *shape[1:]),
                    lambda k, at: (lax.rem(at[0] + CHIPS_Z - k, CHIPS_Z), 0, 0, 0),
                )
                for shape in shapes
            ],
        ),
        out_shape=[jax.ShapeDtypeStruct(shape, jnp.bfloat16) for shape in shapes],
        compiler_params=kernel_params(),
        cost_estimate=pl.CostEstimate(
            flops=0,
            bytes_accessed=4 * CHIPS_Z * len(pieces) * held * unit,
            transcendentals=0,
        ),
    )(place.at, *pieces)
    return [whole.reshape(-1, whole.shape[-1]) for whole in wholes]


def gather_chain(block, layout, split_y, place):
    parts = yield [hop(block, dz=k) for k in range(1, CHIPS_Z)]
    stack = jnp.stack([block, *parts])
    (across,) = yield [hop(stack, dx=1)]
    pieces = [stack, across]
    if split_y:
        pieces = pieces + (yield [hop(piece, dy=1) for piece in pieces])
    others = yield [hop(piece, dc=1) for piece in pieces]
    wholes = place_pieces(
        [item for pair in zip(pieces, others) for item in pair], layout, split_y, place
    )
    rows = sum(units * tall for units, tall in layout)
    return wholes, jnp.stack([stack[:, rows:], across[:, rows:]], axis=1)


class Flow:
    def __init__(self):
        self.running, self.done = {}, {}

    def start(self, name, chain):
        self.running[name] = (chain, next(chain))

    def advance(self, name, arrived):
        chain, _ = self.running.pop(name)
        try:
            self.running[name] = (chain, chain.send(list(arrived)))
        except StopIteration as end:
            self.done[name] = end.value

    def tick(self, main, *names):
        names = [name for name in names if name in self.running]
        pending = [self.running[name][1] for name in names]
        main, pending = lax.optimization_barrier((main, pending))
        for name, arrived in zip(names, pending):
            self.advance(name, arrived)
        return main

    def finish(self, name):
        while name in self.running:
            self.advance(name, self.running[name][1])
        return self.done[name]


def spread_vectors(stack, sizes, place):
    count = CHIPS_Z * CHIPS_X
    stack = stack[:, :, :LAYERS].reshape(count, LAYERS, -1).astype(jnp.float32)
    wanted = jnp.arange(count, dtype=jnp.int32)
    behind = (place.z - wanted // CHIPS_X) % CHIPS_Z * CHIPS_X + (
        place.x - wanted % CHIPS_X
    ) % CHIPS_X
    turn = (behind[:, None] == wanted[None, :]).astype(jnp.float32)
    stack = jnp.sum(turn[:, :, None, None] * stack[None], axis=1)
    out, at = [], 0
    for size in sizes:
        out.append(
            stack[:, :, at : at + size].transpose(1, 0, 2).reshape(LAYERS, count * size)
        )
        at += size
    return out


def first_block(weights, place):
    shard = weights[0][0]
    half = shard.shape[1] // CORES
    block = lax.dynamic_slice_in_dim(shard, place.core * half, half, axis=1)
    vectors = jnp.concatenate([weights[member] for member in VECTORS], axis=1)
    return jnp.concatenate([block, jnp.pad(vectors, ((0, 16 - LAYERS), (0, 0)))])


def pick_sum(at, own, terms, rows, steps):
    groups = [[(array, block, index(k)) for array, block, index in terms] for k in range(CHIPS_Z)]
    return combine(at, steps, groups, [own] * CHIPS_Z)


def reduce_y_first(grad, place):
    at = place.at
    parts, half = grad.parts, grad.half
    rows = grad.rows // CHIPS_Y
    away = grad.product(at, True)
    (near,) = yield [hop(away, dc=1)]
    send, keep = grad.product(at, False, True, near)
    flip = lambda value: 1 - value
    (over,) = yield [hop(send, dy=1)]
    block = (parts, 1, 1, rows, half)
    short = (parts, 1, rows, half)
    index = lambda i, at: (0, i, flip(at[1]), 0, 0)
    (send,) = combine(
        at,
        CHIPS_Z,
        [[(keep, block, index), (over, block, index)]],
        [((parts, CHIPS_Z, rows, half), short, lambda i, at: (0, i, 0, 0))],
    )
    (across,) = yield [hop(send, dx=1)]
    turn = lambda at, k: lax.rem(at[0] + k, CHIPS_Z)
    mine = lambda k: lambda i, at: (0, turn(at, k), at[1], 0, 0)
    piece = (parts, rows, half)
    whole = (piece, piece, lambda i, at: (0, 0, 0))
    own, *sends = pick_sum(
        at,
        whole,
        [
            (keep, block, mine),
            (over, block, mine),
            (across, short, lambda k: lambda i, at: (0, turn(at, k), 0, 0)),
        ],
        rows,
        1,
    )
    landed = yield [hop(send, dz=k) for k, send in zip(range(1, CHIPS_Z), sends)]
    (own,) = combine(at, 1, [[(term, piece, whole[2]) for term in (own, *landed)]], [whole])
    others = yield [hop(own, dy=1), hop(own, dc=1), hop(own, dy=1, dc=1)]
    pieces = [item.reshape(parts * rows, half) for item in (own, *others)]
    return {grad.number: (pieces, 0, rows)}


def reduce_x_first(grads, place):
    at = place.at
    away = [grad.product(at, True) for grad in grads]
    near = yield [hop(item, dc=1) for item in away]
    total = sum(grad.parts * grad.rows for grad in grads)
    starts, flat = [0], ()
    for grad, item in zip(grads, near):
        flat = grad.product(at, False, False, item, starts[-1], total, tuple(flat))
        starts.append(starts[-1] + grad.parts * grad.rows)
    send, keep = flat
    (across,) = yield [hop(send, dx=1)]
    steps = 3
    tall = total // steps
    ahead = lambda k: lambda i, at: (lax.rem(at[0] + k, CHIPS_Z), i, 0)
    piece = ((total, UNIT), (tall, UNIT), lambda i, at: (i, 0))
    own, *sends = pick_sum(
        at, piece, [(item, (1, tall, UNIT), ahead) for item in (keep, across)], tall, steps
    )
    landed = yield [hop(send, dz=k) for k, send in zip(range(1, CHIPS_Z), sends)]
    add = lambda *terms: combine(at, steps, [[(term, *piece[1:]) for term in terms]], [piece])[0]
    own = add(own, *landed)
    (other,) = yield [hop(own, dy=1)]
    own = add(own, other)
    (other,) = yield [hop(own, dc=1)]
    return {
        grad.number: ([own, other], start, grad.rows) for grad, start in zip(grads, starts)
    }


def join_kernel(plan, count, at_ref, *refs):
    for ref, out, layer, outer, parts, dc, dy, start, rows in plan:
        ref, out_ref = refs[ref], refs[count + out]
        half = ref.shape[1]
        core = lax.rem(at_ref[3] + dc, CORES)
        row = 0
        if dy is not None:
            row = pl.multiple_of(lax.rem(at_ref[2] + dy, CHIPS_Y) * rows, 16)
        for part in range(parts):
            column = part * CORES + core if outer else core * parts + part
            column = pl.multiple_of(column * half, 128)
            value = ref[start + part * rows : start + (part + 1) * rows]
            out_ref[layer, pl.ds(row, rows), pl.ds(column, half)] = value.astype(jnp.float32)


def join(at, done, shapes):
    arrays, plan = [], []
    for out, (number, (tall, wide)) in enumerate(shapes.items()):
        for layer in range(LAYERS):
            pieces, start, rows = done[layer][number]
            for place, piece in enumerate(pieces):
                known = [other is piece for other in arrays]
                if not any(known):
                    arrays.append(piece)
                    known.append(True)
                parts = wide // (CORES * piece.shape[1])
                dy, dc = (place % CHIPS_Y, place // CHIPS_Y) if len(pieces) > CORES else (None, place)
                plan.append((known.index(True), out, layer, number == 0, parts, dc, dy, start, rows))
    zeros = lambda i, at: (0, 0)
    outs = [(LAYERS, *shape) for shape in shapes.values()]
    return pl.pallas_call(
        functools.partial(join_kernel, plan, len(arrays)),
        grid_spec=pltpu.PrefetchScalarGridSpec(
            num_scalar_prefetch=1,
            grid=(1,),
            in_specs=[pl.BlockSpec(array.shape, zeros) for array in arrays],
            out_specs=[pl.BlockSpec(out, lambda i, at: (0, 0, 0)) for out in outs],
        ),
        out_shape=[jax.ShapeDtypeStruct(out, jnp.float32) for out in outs],
        compiler_params=kernel_params(),
        cost_estimate=pl.CostEstimate(flops=0, bytes_accessed=4_000_000, transcendentals=0),
    )(at, *arrays)


def reduce_total(total, place):
    for step in (dict(dc=1), dict(dy=1), dict(dx=1), dict(dz=2)):
        (other,) = yield [hop(total, **step)]
        total = total + other
    up, down = yield [hop(total, dz=1), hop(total, dz=3)]
    return total + jnp.where(place.z % 2 == 0, down, up)


def qv_sum(halves):
    own, away, at = halves
    own, away = jnp.sum(own, axis=0), jnp.sum(away, axis=0)
    order = jnp.where(
        at[3] == 0, jnp.concatenate([own, away], axis=0), jnp.concatenate([away, own], axis=0)
    )
    return jnp.concatenate([order[:, part].reshape(D) for part in (0, 2)])


def path_vectors(qv_bias):
    low = qv_bias.astype(jnp.float32)
    return jnp.concatenate([low[:D], jnp.zeros((D,), jnp.float32), low[D:]])


def local(
    fast,
    inputs,
    cotangent,
    segment,
    parent,
    clusters,
    *weights,
):
    flow = Flow()
    if fast:
        place = Place()
        at = place.at
        sizes = [weights[number].shape[1] for number in VECTORS]
        spread_out = []

        blocks = {"first": first_block(weights, place)}

        def get(layer, number):
            if number not in VECTORS:
                for name, (chunk_layer, numbers, _) in CHUNKS.items():
                    if chunk_layer == layer and number in numbers:
                        return flow.finish(name)[0][numbers.index(number)]
            if not spread_out:
                spread_out.extend(spread_vectors(flow.finish("first")[1], sizes, place))
            return spread_out[VECTORS.index(number)][layer]

        def step(point, main):
            advanced, started = FORWARD.get(point, ((), ()))
            main = flow.tick(main, *advanced)
            for name in started:
                _, numbers, split_y = CHUNKS[name]
                layout = chunk_rows(weights, numbers, split_y)
                if name == "first":
                    layout = [(1, layout[0][1])]
                flow.start(name, gather_chain(blocks[name], layout, split_y, place))
            return main

        def reduce(layer, *grads):
            name = ("grad", layer, grads[0].number)
            if grads[0].number in (0, 6):
                flow.start(name, reduce_y_first(*grads, place))
            else:
                flow.start(name, reduce_x_first(grads, place))

        def back_step(main, *held):
            return flow.tick(main, *[name for name in flow.running if name not in held])

        def add_up(name, total):
            flow.start(name, reduce_total(total, place))

    else:
        at = jnp.zeros((4,), jnp.int32)

        def get(layer, number):
            whole = lax.all_gather(weights[number][layer], "shard", axis=0, tiled=True)
            return whole.astype(jnp.float32) if number in VECTORS else whole

        def step(point, main):
            return main

        def reduce(layer, *grads):
            for grad in grads:
                own, away = grad.rights
                if not grad.cut:
                    own = jnp.concatenate([own, away], axis=2)
                    own = own.transpose(1, 0, 2).reshape(own.shape[1], -1)
                total = contract_first(grad.left, own)
                total = lax.psum_scatter(total, "shard", scatter_dimension=0, tiled=True)
                total = lax.psum(total.astype(jnp.bfloat16), "rep").astype(jnp.float32)
                flow.done[("grad", layer, grad.number)] = total

        def back_step(main, *held):
            return main

        def add_up(name, total):
            flow.done[name] = lax.psum(total, AXES)

    step("begin", ())
    if fast:
        blocks.update(pack(weights, [name for name in CHUNKS if name != "first"], place))
        segment, parent, clusters, blocks["rest"] = step(
            "packed", (segment, parent, clusters, blocks["rest"])
        )
    slots, bias = step("prepared", prepare(segment, parent, clusters))
    hidden, hidden_low = inputs, inputs
    saved = []
    for layer in range(LAYERS):
        pull = functools.partial(get, layer)
        weight = pull(0)
        if layer == 0:
            weight = step("ready", weight)
        projected = project(hidden_low, weight, path_vectors(pull(1)))
        first = attend(projected, slots, bias, 0, ())
        first = step((layer, "half"), first)
        context, *heads = attend(projected, slots, bias, 1, first)
        context = step((layer, "context"), context)
        context = step((layer, "waited"), context)
        context, *wide = step((layer, "placed"), (context, pull(2), pull(6), pull(8)))
        entered = hidden_low
        middle, act, slope, *norms, hidden, hidden_low = feed(
            context,
            hidden,
            wide,
            [pull(number) for number in (3, 4, 5, 7, 9, 10, 11)],
        )
        saved.append((entered, heads, context, middle, act, slope, norms))
    result = hidden_low
    above, proj = cotangent, None
    sums = [None] * LAYERS
    for layer in reversed(range(LAYERS)):
        entered, heads, context, middle, act, slope, norms = saved[layer]
        pull = functools.partial(get, layer)
        down, grad_pre, grad_attn, attn_low, grad_context, row_sums, ffin_sum = feed_back(
            above,
            proj,
            None if proj is None else get(layer + 1, 0),
            at,
            [norms[2], norms[3], slope, norms[0], norms[1]],
            [pull(2), pull(6), pull(8)],
            [pull(4), pull(10)],
        )
        sums[layer] = [row_sums, ffin_sum, None]
        down = back_step(down)
        wide = grad_pre.shape[1] // CORES
        grad_8 = Grad(8, act, down, down, True, act.shape[1] // D, UNIT)
        grad_2 = Grad(2, context, attn_low, attn_low, True, 1, UNIT)
        if layer == 0:
            reduce(layer, grad_8, grad_2)
            reduce(layer, Grad(6, middle, grad_pre, grad_pre, True, wide // D, D))
        else:
            grad_6 = Grad(6, middle, grad_pre, grad_pre, True, wide // UNIT, UNIT)
            reduce(layer, grad_8, grad_6, grad_2)
        if layer == 0:
            pieces = [qv_sum(sums[1][2])]
            for row_sums, ffin_sum, _ in sums:
                pieces += [row_sums[:6].reshape(-1), ffin_sum[0]]
            add_up("early", jnp.concatenate(pieces))
        above_chain = () if layer else (("grad", 1, 8),)
        grad_context = back_step(grad_context, *above_chain)
        away, away_sums = attend_back(grad_context, slots, heads, at, True)
        wide_chains = (("grad", layer, 8), ("grad", layer, 6))
        grad_context, away = back_step((grad_context, away), *above_chain, *wide_chains)
        own, own_sums = attend_back(grad_context, slots, heads, at, False)
        proj = (own, away)
        reduce(layer, Grad(0, entered, own, away, False, 3, UNIT))
        sums[layer][2] = (own_sums, away_sums, at)
        proj = back_step(proj, *(wide_chains if layer else ()))
        above = grad_attn
    add_up("late", qv_sum(sums[0][2]))
    grad_input = input_grad(above, proj, get(0, 0), at)
    grad_input = back_step(grad_input)
    while flow.running:
        grad_input = back_step(grad_input)
    early, late = flow.finish("early"), flow.finish("late")
    count = lax.axis_size("shard")
    shard = lax.axis_index("shard")
    ff = sums[0][1].shape[1]
    rest = early[2 * D :].reshape(LAYERS, 6 * D + ff)

    def share(stacked):
        width = stacked.shape[1] // count
        return lax.dynamic_slice_in_dim(stacked, shard * width, width, axis=1)

    grads = {1: share(jnp.stack([late, early[: 2 * D]])), 7: share(rest[:, 6 * D :])}
    for number, row in ((10, 0), (11, 1), (9, 2), (4, 3), (5, 4), (3, 5)):
        grads[number] = share(rest[:, row * D : (row + 1) * D])
    if fast:
        done = [{}, {}]
        for name, value in flow.done.items():
            if name[0] == "grad":
                done[name[1]].update(value)
        for numbers in ((8, 6, 2), (0,)):
            shapes = {number: weights[number].shape[1:] for number in numbers}
            grads.update(zip(numbers, join(at, done, shapes)))
    else:
        for number in MATRICES:
            grads[number] = jnp.stack([flow.done[("grad", layer, number)] for layer in range(LAYERS)])
    return (result, grad_input, *[grads[number] for number in range(12)])


def solution(mesh):
    in_specs = (
        P(("rep", "shard"), None),
        P(("rep", "shard"), None),
        P(("rep", "shard")),
        P(("rep", "shard"), None),
        P(None, ("rep", "shard")),
        P(None, "shard", None),
        P(None, "shard"),
        P(None, "shard", None),
        P(None, "shard"),
        P(None, "shard"),
        P(None, "shard"),
        P(None, "shard", None),
        P(None, "shard"),
        P(None, "shard", None),
        P(None, "shard"),
        P(None, "shard"),
        P(None, "shard"),
    )
    out_specs = (
        P(("rep", "shard"), None),
        P(("rep", "shard"), None),
        P(None, "shard", None),
        P(None, "shard"),
        P(None, "shard", None),
        P(None, "shard"),
        P(None, "shard"),
        P(None, "shard"),
        P(None, "shard", None),
        P(None, "shard"),
        P(None, "shard", None),
        P(None, "shard"),
        P(None, "shard"),
        P(None, "shard"),
    )
    fast = mesh.shape["rep"] == CHIPS_Y * CORES and mesh.shape["shard"] == CHIPS_Z * CHIPS_X
    return jax.shard_map(
        functools.partial(local, fast),
        mesh=mesh,
        in_specs=in_specs,
        out_specs=out_specs,
        check_vma=False,
    )
```

```python
import functools

import jax
import jax.numpy as jnp
from jax import lax
from jax.experimental import pallas as pl
from jax.experimental.pallas import tpu as pltpu
from jax.sharding import PartitionSpec as P

D = 768
HEADS = 12
HEAD_DIM = 64
LAYERS = 2
CLUSTER = 128
TREE_LEN = 1024
SEGMENTS = 13
PAIRS = HEADS // 2
LANES = 2 * HEAD_DIM
KERNEL_VMEM = 60 * 2**20
ROW_TILE = 256
FEED_TILE = 768
DEPTH_TILE = 384
INV_ROOT = (2.0 * 3.141592653589793) ** -0.5
MATRICES = (0, 2, 6, 8)
VECTORS = (1, 3, 4, 5, 7, 9, 10, 11)
UNIT = 384
AXES = ("rep", "shard")
CHIPS_Z, CHIPS_X, CHIPS_Y, CORES = 4, 2, 2, 2
norm_eps = 1e-06


def one_hot_rows(slot_row):
    length = slot_row.shape[-1]
    rows = lax.broadcasted_iota(jnp.int32, (length, length), 0)
    return jnp.where(rows == slot_row, 1.0, 0.0).astype(jnp.bfloat16)


def first_lanes(length):
    return lax.broadcasted_iota(jnp.int32, (length, LANES), 1) < HEAD_DIM


def contract_last(left_side, right_side):
    return lax.dot_general(
        left_side, right_side, (((1,), (1,)), ((), ())), preferred_element_type=jnp.float32
    )


def contract_first(left_side, right_side):
    return lax.dot_general(
        left_side, right_side, (((0,), (0,)), ((), ())), preferred_element_type=jnp.float32
    )


def cluster_blocks(values):
    return [values[at : at + CLUSTER] for at in range(0, values.shape[0], CLUSTER)]


def attend_kernel(slot_ref, query_ref, key_ref, value_ref, bias_ref, *refs):
    ctx_ref, qk_ref, val_ref, p_ref = refs[-4:]
    low = first_lanes(TREE_LEN)
    query = query_ref[...] * jnp.bfloat16(HEAD_DIM**-0.5)
    key = key_ref[...]
    value = value_ref[...]
    packed = (
        jnp.where(low, query, pltpu.roll(key, HEAD_DIM, 1)),
        jnp.where(low, pltpu.roll(query, HEAD_DIM, 1), key),
    )
    context = []
    for head in range(2):
        table = one_hot_rows(slot_ref[0, 0, head : head + 1, :])
        joined = jnp.concatenate([packed[head], value], axis=1)
        slots = jnp.dot(table, joined, preferred_element_type=jnp.float32).astype(jnp.bfloat16)
        both, values = slots[:, :LANES], slots[:, LANES:]
        qk_ref[0, head] = both
        val_ref[0, head] = values
        queries = jnp.where(low, both, jnp.bfloat16(0))
        keys = pltpu.roll(both, HEAD_DIM, 1)
        scores = jnp.concatenate(
            [contract_last(q, k) for q, k in zip(cluster_blocks(queries), cluster_blocks(keys))],
            axis=0,
        )
        scores = scores + bias_ref[0, head].astype(jnp.float32)
        numerator = jnp.exp(scores - jnp.max(scores, axis=1, keepdims=True))
        total = jnp.sum(numerator, axis=1, keepdims=True)
        soft = (numerator * (1.0 / total)).astype(jnp.bfloat16)
        p_ref[0, head] = soft
        out = jnp.concatenate(
            [
                jnp.dot(p, v, preferred_element_type=jnp.float32)
                for p, v in zip(cluster_blocks(soft), cluster_blocks(values))
            ],
            axis=0,
        ).astype(jnp.bfloat16)
        context.append(contract_first(table, out))
    ctx_ref[...] = jnp.where(low, context[0], context[1]).astype(jnp.bfloat16)


def attend_back_kernel(at_ref, slot_ref, grad_ref, qk_ref, val_ref, p_ref, out_ref, sums_ref):
    low = first_lanes(TREE_LEN)
    grads = grad_ref[...]
    placed = []
    for head in range(2):
        table = one_hot_rows(slot_ref[0, 0, head : head + 1, :])
        slots = jnp.dot(table, grads, preferred_element_type=jnp.float32)
        slots = jnp.where(low == (head == 0), slots, 0.0).astype(jnp.bfloat16)
        both, values, soft = qk_ref[0, head], val_ref[0, head], p_ref[0, head]
        grad_soft = jnp.concatenate(
            [contract_last(g, v) for g, v in zip(cluster_blocks(slots), cluster_blocks(values))],
            axis=0,
        )
        grad_value = jnp.concatenate(
            [contract_first(p, g) for p, g in zip(cluster_blocks(soft), cluster_blocks(slots))],
            axis=0,
        ).astype(jnp.bfloat16)
        weights = soft.astype(jnp.float32)
        delta = jnp.sum(weights * grad_soft, axis=1, keepdims=True)
        grad_scores = (weights * (grad_soft - delta)).astype(jnp.bfloat16)
        pairs = list(zip(cluster_blocks(grad_scores), cluster_blocks(both)))
        by_key = jnp.concatenate([contract_first(s, b) for s, b in pairs], axis=0)
        by_query = jnp.concatenate(
            [jnp.dot(s, b, preferred_element_type=jnp.float32) for s, b in pairs], axis=0
        )
        mixed = jnp.where(low, by_key, by_query * HEAD_DIM**-0.5).astype(jnp.bfloat16)
        joined = jnp.concatenate([mixed, grad_value], axis=1)
        placed.append(contract_first(table, joined))
    first, second = placed
    queries = jnp.where(low, pltpu.roll(first[:, :LANES], HEAD_DIM, 1), second[:, :LANES])
    keys = jnp.where(low, first[:, :LANES], pltpu.roll(second[:, :LANES], HEAD_DIM, 1))
    values = jnp.where(low, first[:, LANES:], second[:, LANES:])
    sums = []
    for part, grad in enumerate((queries, keys, values)):
        rounded = grad.astype(jnp.bfloat16)
        out_ref[part] = rounded
        sums.append(rows_sum(rounded.astype(jnp.float32)))
    sums_ref[0, 0] = jnp.concatenate(sums + [jnp.zeros((5, LANES), jnp.float32)], axis=0)


def slot_spec(start=0):
    return pl.BlockSpec((1, 1, 2, TREE_LEN), lambda tree, pair: (tree, start + pair, 0, 0))


def head_spec(start=0):
    return pl.BlockSpec((1, 2, TREE_LEN, LANES), lambda tree, pair: (tree, start + pair, 0, 0))


def column_spec(offset):
    return pl.BlockSpec((TREE_LEN, LANES), lambda tree, pair: (tree, offset + pair))


def kernel_params():
    return pltpu.CompilerParams(vmem_limit_bytes=KERNEL_VMEM)


def attend(projected, slots, bias, half, before):
    trees = slots.shape[0]
    start = half * (PAIRS // 2)
    stored = jax.ShapeDtypeStruct((trees, HEADS, TREE_LEN, LANES), jnp.bfloat16)
    return pl.pallas_call(
        attend_kernel,
        grid=(trees, PAIRS // 2),
        in_specs=[
            slot_spec(start),
            column_spec(start),
            column_spec(PAIRS + start),
            column_spec(2 * PAIRS + start),
            head_spec(start),
        ]
        + [pl.BlockSpec(memory_space=pl.ANY)] * len(before),
        out_specs=[column_spec(start), head_spec(start), head_spec(start), head_spec(start)],
        out_shape=[
            jax.ShapeDtypeStruct((trees * TREE_LEN, D), jnp.bfloat16),
            stored,
            stored,
            stored,
        ],
        input_output_aliases={5 + place: place for place in range(len(before))},
        compiler_params=kernel_params(),
        cost_estimate=pl.CostEstimate(
            flops=trees * 15_000_000_000, bytes_accessed=trees * 10_000_000, transcendentals=0
        ),
    )(slots, projected, projected, projected, bias, *before)


def attend_back(grad_context, slots, kept, at, other):
    trees = slots.shape[0]
    count = PAIRS // CORES
    flip = 1 if other else 0

    def pair_of(pair, at):
        return lax.rem(at[3] + flip, CORES) * count + pair

    head = pl.BlockSpec(
        (1, 2, TREE_LEN, LANES), lambda tree, pair, at: (tree, pair_of(pair, at), 0, 0)
    )
    return pl.pallas_call(
        attend_back_kernel,
        grid_spec=pltpu.PrefetchScalarGridSpec(
            num_scalar_prefetch=1,
            grid=(trees, count),
            in_specs=[
                pl.BlockSpec(
                    (1, 1, 2, TREE_LEN), lambda tree, pair, at: (tree, pair_of(pair, at), 0, 0)
                ),
                pl.BlockSpec((TREE_LEN, LANES), lambda tree, pair, at: (tree, pair_of(pair, at))),
                head,
                head,
                head,
            ],
            out_specs=[
                pl.BlockSpec((3, TREE_LEN, LANES), lambda tree, pair, at: (0, tree, pair)),
                pl.BlockSpec((1, 1, 8, LANES), lambda tree, pair, at: (tree, pair, 0, 0)),
            ],
        ),
        out_shape=[
            jax.ShapeDtypeStruct((3, trees * TREE_LEN, D // CORES), jnp.bfloat16),
            jax.ShapeDtypeStruct((trees, count, 8, LANES), jnp.float32),
        ],
        compiler_params=kernel_params(),
        cost_estimate=pl.CostEstimate(
            flops=trees * 17_000_000_000, bytes_accessed=trees * 10_000_000, transcendentals=0
        ),
    )(at, slots, grad_context, *kept)


def erf_parts(values):
    size = jnp.abs(values)
    turn = 1.0 / (1.0 + (0.3275911 * 0.5**0.5) * size)
    bell = jnp.exp(-0.5 * values * values)
    series = 1.061405429 * 0.5
    for factor in (-1.453152027, 1.421413741, -0.284496736, 0.254829592):
        series = series * turn + factor * 0.5
    tail = series * turn * bell
    return jnp.where(values < 0.0, tail, 1.0 - tail), bell


def norm_parts(values):
    centred = values - jnp.mean(values, axis=-1, keepdims=True)
    scale = lax.rsqrt(jnp.mean(centred * centred, axis=-1, keepdims=True) + norm_eps)
    return centred * scale, scale


def norm_back(grad, normal, scale, gain):
    inner = grad * gain
    mean = jnp.mean(inner, axis=-1, keepdims=True)
    along = jnp.mean(inner * normal, axis=-1, keepdims=True)
    return scale * (inner - mean - normal * along)


def spread(column):
    return jnp.broadcast_to(column, (column.shape[0], 128))


def rows_sum(values):
    return jnp.sum(values, axis=0, keepdims=True)


def project_kernel(rows_ref, weight_ref, bias_ref, out_ref):
    product = jnp.dot(rows_ref[...], weight_ref[...], preferred_element_type=jnp.float32)
    out_ref[...] = (product + bias_ref[...]).astype(jnp.bfloat16)


def feed_kernel(
    context_ref,
    rows_ref,
    out_weight_ref,
    ffin_weight_ref,
    ffout_weight_ref,
    out_bias_ref,
    attn_gain_ref,
    attn_shift_ref,
    ffin_bias_ref,
    ffout_bias_ref,
    ffn_gain_ref,
    ffn_shift_ref,
    hidden_ref,
    act_ref,
    slope_ref,
    attn_normal_ref,
    attn_scale_ref,
    ffn_normal_ref,
    ffn_scale_ref,
    result_ref,
    result_low_ref,
):
    product = jnp.dot(context_ref[...], out_weight_ref[...], preferred_element_type=jnp.float32)
    attn_sum = rows_ref[...].astype(jnp.float32) + product + out_bias_ref[...]
    normal, scale = norm_parts(attn_sum)
    attn_normal_ref[...] = normal
    attn_scale_ref[...] = spread(scale)
    hidden = normal * attn_gain_ref[...] + attn_shift_ref[...]
    hidden_low = hidden.astype(jnp.bfloat16)
    hidden_ref[...] = hidden_low
    total = hidden + ffout_bias_ref[...]
    width = ffin_weight_ref.shape[1]
    for at in range(0, width, FEED_TILE):
        part = slice(at, at + FEED_TILE)
        pre = (
            jnp.dot(hidden_low, ffin_weight_ref[:, part], preferred_element_type=jnp.float32)
            + ffin_bias_ref[:, part]
        )
        below, bell = erf_parts(pre)
        act = (pre * below).astype(jnp.bfloat16)
        act_ref[:, part] = act
        slope_ref[:, part] = (below + pre * bell * INV_ROOT).astype(jnp.bfloat16)
        total = total + jnp.dot(
            act, ffout_weight_ref[part, :], preferred_element_type=jnp.float32
        )
    normal, scale = norm_parts(total)
    ffn_normal_ref[...] = normal
    ffn_scale_ref[...] = spread(scale)
    result = normal * ffn_gain_ref[...] + ffn_shift_ref[...]
    result_ref[...] = result
    result_low_ref[...] = result.astype(jnp.bfloat16)


def add_projected(grad, at_ref, own_ref, away_ref, weight_ref):
    half = own_ref.shape[2]
    for flip, ref in enumerate((own_ref, away_ref)):
        core = lax.rem(at_ref[3] + flip, CORES)
        for part in range(3):
            column = pl.multiple_of((part * CORES + core) * half, 128)
            grad = grad + contract_last(ref[part], weight_ref[:, pl.ds(column, half)])
    return grad


def feed_back_kernel(with_proj, *refs):
    if with_proj:
        above_ref, at_ref, own_ref, away_ref, qkv_weight_ref, *refs = refs
        grad = add_projected(above_ref[...], at_ref, own_ref, away_ref, qkv_weight_ref)
    else:
        above_ref, *refs = refs
        grad = above_ref[...].astype(jnp.float32)
    (
        ffn_normal_ref,
        ffn_scale_ref,
        slope_ref,
        attn_normal_ref,
        attn_scale_ref,
        out_weight_ref,
        ffin_weight_ref,
        ffout_weight_ref,
        attn_gain_ref,
        ffn_gain_ref,
        down_ref,
        pre_ref,
        attn_ref,
        attn_low_ref,
        context_ref,
        sums_ref,
        ffin_sum_ref,
    ) = refs

    @pl.when(pl.program_id(0) == 0)
    def _():
        sums_ref[...] = jnp.zeros_like(sums_ref)
        ffin_sum_ref[...] = jnp.zeros_like(ffin_sum_ref)

    normal = ffn_normal_ref[...]
    sums_ref[0:1] += rows_sum(grad * normal)
    sums_ref[1:2] += rows_sum(grad)
    grad_sum = norm_back(grad, normal, ffn_scale_ref[:, 0:1], ffn_gain_ref[...])
    down = grad_sum.astype(jnp.bfloat16)
    down_ref[...] = down
    sums_ref[2:3] += rows_sum(down.astype(jnp.float32))
    total = grad_sum
    width = ffin_weight_ref.shape[1]
    for at in range(0, width, FEED_TILE):
        part = slice(at, at + FEED_TILE)
        grad_act = contract_last(down, ffout_weight_ref[part, :])
        pre = (grad_act * slope_ref[:, part].astype(jnp.float32)).astype(jnp.bfloat16)
        pre_ref[:, part] = pre
        ffin_sum_ref[:, part] += rows_sum(pre.astype(jnp.float32))
        total = total + contract_last(pre, ffin_weight_ref[:, part])
    normal = attn_normal_ref[...]
    sums_ref[3:4] += rows_sum(total * normal)
    sums_ref[4:5] += rows_sum(total)
    attn = norm_back(total, normal, attn_scale_ref[:, 0:1], attn_gain_ref[...])
    attn_ref[...] = attn
    low = attn.astype(jnp.bfloat16)
    attn_low_ref[...] = low
    sums_ref[5:6] += rows_sum(low.astype(jnp.float32))
    context_ref[...] = contract_last(low, out_weight_ref[...]).astype(jnp.bfloat16)


def input_grad_kernel(above_ref, at_ref, own_ref, away_ref, weight_ref, out_ref):
    out_ref[...] = add_projected(above_ref[...], at_ref, own_ref, away_ref, weight_ref)


def prep_kernel(parent_ref, segment_ref, cluster_ref, slot_ref, bias_ref):
    tree = pl.program_id(0)
    segs = segment_ref[0]
    length = segs.shape[1]

    def parent_of(values):
        found = jnp.zeros_like(values)
        for number in range(SEGMENTS):
            found = jnp.where(values == number, parent_ref[tree, number], found)
        return found

    parents = parent_of(segs)
    grands = parent_of(parents)
    ids = jnp.concatenate([segs, parents, grands, jnp.zeros((5, length), jnp.int32)], axis=0)
    ids = jnp.concatenate([ids, jnp.zeros((8, length), jnp.int32)], axis=0)
    ids = ids.astype(jnp.float32).astype(jnp.bfloat16)
    count = length // CLUSTER
    order = lax.broadcasted_iota(jnp.int32, (count, length), 0)
    lanes = lax.broadcasted_iota(jnp.int32, (count, length), 1)
    for head in range(2):
        member = order == cluster_ref[0, 0, head : head + 1, :]
        ranks = member.astype(jnp.int32)
        step = 1
        while step < length:
            ranks = ranks + jnp.where(lanes >= step, pltpu.roll(ranks, step, 1), 0)
            step *= 2
        slot = jnp.sum(
            jnp.where(member, ranks - 1 + CLUSTER * order, 0), axis=0, keepdims=True
        )
        slot_ref[0, 0, head : head + 1, :] = slot
        table = one_hot_rows(slot)
        rows = contract_last(ids, table)
        columns = jnp.concatenate([rows] * (128 // rows.shape[0]), axis=0).T
        for at in range(0, length, CLUSTER):
            here = rows[0:1, at : at + CLUSTER]
            block = columns[at : at + CLUSTER]
            allowed = (
                (here == block[:, 0:1]) | (here == block[:, 1:2]) | (here == block[:, 2:3])
            )
            bias_ref[0, head, at : at + CLUSTER, :] = jnp.where(allowed, 0.0, -1e30).astype(
                jnp.bfloat16
            )


def row_spec(width, rows=ROW_TILE):
    return pl.BlockSpec((rows, width), lambda i: (i, 0))


def whole_spec(shape):
    return pl.BlockSpec(
        shape, lambda i: (0,) * len(shape), pipeline_mode=pl.Buffered(1)
    )


def part_spec(rows=ROW_TILE):
    return pl.BlockSpec((3, rows, D // CORES), lambda i: (0, i, 0))


def cost(flops, *arrays):
    moved = sum(array.size * array.dtype.itemsize for array in arrays)
    return pl.CostEstimate(flops=int(flops), bytes_accessed=moved, transcendentals=0)


def shape_of(rows, width, kind=jnp.bfloat16):
    return jax.ShapeDtypeStruct((rows, width), kind)


def project(rows, weight, bias):
    count, width = rows.shape[0], weight.shape[1]
    return pl.pallas_call(
        project_kernel,
        grid=(count // ROW_TILE,),
        in_specs=[row_spec(D), whole_spec(weight.shape), whole_spec((1, width))],
        out_specs=row_spec(width),
        out_shape=shape_of(count, width),
        compiler_params=kernel_params(),
        cost_estimate=cost(2.4 * count * D * width, rows, weight),
    )(rows, weight, bias[None])


def feed(context, rows, weights, vectors):
    count = context.shape[0]
    width = weights[1].shape[1]
    f32 = jnp.float32
    vectors = [vector[None] for vector in vectors]
    return pl.pallas_call(
        feed_kernel,
        grid=(count // ROW_TILE,),
        in_specs=[row_spec(D), row_spec(D)]
        + [whole_spec(weight.shape) for weight in weights]
        + [whole_spec(vector.shape) for vector in vectors],
        out_specs=[
            row_spec(D),
            row_spec(width),
            row_spec(width),
            row_spec(D),
            row_spec(128),
            row_spec(D),
            row_spec(128),
            row_spec(D),
            row_spec(D),
        ],
        out_shape=[
            shape_of(count, D),
            shape_of(count, width),
            shape_of(count, width),
            shape_of(count, D, f32),
            shape_of(count, 128, f32),
            shape_of(count, D, f32),
            shape_of(count, 128, f32),
            shape_of(count, D, f32),
            shape_of(count, D),
        ],
        compiler_params=kernel_params(),
        cost_estimate=cost(5 * count * D * (2 * width + D), context, *weights),
    )(context, rows, *weights, *vectors)


def feed_back(above, proj, qkv_weight, at, saved, weights, gains):
    count = above.shape[0]
    width = weights[1].shape[1]
    f32 = jnp.float32
    gains = [gain[None] for gain in gains]
    lead, lead_specs = [above], [row_spec(D)]
    if proj is not None:
        lead += [at, *proj, qkv_weight]
        lead_specs += [
            pl.BlockSpec(memory_space=pltpu.SMEM),
            part_spec(),
            part_spec(),
            whole_spec(qkv_weight.shape),
        ]
    return pl.pallas_call(
        functools.partial(feed_back_kernel, proj is not None),
        grid=(count // ROW_TILE,),
        in_specs=lead_specs
        + [row_spec(D), row_spec(128), row_spec(width), row_spec(D), row_spec(128)]
        + [whole_spec(weight.shape) for weight in weights]
        + [whole_spec(gain.shape) for gain in gains],
        out_specs=[
            row_spec(D),
            row_spec(width),
            row_spec(D),
            row_spec(D),
            row_spec(D),
            pl.BlockSpec((8, D), lambda i: (0, 0)),
            pl.BlockSpec((1, width), lambda i: (0, 0)),
        ],
        out_shape=[
            shape_of(count, D),
            shape_of(count, width),
            shape_of(count, D, f32),
            shape_of(count, D),
            shape_of(count, D),
            shape_of(8, D, f32),
            shape_of(1, width, f32),
        ],
        compiler_params=kernel_params(),
        cost_estimate=cost(5 * count * D * (2 * width + D), above, *weights),
    )(*lead, *saved, *weights, *gains)


def input_grad(above, proj, qkv_weight, at):
    count = above.shape[0]
    return pl.pallas_call(
        input_grad_kernel,
        grid=(count // ROW_TILE,),
        in_specs=[
            row_spec(D),
            pl.BlockSpec(memory_space=pltpu.SMEM),
            part_spec(),
            part_spec(),
            whole_spec(qkv_weight.shape),
        ],
        out_specs=row_spec(D),
        out_shape=shape_of(count, D, jnp.float32),
        compiler_params=kernel_params(),
        cost_estimate=cost(2.4 * count * D * 3 * D, above, qkv_weight),
    )(above, at, *proj, qkv_weight)


def prepare(segment, parent, clusters):
    trees = parent.shape[0]
    segment = segment.reshape(trees, 1, TREE_LEN)
    clusters = clusters.reshape(PAIRS, 2, trees, TREE_LEN).transpose(2, 0, 1, 3)
    return pl.pallas_call(
        prep_kernel,
        grid=(trees, PAIRS),
        in_specs=[
            pl.BlockSpec(memory_space=pltpu.SMEM),
            pl.BlockSpec((1, 1, TREE_LEN), lambda tree, pair: (tree, 0, 0)),
            slot_spec(),
        ],
        out_specs=[slot_spec(), head_spec()],
        out_shape=[
            jax.ShapeDtypeStruct((trees, PAIRS, 2, TREE_LEN), jnp.int32),
            jax.ShapeDtypeStruct((trees, HEADS, TREE_LEN, LANES), jnp.bfloat16),
        ],
        compiler_params=kernel_params(),
        cost_estimate=pl.CostEstimate(
            flops=trees * 20_000_000_000, bytes_accessed=trees * 4_000_000, transcendentals=0
        ),
    )(parent, segment, clusters)


def weight_grad_kernel(split_y, at_ref, left_ref, right_ref, *refs):
    product = contract_first(
        left_ref[...].reshape(left_ref.shape[-2:]), right_ref[...].reshape(right_ref.shape[-2:])
    )
    if split_y is None:
        (out_ref,) = refs
        out_ref[...] = product.astype(jnp.bfloat16).reshape(out_ref.shape)
        return
    near_ref, (send_ref, keep_ref, sum_ref) = refs[0], refs[-3:]
    total = product + near_ref[...].astype(jnp.float32).reshape(product.shape)
    sum_ref[...] = total.astype(jnp.bfloat16).reshape(sum_ref.shape)
    if split_y:
        send_ref[0] = sum_ref[:, :, 1 - at_ref[2]]
        keep_ref[0] = sum_ref[:, :, at_ref[2]]
    else:
        send_ref[...] = sum_ref[:, 1 - at_ref[1]]
        keep_ref[...] = sum_ref[:, at_ref[1]]


class Grad:
    def __init__(self, number, left, own, away, cut, tiles, half):
        self.number = number
        self.left, self.rights = left, (own, away)
        self.cut, self.tiles, self.half = cut, tiles, half
        self.depth = left.shape[1]
        self.parts = 1 if self.depth > D else tiles
        self.rows = self.depth // (CHIPS_Z * CHIPS_X)

    def product(self, at, other, split_y=None, near=None, start=0, total=0, before=()):
        flip = 1 if other else 0
        left, right = self.left, self.rights[flip]
        count = left.shape[0]
        tall = self.depth > D
        core = lambda at: lax.rem(at[3] + flip, CORES)
        in_specs = [
            pl.BlockSpec((count, D), (lambda i, at: (0, i)) if tall else (lambda i, at: (0, 0)))
        ]
        if not self.cut:
            in_specs.append(pl.BlockSpec((1, count, self.half), lambda i, at: (i, 0, 0)))
        elif tall:
            in_specs.append(pl.BlockSpec((count, self.half), lambda i, at: (0, core(at))))
        else:
            in_specs.append(
                pl.BlockSpec((count, self.half), lambda i, at: (0, core(at) * self.tiles + i))
            )
        zs = D // (self.rows * CHIPS_X)
        place = (lambda i: (0, i)) if tall else (lambda i: (i, 0))
        whole = (self.parts, CHIPS_Z, CHIPS_X, self.rows, self.half)
        block = (1, zs, CHIPS_X, self.rows, self.half)
        full = pl.BlockSpec(block, lambda i, at: (*place(i), 0, 0, 0))
        args, scratch = [left, right], []
        if split_y is None:
            out_specs, shapes = full, jax.ShapeDtypeStruct(whole, jnp.bfloat16)
        else:
            in_specs.append(full)
            args.append(near)
            in_specs += [pl.BlockSpec(memory_space=pl.ANY)] * len(before)
            args += before
            if split_y:
                short = self.rows // CHIPS_Y
                kept = (CHIPS_X, short, self.half)
                scratch = [pltpu.VMEM((zs, CHIPS_X, CHIPS_Y, short, self.half), jnp.bfloat16)]
                spec = pl.BlockSpec((1, zs, *kept), lambda i, at: (*place(i), 0, 0, 0))
                shape = (self.parts, CHIPS_Z, *kept)
            else:
                scratch = [pltpu.VMEM((zs, CHIPS_X, self.rows, self.half), jnp.bfloat16)]
                first = start // self.rows
                index = (lambda i, at: (i, first, 0)) if tall else (lambda i, at: (0, first + i, 0))
                spec = pl.BlockSpec((zs, self.rows, self.half), index)
                shape = (CHIPS_Z, total, self.half)
            out_specs, shapes = [spec] * 2, [jax.ShapeDtypeStruct(shape, jnp.bfloat16)] * 2
        return pl.pallas_call(
            functools.partial(weight_grad_kernel, split_y),
            grid_spec=pltpu.PrefetchScalarGridSpec(
                num_scalar_prefetch=1,
                grid=(self.tiles,),
                in_specs=in_specs,
                out_specs=out_specs,
                scratch_shapes=scratch,
            ),
            out_shape=shapes,
            input_output_aliases={4 + place: place for place in range(len(before))},
            compiler_params=kernel_params(),
            cost_estimate=cost(4 * count * D * self.tiles * self.half, left, right),
        )(at, *args)


def combine_kernel(groups, at_ref, *refs):
    total = sum(groups)
    ins, outs = refs[:total], refs[total:]
    first = 0
    for count, out_ref in zip(groups, outs):
        value = None
        for ref in ins[first : first + count]:
            term = ref[...].astype(jnp.float32).reshape(out_ref.shape)
            value = term if value is None else value + term
        out_ref[...] = value.astype(out_ref.dtype)
        first += count


def combine(at, steps, groups, blocks):
    terms = [term for group in groups for term in group]
    return pl.pallas_call(
        functools.partial(combine_kernel, [len(group) for group in groups]),
        grid_spec=pltpu.PrefetchScalarGridSpec(
            num_scalar_prefetch=1,
            grid=(steps,),
            in_specs=[pl.BlockSpec(block, index) for _, block, index in terms],
            out_specs=[pl.BlockSpec(block, index) for _, block, index in blocks],
        ),
        out_shape=[jax.ShapeDtypeStruct(shape, jnp.bfloat16) for shape, _, _ in blocks],
        compiler_params=kernel_params(),
        cost_estimate=pl.CostEstimate(
            flops=0, bytes_accessed=2_000_000, transcendentals=0
        ),
    )(at, *[array for array, _, _ in terms])


CHUNKS = {
    "first": (0, (0,), False),
    "rest": (0, (2, 6, 8), True),
    "next": (1, (0, 2), False),
    "last": (1, (6, 8), False),
}
FORWARD = {
    "begin": ((), ("first",)),
    "packed": (("first",), ("rest",)),
    "prepared": (("first",), ()),
    "ready": (("rest",), ("next",)),
    (0, "half"): (("rest", "next"), ("last",)),
    (0, "context"): (("next",), ()),
    (0, "waited"): (("rest",), ()),
    (0, "placed"): (("last",), ()),
    (1, "half"): (("last",), ()),
}


class Place:
    def __init__(self):
        rep = lax.axis_index("rep")
        shard = lax.axis_index("shard")
        self.y, self.core = rep // CORES, rep % CORES
        self.z, self.x = shard // CHIPS_X, shard % CHIPS_X
        self.at = jnp.stack([self.z, self.x, self.y, self.core]).astype(jnp.int32)


def hop(value, dz=0, dx=0, dy=0, dc=0):
    pairs = []
    for y in range(CHIPS_Y):
        for c in range(CORES):
            for z in range(CHIPS_Z):
                for x in range(CHIPS_X):
                    source = ((y * CORES + c) * CHIPS_Z + z) * CHIPS_X + x
                    y2, c2 = (y + dy) % CHIPS_Y, (c + dc) % CORES
                    z2, x2 = (z + dz) % CHIPS_Z, (x + dx) % CHIPS_X
                    pairs.append((source, ((y2 * CORES + c2) * CHIPS_Z + z2) * CHIPS_X + x2))
    return lax.ppermute(value, AXES, pairs)


def pack_kernel(plan, at_ref, *refs):
    ins, outs = refs[: len(MATRICES)], refs[len(MATRICES) :]
    for out_ref, (layer, numbers, split_y) in zip(outs, plan):
        start = 0
        for number in numbers:
            ref = ins[MATRICES.index(number)]
            rows, half = ref.shape[1], ref.shape[2] // CORES
            first = 0
            if split_y:
                rows = rows // CHIPS_Y
                first = pl.multiple_of(at_ref[2] * rows, 16)
            for at in range(0, half, UNIT):
                column = pl.multiple_of(at_ref[3] * half + at, 128)
                out_ref[start : start + rows] = ref[layer, pl.ds(first, rows), pl.ds(column, UNIT)]
                start += rows


def chunk_rows(weights, numbers, split_y):
    found = []
    for number in numbers:
        _, rows, columns = weights[number].shape
        found.append((columns // (CORES * UNIT), rows // (CHIPS_Y if split_y else 1)))
    return found


def pack(weights, names, place):
    plan = [CHUNKS[name] for name in names]
    shapes = []
    for _, numbers, split_y in plan:
        shapes.append((sum(u * r for u, r in chunk_rows(weights, numbers, split_y)), UNIT))
    matrices = [weights[number] for number in MATRICES]
    packed = pl.pallas_call(
        functools.partial(pack_kernel, plan),
        grid_spec=pltpu.PrefetchScalarGridSpec(
            num_scalar_prefetch=1,
            grid=(1,),
            in_specs=[pl.BlockSpec(matrix.shape, lambda i, at: (0, 0, 0)) for matrix in matrices],
            out_specs=[pl.BlockSpec(shape, lambda i, at: (0, 0)) for shape in shapes],
        ),
        out_shape=[jax.ShapeDtypeStruct(shape, jnp.bfloat16) for shape in shapes],
        compiler_params=kernel_params(),
        cost_estimate=cost(0, *matrices),
    )(place.at, *matrices)
    return dict(zip(names, packed))


def place_kernel(layout, split_y, count, at_ref, *refs):
    pieces, outs = refs[:count], refs[count:]
    for number, piece in enumerate(pieces):
        core = (at_ref[3] + number % CORES) % CORES
        x = (at_ref[1] + number // CORES % CHIPS_X) % CHIPS_X
        row = (at_ref[2] + number // (CORES * CHIPS_X)) % CHIPS_Y if split_y else 0
        start, unit = 0, piece.shape[2]
        for out_ref, (units, rows) in zip(outs, layout):
            for at in range(units):
                column = pl.multiple_of((core * units + at) * unit, 128)
                out_ref[x, row, :, pl.ds(column, unit)] = piece[0, start : start + rows]
                start += rows


def place_pieces(pieces, layout, split_y, place):
    _, held, unit = pieces[0].shape
    splits = CHIPS_Y if split_y else 1
    shapes = [(CHIPS_Z * CHIPS_X, splits, rows, CORES * units * unit) for units, rows in layout]
    wholes = pl.pallas_call(
        functools.partial(place_kernel, layout, split_y, len(pieces)),
        grid_spec=pltpu.PrefetchScalarGridSpec(
            num_scalar_prefetch=1,
            grid=(CHIPS_Z,),
            in_specs=[pl.BlockSpec((1, held, unit), lambda k, at: (k, 0, 0))] * len(pieces),
            out_specs=[
                pl.BlockSpec(
                    (CHIPS_X, *shape[1:]),
                    lambda k, at: (lax.rem(at[0] + CHIPS_Z - k, CHIPS_Z), 0, 0, 0),
                )
                for shape in shapes
            ],
        ),
        out_shape=[jax.ShapeDtypeStruct(shape, jnp.bfloat16) for shape in shapes],
        compiler_params=kernel_params(),
        cost_estimate=pl.CostEstimate(
            flops=0,
            bytes_accessed=4 * CHIPS_Z * len(pieces) * held * unit,
            transcendentals=0,
        ),
    )(place.at, *pieces)
    return [whole.reshape(-1, whole.shape[-1]) for whole in wholes]


def gather_chain(block, layout, split_y, place):
    parts = yield [hop(block, dz=k) for k in range(1, CHIPS_Z)]
    stack = jnp.stack([block, *parts])
    (across,) = yield [hop(stack, dx=1)]
    pieces = [stack, across]
    if split_y:
        pieces = pieces + (yield [hop(piece, dy=1) for piece in pieces])
    others = yield [hop(piece, dc=1) for piece in pieces]
    wholes = place_pieces(
        [item for pair in zip(pieces, others) for item in pair], layout, split_y, place
    )
    rows = sum(units * tall for units, tall in layout)
    return wholes, jnp.stack([stack[:, rows:], across[:, rows:]], axis=1)


class Flow:
    def __init__(self):
        self.running, self.done = {}, {}

    def start(self, name, chain):
        self.running[name] = (chain, next(chain))

    def advance(self, name, arrived):
        chain, _ = self.running.pop(name)
        try:
            self.running[name] = (chain, chain.send(list(arrived)))
        except StopIteration as end:
            self.done[name] = end.value

    def tick(self, main, *names):
        names = [name for name in names if name in self.running]
        pending = [self.running[name][1] for name in names]
        main, pending = lax.optimization_barrier((main, pending))
        for name, arrived in zip(names, pending):
            self.advance(name, arrived)
        return main

    def finish(self, name):
        while name in self.running:
            self.advance(name, self.running[name][1])
        return self.done[name]


def spread_vectors(stack, sizes, place):
    count = CHIPS_Z * CHIPS_X
    stack = stack[:, :, :LAYERS].reshape(count, LAYERS, -1).astype(jnp.float32)
    wanted = jnp.arange(count, dtype=jnp.int32)
    behind = (place.z - wanted // CHIPS_X) % CHIPS_Z * CHIPS_X + (
        place.x - wanted % CHIPS_X
    ) % CHIPS_X
    turn = (behind[:, None] == wanted[None, :]).astype(jnp.float32)
    stack = jnp.sum(turn[:, :, None, None] * stack[None], axis=1)
    out, at = [], 0
    for size in sizes:
        out.append(
            stack[:, :, at : at + size].transpose(1, 0, 2).reshape(LAYERS, count * size)
        )
        at += size
    return out


def first_block(weights, place):
    shard = weights[0][0]
    half = shard.shape[1] // CORES
    block = lax.dynamic_slice_in_dim(shard, place.core * half, half, axis=1)
    vectors = jnp.concatenate([weights[member] for member in VECTORS], axis=1)
    return jnp.concatenate([block, jnp.pad(vectors, ((0, 16 - LAYERS), (0, 0)))])


def pick_sum(at, own, terms, rows, steps):
    groups = [[(array, block, index(k)) for array, block, index in terms] for k in range(CHIPS_Z)]
    return combine(at, steps, groups, [own] * CHIPS_Z)


def reduce_y_first(grad, place, stop=None):
    at = place.at
    parts, half = grad.parts, grad.half
    rows = grad.rows // CHIPS_Y
    away = grad.product(at, True)
    (near,) = yield [hop(away, dc=1)]
    send, keep = grad.product(at, False, True, near)
    if stop == "sums":
        return send, keep, False
    flip = lambda value: 1 - value
    (over,) = yield [hop(send, dy=1)]
    if stop == "y":
        return over, keep, True
    block = (parts, 1, 1, rows, half)
    short = (parts, 1, rows, half)
    index = lambda i, at: (0, i, flip(at[1]), 0, 0)
    (send,) = combine(
        at,
        CHIPS_Z,
        [[(keep, block, index), (over, block, index)]],
        [((parts, CHIPS_Z, rows, half), short, lambda i, at: (0, i, 0, 0))],
    )
    (across,) = yield [hop(send, dx=1)]
    turn = lambda at, k: lax.rem(at[0] + k, CHIPS_Z)
    mine = lambda k: lambda i, at: (0, turn(at, k), at[1], 0, 0)
    piece = (parts, rows, half)
    whole = (piece, piece, lambda i, at: (0, 0, 0))
    own, *sends = pick_sum(
        at,
        whole,
        [
            (keep, block, mine),
            (over, block, mine),
            (across, short, lambda k: lambda i, at: (0, turn(at, k), 0, 0)),
        ],
        rows,
        1,
    )
    landed = yield [hop(send, dz=k) for k, send in zip(range(1, CHIPS_Z), sends)]
    (own,) = combine(at, 1, [[(term, piece, whole[2]) for term in (own, *landed)]], [whole])
    others = yield [hop(own, dy=1), hop(own, dc=1), hop(own, dy=1, dc=1)]
    pieces = [item.reshape(parts * rows, half) for item in (own, *others)]
    return {grad.number: (pieces, 0, rows)}


def reduce_x_first(grads, place, stop):
    at = place.at
    away = [grad.product(at, True) for grad in grads]
    near = yield [hop(item, dc=1) for item in away]
    total = sum(grad.parts * grad.rows for grad in grads)
    starts, flat = [0], ()
    for grad, item in zip(grads, near):
        flat = grad.product(at, False, False, item, starts[-1], total, tuple(flat))
        starts.append(starts[-1] + grad.parts * grad.rows)
    send, keep = flat
    (across,) = yield [hop(send, dx=1)]
    if stop == "x":
        return across, keep
    steps = 3
    tall = total // steps
    ahead = lambda k: lambda i, at: (lax.rem(at[0] + k, CHIPS_Z), i, 0)
    piece = ((total, UNIT), (tall, UNIT), lambda i, at: (i, 0))
    own, *sends = pick_sum(
        at, piece, [(item, (1, tall, UNIT), ahead) for item in (keep, across)], tall, steps
    )
    landed = yield [hop(send, dz=k) for k, send in zip(range(1, CHIPS_Z), sends)]
    add = lambda *terms: combine(at, steps, [[(term, *piece[1:]) for term in terms]], [piece])[0]
    return add(own, *landed)


def tail_kernel(arrived, *refs):
    take = iter(refs)
    count = len(arrived)
    a_in, a_keep = next(take), next(take)
    b_ins = [(next(take), next(take)) for _ in range(count)]
    l_in, vec = next(take), next(take)
    a_own, a_other = next(take), next(take)
    b_outs = [next(take) for _ in range(count)]
    l_own, l_other, vec_out = next(take), next(take), next(take)
    a_zsend, a_zland, a_ysend, a_yland, a_cland = [next(take) for _ in range(5)]
    b_scratch = [[next(take) for _ in range(6)] for _ in range(count)]
    l_yland, l_cland = next(take), next(take)
    v_send, v_land = next(take), next(take)
    a_sems, b_sems, v_sems = next(take), [next(take) for _ in range(count)], next(take)
    rep, shard = lax.axis_index("rep"), lax.axis_index("shard")
    y, core = lax.div(rep, CORES), lax.rem(rep, CORES)
    z, x = lax.div(shard, CHIPS_X), lax.rem(shard, CHIPS_X)

    def device(dz=0, dx=0, dy=0, dc=0):
        to_y, to_core = lax.rem(y + dy, CHIPS_Y), lax.rem(core + dc, CORES)
        to_z, to_x = lax.rem(z + dz, CHIPS_Z), lax.rem(x + dx, CHIPS_X)
        return (to_y * CORES + to_core, to_z * CHIPS_X + to_x)

    flip_z = 1 + 2 * lax.rem(z, 2)
    mates = [dict(dx=1), dict(dy=1), dict(dc=1), dict(dy=1, dc=1)]
    mates += [dict(dz=k) for k in range(1, CHIPS_Z)]
    barrier = pltpu.get_barrier_semaphore()
    for mate in mates:
        pl.semaphore_signal(
            barrier, inc=1, device_id=device(**mate), device_id_type=pl.DeviceIdType.MESH
        )
    pl.semaphore_wait(barrier, len(mates))
    sent = []

    def send(source, target, sems, number, **step):
        copy = pltpu.make_async_remote_copy(
            src_ref=source,
            dst_ref=target,
            send_sem=sems.at[0, number],
            recv_sem=sems.at[1, number],
            device_id=device(**step),
            device_id_type=pl.DeviceIdType.MESH,
        )
        copy.start()
        sent.append(copy)
        return copy

    def wide(value):
        return value.astype(jnp.float32)

    order = (2, 1, 3, 0)
    ahead = [lax.rem(z + k, CHIPS_Z) for k in order]
    v_send[0] = vec[...]
    v_copies = [send(v_send.at[0], v_land.at[0], v_sems, 0, dc=1)]
    a_across = a_in
    l_y = send(l_in, l_yland, a_sems, 0, dy=1)
    b_y = [[] for _ in range(count)]
    for j, to in enumerate(ahead):
        for i, (b_send, _) in enumerate(b_ins):
            if arrived[i]:
                continue
            b_y[i].append(send(b_send.at[:, to], b_scratch[i][0].at[j], b_sems[i], j, dy=1))
    steps = (dict(dc=1), dict(dy=1), dict(dx=1), dict(dz=2), dict(dz=flip_z))

    def add_vectors(s):
        v_copies[s].wait_recv()
        total = v_send[s] + v_land[s]
        if s + 1 == len(steps):
            vec_out[...] = total
        else:
            v_send[s + 1] = total
            v_copies.append(
                send(v_send.at[s + 1], v_land.at[s + 1], v_sems, s + 1, **steps[s + 1])
            )

    def over(i, j, side):
        if arrived[i]:
            return wide(b_ins[i][0][:, ahead[j], side])
        return wide(b_scratch[i][0][j, :, side])

    a_z, b_x, b_z = [], [[] for _ in range(count)], [[] for _ in range(count)]

    def b_along_z(j):
        k = order[j]
        for i, (_, keep) in enumerate(b_ins):
            _, _, x_land, z_send, z_land, _ = b_scratch[i]
            b_x[i][j].wait_recv()
            if k:
                total = wide(keep[:, ahead[j], x]) + over(i, j, x) + wide(x_land[j])
                z_send[k - 1] = total.astype(jnp.bfloat16)
                b_z[i].append(
                    send(z_send.at[k - 1], z_land.at[k - 1], b_sems[i], 7 + k, dz=k)
                )

    for j, k in enumerate(order):
        if k:
            total = wide(a_keep[ahead[j]]) + wide(a_across[ahead[j]])
            a_zsend[k - 1] = total.astype(jnp.bfloat16)
            a_z.append(send(a_zsend.at[k - 1], a_zland.at[k - 1], a_sems, 3 + k, dz=k))
        for i, (_, keep) in enumerate(b_ins):
            _, x_send, x_land, *_ = b_scratch[i]
            if not arrived[i]:
                b_y[i][j].wait_recv()
            total = wide(keep[:, ahead[j], 1 - x]) + over(i, j, 1 - x)
            x_send[j] = total.astype(jnp.bfloat16)
            b_x[i].append(send(x_send.at[j], x_land.at[j], b_sems[i], 4 + j, dx=1))
        if j:
            b_along_z(j - 1)
        add_vectors(j)
    b_along_z(CHIPS_Z - 1)
    l_y.wait_recv()
    l_own[...] = (wide(l_in[...]) + wide(l_yland[...])).astype(jnp.bfloat16)
    ends = [send(l_own, l_cland, a_sems, 1, dc=1)]
    add_vectors(4)
    for copy in a_z:
        copy.wait_recv()
    total = wide(a_keep[z]) + wide(a_across[z])
    for k in range(CHIPS_Z - 1):
        total = total + wide(a_zland[k])
    a_ysend[...] = total.astype(jnp.bfloat16)
    a_y = send(a_ysend, a_yland, a_sems, 7, dy=1)
    for i, (_, keep) in enumerate(b_ins):
        _, _, x_land, _, z_land, end_land = b_scratch[i]
        for copy in b_z[i]:
            copy.wait_recv()
        total = wide(keep[:, z, x]) + over(i, 3, x) + wide(x_land[3])
        for k in range(CHIPS_Z - 1):
            total = total + wide(z_land[k])
        b_outs[i][0] = total.astype(jnp.bfloat16)
        for number, step in enumerate((dict(dy=1), dict(dc=1), dict(dy=1, dc=1))):
            ends.append(
                send(b_outs[i].at[0], end_land.at[number], b_sems[i], 11 + number, **step)
            )
    a_y.wait_recv()
    a_own[...] = (wide(a_ysend[...]) + wide(a_yland[...])).astype(jnp.bfloat16)
    ends.append(send(a_own, a_cland, a_sems, 8, dc=1))
    for copy in ends:
        copy.wait_recv()
    for i in range(count):
        b_outs[i][1:4] = b_scratch[i][5][...]
    a_other[...] = a_cland[...]
    l_other[...] = l_cland[...]
    for copy in sent:
        copy.wait_send()


def reduce_tail(flat, pairs, last, vec):
    low = jnp.bfloat16
    _, total, unit = flat[0].shape
    whole = pl.BlockSpec(memory_space=pltpu.VMEM)
    far = pl.BlockSpec(memory_space=pl.ANY)
    piece = (total, unit)
    outs = [piece, piece]
    scratch = [(CHIPS_Z - 1, *piece), (CHIPS_Z - 1, *piece), piece, piece, piece]
    args, specs, arrived = [*flat], [whole, whole], []
    for first, keep, here in pairs:
        parts, _, _, rows, half = keep.shape
        block = (parts, rows, half)
        args += [first, keep]
        specs += [whole if here else far, whole]
        arrived.append(here)
        outs.append((CORES * CHIPS_Y, *block))
        scratch += [
            (16, 128) if here else (CHIPS_Z, parts, CHIPS_X, rows, half),
            (CHIPS_Z, *block),
            (CHIPS_Z, *block),
            (CHIPS_Z - 1, *block),
            (CHIPS_Z - 1, *block),
            (CORES * CHIPS_Y - 1, *block),
        ]
    outs += [last.shape, last.shape]
    scratch += [last.shape, last.shape]
    shapes = [jax.ShapeDtypeStruct(shape, low) for shape in outs]
    shapes.append(jax.ShapeDtypeStruct(vec.shape, jnp.float32))
    scratch = [pltpu.VMEM(shape, low) for shape in scratch]
    scratch += [pltpu.VMEM((5, *vec.shape), jnp.float32)] * 2
    scratch += [pltpu.SemaphoreType.DMA((2, 9))]
    scratch += [pltpu.SemaphoreType.DMA((2, 14))] * len(pairs)
    scratch += [pltpu.SemaphoreType.DMA((2, 5))]
    own, other, *rest = pl.pallas_call(
        functools.partial(tail_kernel, arrived),
        in_specs=[*specs, whole, whole],
        out_specs=[whole] * len(shapes),
        out_shape=shapes,
        scratch_shapes=scratch,
        compiler_params=pltpu.CompilerParams(
            vmem_limit_bytes=KERNEL_VMEM, collective_id=0, has_side_effects=True
        ),
        cost_estimate=pl.CostEstimate(flops=0, bytes_accessed=200_000_000, transcendentals=0),
    )(*args, last, vec)
    return [own, other], rest[:-3], list(rest[-3:-1]), rest[-1]


def join_kernel(plan, count, at_ref, *refs):
    for ref, out, layer, outer, parts, dc, dy, start, rows in plan:
        ref, out_ref = refs[ref], refs[count + out]
        half = ref.shape[1]
        core = lax.rem(at_ref[3] + dc, CORES)
        row = 0
        if dy is not None:
            row = pl.multiple_of(lax.rem(at_ref[2] + dy, CHIPS_Y) * rows, 16)
        for part in range(parts):
            column = part * CORES + core if outer else core * parts + part
            column = pl.multiple_of(column * half, 128)
            value = ref[start + part * rows : start + (part + 1) * rows]
            out_ref[layer, pl.ds(row, rows), pl.ds(column, half)] = value.astype(jnp.float32)


def join(at, done, shapes):
    arrays, plan = [], []
    for out, (number, (tall, wide)) in enumerate(shapes.items()):
        for layer in range(LAYERS):
            pieces, start, rows = done[layer][number]
            for place, piece in enumerate(pieces):
                known = [other is piece for other in arrays]
                if not any(known):
                    arrays.append(piece)
                    known.append(True)
                parts = wide // (CORES * piece.shape[1])
                dy, dc = (place % CHIPS_Y, place // CHIPS_Y) if len(pieces) > CORES else (None, place)
                plan.append((known.index(True), out, layer, number == 0, parts, dc, dy, start, rows))
    zeros = lambda i, at: (0, 0)
    outs = [(LAYERS, *shape) for shape in shapes.values()]
    return pl.pallas_call(
        functools.partial(join_kernel, plan, len(arrays)),
        grid_spec=pltpu.PrefetchScalarGridSpec(
            num_scalar_prefetch=1,
            grid=(1,),
            in_specs=[pl.BlockSpec(array.shape, zeros) for array in arrays],
            out_specs=[pl.BlockSpec(out, lambda i, at: (0, 0, 0)) for out in outs],
        ),
        out_shape=[jax.ShapeDtypeStruct(out, jnp.float32) for out in outs],
        compiler_params=kernel_params(),
        cost_estimate=pl.CostEstimate(flops=0, bytes_accessed=4_000_000, transcendentals=0),
    )(at, *arrays)


def qv_sum(halves):
    own, away, at = halves
    own, away = jnp.sum(own, axis=0), jnp.sum(away, axis=0)
    order = jnp.where(
        at[3] == 0, jnp.concatenate([own, away], axis=0), jnp.concatenate([away, own], axis=0)
    )
    return jnp.concatenate([order[:, part].reshape(D) for part in (0, 2)])


def path_vectors(qv_bias):
    low = qv_bias.astype(jnp.float32)
    return jnp.concatenate([low[:D], jnp.zeros((D,), jnp.float32), low[D:]])


def local(
    fast,
    inputs,
    cotangent,
    segment,
    parent,
    clusters,
    *weights,
):
    flow = Flow()
    if fast:
        place = Place()
        at = place.at
        sizes = [weights[number].shape[1] for number in VECTORS]
        spread_out = []

        blocks = {"first": first_block(weights, place)}

        def get(layer, number):
            if number not in VECTORS:
                for name, (chunk_layer, numbers, _) in CHUNKS.items():
                    if chunk_layer == layer and number in numbers:
                        return flow.finish(name)[0][numbers.index(number)]
            if not spread_out:
                spread_out.extend(spread_vectors(flow.finish("first")[1], sizes, place))
            return spread_out[VECTORS.index(number)][layer]

        def step(point, main):
            advanced, started = FORWARD.get(point, ((), ()))
            main = flow.tick(main, *advanced)
            for name in started:
                _, numbers, split_y = CHUNKS[name]
                layout = chunk_rows(weights, numbers, split_y)
                if name == "first":
                    layout = [(1, layout[0][1])]
                flow.start(name, gather_chain(blocks[name], layout, split_y, place))
            return main

        def reduce(layer, *grads):
            name = ("grad", layer, grads[0].number)
            if name[2] == 0:
                chain = reduce_y_first(*grads, place, None if layer else "sums")
            elif name[2] == 6:
                chain = reduce_y_first(*grads, place, "y")
            else:
                chain = reduce_x_first(grads, place, "z" if layer else "x")
            flow.start(name, chain)

        def back_step(main, *held):
            return flow.tick(main, *[name for name in flow.running if name not in held])

    else:
        at = jnp.zeros((4,), jnp.int32)

        def get(layer, number):
            whole = lax.all_gather(weights[number][layer], "shard", axis=0, tiled=True)
            return whole.astype(jnp.float32) if number in VECTORS else whole

        def step(point, main):
            return main

        def reduce(layer, *grads):
            for grad in grads:
                own, away = grad.rights
                if not grad.cut:
                    own = jnp.concatenate([own, away], axis=2)
                    own = own.transpose(1, 0, 2).reshape(own.shape[1], -1)
                total = contract_first(grad.left, own)
                total = lax.psum_scatter(total, "shard", scatter_dimension=0, tiled=True)
                total = lax.psum(total.astype(jnp.bfloat16), "rep").astype(jnp.float32)
                flow.done[("grad", layer, grad.number)] = total

        def back_step(main, *held):
            return main

    step("begin", ())
    if fast:
        blocks.update(pack(weights, [name for name in CHUNKS if name != "first"], place))
        segment, parent, clusters, blocks["rest"] = step(
            "packed", (segment, parent, clusters, blocks["rest"])
        )
    slots, bias = step("prepared", prepare(segment, parent, clusters))
    hidden, hidden_low = inputs, inputs
    saved = []
    for layer in range(LAYERS):
        pull = functools.partial(get, layer)
        weight = pull(0)
        if layer == 0:
            weight = step("ready", weight)
        projected = project(hidden_low, weight, path_vectors(pull(1)))
        first = attend(projected, slots, bias, 0, ())
        first = step((layer, "half"), first)
        context, *heads = attend(projected, slots, bias, 1, first)
        context = step((layer, "context"), context)
        context = step((layer, "waited"), context)
        context, *wide = step((layer, "placed"), (context, pull(2), pull(6), pull(8)))
        entered = hidden_low
        middle, act, slope, *norms, hidden, hidden_low = feed(
            context,
            hidden,
            wide,
            [pull(number) for number in (3, 4, 5, 7, 9, 10, 11)],
        )
        saved.append((entered, heads, context, middle, act, slope, norms))
    result = hidden_low
    above, proj = cotangent, None
    sums = [None] * LAYERS
    for layer in reversed(range(LAYERS)):
        entered, heads, context, middle, act, slope, norms = saved[layer]
        pull = functools.partial(get, layer)
        down, grad_pre, grad_attn, attn_low, grad_context, row_sums, ffin_sum = feed_back(
            above,
            proj,
            None if proj is None else get(layer + 1, 0),
            at,
            [norms[2], norms[3], slope, norms[0], norms[1]],
            [pull(2), pull(6), pull(8)],
            [pull(4), pull(10)],
        )
        sums[layer] = [row_sums, ffin_sum, None]
        down = back_step(down)
        wide = grad_pre.shape[1] // CORES
        grad_8 = Grad(8, act, down, down, True, act.shape[1] // D, UNIT)
        grad_2 = Grad(2, context, attn_low, attn_low, True, 1, UNIT)
        if layer == 0:
            reduce(layer, grad_8, grad_2)
            reduce(layer, Grad(6, middle, grad_pre, grad_pre, True, wide // D, D))
        else:
            grad_6 = Grad(6, middle, grad_pre, grad_pre, True, wide // UNIT, UNIT)
            reduce(layer, grad_8, grad_6, grad_2)
        above_chain = () if layer else (("grad", 1, 8),)
        grad_context = back_step(grad_context, *above_chain)
        away, away_sums = attend_back(grad_context, slots, heads, at, True)
        wide_chains = (("grad", layer, 8), ("grad", layer, 6))
        grad_context, away = back_step((grad_context, away), *above_chain, *wide_chains)
        own, own_sums = attend_back(grad_context, slots, heads, at, False)
        proj = (own, away)
        reduce(layer, Grad(0, entered, own, away, False, 3, UNIT))
        sums[layer][2] = (own_sums, away_sums, at)
        proj = back_step(proj, *(wide_chains if layer else ()))
        above = grad_attn
    grad_input = input_grad(above, proj, get(0, 0), at)
    pieces = [qv_sum(sums[layer][2]) for layer in range(LAYERS)]
    for row_sums, ffin_sum, _ in sums:
        pieces += [row_sums[:6].reshape(-1), ffin_sum[0]]
    total = jnp.concatenate(pieces)
    if fast:
        while flow.running:
            grad_input = back_step(grad_input)
        done = flow.done
        vec = total.reshape(-1, 128)
        last, vec, grad_input = lax.optimization_barrier(
            (done["grad", 1, 8], vec, grad_input)
        )
        flat, ends, last, vec = reduce_tail(
            done["grad", 0, 8], [done["grad", 0, 6], done["grad", 0, 0]], last, vec
        )
        total = vec.reshape(-1)
    else:
        total = lax.psum(total, AXES)
    count = lax.axis_size("shard")
    shard = lax.axis_index("shard")
    ff = sums[0][1].shape[1]
    rest = total[4 * D :].reshape(LAYERS, 6 * D + ff)

    def share(stacked):
        width = stacked.shape[1] // count
        return lax.dynamic_slice_in_dim(stacked, shard * width, width, axis=1)

    grads = {1: share(total[: 4 * D].reshape(LAYERS, 2 * D)), 7: share(rest[:, 6 * D :])}
    for number, row in ((10, 0), (11, 1), (9, 2), (4, 3), (5, 4), (3, 5)):
        grads[number] = share(rest[:, row * D : (row + 1) * D])
    if fast:
        rows = {number: weights[number].shape[1] for number in MATRICES}
        parts = {number: weights[number].shape[2] // (CORES * UNIT) for number in MATRICES}
        known = [{}, dict(done["grad", 1, 0])]
        for layer, pieces, numbers in ((0, flat, (8, 2)), (1, last, (8, 6, 2))):
            start = 0
            for number in numbers:
                known[layer][number] = (pieces, start, rows[number])
                start += rows[number] * parts[number]
        for number, end in zip((6, 0), ends):
            end = end.reshape(end.shape[0], -1, end.shape[-1])
            known[0][number] = (list(end), 0, rows[number] // CHIPS_Y)
        for numbers in (MATRICES,):
            shapes = {number: weights[number].shape[1:] for number in numbers}
            grads.update(zip(numbers, join(at, known, shapes)))
    else:
        for number in MATRICES:
            grads[number] = jnp.stack([flow.done[("grad", layer, number)] for layer in range(LAYERS)])
    return (result, grad_input, *[grads[number] for number in range(12)])


def solution(mesh):
    in_specs = (
        P(("rep", "shard"), None),
        P(("rep", "shard"), None),
        P(("rep", "shard")),
        P(("rep", "shard"), None),
        P(None, ("rep", "shard")),
        P(None, "shard", None),
        P(None, "shard"),
        P(None, "shard", None),
        P(None, "shard"),
        P(None, "shard"),
        P(None, "shard"),
        P(None, "shard", None),
        P(None, "shard"),
        P(None, "shard", None),
        P(None, "shard"),
        P(None, "shard"),
        P(None, "shard"),
    )
    out_specs = (
        P(("rep", "shard"), None),
        P(("rep", "shard"), None),
        P(None, "shard", None),
        P(None, "shard"),
        P(None, "shard", None),
        P(None, "shard"),
        P(None, "shard"),
        P(None, "shard"),
        P(None, "shard", None),
        P(None, "shard"),
        P(None, "shard", None),
        P(None, "shard"),
        P(None, "shard"),
        P(None, "shard"),
    )
    fast = mesh.shape["rep"] == CHIPS_Y * CORES and mesh.shape["shard"] == CHIPS_Z * CHIPS_X
    return jax.shard_map(
        functools.partial(local, fast),
        mesh=mesh,
        in_specs=in_specs,
        out_specs=out_specs,
        check_vma=False,
    )
```

```python
import functools

import jax
import jax.numpy as jnp
from jax import lax
from jax.experimental import pallas as pl
from jax.experimental.pallas import tpu as pltpu
from jax.sharding import PartitionSpec as P

D = 768
HEADS = 12
HEAD_DIM = 64
LAYERS = 2
CLUSTER = 128
TREE_LEN = 1024
SEGMENTS = 13
PAIRS = HEADS // 2
LANES = 2 * HEAD_DIM
KERNEL_VMEM = 60 * 2**20
ROW_TILE = 256
FEED_TILE = 768
DEPTH_TILE = 384
INV_ROOT = (2.0 * 3.141592653589793) ** -0.5
MATRICES = (0, 2, 6, 8)
VECTORS = (1, 3, 4, 5, 7, 9, 10, 11)
UNIT = 384
AXES = ("rep", "shard")
CHIPS_Z, CHIPS_X, CHIPS_Y, CORES = 4, 2, 2, 2
norm_eps = 1e-06


def one_hot_rows(slot_row):
    length = slot_row.shape[-1]
    rows = lax.broadcasted_iota(jnp.int32, (length, length), 0)
    return jnp.where(rows == slot_row, 1.0, 0.0).astype(jnp.bfloat16)


def first_lanes(length):
    return lax.broadcasted_iota(jnp.int32, (length, LANES), 1) < HEAD_DIM


def contract_last(left_side, right_side):
    return lax.dot_general(
        left_side, right_side, (((1,), (1,)), ((), ())), preferred_element_type=jnp.float32
    )


def contract_first(left_side, right_side):
    return lax.dot_general(
        left_side, right_side, (((0,), (0,)), ((), ())), preferred_element_type=jnp.float32
    )


def cluster_blocks(values):
    return [values[at : at + CLUSTER] for at in range(0, values.shape[0], CLUSTER)]


def attend_kernel(slot_ref, query_ref, key_ref, value_ref, bias_ref, *refs):
    ctx_ref, qk_ref, val_ref, p_ref = refs[-4:]
    low = first_lanes(TREE_LEN)
    query = query_ref[...] * jnp.bfloat16(HEAD_DIM**-0.5)
    key = key_ref[...]
    value = value_ref[...]
    packed = (
        jnp.where(low, query, pltpu.roll(key, HEAD_DIM, 1)),
        jnp.where(low, pltpu.roll(query, HEAD_DIM, 1), key),
    )
    context = []
    for head in range(2):
        table = one_hot_rows(slot_ref[0, 0, head : head + 1, :])
        joined = jnp.concatenate([packed[head], value], axis=1)
        slots = jnp.dot(table, joined, preferred_element_type=jnp.float32).astype(jnp.bfloat16)
        both, values = slots[:, :LANES], slots[:, LANES:]
        qk_ref[0, head] = both
        val_ref[0, head] = values
        queries = jnp.where(low, both, jnp.bfloat16(0))
        keys = pltpu.roll(both, HEAD_DIM, 1)
        scores = jnp.concatenate(
            [contract_last(q, k) for q, k in zip(cluster_blocks(queries), cluster_blocks(keys))],
            axis=0,
        )
        scores = scores + bias_ref[0, head].astype(jnp.float32)
        numerator = jnp.exp(scores - jnp.max(scores, axis=1, keepdims=True))
        total = jnp.sum(numerator, axis=1, keepdims=True)
        soft = (numerator * (1.0 / total)).astype(jnp.bfloat16)
        p_ref[0, head] = soft
        out = jnp.concatenate(
            [
                jnp.dot(p, v, preferred_element_type=jnp.float32)
                for p, v in zip(cluster_blocks(soft), cluster_blocks(values))
            ],
            axis=0,
        ).astype(jnp.bfloat16)
        context.append(contract_first(table, out))
    ctx_ref[...] = jnp.where(low, context[0], context[1]).astype(jnp.bfloat16)


def attend_back_kernel(at_ref, slot_ref, grad_ref, qk_ref, val_ref, p_ref, out_ref, sums_ref):
    low = first_lanes(TREE_LEN)
    grads = grad_ref[...]
    placed = []
    for head in range(2):
        table = one_hot_rows(slot_ref[0, 0, head : head + 1, :])
        slots = jnp.dot(table, grads, preferred_element_type=jnp.float32)
        slots = jnp.where(low == (head == 0), slots, 0.0).astype(jnp.bfloat16)
        both, values, soft = qk_ref[0, head], val_ref[0, head], p_ref[0, head]
        grad_soft = jnp.concatenate(
            [contract_last(g, v) for g, v in zip(cluster_blocks(slots), cluster_blocks(values))],
            axis=0,
        )
        grad_value = jnp.concatenate(
            [contract_first(p, g) for p, g in zip(cluster_blocks(soft), cluster_blocks(slots))],
            axis=0,
        ).astype(jnp.bfloat16)
        weights = soft.astype(jnp.float32)
        delta = jnp.sum(weights * grad_soft, axis=1, keepdims=True)
        grad_scores = (weights * (grad_soft - delta)).astype(jnp.bfloat16)
        pairs = list(zip(cluster_blocks(grad_scores), cluster_blocks(both)))
        by_key = jnp.concatenate([contract_first(s, b) for s, b in pairs], axis=0)
        by_query = jnp.concatenate(
            [jnp.dot(s, b, preferred_element_type=jnp.float32) for s, b in pairs], axis=0
        )
        mixed = jnp.where(low, by_key, by_query * HEAD_DIM**-0.5).astype(jnp.bfloat16)
        joined = jnp.concatenate([mixed, grad_value], axis=1)
        placed.append(contract_first(table, joined))
    first, second = placed
    queries = jnp.where(low, pltpu.roll(first[:, :LANES], HEAD_DIM, 1), second[:, :LANES])
    keys = jnp.where(low, first[:, :LANES], pltpu.roll(second[:, :LANES], HEAD_DIM, 1))
    values = jnp.where(low, first[:, LANES:], second[:, LANES:])
    sums = []
    for part, grad in enumerate((queries, keys, values)):
        rounded = grad.astype(jnp.bfloat16)
        out_ref[part] = rounded
        sums.append(rows_sum(rounded.astype(jnp.float32)))
    sums_ref[0, 0] = jnp.concatenate(sums + [jnp.zeros((5, LANES), jnp.float32)], axis=0)


def slot_spec(start=0):
    return pl.BlockSpec((1, 1, 2, TREE_LEN), lambda tree, pair: (tree, start + pair, 0, 0))


def head_spec(start=0):
    return pl.BlockSpec((1, 2, TREE_LEN, LANES), lambda tree, pair: (tree, start + pair, 0, 0))


def column_spec(offset):
    return pl.BlockSpec((TREE_LEN, LANES), lambda tree, pair: (tree, offset + pair))


def kernel_params():
    return pltpu.CompilerParams(vmem_limit_bytes=KERNEL_VMEM)


def attend(projected, slots, bias, half, before):
    trees = slots.shape[0]
    start = half * (PAIRS // 2)
    stored = jax.ShapeDtypeStruct((trees, HEADS, TREE_LEN, LANES), jnp.bfloat16)
    return pl.pallas_call(
        attend_kernel,
        grid=(trees, PAIRS // 2),
        in_specs=[
            slot_spec(start),
            column_spec(start),
            column_spec(PAIRS + start),
            column_spec(2 * PAIRS + start),
            head_spec(start),
        ]
        + [pl.BlockSpec(memory_space=pl.ANY)] * len(before),
        out_specs=[column_spec(start), head_spec(start), head_spec(start), head_spec(start)],
        out_shape=[
            jax.ShapeDtypeStruct((trees * TREE_LEN, D), jnp.bfloat16),
            stored,
            stored,
            stored,
        ],
        input_output_aliases={5 + place: place for place in range(len(before))},
        compiler_params=kernel_params(),
        cost_estimate=pl.CostEstimate(
            flops=trees * 15_000_000_000, bytes_accessed=trees * 10_000_000, transcendentals=0
        ),
    )(slots, projected, projected, projected, bias, *before)


def attend_back(grad_context, slots, kept, at, other):
    trees = slots.shape[0]
    count = PAIRS // CORES
    flip = 1 if other else 0

    def pair_of(pair, at):
        return lax.rem(at[3] + flip, CORES) * count + pair

    head = pl.BlockSpec(
        (1, 2, TREE_LEN, LANES), lambda tree, pair, at: (tree, pair_of(pair, at), 0, 0)
    )
    return pl.pallas_call(
        attend_back_kernel,
        grid_spec=pltpu.PrefetchScalarGridSpec(
            num_scalar_prefetch=1,
            grid=(trees, count),
            in_specs=[
                pl.BlockSpec(
                    (1, 1, 2, TREE_LEN), lambda tree, pair, at: (tree, pair_of(pair, at), 0, 0)
                ),
                pl.BlockSpec((TREE_LEN, LANES), lambda tree, pair, at: (tree, pair_of(pair, at))),
                head,
                head,
                head,
            ],
            out_specs=[
                pl.BlockSpec((3, TREE_LEN, LANES), lambda tree, pair, at: (0, tree, pair)),
                pl.BlockSpec((1, 1, 8, LANES), lambda tree, pair, at: (tree, pair, 0, 0)),
            ],
        ),
        out_shape=[
            jax.ShapeDtypeStruct((3, trees * TREE_LEN, D // CORES), jnp.bfloat16),
            jax.ShapeDtypeStruct((trees, count, 8, LANES), jnp.float32),
        ],
        compiler_params=kernel_params(),
        cost_estimate=pl.CostEstimate(
            flops=trees * 17_000_000_000, bytes_accessed=trees * 10_000_000, transcendentals=0
        ),
    )(at, slots, grad_context, *kept)


def erf_parts(values):
    size = jnp.abs(values)
    turn = 1.0 / (1.0 + (0.3275911 * 0.5**0.5) * size)
    bell = jnp.exp(-0.5 * values * values)
    series = 1.061405429 * 0.5
    for factor in (-1.453152027, 1.421413741, -0.284496736, 0.254829592):
        series = series * turn + factor * 0.5
    tail = series * turn * bell
    return jnp.where(values < 0.0, tail, 1.0 - tail), bell


def norm_parts(values):
    centred = values - jnp.mean(values, axis=-1, keepdims=True)
    scale = lax.rsqrt(jnp.mean(centred * centred, axis=-1, keepdims=True) + norm_eps)
    return centred * scale, scale


def norm_back(grad, normal, scale, gain):
    inner = grad * gain
    mean = jnp.mean(inner, axis=-1, keepdims=True)
    along = jnp.mean(inner * normal, axis=-1, keepdims=True)
    return scale * (inner - mean - normal * along)


def spread(column):
    return jnp.broadcast_to(column, (column.shape[0], 128))


def rows_sum(values):
    return jnp.sum(values, axis=0, keepdims=True)


def project_kernel(layer, rows_ref, weight_ref, bias_ref, out_ref):
    product = jnp.dot(rows_ref[...], weight_ref[...], preferred_element_type=jnp.float32)
    bias = bias_ref[layer : layer + 1]
    out_ref[:, :D] = (product[:, :D] + bias[:, :D]).astype(jnp.bfloat16)
    out_ref[:, D : 2 * D] = product[:, D : 2 * D].astype(jnp.bfloat16)
    out_ref[:, 2 * D :] = (product[:, 2 * D :] + bias[:, D:]).astype(jnp.bfloat16)


def feed_kernel(
    layer,
    context_ref,
    rows_ref,
    out_weight_ref,
    ffin_weight_ref,
    ffout_weight_ref,
    out_bias_ref,
    attn_gain_ref,
    attn_shift_ref,
    ffin_bias_ref,
    ffout_bias_ref,
    ffn_gain_ref,
    ffn_shift_ref,
    hidden_ref,
    act_ref,
    slope_ref,
    attn_normal_ref,
    attn_scale_ref,
    ffn_normal_ref,
    ffn_scale_ref,
    result_ref,
    result_low_ref,
):
    here = slice(layer, layer + 1)
    product = jnp.dot(context_ref[...], out_weight_ref[...], preferred_element_type=jnp.float32)
    attn_sum = rows_ref[...].astype(jnp.float32) + product + out_bias_ref[here]
    normal, scale = norm_parts(attn_sum)
    attn_normal_ref[...] = normal
    attn_scale_ref[...] = spread(scale)
    hidden = normal * attn_gain_ref[here] + attn_shift_ref[here]
    hidden_low = hidden.astype(jnp.bfloat16)
    hidden_ref[...] = hidden_low
    total = hidden + ffout_bias_ref[here]
    width = ffin_weight_ref.shape[1]
    for at in range(0, width, FEED_TILE):
        part = slice(at, at + FEED_TILE)
        pre = (
            jnp.dot(hidden_low, ffin_weight_ref[:, part], preferred_element_type=jnp.float32)
            + ffin_bias_ref[here, part]
        )
        below, bell = erf_parts(pre)
        act = (pre * below).astype(jnp.bfloat16)
        act_ref[:, part] = act
        slope_ref[:, part] = (below + pre * bell * INV_ROOT).astype(jnp.bfloat16)
        total = total + jnp.dot(
            act, ffout_weight_ref[part, :], preferred_element_type=jnp.float32
        )
    normal, scale = norm_parts(total)
    ffn_normal_ref[...] = normal
    ffn_scale_ref[...] = spread(scale)
    result = normal * ffn_gain_ref[here] + ffn_shift_ref[here]
    result_ref[...] = result
    result_low_ref[...] = result.astype(jnp.bfloat16)


def add_projected(grad, at_ref, own_ref, away_ref, weight_ref):
    half = own_ref.shape[2]
    for flip, ref in enumerate((own_ref, away_ref)):
        core = lax.rem(at_ref[3] + flip, CORES)
        for part in range(3):
            column = pl.multiple_of((part * CORES + core) * half, 128)
            grad = grad + contract_last(ref[part], weight_ref[:, pl.ds(column, half)])
    return grad


def feed_back_kernel(layer, with_proj, *refs):
    here = slice(layer, layer + 1)
    if with_proj:
        above_ref, at_ref, own_ref, away_ref, qkv_weight_ref, *refs = refs
        grad = add_projected(above_ref[...], at_ref, own_ref, away_ref, qkv_weight_ref)
    else:
        above_ref, *refs = refs
        grad = above_ref[...].astype(jnp.float32)
    (
        ffn_normal_ref,
        ffn_scale_ref,
        slope_ref,
        attn_normal_ref,
        attn_scale_ref,
        out_weight_ref,
        ffin_weight_ref,
        ffout_weight_ref,
        attn_gain_ref,
        ffn_gain_ref,
        down_ref,
        pre_ref,
        attn_ref,
        attn_low_ref,
        context_ref,
        sums_ref,
        ffin_sum_ref,
    ) = refs

    @pl.when(pl.program_id(0) == 0)
    def _():
        sums_ref[...] = jnp.zeros_like(sums_ref)
        ffin_sum_ref[...] = jnp.zeros_like(ffin_sum_ref)

    normal = ffn_normal_ref[...]
    sums_ref[0:1] += rows_sum(grad * normal)
    sums_ref[1:2] += rows_sum(grad)
    grad_sum = norm_back(grad, normal, ffn_scale_ref[:, 0:1], ffn_gain_ref[here])
    down = grad_sum.astype(jnp.bfloat16)
    down_ref[...] = down
    sums_ref[2:3] += rows_sum(down.astype(jnp.float32))
    total = grad_sum
    width = ffin_weight_ref.shape[1]
    for at in range(0, width, FEED_TILE):
        part = slice(at, at + FEED_TILE)
        grad_act = contract_last(down, ffout_weight_ref[part, :])
        pre = (grad_act * slope_ref[:, part].astype(jnp.float32)).astype(jnp.bfloat16)
        pre_ref[:, part] = pre
        ffin_sum_ref[:, part] += rows_sum(pre.astype(jnp.float32))
        total = total + contract_last(pre, ffin_weight_ref[:, part])
    normal = attn_normal_ref[...]
    sums_ref[3:4] += rows_sum(total * normal)
    sums_ref[4:5] += rows_sum(total)
    attn = norm_back(total, normal, attn_scale_ref[:, 0:1], attn_gain_ref[here])
    attn_ref[...] = attn
    low = attn.astype(jnp.bfloat16)
    attn_low_ref[...] = low
    sums_ref[5:6] += rows_sum(low.astype(jnp.float32))
    context_ref[...] = contract_last(low, out_weight_ref[...]).astype(jnp.bfloat16)


def input_grad_kernel(above_ref, at_ref, own_ref, away_ref, weight_ref, out_ref):
    out_ref[...] = add_projected(above_ref[...], at_ref, own_ref, away_ref, weight_ref)


def prep_pair(parent_ref, segment_ref, cluster_ref, slot_ref, bias_ref, row, tree, pair):
    segs = segment_ref[tree]
    length = segs.shape[1]

    def parent_of(values):
        found = jnp.zeros_like(values)
        for number in range(SEGMENTS):
            found = jnp.where(values == number, parent_ref[row, number], found)
        return found

    parents = parent_of(segs)
    grands = parent_of(parents)
    ids = jnp.concatenate([segs, parents, grands, jnp.zeros((5, length), jnp.int32)], axis=0)
    ids = jnp.concatenate([ids, jnp.zeros((8, length), jnp.int32)], axis=0)
    ids = ids.astype(jnp.float32).astype(jnp.bfloat16)
    count = length // CLUSTER
    order = lax.broadcasted_iota(jnp.int32, (count, length), 0)
    lanes = lax.broadcasted_iota(jnp.int32, (count, length), 1)
    for head in range(2):
        member = order == cluster_ref[tree, pair, head : head + 1, :]
        ranks = member.astype(jnp.int32)
        step = 1
        while step < length:
            ranks = ranks + jnp.where(lanes >= step, pltpu.roll(ranks, step, 1), 0)
            step *= 2
        slot = jnp.sum(
            jnp.where(member, ranks - 1 + CLUSTER * order, 0), axis=0, keepdims=True
        )
        slot_ref[tree, pair, head : head + 1, :] = slot
        table = one_hot_rows(slot)
        rows = contract_last(ids, table)
        columns = jnp.concatenate([rows] * (128 // rows.shape[0]), axis=0).T
        for at in range(0, length, CLUSTER):
            here = rows[0:1, at : at + CLUSTER]
            block = columns[at : at + CLUSTER]
            allowed = (
                (here == block[:, 0:1]) | (here == block[:, 1:2]) | (here == block[:, 2:3])
            )
            bias_ref[tree, 2 * pair + head, at : at + CLUSTER, :] = jnp.where(allowed, 0.0, -1e30).astype(
                jnp.bfloat16
            )


def prep_kernel(*refs):
    prep_pair(*refs, pl.program_id(0), 0, 0)


def row_spec(width, rows=ROW_TILE):
    return pl.BlockSpec((rows, width), lambda i: (i, 0))


def whole_spec(shape):
    return pl.BlockSpec(
        shape, lambda i: (0,) * len(shape), pipeline_mode=pl.Buffered(1)
    )


def part_spec(rows=ROW_TILE):
    return pl.BlockSpec((3, rows, D // CORES), lambda i: (0, i, 0))


def cost(flops, *arrays):
    moved = sum(array.size * array.dtype.itemsize for array in arrays)
    return pl.CostEstimate(flops=int(flops), bytes_accessed=moved, transcendentals=0)


def shape_of(rows, width, kind=jnp.bfloat16):
    return jax.ShapeDtypeStruct((rows, width), kind)


def project(layer, rows, weight, bias):
    count, width = rows.shape[0], weight.shape[1]
    return pl.pallas_call(
        functools.partial(project_kernel, layer),
        grid=(count // ROW_TILE,),
        in_specs=[row_spec(D), whole_spec(weight.shape), whole_spec(bias.shape)],
        out_specs=row_spec(width),
        out_shape=shape_of(count, width),
        compiler_params=kernel_params(),
        cost_estimate=cost(2.4 * count * D * width, rows, weight),
    )(rows, weight, bias)


def feed(layer, context, rows, weights, vectors):
    count = context.shape[0]
    width = weights[1].shape[1]
    f32 = jnp.float32
    return pl.pallas_call(
        functools.partial(feed_kernel, layer),
        grid=(count // ROW_TILE,),
        in_specs=[row_spec(D), row_spec(D)]
        + [whole_spec(weight.shape) for weight in weights]
        + [whole_spec(vector.shape) for vector in vectors],
        out_specs=[
            row_spec(D),
            row_spec(width),
            row_spec(width),
            row_spec(D),
            row_spec(128),
            row_spec(D),
            row_spec(128),
            row_spec(D),
            row_spec(D),
        ],
        out_shape=[
            shape_of(count, D),
            shape_of(count, width),
            shape_of(count, width),
            shape_of(count, D, f32),
            shape_of(count, 128, f32),
            shape_of(count, D, f32),
            shape_of(count, 128, f32),
            shape_of(count, D, f32),
            shape_of(count, D),
        ],
        compiler_params=kernel_params(),
        cost_estimate=cost(5 * count * D * (2 * width + D), context, *weights),
    )(context, rows, *weights, *vectors)


def feed_back(layer, above, proj, qkv_weight, at, saved, weights, gains):
    count = above.shape[0]
    width = weights[1].shape[1]
    f32 = jnp.float32
    lead, lead_specs = [above], [row_spec(D)]
    if proj is not None:
        lead += [at, *proj, qkv_weight]
        lead_specs += [
            pl.BlockSpec(memory_space=pltpu.SMEM),
            part_spec(),
            part_spec(),
            whole_spec(qkv_weight.shape),
        ]
    return pl.pallas_call(
        functools.partial(feed_back_kernel, layer, proj is not None),
        grid=(count // ROW_TILE,),
        in_specs=lead_specs
        + [row_spec(D), row_spec(128), row_spec(width), row_spec(D), row_spec(128)]
        + [whole_spec(weight.shape) for weight in weights]
        + [whole_spec(gain.shape) for gain in gains],
        out_specs=[
            row_spec(D),
            row_spec(width),
            row_spec(D),
            row_spec(D),
            row_spec(D),
            pl.BlockSpec((8, D), lambda i: (0, 0)),
            pl.BlockSpec((1, width), lambda i: (0, 0)),
        ],
        out_shape=[
            shape_of(count, D),
            shape_of(count, width),
            shape_of(count, D, f32),
            shape_of(count, D),
            shape_of(count, D),
            shape_of(8, D, f32),
            shape_of(1, width, f32),
        ],
        compiler_params=kernel_params(),
        cost_estimate=cost(5 * count * D * (2 * width + D), above, *weights),
    )(*lead, *saved, *weights, *gains)


def input_grad(above, proj, qkv_weight, at):
    count = above.shape[0]
    return pl.pallas_call(
        input_grad_kernel,
        grid=(count // ROW_TILE,),
        in_specs=[
            row_spec(D),
            pl.BlockSpec(memory_space=pltpu.SMEM),
            part_spec(),
            part_spec(),
            whole_spec(qkv_weight.shape),
        ],
        out_specs=row_spec(D),
        out_shape=shape_of(count, D, jnp.float32),
        compiler_params=kernel_params(),
        cost_estimate=cost(2.4 * count * D * 3 * D, above, qkv_weight),
    )(above, at, *proj, qkv_weight)


def prepare(segment, parent, clusters):
    trees = parent.shape[0]
    segment = segment.reshape(trees, 1, TREE_LEN)
    clusters = clusters.reshape(PAIRS, 2, trees, TREE_LEN).transpose(2, 0, 1, 3)
    return pl.pallas_call(
        prep_kernel,
        grid=(trees, PAIRS),
        in_specs=[
            pl.BlockSpec(memory_space=pltpu.SMEM),
            pl.BlockSpec((1, 1, TREE_LEN), lambda tree, pair: (tree, 0, 0)),
            slot_spec(),
        ],
        out_specs=[slot_spec(), head_spec()],
        out_shape=[
            jax.ShapeDtypeStruct((trees, PAIRS, 2, TREE_LEN), jnp.int32),
            jax.ShapeDtypeStruct((trees, HEADS, TREE_LEN, LANES), jnp.bfloat16),
        ],
        compiler_params=kernel_params(),
        cost_estimate=pl.CostEstimate(
            flops=trees * 20_000_000_000, bytes_accessed=trees * 4_000_000, transcendentals=0
        ),
    )(parent, segment, clusters)


def weight_grad_kernel(split_y, at_ref, left_ref, right_ref, *refs):
    product = contract_first(
        left_ref[...].reshape(left_ref.shape[-2:]), right_ref[...].reshape(right_ref.shape[-2:])
    )
    if split_y is None:
        (out_ref,) = refs
        out_ref[...] = product.astype(jnp.bfloat16).reshape(out_ref.shape)
        return
    near_ref, (send_ref, keep_ref, sum_ref) = refs[0], refs[-3:]
    total = product + near_ref[...].astype(jnp.float32).reshape(product.shape)
    sum_ref[...] = total.astype(jnp.bfloat16).reshape(sum_ref.shape)
    if split_y:
        send_ref[0] = sum_ref[:, :, 1 - at_ref[2]]
        keep_ref[0] = sum_ref[:, :, at_ref[2]]
    else:
        send_ref[...] = sum_ref[:, 1 - at_ref[1]]
        keep_ref[...] = sum_ref[:, at_ref[1]]


class Grad:
    def __init__(self, number, left, own, away, cut, tiles, half):
        self.number = number
        self.left, self.rights = left, (own, away)
        self.cut, self.tiles, self.half = cut, tiles, half
        self.depth = left.shape[1]
        self.parts = 1 if self.depth > D else tiles
        self.rows = self.depth // (CHIPS_Z * CHIPS_X)

    def product(self, at, other, split_y=None, near=None, start=0, total=0, before=()):
        flip = 1 if other else 0
        left, right = self.left, self.rights[flip]
        count = left.shape[0]
        tall = self.depth > D
        core = lambda at: lax.rem(at[3] + flip, CORES)
        in_specs = [
            pl.BlockSpec((count, D), (lambda i, at: (0, i)) if tall else (lambda i, at: (0, 0)))
        ]
        if not self.cut:
            in_specs.append(pl.BlockSpec((1, count, self.half), lambda i, at: (i, 0, 0)))
        elif tall:
            in_specs.append(pl.BlockSpec((count, self.half), lambda i, at: (0, core(at))))
        else:
            in_specs.append(
                pl.BlockSpec((count, self.half), lambda i, at: (0, core(at) * self.tiles + i))
            )
        zs = D // (self.rows * CHIPS_X)
        place = (lambda i: (0, i)) if tall else (lambda i: (i, 0))
        whole = (self.parts, CHIPS_Z, CHIPS_X, self.rows, self.half)
        block = (1, zs, CHIPS_X, self.rows, self.half)
        full = pl.BlockSpec(block, lambda i, at: (*place(i), 0, 0, 0))
        args, scratch = [left, right], []
        if split_y is None:
            out_specs, shapes = full, jax.ShapeDtypeStruct(whole, jnp.bfloat16)
        else:
            in_specs.append(full)
            args.append(near)
            in_specs += [pl.BlockSpec(memory_space=pl.ANY)] * len(before)
            args += before
            if split_y:
                short = self.rows // CHIPS_Y
                kept = (CHIPS_X, short, self.half)
                scratch = [pltpu.VMEM((zs, CHIPS_X, CHIPS_Y, short, self.half), jnp.bfloat16)]
                spec = pl.BlockSpec((1, zs, *kept), lambda i, at: (*place(i), 0, 0, 0))
                shape = (self.parts, CHIPS_Z, *kept)
            else:
                scratch = [pltpu.VMEM((zs, CHIPS_X, self.rows, self.half), jnp.bfloat16)]
                first = start // self.rows
                index = (lambda i, at: (i, first, 0)) if tall else (lambda i, at: (0, first + i, 0))
                spec = pl.BlockSpec((zs, self.rows, self.half), index)
                shape = (CHIPS_Z, total, self.half)
            out_specs, shapes = [spec] * 2, [jax.ShapeDtypeStruct(shape, jnp.bfloat16)] * 2
        return pl.pallas_call(
            functools.partial(weight_grad_kernel, split_y),
            grid_spec=pltpu.PrefetchScalarGridSpec(
                num_scalar_prefetch=1,
                grid=(self.tiles,),
                in_specs=in_specs,
                out_specs=out_specs,
                scratch_shapes=scratch,
            ),
            out_shape=shapes,
            input_output_aliases={4 + place: place for place in range(len(before))},
            compiler_params=kernel_params(),
            cost_estimate=cost(4 * count * D * self.tiles * self.half, left, right),
        )(at, *args)


def combine_kernel(groups, at_ref, *refs):
    total = sum(groups)
    ins, outs = refs[:total], refs[total:]
    first = 0
    for count, out_ref in zip(groups, outs):
        value = None
        for ref in ins[first : first + count]:
            term = ref[...].astype(jnp.float32).reshape(out_ref.shape)
            value = term if value is None else value + term
        out_ref[...] = value.astype(out_ref.dtype)
        first += count


def combine(at, steps, groups, blocks):
    terms = [term for group in groups for term in group]
    return pl.pallas_call(
        functools.partial(combine_kernel, [len(group) for group in groups]),
        grid_spec=pltpu.PrefetchScalarGridSpec(
            num_scalar_prefetch=1,
            grid=(steps,),
            in_specs=[pl.BlockSpec(block, index) for _, block, index in terms],
            out_specs=[pl.BlockSpec(block, index) for _, block, index in blocks],
        ),
        out_shape=[jax.ShapeDtypeStruct(shape, jnp.bfloat16) for shape, _, _ in blocks],
        compiler_params=kernel_params(),
        cost_estimate=pl.CostEstimate(
            flops=0, bytes_accessed=2_000_000, transcendentals=0
        ),
    )(at, *[array for array, _, _ in terms])


CHUNKS = {
    "next": (1, (0, 2), False),
    "last": (1, (6, 8), False),
}
FORWARD = {
    "ready": ((), ("next",)),
    (0, "half"): (("next",), ("last",)),
    (0, "result"): (("next",), ()),
    (1, "projected"): (("last",), ()),
    (1, "context"): (("last",), ()),
}


class Place:
    def __init__(self):
        rep = lax.axis_index("rep")
        shard = lax.axis_index("shard")
        self.y, self.core = rep // CORES, rep % CORES
        self.z, self.x = shard // CHIPS_X, shard % CHIPS_X
        self.at = jnp.stack([self.z, self.x, self.y, self.core]).astype(jnp.int32)


def hop(value, dz=0, dx=0, dy=0, dc=0):
    pairs = []
    for y in range(CHIPS_Y):
        for c in range(CORES):
            for z in range(CHIPS_Z):
                for x in range(CHIPS_X):
                    source = ((y * CORES + c) * CHIPS_Z + z) * CHIPS_X + x
                    y2, c2 = (y + dy) % CHIPS_Y, (c + dc) % CORES
                    z2, x2 = (z + dz) % CHIPS_Z, (x + dx) % CHIPS_X
                    pairs.append((source, ((y2 * CORES + c2) * CHIPS_Z + z2) * CHIPS_X + x2))
    return lax.ppermute(value, AXES, pairs)


def pack_kernel(plan, at_ref, *refs):
    ins, outs = refs[: len(MATRICES)], refs[len(MATRICES) :]
    for out_ref, (layer, numbers, split_y) in zip(outs, plan):
        start = 0
        for number in numbers:
            ref = ins[MATRICES.index(number)]
            rows, half = ref.shape[1], ref.shape[2] // CORES
            first = 0
            if split_y:
                rows = rows // CHIPS_Y
                first = pl.multiple_of(at_ref[2] * rows, 16)
            for at in range(0, half, UNIT):
                column = pl.multiple_of(at_ref[3] * half + at, 128)
                out_ref[start : start + rows] = ref[layer, pl.ds(first, rows), pl.ds(column, UNIT)]
                start += rows


def chunk_rows(weights, numbers, split_y):
    found = []
    for number in numbers:
        _, rows, columns = weights[number].shape
        found.append((columns // (CORES * UNIT), rows // (CHIPS_Y if split_y else 1)))
    return found


def pack(weights, names, place):
    plan = [CHUNKS[name] for name in names]
    shapes = []
    for _, numbers, split_y in plan:
        shapes.append((sum(u * r for u, r in chunk_rows(weights, numbers, split_y)), UNIT))
    matrices = [weights[number] for number in MATRICES]
    packed = pl.pallas_call(
        functools.partial(pack_kernel, plan),
        grid_spec=pltpu.PrefetchScalarGridSpec(
            num_scalar_prefetch=1,
            grid=(1,),
            in_specs=[pl.BlockSpec(matrix.shape, lambda i, at: (0, 0, 0)) for matrix in matrices],
            out_specs=[pl.BlockSpec(shape, lambda i, at: (0, 0)) for shape in shapes],
        ),
        out_shape=[jax.ShapeDtypeStruct(shape, jnp.bfloat16) for shape in shapes],
        compiler_params=kernel_params(),
        cost_estimate=cost(0, *matrices),
    )(place.at, *matrices)
    return dict(zip(names, packed))


def place_kernel(layout, split_y, count, at_ref, *refs):
    pieces, outs = refs[:count], refs[count:]
    for number, piece in enumerate(pieces):
        core = (at_ref[3] + number % CORES) % CORES
        x = (at_ref[1] + number // CORES % CHIPS_X) % CHIPS_X
        row = (at_ref[2] + number // (CORES * CHIPS_X)) % CHIPS_Y if split_y else 0
        start, unit = 0, piece.shape[2]
        for out_ref, (units, rows) in zip(outs, layout):
            for at in range(units):
                column = pl.multiple_of((core * units + at) * unit, 128)
                out_ref[x, row, :, pl.ds(column, unit)] = piece[0, start : start + rows]
                start += rows


def place_pieces(pieces, layout, split_y, place):
    _, held, unit = pieces[0].shape
    splits = CHIPS_Y if split_y else 1
    shapes = [(CHIPS_Z * CHIPS_X, splits, rows, CORES * units * unit) for units, rows in layout]
    wholes = pl.pallas_call(
        functools.partial(place_kernel, layout, split_y, len(pieces)),
        grid_spec=pltpu.PrefetchScalarGridSpec(
            num_scalar_prefetch=1,
            grid=(CHIPS_Z,),
            in_specs=[pl.BlockSpec((1, held, unit), lambda k, at: (k, 0, 0))] * len(pieces),
            out_specs=[
                pl.BlockSpec(
                    (CHIPS_X, *shape[1:]),
                    lambda k, at: (lax.rem(at[0] + CHIPS_Z - k, CHIPS_Z), 0, 0, 0),
                )
                for shape in shapes
            ],
        ),
        out_shape=[jax.ShapeDtypeStruct(shape, jnp.bfloat16) for shape in shapes],
        compiler_params=kernel_params(),
        cost_estimate=pl.CostEstimate(
            flops=0,
            bytes_accessed=4 * CHIPS_Z * len(pieces) * held * unit,
            transcendentals=0,
        ),
    )(place.at, *pieces)
    return [whole.reshape(-1, whole.shape[-1]) for whole in wholes]


def gather_chain(block, layout, split_y, place):
    parts = yield [hop(block, dz=k) for k in range(1, CHIPS_Z)]
    stack = jnp.stack([block, *parts])
    (across,) = yield [hop(stack, dx=1)]
    pieces = [stack, across]
    if split_y:
        pieces = pieces + (yield [hop(piece, dy=1) for piece in pieces])
    others = yield [hop(piece, dc=1) for piece in pieces]
    wholes = place_pieces(
        [item for pair in zip(pieces, others) for item in pair], layout, split_y, place
    )
    return wholes


class Flow:
    def __init__(self):
        self.running, self.done = {}, {}

    def start(self, name, chain):
        self.running[name] = (chain, next(chain))

    def advance(self, name, arrived):
        chain, _ = self.running.pop(name)
        try:
            self.running[name] = (chain, chain.send(list(arrived)))
        except StopIteration as end:
            self.done[name] = end.value

    def tick(self, main, *names):
        names = [name for name in names if name in self.running]
        pending = [self.running[name][1] for name in names]
        main, pending = lax.optimization_barrier((main, pending))
        for name, arrived in zip(names, pending):
            self.advance(name, arrived)
        return main

    def finish(self, name):
        while name in self.running:
            self.advance(name, self.running[name][1])
        return self.done[name]


def spread_vectors(found, sizes):
    found = found[:, :, 0, :LAYERS].reshape(-1, LAYERS, found.shape[-1]).transpose(1, 0, 2)
    out, at = [], 0
    for size in sizes:
        out.append(found[:, :, at : at + size].reshape(LAYERS, -1).astype(jnp.float32))
        at += size
    return out


def pick_sum(at, own, terms, rows, steps):
    groups = [[(array, block, index(k)) for array, block, index in terms] for k in range(CHIPS_Z)]
    return combine(at, steps, groups, [own] * CHIPS_Z)


def reduce_y_first(grad, place, stop=None):
    at = place.at
    parts, half = grad.parts, grad.half
    rows = grad.rows // CHIPS_Y
    away = grad.product(at, True)
    (near,) = yield [hop(away, dc=1)]
    send, keep = grad.product(at, False, True, near)
    if stop == "sums":
        return send, keep, False
    flip = lambda value: 1 - value
    (over,) = yield [hop(send, dy=1)]
    if stop == "y":
        return over, keep, True
    block = (parts, 1, 1, rows, half)
    short = (parts, 1, rows, half)
    index = lambda i, at: (0, i, flip(at[1]), 0, 0)
    (send,) = combine(
        at,
        CHIPS_Z,
        [[(keep, block, index), (over, block, index)]],
        [((parts, CHIPS_Z, rows, half), short, lambda i, at: (0, i, 0, 0))],
    )
    (across,) = yield [hop(send, dx=1)]
    turn = lambda at, k: lax.rem(at[0] + k, CHIPS_Z)
    mine = lambda k: lambda i, at: (0, turn(at, k), at[1], 0, 0)
    piece = (parts, rows, half)
    whole = (piece, piece, lambda i, at: (0, 0, 0))
    own, *sends = pick_sum(
        at,
        whole,
        [
            (keep, block, mine),
            (over, block, mine),
            (across, short, lambda k: lambda i, at: (0, turn(at, k), 0, 0)),
        ],
        rows,
        1,
    )
    landed = yield [hop(send, dz=k) for k, send in zip(range(1, CHIPS_Z), sends)]
    (own,) = combine(at, 1, [[(term, piece, whole[2]) for term in (own, *landed)]], [whole])
    others = yield [hop(own, dy=1), hop(own, dc=1), hop(own, dy=1, dc=1)]
    pieces = [item.reshape(parts * rows, half) for item in (own, *others)]
    return {grad.number: (pieces, 0, rows)}


def reduce_x_first(grads, place, stop):
    at = place.at
    away = [grad.product(at, True) for grad in grads]
    near = yield [hop(item, dc=1) for item in away]
    total = sum(grad.parts * grad.rows for grad in grads)
    starts, flat = [0], ()
    for grad, item in zip(grads, near):
        flat = grad.product(at, False, False, item, starts[-1], total, tuple(flat))
        starts.append(starts[-1] + grad.parts * grad.rows)
    send, keep = flat
    (across,) = yield [hop(send, dx=1)]
    if stop == "x":
        return across, keep
    steps = 3
    tall = total // steps
    ahead = lambda k: lambda i, at: (lax.rem(at[0] + k, CHIPS_Z), i, 0)
    piece = ((total, UNIT), (tall, UNIT), lambda i, at: (i, 0))
    own, *sends = pick_sum(
        at, piece, [(item, (1, tall, UNIT), ahead) for item in (keep, across)], tall, steps
    )
    landed = yield [hop(send, dz=k) for k, send in zip(range(1, CHIPS_Z), sends)]
    add = lambda *terms: combine(at, steps, [[(term, *piece[1:]) for term in terms]], [piece])[0]
    return add(own, *landed)


def gather_kernel(plan, *refs):
    count = len(plan)
    prep_ins, ins, refs = refs[:3], refs[3 : 3 + count], refs[3 + count :]
    prep_outs, outs, sems, local_sem = refs[:2], refs[2 : 2 + count], refs[2 + count : -1], refs[-1]
    rep, shard = lax.axis_index("rep"), lax.axis_index("shard")
    y, core = lax.div(rep, CORES), lax.rem(rep, CORES)
    z, x = lax.div(shard, CHIPS_X), lax.rem(shard, CHIPS_X)

    def device(dz=0, dx=0, dy=0, dc=0):
        to_y, to_core = lax.rem(y + dy, CHIPS_Y), lax.rem(core + dc, CORES)
        to_z, to_x = lax.rem(z + dz, CHIPS_Z), lax.rem(x + dx, CHIPS_X)
        return (to_y * CORES + to_core, to_z * CHIPS_X + to_x)

    mates = [dict(dx=1), dict(dy=1), dict(dc=1)] + [dict(dz=k) for k in range(1, CHIPS_Z)]
    barrier = pltpu.get_barrier_semaphore()
    for mate in mates:
        pl.semaphore_signal(
            barrier, inc=1, device_id=device(**mate), device_id_type=pl.DeviceIdType.MESH
        )
    sent = []

    def send(source, target, m, number, **step):
        copy = pltpu.make_async_remote_copy(
            src_ref=source,
            dst_ref=target,
            send_sem=sems[m].at[0, number],
            recv_sem=sems[m].at[1, number],
            device_id=device(**step),
            device_id_type=pl.DeviceIdType.MESH,
        )
        copy.start()
        sent.append(copy)
        return copy

    def part(m, at_z, at_x, at_y, at_core):
        out, (layer, split_y, by_core) = outs[m], plan[m]
        columns = slice(None)
        if by_core:
            half = out.shape[-1] // CORES
            columns = pl.ds(pl.multiple_of(at_core * half, 128), half)
        at_z = slice(None) if at_z is None else at_z
        at_x = slice(None) if at_x is None else at_x
        return out.at[at_z, at_x, at_y if split_y else 0, :, columns]

    locals_ = []
    for m, (layer, split_y, by_core) in enumerate(plan):
        rows = outs[m].shape[3]
        source = ins[m] if layer is None else ins[m].at[layer]
        if by_core:
            half = outs[m].shape[-1] // CORES
            first = pl.multiple_of(y * rows, 16) if split_y else 0
            source = source.at[pl.ds(first, rows), pl.ds(pl.multiple_of(core * half, 128), half)]
        copy = pltpu.make_async_copy(source, part(m, z, x, y, core), local_sem.at[m])
        copy.start()
        locals_.append(copy)
    pl.semaphore_wait(barrier, len(mates))
    along_z, along_x, over_y, last = {}, {}, {}, []

    def spread(m, at_z, at_x):
        piece = part(m, at_z, at_x, y, core)
        if at_x is x:
            along_x[m].append(send(piece, piece, m, 3 + len(along_x[m]), dx=1))
        if plan[m][1]:
            over_y[m].append(send(piece, piece, m, 7 + len(over_y[m]), dy=1))

    def behind(k):
        return lax.rem(z + CHIPS_Z - k, CHIPS_Z)

    def after_x(m):
        for k in range(CHIPS_Z):
            along_x[m][k].wait_recv()
            spread(m, behind(k), 1 - x)
        if plan[m][2]:
            piece = part(m, None, None, y, core)
            last.append(send(piece, piece, m, 15, dc=1))

    def after_y(m):
        if over_y[m]:
            for copy in over_y[m]:
                copy.wait_recv()
            piece = part(m, None, None, 1 - y, core)
            last.append(send(piece, piece, m, 16, dc=1))

    order = sorted(range(count), key=lambda m: (not plan[m][1], -outs[m].shape[-1]))
    for m in order:
        locals_[m].wait()
        mine = part(m, z, x, y, core)
        along_z[m] = [send(mine, mine, m, k - 1, dz=k) for k in range(1, CHIPS_Z)]
        along_x[m], over_y[m] = [], []
        spread(m, z, x)
    trees, pairs = prep_ins[2].shape[:2]
    todo = [(tree, tree, pair) for tree in range(trees) for pair in range(pairs)]
    for place, m in enumerate(order):
        for k in range(1, CHIPS_Z):
            if todo:
                prep_pair(*prep_ins, *prep_outs, *todo.pop(0))
            along_z[m][k - 1].wait_recv()
            spread(m, behind(k), x)
        if place:
            after_x(order[place - 1])
    for item in todo:
        prep_pair(*prep_ins, *prep_outs, *item)
    after_x(order[-1])
    for m in order:
        after_y(m)
    for copy in last:
        copy.wait_recv()
    for copy in sent:
        copy.wait_send()


def gather_layer(segment, parent, clusters, vectors, weights, layer, tall):
    low = jnp.bfloat16
    args, plan, shapes = [vectors], [(None, False, False)], [(1, *vectors.shape)]
    for number in MATRICES:
        _, rows, columns = weights[number].shape
        split = CHIPS_Y if number in tall else 1
        args.append(weights[number])
        plan.append((layer, split > 1, True))
        shapes.append((split, rows // split, columns))
    shapes = [jax.ShapeDtypeStruct((CHIPS_Z, CHIPS_X, *shape), low) for shape in shapes]
    trees = parent.shape[0]
    segment = segment.reshape(trees, 1, TREE_LEN)
    clusters = clusters.reshape(PAIRS, 2, trees, TREE_LEN).transpose(2, 0, 1, 3)
    prepared = [
        jax.ShapeDtypeStruct(clusters.shape, jnp.int32),
        jax.ShapeDtypeStruct((trees, HEADS, TREE_LEN, LANES), low),
    ]
    whole = pl.BlockSpec(memory_space=pltpu.VMEM)
    slots, bias, *found = pl.pallas_call(
        functools.partial(gather_kernel, plan),
        in_specs=[pl.BlockSpec(memory_space=pltpu.SMEM), whole, whole]
        + [pl.BlockSpec(memory_space=pl.ANY)] * len(args),
        out_specs=[whole] * (2 + len(args)),
        out_shape=prepared + shapes,
        scratch_shapes=[pltpu.SemaphoreType.DMA((2, 17))] * len(args)
        + [pltpu.SemaphoreType.DMA((len(args),))],
        compiler_params=pltpu.CompilerParams(
            vmem_limit_bytes=KERNEL_VMEM, collective_id=1, has_side_effects=True
        ),
        cost_estimate=pl.CostEstimate(flops=0, bytes_accessed=200_000_000, transcendentals=0),
    )(parent, segment, clusters, *args)
    return slots, bias, found[0], [item.reshape(-1, item.shape[-1]) for item in found[1:]]


def pack_sums(out_ref, core, ins):
    rows = 8 * LAYERS
    width = out_ref.shape[1]
    for layer in range(LAYERS):
        sums_ref, ffin_ref, own_ref, away_ref = ins[4 * layer : 4 * layer + 4]
        out_ref[8 * layer : 8 * layer + 8] = sums_ref[...]
        for at in range(0, ffin_ref.shape[1], width):
            out_ref[rows : rows + 1] = ffin_ref[:, at : at + width]
            rows += 1
    for layer in range(LAYERS):
        for flip, ref in enumerate(ins[4 * layer + 2 : 4 * layer + 4]):
            half = lax.rem(core + flip, CORES) * ref.shape[1]
            for pair in range(ref.shape[1]):
                value = ref[0, pair]
                for tree in range(1, ref.shape[0]):
                    value = value + ref[tree, pair]
                column = pl.multiple_of((half + pair) * LANES, LANES)
                out_ref[rows : rows + 8, pl.ds(column, LANES)] = value
        rows += 8


def sum_rows(ffin_width):
    return LAYERS * (16 + ffin_width // D)


def tail_kernel(arrived, *refs):
    take = iter(refs)
    count = len(arrived)
    a_in, a_keep = next(take), next(take)
    b_ins = [(next(take), next(take)) for _ in range(count)]
    l_in, vec_ins = next(take), [next(take) for _ in range(4 * LAYERS)]
    a_own, a_other = next(take), next(take)
    b_outs = [next(take) for _ in range(count)]
    l_own, l_other, vec_out = next(take), next(take), next(take)
    a_zsend, a_zland, a_ysend, a_yland, a_cland = [next(take) for _ in range(5)]
    b_scratch = [[next(take) for _ in range(6)] for _ in range(count)]
    l_yland, l_cland = next(take), next(take)
    v_send, v_land = next(take), next(take)
    a_sems, b_sems, v_sems = next(take), [next(take) for _ in range(count)], next(take)
    rep, shard = lax.axis_index("rep"), lax.axis_index("shard")
    y, core = lax.div(rep, CORES), lax.rem(rep, CORES)
    z, x = lax.div(shard, CHIPS_X), lax.rem(shard, CHIPS_X)

    def device(dz=0, dx=0, dy=0, dc=0):
        to_y, to_core = lax.rem(y + dy, CHIPS_Y), lax.rem(core + dc, CORES)
        to_z, to_x = lax.rem(z + dz, CHIPS_Z), lax.rem(x + dx, CHIPS_X)
        return (to_y * CORES + to_core, to_z * CHIPS_X + to_x)

    flip_z = 1 + 2 * lax.rem(z, 2)
    mates = [dict(dx=1), dict(dy=1), dict(dc=1), dict(dy=1, dc=1)]
    mates += [dict(dz=k) for k in range(1, CHIPS_Z)]
    barrier = pltpu.get_barrier_semaphore()
    for mate in mates:
        pl.semaphore_signal(
            barrier, inc=1, device_id=device(**mate), device_id_type=pl.DeviceIdType.MESH
        )
    pl.semaphore_wait(barrier, len(mates))
    sent = []

    def send(source, target, sems, number, **step):
        copy = pltpu.make_async_remote_copy(
            src_ref=source,
            dst_ref=target,
            send_sem=sems.at[0, number],
            recv_sem=sems.at[1, number],
            device_id=device(**step),
            device_id_type=pl.DeviceIdType.MESH,
        )
        copy.start()
        sent.append(copy)
        return copy

    def wide(value):
        return value.astype(jnp.float32)

    order = (2, 1, 3, 0)
    ahead = [lax.rem(z + k, CHIPS_Z) for k in order]
    pack_sums(v_send.at[0], core, vec_ins)
    v_copies = [send(v_send.at[0], v_land.at[0], v_sems, 0, dc=1)]
    a_across = a_in
    b_y = [[] for _ in range(count)]
    for j, to in enumerate(ahead):
        for i, (b_send, _) in enumerate(b_ins):
            if arrived[i]:
                continue
            b_y[i].append(send(b_send.at[:, to], b_scratch[i][0].at[j], b_sems[i], j, dy=1))
    steps = (dict(dc=1), dict(dy=1), dict(dx=1), dict(dz=2), dict(dz=flip_z))

    def add_vectors(s):
        v_copies[s].wait_recv()
        total = v_send[s] + v_land[s]
        if s + 1 == len(steps):
            vec_out[...] = total
        else:
            v_send[s + 1] = total
            v_copies.append(
                send(v_send.at[s + 1], v_land.at[s + 1], v_sems, s + 1, **steps[s + 1])
            )

    def over(i, j, side):
        if arrived[i]:
            return wide(b_ins[i][0][:, ahead[j], side])
        return wide(b_scratch[i][0][j, :, side])

    a_z, b_x, b_z = [], [[] for _ in range(count)], [[] for _ in range(count)]

    def b_along_z(i, j):
        k, keep = order[j], b_ins[i][1]
        _, _, x_land, z_send, z_land, _ = b_scratch[i]
        b_x[i][j].wait_recv()
        if k:
            total = wide(keep[:, ahead[j], x]) + over(i, j, x) + wide(x_land[j])
            z_send[k - 1] = total.astype(jnp.bfloat16)
            b_z[i].append(send(z_send.at[k - 1], z_land.at[k - 1], b_sems[i], 7 + k, dz=k))

    def b_along_x(i, j):
        keep, (_, x_send, x_land, *_) = b_ins[i][1], b_scratch[i]
        if not arrived[i]:
            b_y[i][j].wait_recv()
        total = wide(keep[:, ahead[j], 1 - x]) + over(i, j, 1 - x)
        x_send[j] = total.astype(jnp.bfloat16)
        b_x[i].append(send(x_send.at[j], x_land.at[j], b_sems[i], 4 + j, dx=1))

    for j, k in enumerate(order):
        if k:
            total = wide(a_keep[ahead[j]]) + wide(a_across[ahead[j]])
            a_zsend[k - 1] = total.astype(jnp.bfloat16)
            a_z.append(send(a_zsend.at[k - 1], a_zland.at[k - 1], a_sems, 3 + k, dz=k))
        for i in range(count):
            if arrived[i]:
                b_along_x(i, j)
    l_y = send(l_in, l_yland, a_sems, 0, dy=1)
    add_vectors(0)
    for j in range(CHIPS_Z):
        for i in range(count):
            if not arrived[i]:
                b_along_x(i, j)
        for i in range(count):
            if arrived[i]:
                b_along_z(i, j)
        add_vectors(j + 1)
    for j in range(CHIPS_Z):
        for i in range(count):
            if not arrived[i]:
                b_along_z(i, j)
    l_y.wait_recv()
    l_own[...] = (wide(l_in[...]) + wide(l_yland[...])).astype(jnp.bfloat16)
    ends = [send(l_own, l_cland, a_sems, 1, dc=1)]
    for copy in a_z:
        copy.wait_recv()
    total = wide(a_keep[z]) + wide(a_across[z])
    for k in range(CHIPS_Z - 1):
        total = total + wide(a_zland[k])
    a_ysend[...] = total.astype(jnp.bfloat16)
    a_y = send(a_ysend, a_yland, a_sems, 7, dy=1)
    for i, (_, keep) in enumerate(b_ins):
        _, _, x_land, _, z_land, end_land = b_scratch[i]
        for copy in b_z[i]:
            copy.wait_recv()
        total = wide(keep[:, z, x]) + over(i, 3, x) + wide(x_land[3])
        for k in range(CHIPS_Z - 1):
            total = total + wide(z_land[k])
        b_outs[i][0] = total.astype(jnp.bfloat16)
        for number, step in enumerate((dict(dy=1), dict(dc=1), dict(dy=1, dc=1))):
            ends.append(
                send(b_outs[i].at[0], end_land.at[number], b_sems[i], 11 + number, **step)
            )
    a_y.wait_recv()
    a_own[...] = (wide(a_ysend[...]) + wide(a_yland[...])).astype(jnp.bfloat16)
    ends.append(send(a_own, a_cland, a_sems, 8, dc=1))
    for copy in ends:
        copy.wait_recv()
    for i in range(count):
        b_outs[i][1:4] = b_scratch[i][5][...]
    a_other[...] = a_cland[...]
    l_other[...] = l_cland[...]
    for copy in sent:
        copy.wait_send()


def reduce_tail(flat, pairs, last, sums):
    low = jnp.bfloat16
    _, total, unit = flat[0].shape
    whole = pl.BlockSpec(memory_space=pltpu.VMEM)
    far = pl.BlockSpec(memory_space=pl.ANY)
    piece = (total, unit)
    outs = [piece, piece]
    scratch = [(CHIPS_Z - 1, *piece), (CHIPS_Z - 1, *piece), piece, piece, piece]
    args, specs, arrived = [*flat], [whole, whole], []
    for first, keep, here in pairs:
        parts, _, _, rows, half = keep.shape
        block = (parts, rows, half)
        args += [first, keep]
        specs += [whole if here else far, whole]
        arrived.append(here)
        outs.append((CORES * CHIPS_Y, *block))
        scratch += [
            (16, 128) if here else (CHIPS_Z, parts, CHIPS_X, rows, half),
            (CHIPS_Z, *block),
            (CHIPS_Z, *block),
            (CHIPS_Z - 1, *block),
            (CHIPS_Z - 1, *block),
            (CORES * CHIPS_Y - 1, *block),
        ]
    outs += [last.shape, last.shape]
    scratch += [last.shape, last.shape]
    shapes = [jax.ShapeDtypeStruct(shape, low) for shape in outs]
    vec = (sum_rows(sums[1].shape[1]), D)
    shapes.append(jax.ShapeDtypeStruct(vec, jnp.float32))
    scratch = [pltpu.VMEM(shape, low) for shape in scratch]
    scratch += [pltpu.VMEM((5, *vec), jnp.float32)] * 2
    scratch += [pltpu.SemaphoreType.DMA((2, 9))]
    scratch += [pltpu.SemaphoreType.DMA((2, 14))] * len(pairs)
    scratch += [pltpu.SemaphoreType.DMA((2, 5))]
    own, other, *rest = pl.pallas_call(
        functools.partial(tail_kernel, arrived),
        in_specs=[*specs, whole] + [whole] * len(sums),
        out_specs=[whole] * len(shapes),
        out_shape=shapes,
        scratch_shapes=scratch,
        compiler_params=pltpu.CompilerParams(
            vmem_limit_bytes=KERNEL_VMEM, collective_id=0, has_side_effects=True
        ),
        cost_estimate=pl.CostEstimate(flops=0, bytes_accessed=200_000_000, transcendentals=0),
    )(*args, last, *sums)
    return [own, other], rest[:-3], list(rest[-3:-1]), rest[-1]


def join_kernel(plan, count, at_ref, *refs):
    for ref, out, layer, outer, parts, dc, dy, start, rows in plan:
        ref, out_ref = refs[ref], refs[count + out]
        half = ref.shape[1]
        core = lax.rem(at_ref[3] + dc, CORES)
        row = 0
        if dy is not None:
            row = pl.multiple_of(lax.rem(at_ref[2] + dy, CHIPS_Y) * rows, 16)
        for part in range(parts):
            column = part * CORES + core if outer else core * parts + part
            column = pl.multiple_of(column * half, 128)
            value = ref[start + part * rows : start + (part + 1) * rows]
            out_ref[layer, pl.ds(row, rows), pl.ds(column, half)] = value.astype(jnp.float32)


def join(at, done, shapes):
    arrays, plan = [], []
    for out, (number, (tall, wide)) in enumerate(shapes.items()):
        for layer in range(LAYERS):
            pieces, start, rows = done[layer][number]
            for place, piece in enumerate(pieces):
                known = [other is piece for other in arrays]
                if not any(known):
                    arrays.append(piece)
                    known.append(True)
                parts = wide // (CORES * piece.shape[1])
                dy, dc = (place % CHIPS_Y, place // CHIPS_Y) if len(pieces) > CORES else (None, place)
                plan.append((known.index(True), out, layer, number == 0, parts, dc, dy, start, rows))
    zeros = lambda i, at: (0, 0)
    outs = [(LAYERS, *shape) for shape in shapes.values()]
    return pl.pallas_call(
        functools.partial(join_kernel, plan, len(arrays)),
        grid_spec=pltpu.PrefetchScalarGridSpec(
            num_scalar_prefetch=1,
            grid=(1,),
            in_specs=[pl.BlockSpec(array.shape, zeros) for array in arrays],
            out_specs=[pl.BlockSpec(out, lambda i, at: (0, 0, 0)) for out in outs],
        ),
        out_shape=[jax.ShapeDtypeStruct(out, jnp.float32) for out in outs],
        compiler_params=kernel_params(),
        cost_estimate=pl.CostEstimate(flops=0, bytes_accessed=4_000_000, transcendentals=0),
    )(at, *arrays)


def local(
    fast,
    inputs,
    cotangent,
    segment,
    parent,
    clusters,
    *weights,
):
    flow = Flow()
    if fast:
        place = Place()
        at = place.at
        blocks = pack(weights, list(CHUNKS), place)
        own_vectors = jnp.concatenate([weights[member] for member in VECTORS], axis=1)
        own_vectors = jnp.pad(own_vectors, ((0, 16 - LAYERS), (0, 0)))
        slots, bias, found, lowest = gather_layer(
            segment, parent, clusters, own_vectors, weights, 0, (6, 8, 2)
        )
        vectors = spread_vectors(found, [weights[number].shape[1] for number in VECTORS])

        def get(layer, number):
            if layer == 0:
                return lowest[MATRICES.index(number)]
            else:
                for name, (chunk_layer, numbers, _) in CHUNKS.items():
                    if chunk_layer == layer and number in numbers:
                        return flow.finish(name)[numbers.index(number)]

        def step(point, main):
            advanced, started = FORWARD.get(point, ((), ()))
            fresh = [blocks[name] for name in started]
            main, fresh = flow.tick((main, fresh), *advanced)
            for name, block in zip(started, fresh):
                _, numbers, split_y = CHUNKS[name]
                layout = chunk_rows(weights, numbers, split_y)
                flow.start(name, gather_chain(block, layout, split_y, place))
            return main

        def reduce(layer, *grads):
            name = ("grad", layer, grads[0].number)
            if name[2] == 0:
                chain = reduce_y_first(*grads, place, None if layer else "sums")
            elif name[2] == 6:
                chain = reduce_y_first(*grads, place, "y")
            else:
                chain = reduce_x_first(grads, place, "z" if layer else "x")
            flow.start(name, chain)

        def back_step(main, *held):
            return flow.tick(main, *[name for name in flow.running if name not in held])

    else:
        at = jnp.zeros((4,), jnp.int32)

        slots, bias = prepare(segment, parent, clusters)
        vectors = [
            lax.all_gather(weights[number], "shard", axis=1, tiled=True).astype(jnp.float32)
            for number in VECTORS
        ]

        def get(layer, number):
            return lax.all_gather(weights[number][layer], "shard", axis=0, tiled=True)

        def step(point, main):
            return main

        def reduce(layer, *grads):
            for grad in grads:
                own, away = grad.rights
                if not grad.cut:
                    own = jnp.concatenate([own, away], axis=2)
                    own = own.transpose(1, 0, 2).reshape(own.shape[1], -1)
                total = contract_first(grad.left, own)
                total = lax.psum_scatter(total, "shard", scatter_dimension=0, tiled=True)
                total = lax.psum(total.astype(jnp.bfloat16), "rep").astype(jnp.float32)
                flow.done[("grad", layer, grad.number)] = total

        def back_step(main, *held):
            return main

    vector = dict(zip(VECTORS, vectors))
    hidden, hidden_low = inputs, inputs
    saved = []
    for layer in range(LAYERS):
        pull = functools.partial(get, layer)
        weight = pull(0)
        if layer == 0:
            weight = step("ready", weight)
        projected = project(layer, hidden_low, weight, vector[1])
        projected = step((layer, "projected"), projected)
        first = attend(projected, slots, bias, 0, ())
        first = step((layer, "half"), first)
        context, *heads = attend(projected, slots, bias, 1, first)
        context = step((layer, "context"), context)
        entered = hidden_low
        middle, act, slope, *norms, hidden, hidden_low = feed(
            layer,
            context,
            hidden,
            [pull(2), pull(6), pull(8)],
            [vector[number] for number in (3, 4, 5, 7, 9, 10, 11)],
        )
        hidden_low = step((layer, "result"), hidden_low)
        saved.append((entered, heads, context, middle, act, slope, norms))
    result = hidden_low
    above, proj = cotangent, None
    sums = [None] * LAYERS
    for layer in reversed(range(LAYERS)):
        entered, heads, context, middle, act, slope, norms = saved[layer]
        pull = functools.partial(get, layer)
        down, grad_pre, grad_attn, attn_low, grad_context, row_sums, ffin_sum = feed_back(
            layer,
            above,
            proj,
            None if proj is None else get(layer + 1, 0),
            at,
            [norms[2], norms[3], slope, norms[0], norms[1]],
            [pull(2), pull(6), pull(8)],
            [vector[4], vector[10]],
        )
        sums[layer] = [row_sums, ffin_sum]
        down = back_step(down)
        wide = grad_pre.shape[1] // CORES
        grad_8 = Grad(8, act, down, down, True, act.shape[1] // D, UNIT)
        grad_2 = Grad(2, context, attn_low, attn_low, True, 1, UNIT)
        if layer == 0:
            reduce(layer, grad_8, grad_2)
            reduce(layer, Grad(6, middle, grad_pre, grad_pre, True, wide // D, D))
        else:
            grad_6 = Grad(6, middle, grad_pre, grad_pre, True, wide // UNIT, UNIT)
            reduce(layer, grad_8, grad_6, grad_2)
        above_chain = () if layer else (("grad", 1, 8),)
        grad_context = back_step(grad_context, *above_chain)
        away, away_sums = attend_back(grad_context, slots, heads, at, True)
        wide_chains = (("grad", layer, 8), ("grad", layer, 6))
        grad_context, away = back_step((grad_context, away), *above_chain, *wide_chains)
        own, own_sums = attend_back(grad_context, slots, heads, at, False)
        proj = (own, away)
        reduce(layer, Grad(0, entered, own, away, False, 3, UNIT))
        sums[layer] += [own_sums, away_sums]
        proj = back_step(proj, *(wide_chains if layer else ()))
        above = grad_attn
    grad_input = input_grad(above, proj, get(0, 0), at)
    sums = [item for layer in sums for item in layer]
    if fast:
        while flow.running:
            grad_input = back_step(grad_input)
        done = flow.done
        last, grad_input = lax.optimization_barrier((done["grad", 1, 8], grad_input))
        flat, ends, last, total = reduce_tail(
            done["grad", 0, 8], [done["grad", 0, 6], done["grad", 0, 0]], last, sums
        )
    else:
        norms, wide, heads = [], [], []
        for row_sums, ffin_sum, own_sums, away_sums in (sums[:4], sums[4:]):
            norms.append(row_sums)
            wide.append(ffin_sum.reshape(-1, D))
            found = jnp.concatenate([own_sums.sum(0), away_sums.sum(0)])
            heads.append(found.transpose(1, 0, 2).reshape(8, D))
        total = lax.psum(jnp.concatenate(norms + wide + heads), AXES)
    count = lax.axis_size("shard")
    shard = lax.axis_index("shard")
    ffin_rows = sums[1].shape[1] // D

    def share(rows):
        stacked = jnp.stack([total[row].reshape(-1) for row in rows])
        width = stacked.shape[1] // count
        return lax.dynamic_slice_in_dim(stacked, shard * width, width, axis=1)

    starts = [0, 8, 16, 16 + ffin_rows]
    heads_at = [16 + 2 * ffin_rows, 24 + 2 * ffin_rows]
    grads = {
        1: share([slice(at, at + 3, 2) for at in heads_at]),
        7: share([slice(at, at + ffin_rows) for at in starts[2:]]),
    }
    for number, row in ((10, 0), (11, 1), (9, 2), (4, 3), (5, 4), (3, 5)):
        grads[number] = share([row, 8 + row])
    if fast:
        rows = {number: weights[number].shape[1] for number in MATRICES}
        parts = {number: weights[number].shape[2] // (CORES * UNIT) for number in MATRICES}
        known = [{}, dict(done["grad", 1, 0])]
        for layer, pieces, numbers in ((0, flat, (8, 2)), (1, last, (8, 6, 2))):
            start = 0
            for number in numbers:
                known[layer][number] = (pieces, start, rows[number])
                start += rows[number] * parts[number]
        for number, end in zip((6, 0), ends):
            end = end.reshape(end.shape[0], -1, end.shape[-1])
            known[0][number] = (list(end), 0, rows[number] // CHIPS_Y)
        for numbers in (MATRICES,):
            shapes = {number: weights[number].shape[1:] for number in numbers}
            grads.update(zip(numbers, join(at, known, shapes)))
    else:
        for number in MATRICES:
            grads[number] = jnp.stack([flow.done[("grad", layer, number)] for layer in range(LAYERS)])
    return (result, grad_input, *[grads[number] for number in range(12)])


def solution(mesh):
    in_specs = (
        P(("rep", "shard"), None),
        P(("rep", "shard"), None),
        P(("rep", "shard")),
        P(("rep", "shard"), None),
        P(None, ("rep", "shard")),
        P(None, "shard", None),
        P(None, "shard"),
        P(None, "shard", None),
        P(None, "shard"),
        P(None, "shard"),
        P(None, "shard"),
        P(None, "shard", None),
        P(None, "shard"),
        P(None, "shard", None),
        P(None, "shard"),
        P(None, "shard"),
        P(None, "shard"),
    )
    out_specs = (
        P(("rep", "shard"), None),
        P(("rep", "shard"), None),
        P(None, "shard", None),
        P(None, "shard"),
        P(None, "shard", None),
        P(None, "shard"),
        P(None, "shard"),
        P(None, "shard"),
        P(None, "shard", None),
        P(None, "shard"),
        P(None, "shard", None),
        P(None, "shard"),
        P(None, "shard"),
        P(None, "shard"),
    )
    fast = mesh.shape["rep"] == CHIPS_Y * CORES and mesh.shape["shard"] == CHIPS_Z * CHIPS_X
    return jax.shard_map(
        functools.partial(local, fast),
        mesh=mesh,
        in_specs=in_specs,
        out_specs=out_specs,
        check_vma=False,
    )
```

```python
import functools

import jax
import jax.numpy as jnp
from jax import lax
from jax.experimental import pallas as pl
from jax.experimental.pallas import tpu as pltpu
from jax.sharding import PartitionSpec as P

D = 768
HEADS = 12
HEAD_DIM = 64
LAYERS = 2
CLUSTER = 128
TREE_LEN = 1024
SEGMENTS = 13
PAIRS = HEADS // 2
LANES = 2 * HEAD_DIM
KERNEL_VMEM = 60 * 2**20
ROW_TILE = 256
FEED_TILE = 768
DEPTH_TILE = 384
INV_ROOT = (2.0 * 3.141592653589793) ** -0.5
MATRICES = (0, 2, 6, 8)
VECTORS = (1, 3, 4, 5, 7, 9, 10, 11)
UNIT = 384
AXES = ("rep", "shard")
CHIPS_Z, CHIPS_X, CHIPS_Y, CORES = 4, 2, 2, 2
norm_eps = 1e-06


def one_hot_rows(slot_row):
    length = slot_row.shape[-1]
    rows = lax.broadcasted_iota(jnp.int32, (length, length), 0)
    return jnp.where(rows == slot_row, 1.0, 0.0).astype(jnp.bfloat16)


def first_lanes(length):
    return lax.broadcasted_iota(jnp.int32, (length, LANES), 1) < HEAD_DIM


def contract_last(left_side, right_side):
    return lax.dot_general(
        left_side, right_side, (((1,), (1,)), ((), ())), preferred_element_type=jnp.float32
    )


def contract_first(left_side, right_side):
    return lax.dot_general(
        left_side, right_side, (((0,), (0,)), ((), ())), preferred_element_type=jnp.float32
    )


def cluster_blocks(values):
    return [values[at : at + CLUSTER] for at in range(0, values.shape[0], CLUSTER)]


def attend_pair(slots, query, key, value, bias, store):
    low = first_lanes(TREE_LEN)
    query = query * jnp.bfloat16(HEAD_DIM**-0.5)
    packed = (
        jnp.where(low, query, pltpu.roll(key, HEAD_DIM, 1)),
        jnp.where(low, pltpu.roll(query, HEAD_DIM, 1), key),
    )
    context = []
    for head in range(2):
        table = one_hot_rows(slots[head : head + 1])
        joined = jnp.concatenate([packed[head], value], axis=1)
        found = jnp.dot(table, joined, preferred_element_type=jnp.float32).astype(jnp.bfloat16)
        both, values = found[:, :LANES], found[:, LANES:]
        store("both", head, both)
        store("values", head, values)
        queries = jnp.where(low, both, jnp.bfloat16(0))
        keys = pltpu.roll(both, HEAD_DIM, 1)
        scores = jnp.concatenate(
            [contract_last(q, k) for q, k in zip(cluster_blocks(queries), cluster_blocks(keys))],
            axis=0,
        )
        scores = scores + bias[head].astype(jnp.float32)
        numerator = jnp.exp(scores - jnp.max(scores, axis=1, keepdims=True))
        total = jnp.sum(numerator, axis=1, keepdims=True)
        soft = (numerator * (1.0 / total)).astype(jnp.bfloat16)
        store("soft", head, soft)
        out = jnp.concatenate(
            [
                jnp.dot(p, v, preferred_element_type=jnp.float32)
                for p, v in zip(cluster_blocks(soft), cluster_blocks(values))
            ],
            axis=0,
        ).astype(jnp.bfloat16)
        context.append(contract_first(table, out))
        if head == 0:
            yield
    store("context", None, jnp.where(low, context[0], context[1]).astype(jnp.bfloat16))


def attend_kernel(slot_ref, query_ref, key_ref, value_ref, bias_ref, ctx_ref, qk_ref, val_ref, p_ref):
    refs = {"both": qk_ref, "values": val_ref, "soft": p_ref}

    def store(name, head, value):
        if head is None:
            ctx_ref[...] = value
        else:
            refs[name][0, head] = value

    for _ in attend_pair(
        slot_ref[0, 0], query_ref[...], key_ref[...], value_ref[...], bias_ref[0], store
    ):
        pass


def attend_steps(ins, outs):
    projected_ref, slot_ref, bias_ref = ins
    ctx_ref, qk_ref, val_ref, p_ref = outs
    refs = {"both": qk_ref, "values": val_ref, "soft": p_ref}
    for tree in range(slot_ref.shape[0]):
        rows = slice(tree * TREE_LEN, (tree + 1) * TREE_LEN)
        for pair in range(PAIRS):
            lanes = [slice((part * PAIRS + pair) * LANES, (part * PAIRS + pair + 1) * LANES) for part in range(3)]
            heads = slice(2 * pair, 2 * pair + 2)

            def store(name, head, value):
                if head is None:
                    ctx_ref[rows, lanes[0]] = value
                else:
                    refs[name][tree, 2 * pair + head] = value

            yield from attend_pair(
                slot_ref[tree, pair],
                *[projected_ref[rows, part] for part in lanes],
                bias_ref[tree, heads],
                store,
            )
            yield


def attend_back_kernel(at_ref, slot_ref, grad_ref, qk_ref, val_ref, p_ref, out_ref, sums_ref):
    low = first_lanes(TREE_LEN)
    grads = grad_ref[...]
    placed = []
    for head in range(2):
        table = one_hot_rows(slot_ref[0, 0, head : head + 1, :])
        slots = jnp.dot(table, grads, preferred_element_type=jnp.float32)
        slots = jnp.where(low == (head == 0), slots, 0.0).astype(jnp.bfloat16)
        both, values, soft = qk_ref[0, head], val_ref[0, head], p_ref[0, head]
        grad_soft = jnp.concatenate(
            [contract_last(g, v) for g, v in zip(cluster_blocks(slots), cluster_blocks(values))],
            axis=0,
        )
        grad_value = jnp.concatenate(
            [contract_first(p, g) for p, g in zip(cluster_blocks(soft), cluster_blocks(slots))],
            axis=0,
        ).astype(jnp.bfloat16)
        weights = soft.astype(jnp.float32)
        delta = jnp.sum(weights * grad_soft, axis=1, keepdims=True)
        grad_scores = (weights * (grad_soft - delta)).astype(jnp.bfloat16)
        pairs = list(zip(cluster_blocks(grad_scores), cluster_blocks(both)))
        by_key = jnp.concatenate([contract_first(s, b) for s, b in pairs], axis=0)
        by_query = jnp.concatenate(
            [jnp.dot(s, b, preferred_element_type=jnp.float32) for s, b in pairs], axis=0
        )
        mixed = jnp.where(low, by_key, by_query * HEAD_DIM**-0.5).astype(jnp.bfloat16)
        joined = jnp.concatenate([mixed, grad_value], axis=1)
        placed.append(contract_first(table, joined))
    first, second = placed
    queries = jnp.where(low, pltpu.roll(first[:, :LANES], HEAD_DIM, 1), second[:, :LANES])
    keys = jnp.where(low, first[:, :LANES], pltpu.roll(second[:, :LANES], HEAD_DIM, 1))
    values = jnp.where(low, first[:, LANES:], second[:, LANES:])
    sums = []
    for part, grad in enumerate((queries, keys, values)):
        rounded = grad.astype(jnp.bfloat16)
        out_ref[part] = rounded
        sums.append(rows_sum(rounded.astype(jnp.float32)))
    sums_ref[0, 0] = jnp.concatenate(sums + [jnp.zeros((5, LANES), jnp.float32)], axis=0)


def slot_spec(start=0):
    return pl.BlockSpec((1, 1, 2, TREE_LEN), lambda tree, pair: (tree, start + pair, 0, 0))


def head_spec(start=0):
    return pl.BlockSpec((1, 2, TREE_LEN, LANES), lambda tree, pair: (tree, start + pair, 0, 0))


def column_spec(offset):
    return pl.BlockSpec((TREE_LEN, LANES), lambda tree, pair: (tree, offset + pair))


def kernel_params():
    return pltpu.CompilerParams(vmem_limit_bytes=KERNEL_VMEM)


def attend_shapes(trees):
    stored = jax.ShapeDtypeStruct((trees, HEADS, TREE_LEN, LANES), jnp.bfloat16)
    return [jax.ShapeDtypeStruct((trees * TREE_LEN, D), jnp.bfloat16), stored, stored, stored]


def attend(projected, slots, bias):
    trees = slots.shape[0]
    return pl.pallas_call(
        attend_kernel,
        grid=(trees, PAIRS),
        in_specs=[
            slot_spec(),
            column_spec(0),
            column_spec(PAIRS),
            column_spec(2 * PAIRS),
            head_spec(),
        ],
        out_specs=[column_spec(0), head_spec(), head_spec(), head_spec()],
        out_shape=attend_shapes(trees),
        compiler_params=kernel_params(),
        cost_estimate=pl.CostEstimate(
            flops=trees * 30_000_000_000, bytes_accessed=trees * 20_000_000, transcendentals=0
        ),
    )(slots, projected, projected, projected, bias)


def attend_back(grad_context, slots, kept, at, other):
    trees = slots.shape[0]
    count = PAIRS // CORES
    flip = 1 if other else 0

    def pair_of(pair, at):
        return lax.rem(at[3] + flip, CORES) * count + pair

    head = pl.BlockSpec(
        (1, 2, TREE_LEN, LANES), lambda tree, pair, at: (tree, pair_of(pair, at), 0, 0)
    )
    return pl.pallas_call(
        attend_back_kernel,
        grid_spec=pltpu.PrefetchScalarGridSpec(
            num_scalar_prefetch=1,
            grid=(trees, count),
            in_specs=[
                pl.BlockSpec(
                    (1, 1, 2, TREE_LEN), lambda tree, pair, at: (tree, pair_of(pair, at), 0, 0)
                ),
                pl.BlockSpec((TREE_LEN, LANES), lambda tree, pair, at: (tree, pair_of(pair, at))),
                head,
                head,
                head,
            ],
            out_specs=[
                pl.BlockSpec((3, TREE_LEN, LANES), lambda tree, pair, at: (0, tree, pair)),
                pl.BlockSpec((1, 1, 8, LANES), lambda tree, pair, at: (tree, pair, 0, 0)),
            ],
        ),
        out_shape=[
            jax.ShapeDtypeStruct((3, trees * TREE_LEN, D // CORES), jnp.bfloat16),
            jax.ShapeDtypeStruct((trees, count, 8, LANES), jnp.float32),
        ],
        compiler_params=kernel_params(),
        cost_estimate=pl.CostEstimate(
            flops=trees * 17_000_000_000, bytes_accessed=trees * 10_000_000, transcendentals=0
        ),
    )(at, slots, grad_context, *kept)


def erf_parts(values):
    size = jnp.abs(values)
    turn = 1.0 / (1.0 + (0.3275911 * 0.5**0.5) * size)
    bell = jnp.exp(-0.5 * values * values)
    series = 1.061405429 * 0.5
    for factor in (-1.453152027, 1.421413741, -0.284496736, 0.254829592):
        series = series * turn + factor * 0.5
    tail = series * turn * bell
    return jnp.where(values < 0.0, tail, 1.0 - tail), bell


def norm_parts(values):
    centred = values - jnp.mean(values, axis=-1, keepdims=True)
    scale = lax.rsqrt(jnp.mean(centred * centred, axis=-1, keepdims=True) + norm_eps)
    return centred * scale, scale


def norm_back(grad, normal, scale, gain):
    inner = grad * gain
    mean = jnp.mean(inner, axis=-1, keepdims=True)
    along = jnp.mean(inner * normal, axis=-1, keepdims=True)
    return scale * (inner - mean - normal * along)


def spread(column):
    return jnp.broadcast_to(column, (column.shape[0], 128))


def rows_sum(values):
    return jnp.sum(values, axis=0, keepdims=True)


def project_kernel(layer, rows_ref, weight_ref, bias_ref, out_ref):
    product = jnp.dot(rows_ref[...], weight_ref[...], preferred_element_type=jnp.float32)
    bias = bias_ref[layer : layer + 1]
    out_ref[:, :D] = (product[:, :D] + bias[:, :D]).astype(jnp.bfloat16)
    out_ref[:, D : 2 * D] = product[:, D : 2 * D].astype(jnp.bfloat16)
    out_ref[:, 2 * D :] = (product[:, 2 * D :] + bias[:, D:]).astype(jnp.bfloat16)


def feed_kernel(
    layer,
    context_ref,
    rows_ref,
    out_weight_ref,
    ffin_weight_ref,
    ffout_weight_ref,
    out_bias_ref,
    attn_gain_ref,
    attn_shift_ref,
    ffin_bias_ref,
    ffout_bias_ref,
    ffn_gain_ref,
    ffn_shift_ref,
    hidden_ref,
    act_ref,
    slope_ref,
    attn_normal_ref,
    attn_scale_ref,
    ffn_normal_ref,
    ffn_scale_ref,
    result_ref,
    result_low_ref,
):
    here = slice(layer, layer + 1)
    product = jnp.dot(context_ref[...], out_weight_ref[...], preferred_element_type=jnp.float32)
    attn_sum = rows_ref[...].astype(jnp.float32) + product + out_bias_ref[here]
    normal, scale = norm_parts(attn_sum)
    attn_normal_ref[...] = normal
    attn_scale_ref[...] = spread(scale)
    hidden = normal * attn_gain_ref[here] + attn_shift_ref[here]
    hidden_low = hidden.astype(jnp.bfloat16)
    hidden_ref[...] = hidden_low
    total = hidden + ffout_bias_ref[here]
    width = ffin_weight_ref.shape[1]
    for at in range(0, width, FEED_TILE):
        part = slice(at, at + FEED_TILE)
        pre = (
            jnp.dot(hidden_low, ffin_weight_ref[:, part], preferred_element_type=jnp.float32)
            + ffin_bias_ref[here, part]
        )
        below, bell = erf_parts(pre)
        act = (pre * below).astype(jnp.bfloat16)
        act_ref[:, part] = act
        slope_ref[:, part] = (below + pre * bell * INV_ROOT).astype(jnp.bfloat16)
        total = total + jnp.dot(
            act, ffout_weight_ref[part, :], preferred_element_type=jnp.float32
        )
    normal, scale = norm_parts(total)
    ffn_normal_ref[...] = normal
    ffn_scale_ref[...] = spread(scale)
    result = normal * ffn_gain_ref[here] + ffn_shift_ref[here]
    result_ref[...] = result
    result_low_ref[...] = result.astype(jnp.bfloat16)


def add_projected(grad, at_ref, own_ref, away_ref, weight_ref):
    half = own_ref.shape[2]
    for flip, ref in enumerate((own_ref, away_ref)):
        core = lax.rem(at_ref[3] + flip, CORES)
        for part in range(3):
            column = pl.multiple_of((part * CORES + core) * half, 128)
            grad = grad + contract_last(ref[part], weight_ref[:, pl.ds(column, half)])
    return grad


def feed_back_kernel(layer, with_proj, *refs):
    here = slice(layer, layer + 1)
    if with_proj:
        above_ref, at_ref, own_ref, away_ref, qkv_weight_ref, *refs = refs
        grad = add_projected(above_ref[...], at_ref, own_ref, away_ref, qkv_weight_ref)
    else:
        above_ref, *refs = refs
        grad = above_ref[...].astype(jnp.float32)
    (
        ffn_normal_ref,
        ffn_scale_ref,
        slope_ref,
        attn_normal_ref,
        attn_scale_ref,
        out_weight_ref,
        ffin_weight_ref,
        ffout_weight_ref,
        attn_gain_ref,
        ffn_gain_ref,
        down_ref,
        pre_ref,
        attn_ref,
        attn_low_ref,
        context_ref,
        sums_ref,
        ffin_sum_ref,
    ) = refs

    @pl.when(pl.program_id(0) == 0)
    def _():
        sums_ref[...] = jnp.zeros_like(sums_ref)
        ffin_sum_ref[...] = jnp.zeros_like(ffin_sum_ref)

    normal = ffn_normal_ref[...]
    sums_ref[0:1] += rows_sum(grad * normal)
    sums_ref[1:2] += rows_sum(grad)
    grad_sum = norm_back(grad, normal, ffn_scale_ref[:, 0:1], ffn_gain_ref[here])
    down = grad_sum.astype(jnp.bfloat16)
    down_ref[...] = down
    sums_ref[2:3] += rows_sum(down.astype(jnp.float32))
    total = grad_sum
    width = ffin_weight_ref.shape[1]
    for at in range(0, width, FEED_TILE):
        part = slice(at, at + FEED_TILE)
        grad_act = contract_last(down, ffout_weight_ref[part, :])
        pre = (grad_act * slope_ref[:, part].astype(jnp.float32)).astype(jnp.bfloat16)
        pre_ref[:, part] = pre
        ffin_sum_ref[:, part] += rows_sum(pre.astype(jnp.float32))
        total = total + contract_last(pre, ffin_weight_ref[:, part])
    normal = attn_normal_ref[...]
    sums_ref[3:4] += rows_sum(total * normal)
    sums_ref[4:5] += rows_sum(total)
    attn = norm_back(total, normal, attn_scale_ref[:, 0:1], attn_gain_ref[here])
    attn_ref[...] = attn
    low = attn.astype(jnp.bfloat16)
    attn_low_ref[...] = low
    sums_ref[5:6] += rows_sum(low.astype(jnp.float32))
    context_ref[...] = contract_last(low, out_weight_ref[...]).astype(jnp.bfloat16)


def input_grad_kernel(above_ref, at_ref, own_ref, away_ref, weight_ref, out_ref):
    out_ref[...] = add_projected(above_ref[...], at_ref, own_ref, away_ref, weight_ref)


def prep_pair(parent_ref, segment_ref, cluster_ref, slot_ref, bias_ref, row, tree, pair):
    segs = segment_ref[tree]
    length = segs.shape[1]

    def parent_of(values):
        found = jnp.zeros_like(values)
        for number in range(SEGMENTS):
            found = jnp.where(values == number, parent_ref[row, number], found)
        return found

    parents = parent_of(segs)
    grands = parent_of(parents)
    ids = jnp.concatenate([segs, parents, grands, jnp.zeros((5, length), jnp.int32)], axis=0)
    ids = jnp.concatenate([ids, jnp.zeros((8, length), jnp.int32)], axis=0)
    ids = ids.astype(jnp.float32).astype(jnp.bfloat16)
    count = length // CLUSTER
    order = lax.broadcasted_iota(jnp.int32, (count, length), 0)
    lanes = lax.broadcasted_iota(jnp.int32, (count, length), 1)
    for head in range(2):
        member = order == cluster_ref[tree, pair, head : head + 1, :]
        ranks = member.astype(jnp.int32)
        step = 1
        while step < length:
            ranks = ranks + jnp.where(lanes >= step, pltpu.roll(ranks, step, 1), 0)
            step *= 2
        slot = jnp.sum(
            jnp.where(member, ranks - 1 + CLUSTER * order, 0), axis=0, keepdims=True
        )
        slot_ref[tree, pair, head : head + 1, :] = slot
        table = one_hot_rows(slot)
        rows = contract_last(ids, table)
        columns = jnp.concatenate([rows] * (128 // rows.shape[0]), axis=0).T
        for at in range(0, length, CLUSTER):
            here = rows[0:1, at : at + CLUSTER]
            block = columns[at : at + CLUSTER]
            allowed = (
                (here == block[:, 0:1]) | (here == block[:, 1:2]) | (here == block[:, 2:3])
            )
            bias_ref[tree, 2 * pair + head, at : at + CLUSTER, :] = jnp.where(allowed, 0.0, -1e30).astype(
                jnp.bfloat16
            )


def prep_kernel(*refs):
    prep_pair(*refs, pl.program_id(0), 0, 0)


def row_spec(width, rows=ROW_TILE):
    return pl.BlockSpec((rows, width), lambda i: (i, 0))


def whole_spec(shape):
    return pl.BlockSpec(
        shape, lambda i: (0,) * len(shape), pipeline_mode=pl.Buffered(1)
    )


def part_spec(rows=ROW_TILE):
    return pl.BlockSpec((3, rows, D // CORES), lambda i: (0, i, 0))


def cost(flops, *arrays):
    moved = sum(array.size * array.dtype.itemsize for array in arrays)
    return pl.CostEstimate(flops=int(flops), bytes_accessed=moved, transcendentals=0)


def shape_of(rows, width, kind=jnp.bfloat16):
    return jax.ShapeDtypeStruct((rows, width), kind)


def project(layer, rows, weight, bias):
    count, width = rows.shape[0], weight.shape[1]
    return pl.pallas_call(
        functools.partial(project_kernel, layer),
        grid=(count // ROW_TILE,),
        in_specs=[row_spec(D), whole_spec(weight.shape), whole_spec(bias.shape)],
        out_specs=row_spec(width),
        out_shape=shape_of(count, width),
        compiler_params=kernel_params(),
        cost_estimate=cost(2.4 * count * D * width, rows, weight),
    )(rows, weight, bias)


def feed(layer, context, rows, weights, vectors):
    count = context.shape[0]
    width = weights[1].shape[1]
    f32 = jnp.float32
    return pl.pallas_call(
        functools.partial(feed_kernel, layer),
        grid=(count // ROW_TILE,),
        in_specs=[row_spec(D), row_spec(D)]
        + [whole_spec(weight.shape) for weight in weights]
        + [whole_spec(vector.shape) for vector in vectors],
        out_specs=[
            row_spec(D),
            row_spec(width),
            row_spec(width),
            row_spec(D),
            row_spec(128),
            row_spec(D),
            row_spec(128),
            row_spec(D),
            row_spec(D),
        ],
        out_shape=[
            shape_of(count, D),
            shape_of(count, width),
            shape_of(count, width),
            shape_of(count, D, f32),
            shape_of(count, 128, f32),
            shape_of(count, D, f32),
            shape_of(count, 128, f32),
            shape_of(count, D, f32),
            shape_of(count, D),
        ],
        compiler_params=kernel_params(),
        cost_estimate=cost(5 * count * D * (2 * width + D), context, *weights),
    )(context, rows, *weights, *vectors)


def feed_back(layer, above, proj, qkv_weight, at, saved, weights, gains):
    count = above.shape[0]
    width = weights[1].shape[1]
    f32 = jnp.float32
    lead, lead_specs = [above], [row_spec(D)]
    if proj is not None:
        lead += [at, *proj, qkv_weight]
        lead_specs += [
            pl.BlockSpec(memory_space=pltpu.SMEM),
            part_spec(),
            part_spec(),
            whole_spec(qkv_weight.shape),
        ]
    return pl.pallas_call(
        functools.partial(feed_back_kernel, layer, proj is not None),
        grid=(count // ROW_TILE,),
        in_specs=lead_specs
        + [row_spec(D), row_spec(128), row_spec(width), row_spec(D), row_spec(128)]
        + [whole_spec(weight.shape) for weight in weights]
        + [whole_spec(gain.shape) for gain in gains],
        out_specs=[
            row_spec(D),
            row_spec(width),
            row_spec(D),
            row_spec(D),
            row_spec(D),
            pl.BlockSpec((8, D), lambda i: (0, 0)),
            pl.BlockSpec((1, width), lambda i: (0, 0)),
        ],
        out_shape=[
            shape_of(count, D),
            shape_of(count, width),
            shape_of(count, D, f32),
            shape_of(count, D),
            shape_of(count, D),
            shape_of(8, D, f32),
            shape_of(1, width, f32),
        ],
        compiler_params=kernel_params(),
        cost_estimate=cost(5 * count * D * (2 * width + D), above, *weights),
    )(*lead, *saved, *weights, *gains)


def input_grad(above, proj, qkv_weight, at):
    count = above.shape[0]
    return pl.pallas_call(
        input_grad_kernel,
        grid=(count // ROW_TILE,),
        in_specs=[
            row_spec(D),
            pl.BlockSpec(memory_space=pltpu.SMEM),
            part_spec(),
            part_spec(),
            whole_spec(qkv_weight.shape),
        ],
        out_specs=row_spec(D),
        out_shape=shape_of(count, D, jnp.float32),
        compiler_params=kernel_params(),
        cost_estimate=cost(2.4 * count * D * 3 * D, above, qkv_weight),
    )(above, at, *proj, qkv_weight)


def prepare(segment, parent, clusters):
    trees = parent.shape[0]
    segment = segment.reshape(trees, 1, TREE_LEN)
    clusters = clusters.reshape(PAIRS, 2, trees, TREE_LEN).transpose(2, 0, 1, 3)
    return pl.pallas_call(
        prep_kernel,
        grid=(trees, PAIRS),
        in_specs=[
            pl.BlockSpec(memory_space=pltpu.SMEM),
            pl.BlockSpec((1, 1, TREE_LEN), lambda tree, pair: (tree, 0, 0)),
            slot_spec(),
        ],
        out_specs=[slot_spec(), head_spec()],
        out_shape=[
            jax.ShapeDtypeStruct((trees, PAIRS, 2, TREE_LEN), jnp.int32),
            jax.ShapeDtypeStruct((trees, HEADS, TREE_LEN, LANES), jnp.bfloat16),
        ],
        compiler_params=kernel_params(),
        cost_estimate=pl.CostEstimate(
            flops=trees * 20_000_000_000, bytes_accessed=trees * 4_000_000, transcendentals=0
        ),
    )(parent, segment, clusters)


def weight_grad_kernel(split_y, at_ref, left_ref, right_ref, *refs):
    product = contract_first(
        left_ref[...].reshape(left_ref.shape[-2:]), right_ref[...].reshape(right_ref.shape[-2:])
    )
    if split_y is None:
        (out_ref,) = refs
        out_ref[...] = product.astype(jnp.bfloat16).reshape(out_ref.shape)
        return
    near_ref, (send_ref, keep_ref, sum_ref) = refs[0], refs[-3:]
    total = product + near_ref[...].astype(jnp.float32).reshape(product.shape)
    sum_ref[...] = total.astype(jnp.bfloat16).reshape(sum_ref.shape)
    if split_y:
        send_ref[0] = sum_ref[:, :, 1 - at_ref[2]]
        keep_ref[0] = sum_ref[:, :, at_ref[2]]
    else:
        send_ref[...] = sum_ref[:, 1 - at_ref[1]]
        keep_ref[...] = sum_ref[:, at_ref[1]]


class Grad:
    def __init__(self, number, left, own, away, cut, tiles, half):
        self.number = number
        self.left, self.rights = left, (own, away)
        self.cut, self.tiles, self.half = cut, tiles, half
        self.depth = left.shape[1]
        self.parts = 1 if self.depth > D else tiles
        self.rows = self.depth // (CHIPS_Z * CHIPS_X)

    def product(self, at, other, split_y=None, near=None, start=0, total=0, before=()):
        flip = 1 if other else 0
        left, right = self.left, self.rights[flip]
        count = left.shape[0]
        tall = self.depth > D
        core = lambda at: lax.rem(at[3] + flip, CORES)
        in_specs = [
            pl.BlockSpec((count, D), (lambda i, at: (0, i)) if tall else (lambda i, at: (0, 0)))
        ]
        if not self.cut:
            in_specs.append(pl.BlockSpec((1, count, self.half), lambda i, at: (i, 0, 0)))
        elif tall:
            in_specs.append(pl.BlockSpec((count, self.half), lambda i, at: (0, core(at))))
        else:
            in_specs.append(
                pl.BlockSpec((count, self.half), lambda i, at: (0, core(at) * self.tiles + i))
            )
        zs = D // (self.rows * CHIPS_X)
        place = (lambda i: (0, i)) if tall else (lambda i: (i, 0))
        whole = (self.parts, CHIPS_Z, CHIPS_X, self.rows, self.half)
        block = (1, zs, CHIPS_X, self.rows, self.half)
        full = pl.BlockSpec(block, lambda i, at: (*place(i), 0, 0, 0))
        args, scratch = [left, right], []
        if split_y is None:
            out_specs, shapes = full, jax.ShapeDtypeStruct(whole, jnp.bfloat16)
        else:
            in_specs.append(full)
            args.append(near)
            in_specs += [pl.BlockSpec(memory_space=pl.ANY)] * len(before)
            args += before
            if split_y:
                short = self.rows // CHIPS_Y
                kept = (CHIPS_X, short, self.half)
                scratch = [pltpu.VMEM((zs, CHIPS_X, CHIPS_Y, short, self.half), jnp.bfloat16)]
                spec = pl.BlockSpec((1, zs, *kept), lambda i, at: (*place(i), 0, 0, 0))
                shape = (self.parts, CHIPS_Z, *kept)
            else:
                scratch = [pltpu.VMEM((zs, CHIPS_X, self.rows, self.half), jnp.bfloat16)]
                first = start // self.rows
                index = (lambda i, at: (i, first, 0)) if tall else (lambda i, at: (0, first + i, 0))
                spec = pl.BlockSpec((zs, self.rows, self.half), index)
                shape = (CHIPS_Z, total, self.half)
            out_specs, shapes = [spec] * 2, [jax.ShapeDtypeStruct(shape, jnp.bfloat16)] * 2
        return pl.pallas_call(
            functools.partial(weight_grad_kernel, split_y),
            grid_spec=pltpu.PrefetchScalarGridSpec(
                num_scalar_prefetch=1,
                grid=(self.tiles,),
                in_specs=in_specs,
                out_specs=out_specs,
                scratch_shapes=scratch,
            ),
            out_shape=shapes,
            input_output_aliases={4 + place: place for place in range(len(before))},
            compiler_params=kernel_params(),
            cost_estimate=cost(4 * count * D * self.tiles * self.half, left, right),
        )(at, *args)


def combine_kernel(groups, at_ref, *refs):
    total = sum(groups)
    ins, outs = refs[:total], refs[total:]
    first = 0
    for count, out_ref in zip(groups, outs):
        value = None
        for ref in ins[first : first + count]:
            term = ref[...].astype(jnp.float32).reshape(out_ref.shape)
            value = term if value is None else value + term
        out_ref[...] = value.astype(out_ref.dtype)
        first += count


def combine(at, steps, groups, blocks):
    terms = [term for group in groups for term in group]
    return pl.pallas_call(
        functools.partial(combine_kernel, [len(group) for group in groups]),
        grid_spec=pltpu.PrefetchScalarGridSpec(
            num_scalar_prefetch=1,
            grid=(steps,),
            in_specs=[pl.BlockSpec(block, index) for _, block, index in terms],
            out_specs=[pl.BlockSpec(block, index) for _, block, index in blocks],
        ),
        out_shape=[jax.ShapeDtypeStruct(shape, jnp.bfloat16) for shape, _, _ in blocks],
        compiler_params=kernel_params(),
        cost_estimate=pl.CostEstimate(
            flops=0, bytes_accessed=2_000_000, transcendentals=0
        ),
    )(at, *[array for array, _, _ in terms])


class Place:
    def __init__(self):
        rep = lax.axis_index("rep")
        shard = lax.axis_index("shard")
        self.y, self.core = rep // CORES, rep % CORES
        self.z, self.x = shard // CHIPS_X, shard % CHIPS_X
        self.at = jnp.stack([self.z, self.x, self.y, self.core]).astype(jnp.int32)


def hop(value, dz=0, dx=0, dy=0, dc=0):
    pairs = []
    for y in range(CHIPS_Y):
        for c in range(CORES):
            for z in range(CHIPS_Z):
                for x in range(CHIPS_X):
                    source = ((y * CORES + c) * CHIPS_Z + z) * CHIPS_X + x
                    y2, c2 = (y + dy) % CHIPS_Y, (c + dc) % CORES
                    z2, x2 = (z + dz) % CHIPS_Z, (x + dx) % CHIPS_X
                    pairs.append((source, ((y2 * CORES + c2) * CHIPS_Z + z2) * CHIPS_X + x2))
    return lax.ppermute(value, AXES, pairs)


class Flow:
    def __init__(self):
        self.running, self.done = {}, {}

    def start(self, name, chain):
        self.running[name] = (chain, next(chain))

    def advance(self, name, arrived):
        chain, _ = self.running.pop(name)
        try:
            self.running[name] = (chain, chain.send(list(arrived)))
        except StopIteration as end:
            self.done[name] = end.value

    def tick(self, main, *names):
        names = [name for name in names if name in self.running]
        pending = [self.running[name][1] for name in names]
        main, pending = lax.optimization_barrier((main, pending))
        for name, arrived in zip(names, pending):
            self.advance(name, arrived)
        return main

    def finish(self, name):
        while name in self.running:
            self.advance(name, self.running[name][1])
        return self.done[name]


def spread_vectors(found, sizes):
    found = found[:, :, 0, :LAYERS].reshape(-1, LAYERS, found.shape[-1]).transpose(1, 0, 2)
    out, at = [], 0
    for size in sizes:
        out.append(found[:, :, at : at + size].reshape(LAYERS, -1).astype(jnp.float32))
        at += size
    return out


def pick_sum(at, own, terms, rows, steps):
    groups = [[(array, block, index(k)) for array, block, index in terms] for k in range(CHIPS_Z)]
    return combine(at, steps, groups, [own] * CHIPS_Z)


def reduce_y_first(grad, place, stop=None):
    at = place.at
    parts, half = grad.parts, grad.half
    rows = grad.rows // CHIPS_Y
    away = grad.product(at, True)
    (near,) = yield [hop(away, dc=1)]
    send, keep = grad.product(at, False, True, near)
    if stop == "sums":
        return send, keep, False
    flip = lambda value: 1 - value
    (over,) = yield [hop(send, dy=1)]
    if stop == "y":
        return over, keep, True
    block = (parts, 1, 1, rows, half)
    short = (parts, 1, rows, half)
    index = lambda i, at: (0, i, flip(at[1]), 0, 0)
    (send,) = combine(
        at,
        CHIPS_Z,
        [[(keep, block, index), (over, block, index)]],
        [((parts, CHIPS_Z, rows, half), short, lambda i, at: (0, i, 0, 0))],
    )
    (across,) = yield [hop(send, dx=1)]
    turn = lambda at, k: lax.rem(at[0] + k, CHIPS_Z)
    mine = lambda k: lambda i, at: (0, turn(at, k), at[1], 0, 0)
    piece = (parts, rows, half)
    whole = (piece, piece, lambda i, at: (0, 0, 0))
    own, *sends = pick_sum(
        at,
        whole,
        [
            (keep, block, mine),
            (over, block, mine),
            (across, short, lambda k: lambda i, at: (0, turn(at, k), 0, 0)),
        ],
        rows,
        1,
    )
    landed = yield [hop(send, dz=k) for k, send in zip(range(1, CHIPS_Z), sends)]
    (own,) = combine(at, 1, [[(term, piece, whole[2]) for term in (own, *landed)]], [whole])
    others = yield [hop(own, dy=1), hop(own, dc=1), hop(own, dy=1, dc=1)]
    pieces = [item.reshape(parts * rows, half) for item in (own, *others)]
    return {grad.number: (pieces, 0, rows)}


def reduce_x_first(grads, place, stop):
    at = place.at
    away = [grad.product(at, True) for grad in grads]
    near = yield [hop(item, dc=1) for item in away]
    total = sum(grad.parts * grad.rows for grad in grads)
    starts, flat = [0], ()
    for grad, item in zip(grads, near):
        flat = grad.product(at, False, False, item, starts[-1], total, tuple(flat))
        starts.append(starts[-1] + grad.parts * grad.rows)
    send, keep = flat
    (across,) = yield [hop(send, dx=1)]
    if stop == "x":
        return across, keep
    steps = 3
    tall = total // steps
    ahead = lambda k: lambda i, at: (lax.rem(at[0] + k, CHIPS_Z), i, 0)
    piece = ((total, UNIT), (tall, UNIT), lambda i, at: (i, 0))
    own, *sends = pick_sum(
        at, piece, [(item, (1, tall, UNIT), ahead) for item in (keep, across)], tall, steps
    )
    landed = yield [hop(send, dz=k) for k, send in zip(range(1, CHIPS_Z), sends)]
    add = lambda *terms: combine(at, steps, [[(term, *piece[1:]) for term in terms]], [piece])[0]
    return add(own, *landed)


def prep_steps(ins, outs):
    trees, pairs = ins[2].shape[:2]
    for tree in range(trees):
        for pair in range(pairs):
            prep_pair(*ins, *outs, tree, tree, pair)
            yield


def gather_kernel(plan, work, work_ins, work_outs, *refs):
    count = len(plan)
    own_ins, ins, refs = refs[:work_ins], refs[work_ins : work_ins + count], refs[work_ins + count :]
    own_outs, outs = refs[:work_outs], refs[work_outs : work_outs + count]
    sems, local_sem = refs[work_outs + count : -1], refs[-1]
    todo = work(own_ins, own_outs)
    rep, shard = lax.axis_index("rep"), lax.axis_index("shard")
    y, core = lax.div(rep, CORES), lax.rem(rep, CORES)
    z, x = lax.div(shard, CHIPS_X), lax.rem(shard, CHIPS_X)

    def device(dz=0, dx=0, dy=0, dc=0):
        to_y, to_core = lax.rem(y + dy, CHIPS_Y), lax.rem(core + dc, CORES)
        to_z, to_x = lax.rem(z + dz, CHIPS_Z), lax.rem(x + dx, CHIPS_X)
        return (to_y * CORES + to_core, to_z * CHIPS_X + to_x)

    mates = [dict(dx=1), dict(dy=1), dict(dc=1)] + [dict(dz=k) for k in range(1, CHIPS_Z)]
    barrier = pltpu.get_barrier_semaphore()
    for mate in mates:
        pl.semaphore_signal(
            barrier, inc=1, device_id=device(**mate), device_id_type=pl.DeviceIdType.MESH
        )
    sent = []

    def send(source, target, m, number, **step):
        copy = pltpu.make_async_remote_copy(
            src_ref=source,
            dst_ref=target,
            send_sem=sems[m].at[0, number],
            recv_sem=sems[m].at[1, number],
            device_id=device(**step),
            device_id_type=pl.DeviceIdType.MESH,
        )
        copy.start()
        sent.append(copy)
        return copy

    def part(m, at_z, at_x, at_y, at_core):
        out, (layer, split_y, by_core) = outs[m], plan[m]
        columns = slice(None)
        if by_core:
            half = out.shape[-1] // CORES
            columns = pl.ds(pl.multiple_of(at_core * half, 128), half)
        at_z = slice(None) if at_z is None else at_z
        at_x = slice(None) if at_x is None else at_x
        return out.at[at_z, at_x, at_y if split_y else 0, :, columns]

    locals_ = []
    for m, (layer, split_y, by_core) in enumerate(plan):
        rows = outs[m].shape[3]
        source = ins[m] if layer is None else ins[m].at[layer]
        if by_core:
            half = outs[m].shape[-1] // CORES
            first = pl.multiple_of(y * rows, 16) if split_y else 0
            source = source.at[pl.ds(first, rows), pl.ds(pl.multiple_of(core * half, 128), half)]
        copy = pltpu.make_async_copy(source, part(m, z, x, y, core), local_sem.at[m])
        copy.start()
        locals_.append(copy)
    pl.semaphore_wait(barrier, len(mates))
    along_z, along_x, over_y, last = {}, {}, {}, []

    def spread(m, at_z, at_x):
        piece = part(m, at_z, at_x, y, core)
        if at_x is x:
            along_x[m].append(send(piece, piece, m, 3 + len(along_x[m]), dx=1))
        if plan[m][1]:
            over_y[m].append(send(piece, piece, m, 7 + len(over_y[m]), dy=1))

    def behind(k):
        return lax.rem(z + CHIPS_Z - k, CHIPS_Z)

    def after_x(m):
        for k in range(CHIPS_Z):
            if k % 2:
                next(todo, None)
            along_x[m][k].wait_recv()
            spread(m, behind(k), 1 - x)
        if plan[m][2]:
            piece = part(m, None, None, y, core)
            last.append(send(piece, piece, m, 15, dc=1))

    def after_y(m):
        if over_y[m]:
            for copy in over_y[m]:
                copy.wait_recv()
            piece = part(m, None, None, 1 - y, core)
            last.append(send(piece, piece, m, 16, dc=1))

    order = sorted(range(count), key=lambda m: (not plan[m][1], -outs[m].shape[-1]))
    for m in order:
        locals_[m].wait()
        mine = part(m, z, x, y, core)
        along_z[m] = [send(mine, mine, m, k - 1, dz=k) for k in range(1, CHIPS_Z)]
        along_x[m], over_y[m] = [], []
        spread(m, z, x)
    for place, m in enumerate(order):
        for k in range(1, CHIPS_Z):
            next(todo, None)
            along_z[m][k - 1].wait_recv()
            spread(m, behind(k), x)
        if place:
            after_x(order[place - 1])
    after_x(order[-1])
    for m in order:
        after_y(m)
        next(todo, None)
    for _ in todo:
        pass
    for copy in last:
        copy.wait_recv()
    for copy in sent:
        copy.wait_send()


def gather(weights, wanted, work, work_args, work_shapes, number):
    low = jnp.bfloat16
    args, plan, shapes = [], [], []
    for which, layer, split_y in wanted:
        args.append(weights[which])
        plan.append((layer, split_y, layer is not None))
        rows, columns = weights[which].shape[-2:]
        split = CHIPS_Y if split_y else 1
        shapes.append((CHIPS_Z, CHIPS_X, split, rows // split, columns))
    whole = pl.BlockSpec(memory_space=pltpu.VMEM)
    small = pl.BlockSpec(memory_space=pltpu.SMEM)
    found = pl.pallas_call(
        functools.partial(gather_kernel, plan, work, len(work_args), len(work_shapes)),
        in_specs=[small if arg.shape[-1] == SEGMENTS else whole for arg in work_args]
        + [pl.BlockSpec(memory_space=pl.ANY)] * len(args),
        out_specs=[whole] * (len(work_shapes) + len(args)),
        out_shape=work_shapes + [jax.ShapeDtypeStruct(shape, low) for shape in shapes],
        scratch_shapes=[pltpu.SemaphoreType.DMA((2, 17))] * len(args)
        + [pltpu.SemaphoreType.DMA((len(args),))],
        compiler_params=pltpu.CompilerParams(
            vmem_limit_bytes=KERNEL_VMEM, collective_id=number, has_side_effects=True
        ),
        cost_estimate=pl.CostEstimate(flops=0, bytes_accessed=200_000_000, transcendentals=0),
    )(*work_args, *args)
    results, arrays = list(found[: len(work_shapes)]), found[len(work_shapes) :]
    for item, array in zip(wanted, arrays):
        results.append(array if item[1] is None else array.reshape(-1, array.shape[-1]))
    return results


def pack_sums(out_ref, core, ins):
    rows = 8 * LAYERS
    width = out_ref.shape[1]
    for layer in range(LAYERS):
        sums_ref, ffin_ref, own_ref, away_ref = ins[4 * layer : 4 * layer + 4]
        out_ref[8 * layer : 8 * layer + 8] = sums_ref[...]
        for at in range(0, ffin_ref.shape[1], width):
            out_ref[rows : rows + 1] = ffin_ref[:, at : at + width]
            rows += 1
    for layer in range(LAYERS):
        for flip, ref in enumerate(ins[4 * layer + 2 : 4 * layer + 4]):
            half = lax.rem(core + flip, CORES) * ref.shape[1]
            for pair in range(ref.shape[1]):
                value = ref[0, pair]
                for tree in range(1, ref.shape[0]):
                    value = value + ref[tree, pair]
                column = pl.multiple_of((half + pair) * LANES, LANES)
                out_ref[rows : rows + 8, pl.ds(column, LANES)] = value
        rows += 8


def sum_rows(ffin_width):
    return LAYERS * (16 + ffin_width // D)


def tail_kernel(arrived, *refs):
    take = iter(refs)
    count = len(arrived)
    a_in, a_keep = next(take), next(take)
    b_ins = [(next(take), next(take)) for _ in range(count)]
    l_in, vec_ins = next(take), [next(take) for _ in range(4 * LAYERS)]
    a_own, a_other = next(take), next(take)
    b_outs = [next(take) for _ in range(count)]
    l_own, l_other, vec_out = next(take), next(take), next(take)
    a_zsend, a_zland, a_ysend, a_yland, a_cland = [next(take) for _ in range(5)]
    b_scratch = [[next(take) for _ in range(6)] for _ in range(count)]
    l_yland, l_cland = next(take), next(take)
    v_send, v_land = next(take), next(take)
    a_sems, b_sems, v_sems = next(take), [next(take) for _ in range(count)], next(take)
    rep, shard = lax.axis_index("rep"), lax.axis_index("shard")
    y, core = lax.div(rep, CORES), lax.rem(rep, CORES)
    z, x = lax.div(shard, CHIPS_X), lax.rem(shard, CHIPS_X)

    def device(dz=0, dx=0, dy=0, dc=0):
        to_y, to_core = lax.rem(y + dy, CHIPS_Y), lax.rem(core + dc, CORES)
        to_z, to_x = lax.rem(z + dz, CHIPS_Z), lax.rem(x + dx, CHIPS_X)
        return (to_y * CORES + to_core, to_z * CHIPS_X + to_x)

    flip_z = 1 + 2 * lax.rem(z, 2)
    mates = [dict(dx=1), dict(dy=1), dict(dc=1), dict(dy=1, dc=1)]
    mates += [dict(dz=k) for k in range(1, CHIPS_Z)]
    barrier = pltpu.get_barrier_semaphore()
    for mate in mates:
        pl.semaphore_signal(
            barrier, inc=1, device_id=device(**mate), device_id_type=pl.DeviceIdType.MESH
        )
    pl.semaphore_wait(barrier, len(mates))
    sent = []

    def send(source, target, sems, number, **step):
        copy = pltpu.make_async_remote_copy(
            src_ref=source,
            dst_ref=target,
            send_sem=sems.at[0, number],
            recv_sem=sems.at[1, number],
            device_id=device(**step),
            device_id_type=pl.DeviceIdType.MESH,
        )
        copy.start()
        sent.append(copy)
        return copy

    def wide(value):
        return value.astype(jnp.float32)

    order = (2, 1, 3, 0)
    ahead = [lax.rem(z + k, CHIPS_Z) for k in order]
    pack_sums(v_send.at[0], core, vec_ins)
    v_copies = [send(v_send.at[0], v_land.at[0], v_sems, 0, dc=1)]
    a_across = a_in
    b_y = [[] for _ in range(count)]
    for j, to in enumerate(ahead):
        for i, (b_send, _) in enumerate(b_ins):
            if arrived[i]:
                continue
            b_y[i].append(send(b_send.at[:, to], b_scratch[i][0].at[j], b_sems[i], j, dy=1))
    steps = (dict(dc=1), dict(dy=1), dict(dx=1), dict(dz=2), dict(dz=flip_z))

    def add_vectors(s):
        v_copies[s].wait_recv()
        total = v_send[s] + v_land[s]
        if s + 1 == len(steps):
            vec_out[...] = total
        else:
            v_send[s + 1] = total
            v_copies.append(
                send(v_send.at[s + 1], v_land.at[s + 1], v_sems, s + 1, **steps[s + 1])
            )

    def over(i, j, side):
        if arrived[i]:
            return wide(b_ins[i][0][:, ahead[j], side])
        return wide(b_scratch[i][0][j, :, side])

    a_z, b_x, b_z = [], [[] for _ in range(count)], [[] for _ in range(count)]

    def b_along_z(i, j):
        k, keep = order[j], b_ins[i][1]
        _, _, x_land, z_send, z_land, _ = b_scratch[i]
        b_x[i][j].wait_recv()
        if k:
            total = wide(keep[:, ahead[j], x]) + over(i, j, x) + wide(x_land[j])
            z_send[k - 1] = total.astype(jnp.bfloat16)
            b_z[i].append(send(z_send.at[k - 1], z_land.at[k - 1], b_sems[i], 7 + k, dz=k))

    def b_along_x(i, j):
        keep, (_, x_send, x_land, *_) = b_ins[i][1], b_scratch[i]
        if not arrived[i]:
            b_y[i][j].wait_recv()
        total = wide(keep[:, ahead[j], 1 - x]) + over(i, j, 1 - x)
        x_send[j] = total.astype(jnp.bfloat16)
        b_x[i].append(send(x_send.at[j], x_land.at[j], b_sems[i], 4 + j, dx=1))

    for j, k in enumerate(order):
        if k:
            total = wide(a_keep[ahead[j]]) + wide(a_across[ahead[j]])
            a_zsend[k - 1] = total.astype(jnp.bfloat16)
            a_z.append(send(a_zsend.at[k - 1], a_zland.at[k - 1], a_sems, 3 + k, dz=k))
        for i in range(count):
            if arrived[i]:
                b_along_x(i, j)
    l_y = send(l_in, l_yland, a_sems, 0, dy=1)
    add_vectors(0)
    for j in range(CHIPS_Z):
        for i in range(count):
            if not arrived[i]:
                b_along_x(i, j)
        for i in range(count):
            if arrived[i]:
                b_along_z(i, j)
        add_vectors(j + 1)
    for j in range(CHIPS_Z):
        for i in range(count):
            if not arrived[i]:
                b_along_z(i, j)
    l_y.wait_recv()
    l_own[...] = (wide(l_in[...]) + wide(l_yland[...])).astype(jnp.bfloat16)
    ends = [send(l_own, l_cland, a_sems, 1, dc=1)]
    for copy in a_z:
        copy.wait_recv()
    total = wide(a_keep[z]) + wide(a_across[z])
    for k in range(CHIPS_Z - 1):
        total = total + wide(a_zland[k])
    a_ysend[...] = total.astype(jnp.bfloat16)
    a_y = send(a_ysend, a_yland, a_sems, 7, dy=1)
    for i, (_, keep) in enumerate(b_ins):
        _, _, x_land, _, z_land, end_land = b_scratch[i]
        for copy in b_z[i]:
            copy.wait_recv()
        total = wide(keep[:, z, x]) + over(i, 3, x) + wide(x_land[3])
        for k in range(CHIPS_Z - 1):
            total = total + wide(z_land[k])
        b_outs[i][0] = total.astype(jnp.bfloat16)
        for number, step in enumerate((dict(dy=1), dict(dc=1), dict(dy=1, dc=1))):
            ends.append(
                send(b_outs[i].at[0], end_land.at[number], b_sems[i], 11 + number, **step)
            )
    a_y.wait_recv()
    a_own[...] = (wide(a_ysend[...]) + wide(a_yland[...])).astype(jnp.bfloat16)
    ends.append(send(a_own, a_cland, a_sems, 8, dc=1))
    for copy in ends:
        copy.wait_recv()
    for i in range(count):
        b_outs[i][1:4] = b_scratch[i][5][...]
    a_other[...] = a_cland[...]
    l_other[...] = l_cland[...]
    for copy in sent:
        copy.wait_send()


def reduce_tail(flat, pairs, last, sums):
    low = jnp.bfloat16
    _, total, unit = flat[0].shape
    whole = pl.BlockSpec(memory_space=pltpu.VMEM)
    far = pl.BlockSpec(memory_space=pl.ANY)
    piece = (total, unit)
    outs = [piece, piece]
    scratch = [(CHIPS_Z - 1, *piece), (CHIPS_Z - 1, *piece), piece, piece, piece]
    args, specs, arrived = [*flat], [whole, whole], []
    for first, keep, here in pairs:
        parts, _, _, rows, half = keep.shape
        block = (parts, rows, half)
        args += [first, keep]
        specs += [whole if here else far, whole]
        arrived.append(here)
        outs.append((CORES * CHIPS_Y, *block))
        scratch += [
            (16, 128) if here else (CHIPS_Z, parts, CHIPS_X, rows, half),
            (CHIPS_Z, *block),
            (CHIPS_Z, *block),
            (CHIPS_Z - 1, *block),
            (CHIPS_Z - 1, *block),
            (CORES * CHIPS_Y - 1, *block),
        ]
    outs += [last.shape, last.shape]
    scratch += [last.shape, last.shape]
    shapes = [jax.ShapeDtypeStruct(shape, low) for shape in outs]
    vec = (sum_rows(sums[1].shape[1]), D)
    shapes.append(jax.ShapeDtypeStruct(vec, jnp.float32))
    scratch = [pltpu.VMEM(shape, low) for shape in scratch]
    scratch += [pltpu.VMEM((5, *vec), jnp.float32)] * 2
    scratch += [pltpu.SemaphoreType.DMA((2, 9))]
    scratch += [pltpu.SemaphoreType.DMA((2, 14))] * len(pairs)
    scratch += [pltpu.SemaphoreType.DMA((2, 5))]
    own, other, *rest = pl.pallas_call(
        functools.partial(tail_kernel, arrived),
        in_specs=[*specs, whole] + [whole] * len(sums),
        out_specs=[whole] * len(shapes),
        out_shape=shapes,
        scratch_shapes=scratch,
        compiler_params=pltpu.CompilerParams(
            vmem_limit_bytes=KERNEL_VMEM, collective_id=0, has_side_effects=True
        ),
        cost_estimate=pl.CostEstimate(flops=0, bytes_accessed=200_000_000, transcendentals=0),
    )(*args, last, *sums)
    return [own, other], rest[:-3], list(rest[-3:-1]), rest[-1]


def join_kernel(plan, count, at_ref, *refs):
    for ref, out, layer, outer, parts, dc, dy, start, rows in plan:
        ref, out_ref = refs[ref], refs[count + out]
        half = ref.shape[1]
        core = lax.rem(at_ref[3] + dc, CORES)
        row = 0
        if dy is not None:
            row = pl.multiple_of(lax.rem(at_ref[2] + dy, CHIPS_Y) * rows, 16)
        for part in range(parts):
            column = part * CORES + core if outer else core * parts + part
            column = pl.multiple_of(column * half, 128)
            value = ref[start + part * rows : start + (part + 1) * rows]
            out_ref[layer, pl.ds(row, rows), pl.ds(column, half)] = value.astype(jnp.float32)


def join(at, done, shapes):
    arrays, plan = [], []
    for out, (number, (tall, wide)) in enumerate(shapes.items()):
        for layer in range(LAYERS):
            pieces, start, rows = done[layer][number]
            for place, piece in enumerate(pieces):
                known = [other is piece for other in arrays]
                if not any(known):
                    arrays.append(piece)
                    known.append(True)
                parts = wide // (CORES * piece.shape[1])
                dy, dc = (place % CHIPS_Y, place // CHIPS_Y) if len(pieces) > CORES else (None, place)
                plan.append((known.index(True), out, layer, number == 0, parts, dc, dy, start, rows))
    zeros = lambda i, at: (0, 0)
    outs = [(LAYERS, *shape) for shape in shapes.values()]
    return pl.pallas_call(
        functools.partial(join_kernel, plan, len(arrays)),
        grid_spec=pltpu.PrefetchScalarGridSpec(
            num_scalar_prefetch=1,
            grid=(1,),
            in_specs=[pl.BlockSpec(array.shape, zeros) for array in arrays],
            out_specs=[pl.BlockSpec(out, lambda i, at: (0, 0, 0)) for out in outs],
        ),
        out_shape=[jax.ShapeDtypeStruct(out, jnp.float32) for out in outs],
        compiler_params=kernel_params(),
        cost_estimate=pl.CostEstimate(flops=0, bytes_accessed=4_000_000, transcendentals=0),
    )(at, *arrays)


def local(
    fast,
    inputs,
    cotangent,
    segment,
    parent,
    clusters,
    *weights,
):
    flow = Flow()
    if fast:
        place = Place()
        at = place.at
        shards = dict(enumerate(weights))
        shards["vectors"] = jnp.pad(
            jnp.concatenate([weights[member] for member in VECTORS], axis=1),
            ((0, 16 - LAYERS), (0, 0)),
        )
        trees = parent.shape[0]
        slots, bias, found, qkv = gather(
            shards,
            (("vectors", None, False), (0, 0, True)),
            prep_steps,
            (
                parent,
                segment.reshape(trees, 1, TREE_LEN),
                clusters.reshape(PAIRS, 2, trees, TREE_LEN).transpose(2, 0, 1, 3),
            ),
            [
                jax.ShapeDtypeStruct((trees, PAIRS, 2, TREE_LEN), jnp.int32),
                jax.ShapeDtypeStruct((trees, HEADS, TREE_LEN, LANES), jnp.bfloat16),
            ],
            1,
        )
        vectors = spread_vectors(found, [weights[number].shape[1] for number in VECTORS])
        whole = {(0, 0): qkv}

        def attend_layer(layer, projected):
            wanted = [(6, layer, True), (8, layer, True), (2, layer, True)]
            if layer + 1 < LAYERS:
                wanted.insert(2, (0, layer + 1, False))
            results = gather(
                shards, wanted, attend_steps, (projected, slots, bias), attend_shapes(trees), 2 + layer
            )
            for (number, at_layer, _), array in zip(wanted, results[4:]):
                whole[at_layer, number] = array
            return results[:4]

        def get(layer, number):
            return whole[layer, number]

        def reduce(layer, *grads):
            name = ("grad", layer, grads[0].number)
            if name[2] == 0:
                chain = reduce_y_first(*grads, place, None if layer else "sums")
            elif name[2] == 6:
                chain = reduce_y_first(*grads, place, "y")
            else:
                chain = reduce_x_first(grads, place, "z" if layer else "x")
            flow.start(name, chain)

        def back_step(main, *held):
            return flow.tick(main, *[name for name in flow.running if name not in held])

    else:
        at = jnp.zeros((4,), jnp.int32)

        slots, bias = prepare(segment, parent, clusters)
        vectors = [
            lax.all_gather(weights[number], "shard", axis=1, tiled=True).astype(jnp.float32)
            for number in VECTORS
        ]

        def attend_layer(layer, projected):
            return attend(projected, slots, bias)

        def get(layer, number):
            return lax.all_gather(weights[number][layer], "shard", axis=0, tiled=True)

        def reduce(layer, *grads):
            for grad in grads:
                own, away = grad.rights
                if not grad.cut:
                    own = jnp.concatenate([own, away], axis=2)
                    own = own.transpose(1, 0, 2).reshape(own.shape[1], -1)
                total = contract_first(grad.left, own)
                total = lax.psum_scatter(total, "shard", scatter_dimension=0, tiled=True)
                total = lax.psum(total.astype(jnp.bfloat16), "rep").astype(jnp.float32)
                flow.done[("grad", layer, grad.number)] = total

        def back_step(main, *held):
            return main

    vector = dict(zip(VECTORS, vectors))
    hidden, hidden_low = inputs, inputs
    saved = []
    for layer in range(LAYERS):
        pull = functools.partial(get, layer)
        projected = project(layer, hidden_low, pull(0), vector[1])
        context, *heads = attend_layer(layer, projected)
        entered = hidden_low
        middle, act, slope, *norms, hidden, hidden_low = feed(
            layer,
            context,
            hidden,
            [pull(2), pull(6), pull(8)],
            [vector[number] for number in (3, 4, 5, 7, 9, 10, 11)],
        )
        saved.append((entered, heads, context, middle, act, slope, norms))
    result = hidden_low
    above, proj = cotangent, None
    sums = [None] * LAYERS
    for layer in reversed(range(LAYERS)):
        entered, heads, context, middle, act, slope, norms = saved[layer]
        pull = functools.partial(get, layer)
        down, grad_pre, grad_attn, attn_low, grad_context, row_sums, ffin_sum = feed_back(
            layer,
            above,
            proj,
            None if proj is None else get(layer + 1, 0),
            at,
            [norms[2], norms[3], slope, norms[0], norms[1]],
            [pull(2), pull(6), pull(8)],
            [vector[4], vector[10]],
        )
        sums[layer] = [row_sums, ffin_sum]
        down = back_step(down)
        wide = grad_pre.shape[1] // CORES
        grad_8 = Grad(8, act, down, down, True, act.shape[1] // D, UNIT)
        grad_2 = Grad(2, context, attn_low, attn_low, True, 1, UNIT)
        if layer == 0:
            reduce(layer, grad_8, grad_2)
            reduce(layer, Grad(6, middle, grad_pre, grad_pre, True, wide // D, D))
        else:
            grad_6 = Grad(6, middle, grad_pre, grad_pre, True, wide // UNIT, UNIT)
            reduce(layer, grad_8, grad_6, grad_2)
        above_chain = () if layer else (("grad", 1, 8),)
        grad_context = back_step(grad_context, *above_chain)
        away, away_sums = attend_back(grad_context, slots, heads, at, True)
        wide_chains = (("grad", layer, 8), ("grad", layer, 6))
        grad_context, away = back_step((grad_context, away), *above_chain, *wide_chains)
        own, own_sums = attend_back(grad_context, slots, heads, at, False)
        proj = (own, away)
        reduce(layer, Grad(0, entered, own, away, False, 3, UNIT))
        sums[layer] += [own_sums, away_sums]
        proj = back_step(proj, *(wide_chains if layer else ()))
        above = grad_attn
    grad_input = input_grad(above, proj, get(0, 0), at)
    sums = [item for layer in sums for item in layer]
    if fast:
        while flow.running:
            grad_input = back_step(grad_input)
        done = flow.done
        last, grad_input = lax.optimization_barrier((done["grad", 1, 8], grad_input))
        flat, ends, last, total = reduce_tail(
            done["grad", 0, 8], [done["grad", 0, 6], done["grad", 0, 0]], last, sums
        )
    else:
        norms, wide, heads = [], [], []
        for row_sums, ffin_sum, own_sums, away_sums in (sums[:4], sums[4:]):
            norms.append(row_sums)
            wide.append(ffin_sum.reshape(-1, D))
            found = jnp.concatenate([own_sums.sum(0), away_sums.sum(0)])
            heads.append(found.transpose(1, 0, 2).reshape(8, D))
        total = lax.psum(jnp.concatenate(norms + wide + heads), AXES)
    count = lax.axis_size("shard")
    shard = lax.axis_index("shard")
    ffin_rows = sums[1].shape[1] // D

    def share(rows):
        stacked = jnp.stack([total[row].reshape(-1) for row in rows])
        width = stacked.shape[1] // count
        return lax.dynamic_slice_in_dim(stacked, shard * width, width, axis=1)

    starts = [0, 8, 16, 16 + ffin_rows]
    heads_at = [16 + 2 * ffin_rows, 24 + 2 * ffin_rows]
    grads = {
        1: share([slice(at, at + 3, 2) for at in heads_at]),
        7: share([slice(at, at + ffin_rows) for at in starts[2:]]),
    }
    for number, row in ((10, 0), (11, 1), (9, 2), (4, 3), (5, 4), (3, 5)):
        grads[number] = share([row, 8 + row])
    if fast:
        rows = {number: weights[number].shape[1] for number in MATRICES}
        parts = {number: weights[number].shape[2] // (CORES * UNIT) for number in MATRICES}
        known = [{}, dict(done["grad", 1, 0])]
        for layer, pieces, numbers in ((0, flat, (8, 2)), (1, last, (8, 6, 2))):
            start = 0
            for number in numbers:
                known[layer][number] = (pieces, start, rows[number])
                start += rows[number] * parts[number]
        for number, end in zip((6, 0), ends):
            end = end.reshape(end.shape[0], -1, end.shape[-1])
            known[0][number] = (list(end), 0, rows[number] // CHIPS_Y)
        for numbers in (MATRICES,):
            shapes = {number: weights[number].shape[1:] for number in numbers}
            grads.update(zip(numbers, join(at, known, shapes)))
    else:
        for number in MATRICES:
            grads[number] = jnp.stack([flow.done[("grad", layer, number)] for layer in range(LAYERS)])
    return (result, grad_input, *[grads[number] for number in range(12)])


def solution(mesh):
    in_specs = (
        P(("rep", "shard"), None),
        P(("rep", "shard"), None),
        P(("rep", "shard")),
        P(("rep", "shard"), None),
        P(None, ("rep", "shard")),
        P(None, "shard", None),
        P(None, "shard"),
        P(None, "shard", None),
        P(None, "shard"),
        P(None, "shard"),
        P(None, "shard"),
        P(None, "shard", None),
        P(None, "shard"),
        P(None, "shard", None),
        P(None, "shard"),
        P(None, "shard"),
        P(None, "shard"),
    )
    out_specs = (
        P(("rep", "shard"), None),
        P(("rep", "shard"), None),
        P(None, "shard", None),
        P(None, "shard"),
        P(None, "shard", None),
        P(None, "shard"),
        P(None, "shard"),
        P(None, "shard"),
        P(None, "shard", None),
        P(None, "shard"),
        P(None, "shard", None),
        P(None, "shard"),
        P(None, "shard"),
        P(None, "shard"),
    )
    fast = mesh.shape["rep"] == CHIPS_Y * CORES and mesh.shape["shard"] == CHIPS_Z * CHIPS_X
    return jax.shard_map(
        functools.partial(local, fast),
        mesh=mesh,
        in_specs=in_specs,
        out_specs=out_specs,
        check_vma=False,
    )
```

```python
import functools

import jax
import jax.numpy as jnp
from jax import lax
from jax.experimental import pallas as pl
from jax.experimental.pallas import tpu as pltpu
from jax.sharding import PartitionSpec as P

D = 768
HEADS = 12
HEAD_DIM = 64
LAYERS = 2
CLUSTER = 128
TREE_LEN = 1024
SEGMENTS = 13
PAIRS = HEADS // 2
LANES = 2 * HEAD_DIM
KERNEL_VMEM = 60 * 2**20
ROW_TILE = 256
FEED_TILE = 768
DEPTH_TILE = 384
INV_ROOT = (2.0 * 3.141592653589793) ** -0.5
MATRICES = (0, 2, 6, 8)
VECTORS = (1, 3, 4, 5, 7, 9, 10, 11)
UNIT = 384
AXES = ("rep", "shard")
CHIPS_Z, CHIPS_X, CHIPS_Y, CORES = 4, 2, 2, 2
norm_eps = 1e-06


def one_hot_rows(slot_row):
    length = slot_row.shape[-1]
    rows = lax.broadcasted_iota(jnp.int32, (length, length), 0)
    return jnp.where(rows == slot_row, 1.0, 0.0).astype(jnp.bfloat16)


def first_lanes(length):
    return lax.broadcasted_iota(jnp.int32, (length, LANES), 1) < HEAD_DIM


def contract_last(left_side, right_side):
    return lax.dot_general(
        left_side, right_side, (((1,), (1,)), ((), ())), preferred_element_type=jnp.float32
    )


def contract_first(left_side, right_side):
    return lax.dot_general(
        left_side, right_side, (((0,), (0,)), ((), ())), preferred_element_type=jnp.float32
    )


def cluster_blocks(values):
    return [values[at : at + CLUSTER] for at in range(0, values.shape[0], CLUSTER)]


def attend_pair(slots, query, key, value, bias, store):
    low = first_lanes(TREE_LEN)
    query = query * jnp.bfloat16(HEAD_DIM**-0.5)
    packed = (
        jnp.where(low, query, pltpu.roll(key, HEAD_DIM, 1)),
        jnp.where(low, pltpu.roll(query, HEAD_DIM, 1), key),
    )
    context = []
    for head in range(2):
        table = one_hot_rows(slots[head : head + 1])
        joined = jnp.concatenate([packed[head], value], axis=1)
        found = jnp.dot(table, joined, preferred_element_type=jnp.float32).astype(jnp.bfloat16)
        both, values = found[:, :LANES], found[:, LANES:]
        store("both", head, both)
        store("values", head, values)
        queries = jnp.where(low, both, jnp.bfloat16(0))
        keys = pltpu.roll(both, HEAD_DIM, 1)
        scores = jnp.concatenate(
            [contract_last(q, k) for q, k in zip(cluster_blocks(queries), cluster_blocks(keys))],
            axis=0,
        )
        scores = scores + bias[head].astype(jnp.float32)
        numerator = jnp.exp(scores - jnp.max(scores, axis=1, keepdims=True))
        total = jnp.sum(numerator, axis=1, keepdims=True)
        soft = (numerator * (1.0 / total)).astype(jnp.bfloat16)
        store("soft", head, soft)
        out = jnp.concatenate(
            [
                jnp.dot(p, v, preferred_element_type=jnp.float32)
                for p, v in zip(cluster_blocks(soft), cluster_blocks(values))
            ],
            axis=0,
        ).astype(jnp.bfloat16)
        context.append(contract_first(table, out))
        if head == 0:
            yield
    store("context", None, jnp.where(low, context[0], context[1]).astype(jnp.bfloat16))


def attend_kernel(slot_ref, query_ref, key_ref, value_ref, bias_ref, ctx_ref, qk_ref, val_ref, p_ref):
    refs = {"both": qk_ref, "values": val_ref, "soft": p_ref}

    def store(name, head, value):
        if head is None:
            ctx_ref[...] = value
        else:
            refs[name][0, head] = value

    for _ in attend_pair(
        slot_ref[0, 0], query_ref[...], key_ref[...], value_ref[...], bias_ref[0], store
    ):
        pass


def attend_steps(ins, outs):
    projected_ref, slot_ref, bias_ref = ins
    ctx_ref, qk_ref, val_ref, p_ref = outs
    refs = {"both": qk_ref, "values": val_ref, "soft": p_ref}
    for tree in range(slot_ref.shape[0]):
        rows = slice(tree * TREE_LEN, (tree + 1) * TREE_LEN)
        for pair in range(PAIRS):
            lanes = [slice((part * PAIRS + pair) * LANES, (part * PAIRS + pair + 1) * LANES) for part in range(3)]
            heads = slice(2 * pair, 2 * pair + 2)

            def store(name, head, value):
                if head is None:
                    ctx_ref[rows, lanes[0]] = value
                else:
                    refs[name][tree, 2 * pair + head] = value

            yield from attend_pair(
                slot_ref[tree, pair],
                *[projected_ref[rows, part] for part in lanes],
                bias_ref[tree, heads],
                store,
            )
            yield


def attend_back_pair(slots, grads, both_of, values_of, soft_of, store):
    low = first_lanes(TREE_LEN)
    placed = []
    for head in range(2):
        table = one_hot_rows(slots[head : head + 1])
        found = jnp.dot(table, grads, preferred_element_type=jnp.float32)
        found = jnp.where(low == (head == 0), found, 0.0).astype(jnp.bfloat16)
        both, values, soft = both_of(head), values_of(head), soft_of(head)
        grad_soft = jnp.concatenate(
            [contract_last(g, v) for g, v in zip(cluster_blocks(found), cluster_blocks(values))],
            axis=0,
        )
        grad_value = jnp.concatenate(
            [contract_first(p, g) for p, g in zip(cluster_blocks(soft), cluster_blocks(found))],
            axis=0,
        ).astype(jnp.bfloat16)
        weights = soft.astype(jnp.float32)
        delta = jnp.sum(weights * grad_soft, axis=1, keepdims=True)
        grad_scores = (weights * (grad_soft - delta)).astype(jnp.bfloat16)
        pairs = list(zip(cluster_blocks(grad_scores), cluster_blocks(both)))
        by_key = jnp.concatenate([contract_first(s, b) for s, b in pairs], axis=0)
        by_query = jnp.concatenate(
            [jnp.dot(s, b, preferred_element_type=jnp.float32) for s, b in pairs], axis=0
        )
        mixed = jnp.where(low, by_key, by_query * HEAD_DIM**-0.5).astype(jnp.bfloat16)
        joined = jnp.concatenate([mixed, grad_value], axis=1)
        placed.append(contract_first(table, joined))
        if head == 0:
            yield
    first, second = placed
    queries = jnp.where(low, pltpu.roll(first[:, :LANES], HEAD_DIM, 1), second[:, :LANES])
    keys = jnp.where(low, first[:, :LANES], pltpu.roll(second[:, :LANES], HEAD_DIM, 1))
    values = jnp.where(low, first[:, LANES:], second[:, LANES:])
    sums = []
    for part, grad in enumerate((queries, keys, values)):
        rounded = grad.astype(jnp.bfloat16)
        store(part, rounded)
        sums.append(rows_sum(rounded.astype(jnp.float32)))
    store(None, jnp.concatenate(sums + [jnp.zeros((5, LANES), jnp.float32)], axis=0))


def attend_back_kernel(slot_ref, grad_ref, qk_ref, val_ref, p_ref, out_ref, sums_ref):
    def store(part, value):
        if part is None:
            sums_ref[0, 0] = value
        else:
            out_ref[part] = value

    refs = [lambda head, ref=ref: ref[0, head] for ref in (qk_ref, val_ref, p_ref)]
    for _ in attend_back_pair(slot_ref[0, 0], grad_ref[...], *refs, store):
        pass


def attend_back_steps(ins, outs):
    slot_ref, grad_ref, *kept = ins
    out_ref, sums_ref = outs
    for tree in range(slot_ref.shape[0]):
        rows = slice(tree * TREE_LEN, (tree + 1) * TREE_LEN)
        for pair in range(PAIRS):
            lanes = slice(pair * LANES, (pair + 1) * LANES)

            def store(part, value):
                if part is None:
                    sums_ref[tree, pair] = value
                else:
                    out_ref[part, rows, lanes] = value

            refs = [lambda head, ref=ref: ref[tree, 2 * pair + head] for ref in kept]
            yield from attend_back_pair(slot_ref[tree, pair], grad_ref[rows, lanes], *refs, store)
            yield


def slot_spec(start=0):
    return pl.BlockSpec((1, 1, 2, TREE_LEN), lambda tree, pair: (tree, start + pair, 0, 0))


def head_spec(start=0):
    return pl.BlockSpec((1, 2, TREE_LEN, LANES), lambda tree, pair: (tree, start + pair, 0, 0))


def column_spec(offset):
    return pl.BlockSpec((TREE_LEN, LANES), lambda tree, pair: (tree, offset + pair))


def kernel_params():
    return pltpu.CompilerParams(vmem_limit_bytes=KERNEL_VMEM)


def attend_shapes(trees):
    stored = jax.ShapeDtypeStruct((trees, HEADS, TREE_LEN, LANES), jnp.bfloat16)
    return [jax.ShapeDtypeStruct((trees * TREE_LEN, D), jnp.bfloat16), stored, stored, stored]


def attend(projected, slots, bias):
    trees = slots.shape[0]
    return pl.pallas_call(
        attend_kernel,
        grid=(trees, PAIRS),
        in_specs=[
            slot_spec(),
            column_spec(0),
            column_spec(PAIRS),
            column_spec(2 * PAIRS),
            head_spec(),
        ],
        out_specs=[column_spec(0), head_spec(), head_spec(), head_spec()],
        out_shape=attend_shapes(trees),
        compiler_params=kernel_params(),
        cost_estimate=pl.CostEstimate(
            flops=trees * 30_000_000_000, bytes_accessed=trees * 20_000_000, transcendentals=0
        ),
    )(slots, projected, projected, projected, bias)


def attend_back_shapes(trees):
    return [
        jax.ShapeDtypeStruct((3, trees * TREE_LEN, D), jnp.bfloat16),
        jax.ShapeDtypeStruct((trees, PAIRS, 8, LANES), jnp.float32),
    ]


def attend_back(grad_context, slots, kept):
    trees = slots.shape[0]
    return pl.pallas_call(
        attend_back_kernel,
        grid=(trees, PAIRS),
        in_specs=[slot_spec(), column_spec(0), head_spec(), head_spec(), head_spec()],
        out_specs=[
            pl.BlockSpec((3, TREE_LEN, LANES), lambda tree, pair: (0, tree, pair)),
            pl.BlockSpec((1, 1, 8, LANES), lambda tree, pair: (tree, pair, 0, 0)),
        ],
        out_shape=attend_back_shapes(trees),
        compiler_params=kernel_params(),
        cost_estimate=pl.CostEstimate(
            flops=trees * 35_000_000_000, bytes_accessed=trees * 20_000_000, transcendentals=0
        ),
    )(slots, grad_context, *kept)


def erf_parts(values):
    size = jnp.abs(values)
    turn = 1.0 / (1.0 + (0.3275911 * 0.5**0.5) * size)
    bell = jnp.exp(-0.5 * values * values)
    series = 1.061405429 * 0.5
    for factor in (-1.453152027, 1.421413741, -0.284496736, 0.254829592):
        series = series * turn + factor * 0.5
    tail = series * turn * bell
    return jnp.where(values < 0.0, tail, 1.0 - tail), bell


def norm_parts(values):
    centred = values - jnp.mean(values, axis=-1, keepdims=True)
    scale = lax.rsqrt(jnp.mean(centred * centred, axis=-1, keepdims=True) + norm_eps)
    return centred * scale, scale


def norm_back(grad, normal, scale, gain):
    inner = grad * gain
    mean = jnp.mean(inner, axis=-1, keepdims=True)
    along = jnp.mean(inner * normal, axis=-1, keepdims=True)
    return scale * (inner - mean - normal * along)


def spread(column):
    return jnp.broadcast_to(column, (column.shape[0], 128))


def rows_sum(values):
    return jnp.sum(values, axis=0, keepdims=True)


def project_kernel(layer, rows_ref, weight_ref, bias_ref, out_ref):
    product = jnp.dot(rows_ref[...], weight_ref[...], preferred_element_type=jnp.float32)
    bias = bias_ref[layer : layer + 1]
    out_ref[:, :D] = (product[:, :D] + bias[:, :D]).astype(jnp.bfloat16)
    out_ref[:, D : 2 * D] = product[:, D : 2 * D].astype(jnp.bfloat16)
    out_ref[:, 2 * D :] = (product[:, 2 * D :] + bias[:, D:]).astype(jnp.bfloat16)


def feed_kernel(
    layer,
    context_ref,
    rows_ref,
    out_weight_ref,
    ffin_weight_ref,
    ffout_weight_ref,
    out_bias_ref,
    attn_gain_ref,
    attn_shift_ref,
    ffin_bias_ref,
    ffout_bias_ref,
    ffn_gain_ref,
    ffn_shift_ref,
    hidden_ref,
    act_ref,
    slope_ref,
    attn_normal_ref,
    attn_scale_ref,
    ffn_normal_ref,
    ffn_scale_ref,
    result_ref,
    result_low_ref,
):
    here = slice(layer, layer + 1)
    product = jnp.dot(context_ref[...], out_weight_ref[...], preferred_element_type=jnp.float32)
    attn_sum = rows_ref[...].astype(jnp.float32) + product + out_bias_ref[here]
    normal, scale = norm_parts(attn_sum)
    attn_normal_ref[...] = normal
    attn_scale_ref[...] = spread(scale)
    hidden = normal * attn_gain_ref[here] + attn_shift_ref[here]
    hidden_low = hidden.astype(jnp.bfloat16)
    hidden_ref[...] = hidden_low
    total = hidden + ffout_bias_ref[here]
    width = ffin_weight_ref.shape[1]
    for at in range(0, width, FEED_TILE):
        part = slice(at, at + FEED_TILE)
        pre = (
            jnp.dot(hidden_low, ffin_weight_ref[:, part], preferred_element_type=jnp.float32)
            + ffin_bias_ref[here, part]
        )
        below, bell = erf_parts(pre)
        act = (pre * below).astype(jnp.bfloat16)
        act_ref[:, part] = act
        slope_ref[:, part] = (below + pre * bell * INV_ROOT).astype(jnp.bfloat16)
        total = total + jnp.dot(
            act, ffout_weight_ref[part, :], preferred_element_type=jnp.float32
        )
    normal, scale = norm_parts(total)
    ffn_normal_ref[...] = normal
    ffn_scale_ref[...] = spread(scale)
    result = normal * ffn_gain_ref[here] + ffn_shift_ref[here]
    result_ref[...] = result
    result_low_ref[...] = result.astype(jnp.bfloat16)


def add_projected(grad, proj_ref, weight_ref):
    for part in range(3):
        grad = grad + contract_last(proj_ref[part], weight_ref[:, part * D : (part + 1) * D])
    return grad


def feed_back_kernel(layer, with_proj, *refs):
    here = slice(layer, layer + 1)
    if with_proj:
        above_ref, proj_ref, qkv_weight_ref, *refs = refs
        grad = add_projected(above_ref[...], proj_ref, qkv_weight_ref)
    else:
        above_ref, *refs = refs
        grad = above_ref[...].astype(jnp.float32)
    (
        ffn_normal_ref,
        ffn_scale_ref,
        slope_ref,
        attn_normal_ref,
        attn_scale_ref,
        out_weight_ref,
        ffin_weight_ref,
        ffout_weight_ref,
        attn_gain_ref,
        ffn_gain_ref,
        down_ref,
        pre_ref,
        attn_ref,
        attn_low_ref,
        context_ref,
        sums_ref,
        ffin_sum_ref,
    ) = refs

    @pl.when(pl.program_id(0) == 0)
    def _():
        sums_ref[...] = jnp.zeros_like(sums_ref)
        ffin_sum_ref[...] = jnp.zeros_like(ffin_sum_ref)

    normal = ffn_normal_ref[...]
    sums_ref[0:1] += rows_sum(grad * normal)
    sums_ref[1:2] += rows_sum(grad)
    grad_sum = norm_back(grad, normal, ffn_scale_ref[:, 0:1], ffn_gain_ref[here])
    down = grad_sum.astype(jnp.bfloat16)
    down_ref[...] = down
    sums_ref[2:3] += rows_sum(down.astype(jnp.float32))
    total = grad_sum
    width = ffin_weight_ref.shape[1]
    for at in range(0, width, FEED_TILE):
        part = slice(at, at + FEED_TILE)
        grad_act = contract_last(down, ffout_weight_ref[part, :])
        pre = (grad_act * slope_ref[:, part].astype(jnp.float32)).astype(jnp.bfloat16)
        pre_ref[:, part] = pre
        ffin_sum_ref[:, part] += rows_sum(pre.astype(jnp.float32))
        total = total + contract_last(pre, ffin_weight_ref[:, part])
    normal = attn_normal_ref[...]
    sums_ref[3:4] += rows_sum(total * normal)
    sums_ref[4:5] += rows_sum(total)
    attn = norm_back(total, normal, attn_scale_ref[:, 0:1], attn_gain_ref[here])
    attn_ref[...] = attn
    low = attn.astype(jnp.bfloat16)
    attn_low_ref[...] = low
    sums_ref[5:6] += rows_sum(low.astype(jnp.float32))
    context_ref[...] = contract_last(low, out_weight_ref[...]).astype(jnp.bfloat16)


def input_grad_kernel(above_ref, proj_ref, weight_ref, out_ref):
    out_ref[...] = add_projected(above_ref[...], proj_ref, weight_ref)


def prep_pair(parent_ref, segment_ref, cluster_ref, slot_ref, bias_ref, row, tree, pair):
    segs = segment_ref[tree]
    length = segs.shape[1]

    def parent_of(values):
        found = jnp.zeros_like(values)
        for number in range(SEGMENTS):
            found = jnp.where(values == number, parent_ref[row, number], found)
        return found

    parents = parent_of(segs)
    grands = parent_of(parents)
    ids = jnp.concatenate([segs, parents, grands, jnp.zeros((5, length), jnp.int32)], axis=0)
    ids = jnp.concatenate([ids, jnp.zeros((8, length), jnp.int32)], axis=0)
    ids = ids.astype(jnp.float32).astype(jnp.bfloat16)
    count = length // CLUSTER
    order = lax.broadcasted_iota(jnp.int32, (count, length), 0)
    lanes = lax.broadcasted_iota(jnp.int32, (count, length), 1)
    for head in range(2):
        member = order == cluster_ref[tree, pair, head : head + 1, :]
        ranks = member.astype(jnp.int32)
        step = 1
        while step < length:
            ranks = ranks + jnp.where(lanes >= step, pltpu.roll(ranks, step, 1), 0)
            step *= 2
        slot = jnp.sum(
            jnp.where(member, ranks - 1 + CLUSTER * order, 0), axis=0, keepdims=True
        )
        slot_ref[tree, pair, head : head + 1, :] = slot
        table = one_hot_rows(slot)
        rows = contract_last(ids, table)
        columns = jnp.concatenate([rows] * (128 // rows.shape[0]), axis=0).T
        for at in range(0, length, CLUSTER):
            here = rows[0:1, at : at + CLUSTER]
            block = columns[at : at + CLUSTER]
            allowed = (
                (here == block[:, 0:1]) | (here == block[:, 1:2]) | (here == block[:, 2:3])
            )
            bias_ref[tree, 2 * pair + head, at : at + CLUSTER, :] = jnp.where(allowed, 0.0, -1e30).astype(
                jnp.bfloat16
            )


def prep_kernel(*refs):
    prep_pair(*refs, pl.program_id(0), 0, 0)


def row_spec(width, rows=ROW_TILE):
    return pl.BlockSpec((rows, width), lambda i: (i, 0))


def whole_spec(shape):
    return pl.BlockSpec(
        shape, lambda i: (0,) * len(shape), pipeline_mode=pl.Buffered(1)
    )


def part_spec(rows=ROW_TILE):
    return pl.BlockSpec((3, rows, D), lambda i: (0, i, 0))


def cost(flops, *arrays):
    moved = sum(array.size * array.dtype.itemsize for array in arrays)
    return pl.CostEstimate(flops=int(flops), bytes_accessed=moved, transcendentals=0)


def shape_of(rows, width, kind=jnp.bfloat16):
    return jax.ShapeDtypeStruct((rows, width), kind)


def project(layer, rows, weight, bias):
    count, width = rows.shape[0], weight.shape[1]
    return pl.pallas_call(
        functools.partial(project_kernel, layer),
        grid=(count // ROW_TILE,),
        in_specs=[row_spec(D), whole_spec(weight.shape), whole_spec(bias.shape)],
        out_specs=row_spec(width),
        out_shape=shape_of(count, width),
        compiler_params=kernel_params(),
        cost_estimate=cost(2.4 * count * D * width, rows, weight),
    )(rows, weight, bias)


def feed(layer, context, rows, weights, vectors):
    count = context.shape[0]
    width = weights[1].shape[1]
    f32 = jnp.float32
    return pl.pallas_call(
        functools.partial(feed_kernel, layer),
        grid=(count // ROW_TILE,),
        in_specs=[row_spec(D), row_spec(D)]
        + [whole_spec(weight.shape) for weight in weights]
        + [whole_spec(vector.shape) for vector in vectors],
        out_specs=[
            row_spec(D),
            row_spec(width),
            row_spec(width),
            row_spec(D),
            row_spec(128),
            row_spec(D),
            row_spec(128),
            row_spec(D),
            row_spec(D),
        ],
        out_shape=[
            shape_of(count, D),
            shape_of(count, width),
            shape_of(count, width),
            shape_of(count, D, f32),
            shape_of(count, 128, f32),
            shape_of(count, D, f32),
            shape_of(count, 128, f32),
            shape_of(count, D, f32),
            shape_of(count, D),
        ],
        compiler_params=kernel_params(),
        cost_estimate=cost(5 * count * D * (2 * width + D), context, *weights),
    )(context, rows, *weights, *vectors)


def feed_back(layer, above, proj, qkv_weight, saved, weights, gains):
    count = above.shape[0]
    width = weights[1].shape[1]
    f32 = jnp.float32
    lead, lead_specs = [above], [row_spec(D)]
    if proj is not None:
        lead += [proj, qkv_weight]
        lead_specs += [part_spec(), whole_spec(qkv_weight.shape)]
    return pl.pallas_call(
        functools.partial(feed_back_kernel, layer, proj is not None),
        grid=(count // ROW_TILE,),
        in_specs=lead_specs
        + [row_spec(D), row_spec(128), row_spec(width), row_spec(D), row_spec(128)]
        + [whole_spec(weight.shape) for weight in weights]
        + [whole_spec(gain.shape) for gain in gains],
        out_specs=[
            row_spec(D),
            row_spec(width),
            row_spec(D),
            row_spec(D),
            row_spec(D),
            pl.BlockSpec((8, D), lambda i: (0, 0)),
            pl.BlockSpec((1, width), lambda i: (0, 0)),
        ],
        out_shape=[
            shape_of(count, D),
            shape_of(count, width),
            shape_of(count, D, f32),
            shape_of(count, D),
            shape_of(count, D),
            shape_of(8, D, f32),
            shape_of(1, width, f32),
        ],
        compiler_params=kernel_params(),
        cost_estimate=cost(5 * count * D * (2 * width + D), above, *weights),
    )(*lead, *saved, *weights, *gains)


def input_grad(above, proj, qkv_weight):
    count = above.shape[0]
    return pl.pallas_call(
        input_grad_kernel,
        grid=(count // ROW_TILE,),
        in_specs=[
            row_spec(D),
            part_spec(),
            whole_spec(qkv_weight.shape),
        ],
        out_specs=row_spec(D),
        out_shape=shape_of(count, D, jnp.float32),
        compiler_params=kernel_params(),
        cost_estimate=cost(2.4 * count * D * 3 * D, above, qkv_weight),
    )(above, proj, qkv_weight)


def prepare(segment, parent, clusters):
    trees = parent.shape[0]
    segment = segment.reshape(trees, 1, TREE_LEN)
    clusters = clusters.reshape(PAIRS, 2, trees, TREE_LEN).transpose(2, 0, 1, 3)
    return pl.pallas_call(
        prep_kernel,
        grid=(trees, PAIRS),
        in_specs=[
            pl.BlockSpec(memory_space=pltpu.SMEM),
            pl.BlockSpec((1, 1, TREE_LEN), lambda tree, pair: (tree, 0, 0)),
            slot_spec(),
        ],
        out_specs=[slot_spec(), head_spec()],
        out_shape=[
            jax.ShapeDtypeStruct((trees, PAIRS, 2, TREE_LEN), jnp.int32),
            jax.ShapeDtypeStruct((trees, HEADS, TREE_LEN, LANES), jnp.bfloat16),
        ],
        compiler_params=kernel_params(),
        cost_estimate=pl.CostEstimate(
            flops=trees * 20_000_000_000, bytes_accessed=trees * 4_000_000, transcendentals=0
        ),
    )(parent, segment, clusters)


def weight_grad_kernel(split_y, at_ref, left_ref, right_ref, *refs):
    product = contract_first(
        left_ref[...].reshape(left_ref.shape[-2:]), right_ref[...].reshape(right_ref.shape[-2:])
    )
    if split_y is None:
        (out_ref,) = refs
        out_ref[...] = product.astype(jnp.bfloat16).reshape(out_ref.shape)
        return
    near_ref, (send_ref, keep_ref, sum_ref) = refs[0], refs[-3:]
    total = product + near_ref[...].astype(jnp.float32).reshape(product.shape)
    sum_ref[...] = total.astype(jnp.bfloat16).reshape(sum_ref.shape)
    if split_y:
        send_ref[0] = sum_ref[:, :, 1 - at_ref[2]]
        keep_ref[0] = sum_ref[:, :, at_ref[2]]
    else:
        send_ref[...] = sum_ref[:, 1 - at_ref[1]]
        keep_ref[...] = sum_ref[:, at_ref[1]]


class Grad:
    def __init__(self, number, left, right, tiles, half):
        self.number = number
        self.left, self.right = left, right
        self.tiles, self.half = tiles, half
        self.depth = left.shape[1]
        self.parts = 1 if self.depth > D else tiles
        self.rows = self.depth // (CHIPS_Z * CHIPS_X)

    def product(self, at, other, split_y=None, near=None, start=0, total=0, before=()):
        flip = 1 if other else 0
        left, right = self.left, self.right
        count = left.shape[0]
        tall = self.depth > D
        core = lambda at: lax.rem(at[3] + flip, CORES)
        in_specs = [
            pl.BlockSpec((count, D), (lambda i, at: (0, i)) if tall else (lambda i, at: (0, 0)))
        ]
        if right.ndim == 3:
            in_specs.append(pl.BlockSpec((1, count, self.half), lambda i, at: (i, 0, core(at))))
        elif tall:
            in_specs.append(pl.BlockSpec((count, self.half), lambda i, at: (0, core(at))))
        else:
            in_specs.append(
                pl.BlockSpec((count, self.half), lambda i, at: (0, core(at) * self.tiles + i))
            )
        zs = D // (self.rows * CHIPS_X)
        place = (lambda i: (0, i)) if tall else (lambda i: (i, 0))
        whole = (self.parts, CHIPS_Z, CHIPS_X, self.rows, self.half)
        block = (1, zs, CHIPS_X, self.rows, self.half)
        full = pl.BlockSpec(block, lambda i, at: (*place(i), 0, 0, 0))
        args, scratch = [left, right], []
        if split_y is None:
            out_specs, shapes = full, jax.ShapeDtypeStruct(whole, jnp.bfloat16)
        else:
            in_specs.append(full)
            args.append(near)
            in_specs += [pl.BlockSpec(memory_space=pl.ANY)] * len(before)
            args += before
            if split_y:
                short = self.rows // CHIPS_Y
                kept = (CHIPS_X, short, self.half)
                scratch = [pltpu.VMEM((zs, CHIPS_X, CHIPS_Y, short, self.half), jnp.bfloat16)]
                spec = pl.BlockSpec((1, zs, *kept), lambda i, at: (*place(i), 0, 0, 0))
                shape = (self.parts, CHIPS_Z, *kept)
            else:
                scratch = [pltpu.VMEM((zs, CHIPS_X, self.rows, self.half), jnp.bfloat16)]
                first = start // self.rows
                index = (lambda i, at: (i, first, 0)) if tall else (lambda i, at: (0, first + i, 0))
                spec = pl.BlockSpec((zs, self.rows, self.half), index)
                shape = (CHIPS_Z, total, self.half)
            out_specs, shapes = [spec] * 2, [jax.ShapeDtypeStruct(shape, jnp.bfloat16)] * 2
        return pl.pallas_call(
            functools.partial(weight_grad_kernel, split_y),
            grid_spec=pltpu.PrefetchScalarGridSpec(
                num_scalar_prefetch=1,
                grid=(self.tiles,),
                in_specs=in_specs,
                out_specs=out_specs,
                scratch_shapes=scratch,
            ),
            out_shape=shapes,
            input_output_aliases={4 + place: place for place in range(len(before))},
            compiler_params=kernel_params(),
            cost_estimate=cost(4 * count * D * self.tiles * self.half, left, right),
        )(at, *args)


class Place:
    def __init__(self):
        rep = lax.axis_index("rep")
        shard = lax.axis_index("shard")
        self.y, self.core = rep // CORES, rep % CORES
        self.z, self.x = shard // CHIPS_X, shard % CHIPS_X
        self.at = jnp.stack([self.z, self.x, self.y, self.core]).astype(jnp.int32)


def hop(value, dz=0, dx=0, dy=0, dc=0):
    pairs = []
    for y in range(CHIPS_Y):
        for c in range(CORES):
            for z in range(CHIPS_Z):
                for x in range(CHIPS_X):
                    source = ((y * CORES + c) * CHIPS_Z + z) * CHIPS_X + x
                    y2, c2 = (y + dy) % CHIPS_Y, (c + dc) % CORES
                    z2, x2 = (z + dz) % CHIPS_Z, (x + dx) % CHIPS_X
                    pairs.append((source, ((y2 * CORES + c2) * CHIPS_Z + z2) * CHIPS_X + x2))
    return lax.ppermute(value, AXES, pairs)


def spread_vectors(found, sizes):
    found = found[:, :, 0, :LAYERS].reshape(-1, LAYERS, found.shape[-1]).transpose(1, 0, 2)
    out, at = [], 0
    for size in sizes:
        out.append(found[:, :, at : at + size].reshape(LAYERS, -1).astype(jnp.float32))
        at += size
    return out


def cut_sums(place, groups):
    at = place.at
    arrived = []
    for grads, _ in groups:
        arrived.append([hop(grad.product(at, True), dc=1) for grad in grads])
    found = []
    for (grads, y_first), near in zip(groups, arrived):
        total = sum(grad.parts * grad.rows for grad in grads)
        start, pair = 0, ()
        for grad, item in zip(grads, near):
            if y_first:
                pair = grad.product(at, False, True, item)
            else:
                pair = grad.product(at, False, False, item, start, total, tuple(pair))
            start += grad.parts * grad.rows
        found.append(tuple(pair))
    return found


def prep_steps(ins, outs):
    trees, pairs = ins[2].shape[:2]
    for tree in range(trees):
        for pair in range(pairs):
            prep_pair(*ins, *outs, tree, tree, pair)
            yield


def gather_kernel(plan, work, work_ins, work_outs, *refs):
    count = len(plan)
    own_ins, ins, refs = refs[:work_ins], refs[work_ins : work_ins + count], refs[work_ins + count :]
    own_outs, outs = refs[:work_outs], refs[work_outs : work_outs + count]
    sems, local_sem = refs[work_outs + count : -1], refs[-1]
    todo = work(own_ins, own_outs)
    rep, shard = lax.axis_index("rep"), lax.axis_index("shard")
    y, core = lax.div(rep, CORES), lax.rem(rep, CORES)
    z, x = lax.div(shard, CHIPS_X), lax.rem(shard, CHIPS_X)

    def device(dz=0, dx=0, dy=0, dc=0):
        to_y, to_core = lax.rem(y + dy, CHIPS_Y), lax.rem(core + dc, CORES)
        to_z, to_x = lax.rem(z + dz, CHIPS_Z), lax.rem(x + dx, CHIPS_X)
        return (to_y * CORES + to_core, to_z * CHIPS_X + to_x)

    mates = [dict(dx=1), dict(dy=1), dict(dc=1)] + [dict(dz=k) for k in range(1, CHIPS_Z)]
    barrier = pltpu.get_barrier_semaphore()
    for mate in mates:
        pl.semaphore_signal(
            barrier, inc=1, device_id=device(**mate), device_id_type=pl.DeviceIdType.MESH
        )
    sent = []

    def send(source, target, m, number, **step):
        copy = pltpu.make_async_remote_copy(
            src_ref=source,
            dst_ref=target,
            send_sem=sems[m].at[0, number],
            recv_sem=sems[m].at[1, number],
            device_id=device(**step),
            device_id_type=pl.DeviceIdType.MESH,
        )
        copy.start()
        sent.append(copy)
        return copy

    def part(m, at_z, at_x, at_y, at_core):
        out, (layer, split_y, by_core) = outs[m], plan[m]
        columns = slice(None)
        if by_core:
            half = out.shape[-1] // CORES
            columns = pl.ds(pl.multiple_of(at_core * half, 128), half)
        at_z = slice(None) if at_z is None else at_z
        at_x = slice(None) if at_x is None else at_x
        return out.at[at_z, at_x, at_y if split_y else 0, :, columns]

    locals_ = []
    for m, (layer, split_y, by_core) in enumerate(plan):
        rows = outs[m].shape[3]
        source = ins[m] if layer is None else ins[m].at[layer]
        if by_core:
            half = outs[m].shape[-1] // CORES
            first = pl.multiple_of(y * rows, 16) if split_y else 0
            source = source.at[pl.ds(first, rows), pl.ds(pl.multiple_of(core * half, 128), half)]
        copy = pltpu.make_async_copy(source, part(m, z, x, y, core), local_sem.at[m])
        copy.start()
        locals_.append(copy)
    pl.semaphore_wait(barrier, len(mates))
    along_z, along_x, over_y, last = {}, {}, {}, []

    def spread(m, at_z, at_x):
        piece = part(m, at_z, at_x, y, core)
        if at_x is x:
            along_x[m].append(send(piece, piece, m, 3 + len(along_x[m]), dx=1))
        if plan[m][1]:
            over_y[m].append(send(piece, piece, m, 7 + len(over_y[m]), dy=1))

    def behind(k):
        return lax.rem(z + CHIPS_Z - k, CHIPS_Z)

    def after_x(m):
        for k in range(CHIPS_Z):
            if k % 2:
                next(todo, None)
            along_x[m][k].wait_recv()
            spread(m, behind(k), 1 - x)
        if plan[m][2]:
            piece = part(m, None, None, y, core)
            last.append(send(piece, piece, m, 15, dc=1))

    def after_y(m):
        if over_y[m]:
            for copy in over_y[m]:
                copy.wait_recv()
            piece = part(m, None, None, 1 - y, core)
            last.append(send(piece, piece, m, 16, dc=1))

    order = sorted(range(count), key=lambda m: (not plan[m][1], -outs[m].shape[-1]))
    for m in order:
        locals_[m].wait()
        mine = part(m, z, x, y, core)
        along_z[m] = [send(mine, mine, m, k - 1, dz=k) for k in range(1, CHIPS_Z)]
        along_x[m], over_y[m] = [], []
        spread(m, z, x)
    for place, m in enumerate(order):
        for k in range(1, CHIPS_Z):
            next(todo, None)
            along_z[m][k - 1].wait_recv()
            spread(m, behind(k), x)
        if place:
            after_x(order[place - 1])
    after_x(order[-1])
    for m in order:
        after_y(m)
        next(todo, None)
    for _ in todo:
        pass
    for copy in last:
        copy.wait_recv()
    for copy in sent:
        copy.wait_send()


def gather(weights, wanted, work, work_args, work_shapes, number):
    low = jnp.bfloat16
    args, plan, shapes = [], [], []
    for which, layer, split_y in wanted:
        args.append(weights[which])
        plan.append((layer, split_y, layer is not None))
        rows, columns = weights[which].shape[-2:]
        split = CHIPS_Y if split_y else 1
        shapes.append((CHIPS_Z, CHIPS_X, split, rows // split, columns))
    whole = pl.BlockSpec(memory_space=pltpu.VMEM)
    small = pl.BlockSpec(memory_space=pltpu.SMEM)
    found = pl.pallas_call(
        functools.partial(gather_kernel, plan, work, len(work_args), len(work_shapes)),
        in_specs=[small if arg.shape[-1] == SEGMENTS else whole for arg in work_args]
        + [pl.BlockSpec(memory_space=pl.ANY)] * len(args),
        out_specs=[whole] * (len(work_shapes) + len(args)),
        out_shape=work_shapes + [jax.ShapeDtypeStruct(shape, low) for shape in shapes],
        scratch_shapes=[pltpu.SemaphoreType.DMA((2, 17))] * len(args)
        + [pltpu.SemaphoreType.DMA((len(args),))],
        compiler_params=pltpu.CompilerParams(
            vmem_limit_bytes=KERNEL_VMEM, collective_id=number, has_side_effects=True
        ),
        cost_estimate=pl.CostEstimate(flops=0, bytes_accessed=200_000_000, transcendentals=0),
    )(*work_args, *args)
    results, arrays = list(found[: len(work_shapes)]), found[len(work_shapes) :]
    for item, array in zip(wanted, arrays):
        results.append(array if item[1] is None else array.reshape(-1, array.shape[-1]))
    return results


def pack_sums(out_ref, ins):
    rows = 8 * LAYERS
    width = out_ref.shape[1]
    for layer in range(LAYERS):
        sums_ref, ffin_ref, _ = ins[3 * layer : 3 * layer + 3]
        out_ref[8 * layer : 8 * layer + 8] = sums_ref[...]
        for at in range(0, ffin_ref.shape[1], width):
            out_ref[rows : rows + 1] = ffin_ref[:, at : at + width]
            rows += 1
    for layer in range(LAYERS):
        ref = ins[3 * layer + 2]
        for pair in range(ref.shape[1]):
            value = ref[0, pair]
            for tree in range(1, ref.shape[0]):
                value = value + ref[tree, pair]
            out_ref[rows : rows + 8, pair * LANES : (pair + 1) * LANES] = value
        rows += 8


def sum_rows(ffin_width):
    return LAYERS * (16 + ffin_width // D)


def reduce_kernel(flats, count, vectors, work, work_ins, work_outs, *refs):
    take = iter(refs)

    def some(number):
        return [next(take) for _ in range(number)]

    own_ins = some(work_ins)
    a_ins = [some(2) for _ in range(flats)]
    b_ins = [some(2) for _ in range(count)]
    vec_ins = some(vectors)
    own_outs = some(work_outs)
    a_outs = [some(2) for _ in range(flats)]
    b_outs = some(count)
    vec_outs = some(1 if vectors else 0)
    a_scratch = [some(6) for _ in range(flats)]
    b_scratch = [some(6) for _ in range(count)]
    v_send, v_land = some(2) if vectors else (None, None)
    a_sems, b_sems = some(flats), some(count)
    v_sems = next(take) if vectors else None
    todo = work(own_ins, own_outs)
    rep, shard = lax.axis_index("rep"), lax.axis_index("shard")
    y, core = lax.div(rep, CORES), lax.rem(rep, CORES)
    z, x = lax.div(shard, CHIPS_X), lax.rem(shard, CHIPS_X)

    def device(dz=0, dx=0, dy=0, dc=0):
        to_y, to_core = lax.rem(y + dy, CHIPS_Y), lax.rem(core + dc, CORES)
        to_z, to_x = lax.rem(z + dz, CHIPS_Z), lax.rem(x + dx, CHIPS_X)
        return (to_y * CORES + to_core, to_z * CHIPS_X + to_x)

    flip_z = 1 + 2 * lax.rem(z, 2)
    mates = [dict(dx=1), dict(dy=1), dict(dc=1), dict(dy=1, dc=1)]
    mates += [dict(dz=k) for k in range(1, CHIPS_Z)]
    barrier = pltpu.get_barrier_semaphore()
    for mate in mates:
        pl.semaphore_signal(
            barrier, inc=1, device_id=device(**mate), device_id_type=pl.DeviceIdType.MESH
        )
    pl.semaphore_wait(barrier, len(mates))
    sent = []

    def send(source, target, sems, number, **step):
        copy = pltpu.make_async_remote_copy(
            src_ref=source,
            dst_ref=target,
            send_sem=sems.at[0, number],
            recv_sem=sems.at[1, number],
            device_id=device(**step),
            device_id_type=pl.DeviceIdType.MESH,
        )
        copy.start()
        sent.append(copy)
        return copy

    def wide(value):
        return value.astype(jnp.float32)

    order = (2, 1, 3, 0)
    ahead = [lax.rem(z + k, CHIPS_Z) for k in order]
    v_copies = []
    if vectors:
        pack_sums(v_send.at[0], vec_ins)
        v_copies.append(send(v_send.at[0], v_land.at[0], v_sems, 0, dc=1))
    a_x, b_y = [[] for _ in range(flats)], [[] for _ in range(count)]
    for j, to in enumerate(ahead):
        for i, (first, _) in enumerate(a_ins):
            a_x[i].append(send(first.at[to], a_scratch[i][0].at[j], a_sems[i], j, dx=1))
        for i, (first, _) in enumerate(b_ins):
            b_y[i].append(send(first.at[:, to], b_scratch[i][0].at[j], b_sems[i], j, dy=1))
    steps = (dict(dc=1), dict(dy=1), dict(dx=1), dict(dz=2), dict(dz=flip_z))

    def add_vectors(s):
        if not vectors:
            return
        v_copies[s].wait_recv()
        total = v_send[s] + v_land[s]
        if s + 1 == len(steps):
            vec_outs[0][...] = total
        else:
            v_send[s + 1] = total
            v_copies.append(
                send(v_send.at[s + 1], v_land.at[s + 1], v_sems, s + 1, **steps[s + 1])
            )

    a_z, b_x, b_z = ([[] for _ in range(number)] for number in (flats, count, count))

    def b_along_z(i, j):
        k, keep = order[j], b_ins[i][1]
        over, _, x_land, z_send, z_land, _ = b_scratch[i]
        b_x[i][j].wait_recv()
        if k:
            total = wide(keep[:, ahead[j], x]) + wide(over[j, :, x]) + wide(x_land[j])
            z_send[k - 1] = total.astype(jnp.bfloat16)
            b_z[i].append(send(z_send.at[k - 1], z_land.at[k - 1], b_sems[i], 7 + k, dz=k))

    def b_along_x(i, j):
        keep, (over, x_send, x_land, *_) = b_ins[i][1], b_scratch[i]
        b_y[i][j].wait_recv()
        total = wide(keep[:, ahead[j], 1 - x]) + wide(over[j, :, 1 - x])
        x_send[j] = total.astype(jnp.bfloat16)
        b_x[i].append(send(x_send.at[j], x_land.at[j], b_sems[i], 4 + j, dx=1))

    for j, k in enumerate(order):
        next(todo, None)
        for i, (_, keep) in enumerate(a_ins):
            across, z_send, z_land, *_ = a_scratch[i]
            a_x[i][j].wait_recv()
            if k:
                total = wide(keep[ahead[j]]) + wide(across[j])
                z_send[k - 1] = total.astype(jnp.bfloat16)
                a_z[i].append(
                    send(z_send.at[k - 1], z_land.at[k - 1], a_sems[i], 3 + k, dz=k)
                )
        next(todo, None)
        for i in range(count):
            b_along_x(i, j)
        if j:
            for i in range(count):
                b_along_z(i, j - 1)
        next(todo, None)
        add_vectors(j)
    for i in range(count):
        b_along_z(i, CHIPS_Z - 1)
    add_vectors(4)
    for _ in todo:
        pass
    over_y, ends = [], []
    for i, (_, keep) in enumerate(a_ins):
        across, _, z_land, y_send, y_land, _ = a_scratch[i]
        for copy in a_z[i]:
            copy.wait_recv()
        total = wide(keep[z]) + wide(across[CHIPS_Z - 1])
        for k in range(CHIPS_Z - 1):
            total = total + wide(z_land[k])
        y_send[...] = total.astype(jnp.bfloat16)
        over_y.append(send(y_send, y_land, a_sems[i], 7, dy=1))
    for i, (_, keep) in enumerate(b_ins):
        over, _, x_land, _, z_land, end_land = b_scratch[i]
        for copy in b_z[i]:
            copy.wait_recv()
        total = wide(keep[:, z, x]) + wide(over[3, :, x]) + wide(x_land[3])
        for k in range(CHIPS_Z - 1):
            total = total + wide(z_land[k])
        b_outs[i][0] = total.astype(jnp.bfloat16)
        for number, step in enumerate((dict(dy=1), dict(dc=1), dict(dy=1, dc=1))):
            ends.append(
                send(b_outs[i].at[0], end_land.at[number], b_sems[i], 11 + number, **step)
            )
    for i, (own, _) in enumerate(a_outs):
        *_, y_send, y_land, c_land = a_scratch[i]
        over_y[i].wait_recv()
        own[...] = (wide(y_send[...]) + wide(y_land[...])).astype(jnp.bfloat16)
        ends.append(send(own, c_land, a_sems[i], 8, dc=1))
    for copy in ends:
        copy.wait_recv()
    for i in range(count):
        b_outs[i][1:4] = b_scratch[i][5][...]
    for i, (_, other) in enumerate(a_outs):
        other[...] = a_scratch[i][5][...]
    for copy in sent:
        copy.wait_send()


def no_work(ins, outs):
    return iter(())


def reduce_sums(flats, pairs, sums, number, work=no_work, work_args=(), work_shapes=()):
    low = jnp.bfloat16
    whole = pl.BlockSpec(memory_space=pltpu.VMEM)
    far = pl.BlockSpec(memory_space=pl.ANY)
    args, specs = list(work_args), [whole] * len(work_args)
    outs, scratch = [], []
    for first, keep in flats:
        piece = keep.shape[1:]
        args += [first, keep]
        specs += [far, whole]
        outs += [piece, piece]
        scratch += [(CHIPS_Z, *piece), (CHIPS_Z - 1, *piece), (CHIPS_Z - 1, *piece)]
        scratch += [piece] * 3
    for first, keep in pairs:
        parts, _, _, rows, half = keep.shape
        block = (parts, rows, half)
        args += [first, keep]
        specs += [far, whole]
        outs.append((CORES * CHIPS_Y, *block))
        scratch += [
            (CHIPS_Z, parts, CHIPS_X, rows, half),
            (CHIPS_Z, *block),
            (CHIPS_Z, *block),
            (CHIPS_Z - 1, *block),
            (CHIPS_Z - 1, *block),
            (CORES * CHIPS_Y - 1, *block),
        ]
    args += sums
    specs += [whole] * len(sums)
    shapes = list(work_shapes) + [jax.ShapeDtypeStruct(shape, low) for shape in outs]
    scratch = [pltpu.VMEM(shape, low) for shape in scratch]
    if sums:
        vec = (sum_rows(sums[1].shape[1]), D)
        shapes.append(jax.ShapeDtypeStruct(vec, jnp.float32))
        scratch += [pltpu.VMEM((5, *vec), jnp.float32)] * 2
    scratch += [pltpu.SemaphoreType.DMA((2, 9))] * len(flats)
    scratch += [pltpu.SemaphoreType.DMA((2, 14))] * len(pairs)
    if sums:
        scratch.append(pltpu.SemaphoreType.DMA((2, 5)))
    return pl.pallas_call(
        functools.partial(
            reduce_kernel, len(flats), len(pairs), len(sums), work, len(work_args), len(work_shapes)
        ),
        in_specs=specs,
        out_specs=[whole] * len(shapes),
        out_shape=shapes,
        scratch_shapes=scratch,
        compiler_params=pltpu.CompilerParams(
            vmem_limit_bytes=KERNEL_VMEM, collective_id=number, has_side_effects=True
        ),
        cost_estimate=pl.CostEstimate(flops=0, bytes_accessed=200_000_000, transcendentals=0),
    )(*args)


def join_kernel(plan, count, at_ref, *refs):
    for ref, out, layer, outer, parts, dc, dy, start, rows in plan:
        ref, out_ref = refs[ref], refs[count + out]
        half = ref.shape[1]
        core = lax.rem(at_ref[3] + dc, CORES)
        row = 0
        if dy is not None:
            row = pl.multiple_of(lax.rem(at_ref[2] + dy, CHIPS_Y) * rows, 16)
        for part in range(parts):
            column = part * CORES + core if outer else core * parts + part
            column = pl.multiple_of(column * half, 128)
            value = ref[start + part * rows : start + (part + 1) * rows]
            out_ref[layer, pl.ds(row, rows), pl.ds(column, half)] = value.astype(jnp.float32)


def join(at, done, shapes):
    arrays, plan = [], []
    for out, (number, (tall, wide)) in enumerate(shapes.items()):
        for layer in range(LAYERS):
            pieces, start, rows = done[layer][number]
            for place, piece in enumerate(pieces):
                known = [other is piece for other in arrays]
                if not any(known):
                    arrays.append(piece)
                    known.append(True)
                parts = wide // (CORES * piece.shape[1])
                dy, dc = (place % CHIPS_Y, place // CHIPS_Y) if len(pieces) > CORES else (None, place)
                plan.append((known.index(True), out, layer, number == 0, parts, dc, dy, start, rows))
    zeros = lambda i, at: (0, 0)
    outs = [(LAYERS, *shape) for shape in shapes.values()]
    return pl.pallas_call(
        functools.partial(join_kernel, plan, len(arrays)),
        grid_spec=pltpu.PrefetchScalarGridSpec(
            num_scalar_prefetch=1,
            grid=(1,),
            in_specs=[pl.BlockSpec(array.shape, zeros) for array in arrays],
            out_specs=[pl.BlockSpec(out, lambda i, at: (0, 0, 0)) for out in outs],
        ),
        out_shape=[jax.ShapeDtypeStruct(out, jnp.float32) for out in outs],
        compiler_params=kernel_params(),
        cost_estimate=pl.CostEstimate(flops=0, bytes_accessed=4_000_000, transcendentals=0),
    )(at, *arrays)


def local(
    fast,
    inputs,
    cotangent,
    segment,
    parent,
    clusters,
    *weights,
):
    pieces = {}
    if fast:
        place = Place()
        at = place.at
        shards = dict(enumerate(weights))
        shards["vectors"] = jnp.pad(
            jnp.concatenate([weights[member] for member in VECTORS], axis=1),
            ((0, 16 - LAYERS), (0, 0)),
        )
        trees = parent.shape[0]
        slots, bias, found, qkv = gather(
            shards,
            (("vectors", None, False), (0, 0, True)),
            prep_steps,
            (
                parent,
                segment.reshape(trees, 1, TREE_LEN),
                clusters.reshape(PAIRS, 2, trees, TREE_LEN).transpose(2, 0, 1, 3),
            ),
            [
                jax.ShapeDtypeStruct((trees, PAIRS, 2, TREE_LEN), jnp.int32),
                jax.ShapeDtypeStruct((trees, HEADS, TREE_LEN, LANES), jnp.bfloat16),
            ],
            1,
        )
        vectors = spread_vectors(found, [weights[number].shape[1] for number in VECTORS])
        whole = {(0, 0): qkv}

        def attend_layer(layer, projected):
            last = layer + 1 == LAYERS
            wanted = [(6, layer, True), (8, layer, not last), (2, layer, last)]
            if not last:
                wanted.insert(2, (0, layer + 1, False))
            results = gather(
                shards, wanted, attend_steps, (projected, slots, bias), attend_shapes(trees), 2 + layer
            )
            for (number, at_layer, _), array in zip(wanted, results[4:]):
                whole[at_layer, number] = array
            return results[:4]

        def get(layer, number):
            return whole[layer, number]

        def attend_back_layer(layer, grad_context, heads, groups, waiting):
            flat, pair = cut_sums(place, groups)
            proj, head_sums, *ends = reduce_sums(
                [flat],
                [pair, *waiting],
                [],
                2 + LAYERS + layer,
                attend_back_steps,
                (slots, grad_context, *heads),
                attend_back_shapes(trees),
            )
            pieces[layer, "flat"] = ends[:2]
            pieces[layer, 6] = ends[2]
            if waiting:
                pieces[layer + 1, 0] = ends[3]
            return proj, head_sums

    else:
        slots, bias = prepare(segment, parent, clusters)
        vectors = [
            lax.all_gather(weights[number], "shard", axis=1, tiled=True).astype(jnp.float32)
            for number in VECTORS
        ]

        def attend_layer(layer, projected):
            return attend(projected, slots, bias)

        def get(layer, number):
            return lax.all_gather(weights[number][layer], "shard", axis=0, tiled=True)

        def own_sum(left, right):
            if right.ndim == 3:
                right = right.transpose(1, 0, 2).reshape(right.shape[1], -1)
            total = contract_first(left, right)
            total = lax.psum_scatter(total, "shard", scatter_dimension=0, tiled=True)
            return lax.psum(total.astype(jnp.bfloat16), "rep").astype(jnp.float32)

        def attend_back_layer(layer, grad_context, heads, groups, waiting):
            for grads, _ in groups:
                for grad in grads:
                    pieces[layer, grad.number] = own_sum(grad.left, grad.right)
            return attend_back(grad_context, slots, heads)

    vector = dict(zip(VECTORS, vectors))
    hidden, hidden_low = inputs, inputs
    saved = []
    for layer in range(LAYERS):
        pull = functools.partial(get, layer)
        projected = project(layer, hidden_low, pull(0), vector[1])
        context, *heads = attend_layer(layer, projected)
        entered = hidden_low
        middle, act, slope, *norms, hidden, hidden_low = feed(
            layer,
            context,
            hidden,
            [pull(2), pull(6), pull(8)],
            [vector[number] for number in (3, 4, 5, 7, 9, 10, 11)],
        )
        saved.append((entered, heads, context, middle, act, slope, norms))
    result = hidden_low
    above, proj = cotangent, None
    sums, waiting = [None] * LAYERS, []
    for layer in reversed(range(LAYERS)):
        entered, heads, context, middle, act, slope, norms = saved[layer]
        pull = functools.partial(get, layer)
        down, grad_pre, grad_attn, attn_low, grad_context, row_sums, ffin_sum = feed_back(
            layer,
            above,
            proj,
            None if proj is None else get(layer + 1, 0),
            [norms[2], norms[3], slope, norms[0], norms[1]],
            [pull(2), pull(6), pull(8)],
            [vector[4], vector[10]],
        )
        wide = grad_pre.shape[1] // CORES
        groups = (
            (
                (
                    Grad(8, act, down, act.shape[1] // D, UNIT),
                    Grad(2, context, attn_low, 1, UNIT),
                ),
                False,
            ),
            ((Grad(6, middle, grad_pre, wide // D, D),), True),
        )
        proj, head_sums = attend_back_layer(layer, grad_context, heads, groups, waiting)
        sums[layer] = [row_sums, ffin_sum, head_sums]
        above = grad_attn
        last = Grad(0, entered, proj, 3, UNIT)
        if not fast:
            pieces[layer, 0] = own_sum(last.left, last.right)
        elif layer:
            waiting = cut_sums(place, [((last,), True)])
    grad_input = input_grad(above, proj, get(0, 0))
    sums = [item for layer in sums for item in layer]
    if fast:
        (pair,) = cut_sums(place, [((last,), True)])
        pair, grad_input = lax.optimization_barrier((pair, grad_input))
        pieces[0, 0], total = reduce_sums([], [pair], sums, 0)
    else:
        norms, wide, heads = [], [], []
        for row_sums, ffin_sum, head_sums in (sums[:3], sums[3:]):
            norms.append(row_sums)
            wide.append(ffin_sum.reshape(-1, D))
            heads.append(head_sums.sum(0).transpose(1, 0, 2).reshape(8, D))
        total = lax.psum(jnp.concatenate(norms + wide + heads), AXES)
    count = lax.axis_size("shard")
    shard = lax.axis_index("shard")
    ffin_rows = sums[1].shape[1] // D

    def share(rows):
        stacked = jnp.stack([total[row].reshape(-1) for row in rows])
        width = stacked.shape[1] // count
        return lax.dynamic_slice_in_dim(stacked, shard * width, width, axis=1)

    starts = [0, 8, 16, 16 + ffin_rows]
    heads_at = [16 + 2 * ffin_rows, 24 + 2 * ffin_rows]
    grads = {
        1: share([slice(at, at + 3, 2) for at in heads_at]),
        7: share([slice(at, at + ffin_rows) for at in starts[2:]]),
    }
    for number, row in ((10, 0), (11, 1), (9, 2), (4, 3), (5, 4), (3, 5)):
        grads[number] = share([row, 8 + row])
    if fast:
        rows = {number: weights[number].shape[1] for number in MATRICES}
        parts = {number: weights[number].shape[2] // (CORES * UNIT) for number in MATRICES}
        known = [{} for _ in range(LAYERS)]
        for layer in range(LAYERS):
            start = 0
            for number in (8, 2):
                known[layer][number] = (pieces[layer, "flat"], start, rows[number])
                start += rows[number] * parts[number]
            for number in (6, 0):
                end = pieces[layer, number]
                end = end.reshape(end.shape[0], -1, end.shape[-1])
                known[layer][number] = (list(end), 0, rows[number] // CHIPS_Y)
        for numbers in (MATRICES,):
            shapes = {number: weights[number].shape[1:] for number in numbers}
            grads.update(zip(numbers, join(place.at, known, shapes)))
    else:
        for number in MATRICES:
            grads[number] = jnp.stack([pieces[layer, number] for layer in range(LAYERS)])
    return (result, grad_input, *[grads[number] for number in range(12)])


def solution(mesh):
    in_specs = (
        P(("rep", "shard"), None),
        P(("rep", "shard"), None),
        P(("rep", "shard")),
        P(("rep", "shard"), None),
        P(None, ("rep", "shard")),
        P(None, "shard", None),
        P(None, "shard"),
        P(None, "shard", None),
        P(None, "shard"),
        P(None, "shard"),
        P(None, "shard"),
        P(None, "shard", None),
        P(None, "shard"),
        P(None, "shard", None),
        P(None, "shard"),
        P(None, "shard"),
        P(None, "shard"),
    )
    out_specs = (
        P(("rep", "shard"), None),
        P(("rep", "shard"), None),
        P(None, "shard", None),
        P(None, "shard"),
        P(None, "shard", None),
        P(None, "shard"),
        P(None, "shard"),
        P(None, "shard"),
        P(None, "shard", None),
        P(None, "shard"),
        P(None, "shard", None),
        P(None, "shard"),
        P(None, "shard"),
        P(None, "shard"),
    )
    fast = mesh.shape["rep"] == CHIPS_Y * CORES and mesh.shape["shard"] == CHIPS_Z * CHIPS_X
    return jax.shard_map(
        functools.partial(local, fast),
        mesh=mesh,
        in_specs=in_specs,
        out_specs=out_specs,
        check_vma=False,
    )
```

```python
import functools

import jax
import jax.numpy as jnp
from jax import lax
from jax.experimental import pallas as pl
from jax.experimental.pallas import tpu as pltpu
from jax.sharding import PartitionSpec as P

D = 768
HEADS = 12
HEAD_DIM = 64
LAYERS = 2
CLUSTER = 128
TREE_LEN = 1024
SEGMENTS = 13
PAIRS = HEADS // 2
LANES = 2 * HEAD_DIM
KERNEL_VMEM = 60 * 2**20
ROW_TILE = 256
FEED_TILE = 768
DEPTH_TILE = 384
INV_ROOT = (2.0 * 3.141592653589793) ** -0.5
MATRICES = (0, 2, 6, 8)
VECTORS = (1, 3, 4, 5, 7, 9, 10, 11)
UNIT = 384
AXES = ("rep", "shard")
CHIPS_Z, CHIPS_X, CHIPS_Y, CORES = 4, 2, 2, 2
norm_eps = 1e-06


def one_hot_rows(slot_row):
    length = slot_row.shape[-1]
    rows = lax.broadcasted_iota(jnp.int32, (length, length), 0)
    return jnp.where(rows == slot_row, 1.0, 0.0).astype(jnp.bfloat16)


def first_lanes(length):
    return lax.broadcasted_iota(jnp.int32, (length, LANES), 1) < HEAD_DIM


def contract_last(left_side, right_side):
    return lax.dot_general(
        left_side, right_side, (((1,), (1,)), ((), ())), preferred_element_type=jnp.float32
    )


def contract_first(left_side, right_side):
    return lax.dot_general(
        left_side, right_side, (((0,), (0,)), ((), ())), preferred_element_type=jnp.float32
    )


def cluster_blocks(values):
    return [values[at : at + CLUSTER] for at in range(0, values.shape[0], CLUSTER)]


def attend_pair(slots, query, key, value, bias, store):
    low = first_lanes(TREE_LEN)
    query = query * jnp.bfloat16(HEAD_DIM**-0.5)
    packed = (
        jnp.where(low, query, pltpu.roll(key, HEAD_DIM, 1)),
        jnp.where(low, pltpu.roll(query, HEAD_DIM, 1), key),
    )
    context = []
    for head in range(2):
        table = one_hot_rows(slots[head : head + 1])
        joined = jnp.concatenate([packed[head], value], axis=1)
        found = jnp.dot(table, joined, preferred_element_type=jnp.float32).astype(jnp.bfloat16)
        both, values = found[:, :LANES], found[:, LANES:]
        store("both", head, both)
        store("values", head, values)
        queries = jnp.where(low, both, jnp.bfloat16(0))
        keys = pltpu.roll(both, HEAD_DIM, 1)
        scores = jnp.concatenate(
            [contract_last(q, k) for q, k in zip(cluster_blocks(queries), cluster_blocks(keys))],
            axis=0,
        )
        scores = scores + bias[head].astype(jnp.float32)
        numerator = jnp.exp(scores - jnp.max(scores, axis=1, keepdims=True))
        total = jnp.sum(numerator, axis=1, keepdims=True)
        soft = (numerator * (1.0 / total)).astype(jnp.bfloat16)
        store("soft", head, soft)
        out = jnp.concatenate(
            [
                jnp.dot(p, v, preferred_element_type=jnp.float32)
                for p, v in zip(cluster_blocks(soft), cluster_blocks(values))
            ],
            axis=0,
        ).astype(jnp.bfloat16)
        context.append(contract_first(table, out))
        if head == 0:
            yield
    store("context", None, jnp.where(low, context[0], context[1]).astype(jnp.bfloat16))


def attend_kernel(slot_ref, query_ref, key_ref, value_ref, bias_ref, ctx_ref, qk_ref, val_ref, p_ref):
    refs = {"both": qk_ref, "values": val_ref, "soft": p_ref}

    def store(name, head, value):
        if head is None:
            ctx_ref[...] = value
        else:
            refs[name][0, head] = value

    for _ in attend_pair(
        slot_ref[0, 0], query_ref[...], key_ref[...], value_ref[...], bias_ref[0], store
    ):
        pass


def attend_steps(ins, outs):
    projected_ref, slot_ref, bias_ref = ins
    ctx_ref, qk_ref, val_ref, p_ref = outs
    refs = {"both": qk_ref, "values": val_ref, "soft": p_ref}
    for tree in range(slot_ref.shape[0]):
        rows = slice(tree * TREE_LEN, (tree + 1) * TREE_LEN)
        for pair in range(PAIRS):
            lanes = [slice((part * PAIRS + pair) * LANES, (part * PAIRS + pair + 1) * LANES) for part in range(3)]
            heads = slice(2 * pair, 2 * pair + 2)

            def store(name, head, value):
                if head is None:
                    ctx_ref[rows, lanes[0]] = value
                else:
                    refs[name][tree, 2 * pair + head] = value

            yield from attend_pair(
                slot_ref[tree, pair],
                *[projected_ref[rows, part] for part in lanes],
                bias_ref[tree, heads],
                store,
            )
            yield


def attend_back_pair(slots, grads, both_of, values_of, soft_of, store):
    low = first_lanes(TREE_LEN)
    placed = []
    for head in range(2):
        table = one_hot_rows(slots[head : head + 1])
        found = jnp.dot(table, grads, preferred_element_type=jnp.float32)
        found = jnp.where(low == (head == 0), found, 0.0).astype(jnp.bfloat16)
        both, values, soft = both_of(head), values_of(head), soft_of(head)
        grad_soft = jnp.concatenate(
            [contract_last(g, v) for g, v in zip(cluster_blocks(found), cluster_blocks(values))],
            axis=0,
        )
        grad_value = jnp.concatenate(
            [contract_first(p, g) for p, g in zip(cluster_blocks(soft), cluster_blocks(found))],
            axis=0,
        ).astype(jnp.bfloat16)
        weights = soft.astype(jnp.float32)
        delta = jnp.sum(weights * grad_soft, axis=1, keepdims=True)
        grad_scores = (weights * (grad_soft - delta)).astype(jnp.bfloat16)
        pairs = list(zip(cluster_blocks(grad_scores), cluster_blocks(both)))
        by_key = jnp.concatenate([contract_first(s, b) for s, b in pairs], axis=0)
        by_query = jnp.concatenate(
            [jnp.dot(s, b, preferred_element_type=jnp.float32) for s, b in pairs], axis=0
        )
        mixed = jnp.where(low, by_key, by_query * HEAD_DIM**-0.5).astype(jnp.bfloat16)
        joined = jnp.concatenate([mixed, grad_value], axis=1)
        placed.append(contract_first(table, joined))
        if head == 0:
            yield
    first, second = placed
    queries = jnp.where(low, pltpu.roll(first[:, :LANES], HEAD_DIM, 1), second[:, :LANES])
    keys = jnp.where(low, first[:, :LANES], pltpu.roll(second[:, :LANES], HEAD_DIM, 1))
    values = jnp.where(low, first[:, LANES:], second[:, LANES:])
    sums = []
    for part, grad in enumerate((queries, keys, values)):
        rounded = grad.astype(jnp.bfloat16)
        store(part, rounded)
        sums.append(rows_sum(rounded.astype(jnp.float32)))
    store(None, jnp.concatenate(sums + [jnp.zeros((5, LANES), jnp.float32)], axis=0))


def attend_back_kernel(slot_ref, grad_ref, qk_ref, val_ref, p_ref, out_ref, sums_ref):
    def store(part, value):
        if part is None:
            sums_ref[0, 0] = value
        else:
            out_ref[part] = value

    refs = [lambda head, ref=ref: ref[0, head] for ref in (qk_ref, val_ref, p_ref)]
    for _ in attend_back_pair(slot_ref[0, 0], grad_ref[...], *refs, store):
        pass


def attend_back_steps(ins, outs):
    slot_ref, grad_ref, *kept = ins
    out_ref, sums_ref = outs
    for tree in range(slot_ref.shape[0]):
        rows = slice(tree * TREE_LEN, (tree + 1) * TREE_LEN)
        for pair in range(PAIRS):
            lanes = slice(pair * LANES, (pair + 1) * LANES)

            def store(part, value):
                if part is None:
                    sums_ref[tree, pair] = value
                else:
                    out_ref[part, rows, lanes] = value

            refs = [lambda head, ref=ref: ref[tree, 2 * pair + head] for ref in kept]
            yield from attend_back_pair(slot_ref[tree, pair], grad_ref[rows, lanes], *refs, store)
            yield


def slot_spec(start=0):
    return pl.BlockSpec((1, 1, 2, TREE_LEN), lambda tree, pair: (tree, start + pair, 0, 0))


def head_spec(start=0):
    return pl.BlockSpec((1, 2, TREE_LEN, LANES), lambda tree, pair: (tree, start + pair, 0, 0))


def column_spec(offset):
    return pl.BlockSpec((TREE_LEN, LANES), lambda tree, pair: (tree, offset + pair))


def kernel_params():
    return pltpu.CompilerParams(vmem_limit_bytes=KERNEL_VMEM)


def attend_shapes(trees):
    stored = jax.ShapeDtypeStruct((trees, HEADS, TREE_LEN, LANES), jnp.bfloat16)
    return [jax.ShapeDtypeStruct((trees * TREE_LEN, D), jnp.bfloat16), stored, stored, stored]


def attend(projected, slots, bias):
    trees = slots.shape[0]
    return pl.pallas_call(
        attend_kernel,
        grid=(trees, PAIRS),
        in_specs=[
            slot_spec(),
            column_spec(0),
            column_spec(PAIRS),
            column_spec(2 * PAIRS),
            head_spec(),
        ],
        out_specs=[column_spec(0), head_spec(), head_spec(), head_spec()],
        out_shape=attend_shapes(trees),
        compiler_params=kernel_params(),
        cost_estimate=pl.CostEstimate(
            flops=trees * 30_000_000_000, bytes_accessed=trees * 20_000_000, transcendentals=0
        ),
    )(slots, projected, projected, projected, bias)


def attend_back_shapes(trees):
    return [
        jax.ShapeDtypeStruct((3, trees * TREE_LEN, D), jnp.bfloat16),
        jax.ShapeDtypeStruct((trees, PAIRS, 8, LANES), jnp.float32),
    ]


def attend_back(grad_context, slots, kept):
    trees = slots.shape[0]
    return pl.pallas_call(
        attend_back_kernel,
        grid=(trees, PAIRS),
        in_specs=[slot_spec(), column_spec(0), head_spec(), head_spec(), head_spec()],
        out_specs=[
            pl.BlockSpec((3, TREE_LEN, LANES), lambda tree, pair: (0, tree, pair)),
            pl.BlockSpec((1, 1, 8, LANES), lambda tree, pair: (tree, pair, 0, 0)),
        ],
        out_shape=attend_back_shapes(trees),
        compiler_params=kernel_params(),
        cost_estimate=pl.CostEstimate(
            flops=trees * 35_000_000_000, bytes_accessed=trees * 20_000_000, transcendentals=0
        ),
    )(slots, grad_context, *kept)


def erf_parts(values):
    size = jnp.abs(values)
    turn = 1.0 / (1.0 + (0.3275911 * 0.5**0.5) * size)
    bell = jnp.exp(-0.5 * values * values)
    series = 1.061405429 * 0.5
    for factor in (-1.453152027, 1.421413741, -0.284496736, 0.254829592):
        series = series * turn + factor * 0.5
    tail = series * turn * bell
    return jnp.where(values < 0.0, tail, 1.0 - tail), bell


def norm_parts(values):
    centred = values - jnp.mean(values, axis=-1, keepdims=True)
    scale = lax.rsqrt(jnp.mean(centred * centred, axis=-1, keepdims=True) + norm_eps)
    return centred * scale, scale


def norm_back(grad, normal, scale, gain):
    inner = grad * gain
    mean = jnp.mean(inner, axis=-1, keepdims=True)
    along = jnp.mean(inner * normal, axis=-1, keepdims=True)
    return scale * (inner - mean - normal * along)


def spread(column):
    return jnp.broadcast_to(column, (column.shape[0], 128))


def rows_sum(values):
    return jnp.sum(values, axis=0, keepdims=True)


def project_kernel(layer, rows_ref, weight_ref, bias_ref, out_ref):
    product = jnp.dot(rows_ref[...], weight_ref[...], preferred_element_type=jnp.float32)
    bias = bias_ref[layer : layer + 1]
    out_ref[:, :D] = (product[:, :D] + bias[:, :D]).astype(jnp.bfloat16)
    out_ref[:, D : 2 * D] = product[:, D : 2 * D].astype(jnp.bfloat16)
    out_ref[:, 2 * D :] = (product[:, 2 * D :] + bias[:, D:]).astype(jnp.bfloat16)


def feed_kernel(
    layer,
    context_ref,
    rows_ref,
    out_weight_ref,
    ffin_weight_ref,
    ffout_weight_ref,
    out_bias_ref,
    attn_gain_ref,
    attn_shift_ref,
    ffin_bias_ref,
    ffout_bias_ref,
    ffn_gain_ref,
    ffn_shift_ref,
    hidden_ref,
    act_ref,
    slope_ref,
    attn_normal_ref,
    attn_scale_ref,
    ffn_normal_ref,
    ffn_scale_ref,
    result_ref,
    result_low_ref,
):
    here = slice(layer, layer + 1)
    product = jnp.dot(context_ref[...], out_weight_ref[...], preferred_element_type=jnp.float32)
    attn_sum = rows_ref[...].astype(jnp.float32) + product + out_bias_ref[here]
    normal, scale = norm_parts(attn_sum)
    attn_normal_ref[...] = normal
    attn_scale_ref[...] = spread(scale)
    hidden = normal * attn_gain_ref[here] + attn_shift_ref[here]
    hidden_low = hidden.astype(jnp.bfloat16)
    hidden_ref[...] = hidden_low
    total = hidden + ffout_bias_ref[here]
    width = ffin_weight_ref.shape[1]
    for at in range(0, width, FEED_TILE):
        part = slice(at, at + FEED_TILE)
        pre = (
            jnp.dot(hidden_low, ffin_weight_ref[:, part], preferred_element_type=jnp.float32)
            + ffin_bias_ref[here, part]
        )
        below, bell = erf_parts(pre)
        act = (pre * below).astype(jnp.bfloat16)
        act_ref[:, part] = act
        slope_ref[:, part] = (below + pre * bell * INV_ROOT).astype(jnp.bfloat16)
        total = total + jnp.dot(
            act, ffout_weight_ref[part, :], preferred_element_type=jnp.float32
        )
    normal, scale = norm_parts(total)
    ffn_normal_ref[...] = normal
    ffn_scale_ref[...] = spread(scale)
    result = normal * ffn_gain_ref[here] + ffn_shift_ref[here]
    result_ref[...] = result
    result_low_ref[...] = result.astype(jnp.bfloat16)


def add_projected(grad, proj_ref, weight_ref):
    for part in range(3):
        grad = grad + contract_last(proj_ref[part], weight_ref[:, part * D : (part + 1) * D])
    return grad


def feed_back_kernel(layer, with_proj, *refs):
    here = slice(layer, layer + 1)
    if with_proj:
        above_ref, proj_ref, qkv_weight_ref, *refs = refs
        grad = add_projected(above_ref[...], proj_ref, qkv_weight_ref)
    else:
        above_ref, *refs = refs
        grad = above_ref[...].astype(jnp.float32)
    (
        ffn_normal_ref,
        ffn_scale_ref,
        slope_ref,
        attn_normal_ref,
        attn_scale_ref,
        out_weight_ref,
        ffin_weight_ref,
        ffout_weight_ref,
        attn_gain_ref,
        ffn_gain_ref,
        down_ref,
        pre_ref,
        attn_ref,
        attn_low_ref,
        context_ref,
        sums_ref,
        ffin_sum_ref,
    ) = refs

    @pl.when(pl.program_id(0) == 0)
    def _():
        sums_ref[...] = jnp.zeros_like(sums_ref)
        ffin_sum_ref[...] = jnp.zeros_like(ffin_sum_ref)

    normal = ffn_normal_ref[...]
    sums_ref[0:1] += rows_sum(grad * normal)
    sums_ref[1:2] += rows_sum(grad)
    grad_sum = norm_back(grad, normal, ffn_scale_ref[:, 0:1], ffn_gain_ref[here])
    down = grad_sum.astype(jnp.bfloat16)
    down_ref[...] = down
    sums_ref[2:3] += rows_sum(down.astype(jnp.float32))
    total = grad_sum
    width = ffin_weight_ref.shape[1]
    for at in range(0, width, FEED_TILE):
        part = slice(at, at + FEED_TILE)
        grad_act = contract_last(down, ffout_weight_ref[part, :])
        pre = (grad_act * slope_ref[:, part].astype(jnp.float32)).astype(jnp.bfloat16)
        pre_ref[:, part] = pre
        ffin_sum_ref[:, part] += rows_sum(pre.astype(jnp.float32))
        total = total + contract_last(pre, ffin_weight_ref[:, part])
    normal = attn_normal_ref[...]
    sums_ref[3:4] += rows_sum(total * normal)
    sums_ref[4:5] += rows_sum(total)
    attn = norm_back(total, normal, attn_scale_ref[:, 0:1], attn_gain_ref[here])
    attn_ref[...] = attn
    low = attn.astype(jnp.bfloat16)
    attn_low_ref[...] = low
    sums_ref[5:6] += rows_sum(low.astype(jnp.float32))
    context_ref[...] = contract_last(low, out_weight_ref[...]).astype(jnp.bfloat16)


def input_grad_kernel(above_ref, proj_ref, weight_ref, out_ref):
    out_ref[...] = add_projected(above_ref[...], proj_ref, weight_ref)


def prep_pair(parent_ref, segment_ref, cluster_ref, slot_ref, bias_ref, row, tree, pair):
    segs = segment_ref[tree]
    length = segs.shape[1]

    def parent_of(values):
        found = jnp.zeros_like(values)
        for number in range(SEGMENTS):
            found = jnp.where(values == number, parent_ref[row, number], found)
        return found

    parents = parent_of(segs)
    grands = parent_of(parents)
    ids = jnp.concatenate([segs, parents, grands, jnp.zeros((5, length), jnp.int32)], axis=0)
    ids = jnp.concatenate([ids, jnp.zeros((8, length), jnp.int32)], axis=0)
    ids = ids.astype(jnp.float32).astype(jnp.bfloat16)
    count = length // CLUSTER
    order = lax.broadcasted_iota(jnp.int32, (count, length), 0)
    lanes = lax.broadcasted_iota(jnp.int32, (count, length), 1)
    for head in range(2):
        member = order == cluster_ref[tree, pair, head : head + 1, :]
        ranks = member.astype(jnp.int32)
        step = 1
        while step < length:
            ranks = ranks + jnp.where(lanes >= step, pltpu.roll(ranks, step, 1), 0)
            step *= 2
        slot = jnp.sum(
            jnp.where(member, ranks - 1 + CLUSTER * order, 0), axis=0, keepdims=True
        )
        slot_ref[tree, pair, head : head + 1, :] = slot
        table = one_hot_rows(slot)
        rows = contract_last(ids, table)
        columns = jnp.concatenate([rows] * (128 // rows.shape[0]), axis=0).T
        for at in range(0, length, CLUSTER):
            here = rows[0:1, at : at + CLUSTER]
            block = columns[at : at + CLUSTER]
            allowed = (
                (here == block[:, 0:1]) | (here == block[:, 1:2]) | (here == block[:, 2:3])
            )
            bias_ref[tree, 2 * pair + head, at : at + CLUSTER, :] = jnp.where(allowed, 0.0, -1e30).astype(
                jnp.bfloat16
            )


def prep_kernel(*refs):
    prep_pair(*refs, pl.program_id(0), 0, 0)


def row_spec(width, rows=ROW_TILE):
    return pl.BlockSpec((rows, width), lambda i: (i, 0))


def whole_spec(shape):
    return pl.BlockSpec(
        shape, lambda i: (0,) * len(shape), pipeline_mode=pl.Buffered(1)
    )


def part_spec(rows=ROW_TILE):
    return pl.BlockSpec((3, rows, D), lambda i: (0, i, 0))


def cost(flops, *arrays):
    moved = sum(array.size * array.dtype.itemsize for array in arrays)
    return pl.CostEstimate(flops=int(flops), bytes_accessed=moved, transcendentals=0)


def shape_of(rows, width, kind=jnp.bfloat16):
    return jax.ShapeDtypeStruct((rows, width), kind)


def project(layer, rows, weight, bias):
    count, width = rows.shape[0], weight.shape[1]
    return pl.pallas_call(
        functools.partial(project_kernel, layer),
        grid=(count // ROW_TILE,),
        in_specs=[row_spec(D), whole_spec(weight.shape), whole_spec(bias.shape)],
        out_specs=row_spec(width),
        out_shape=shape_of(count, width),
        compiler_params=kernel_params(),
        cost_estimate=cost(2.4 * count * D * width, rows, weight),
    )(rows, weight, bias)


def feed(layer, context, rows, weights, vectors):
    count = context.shape[0]
    width = weights[1].shape[1]
    f32 = jnp.float32
    return pl.pallas_call(
        functools.partial(feed_kernel, layer),
        grid=(count // ROW_TILE,),
        in_specs=[row_spec(D), row_spec(D)]
        + [whole_spec(weight.shape) for weight in weights]
        + [whole_spec(vector.shape) for vector in vectors],
        out_specs=[
            row_spec(D),
            row_spec(width),
            row_spec(width),
            row_spec(D),
            row_spec(128),
            row_spec(D),
            row_spec(128),
            row_spec(D),
            row_spec(D),
        ],
        out_shape=[
            shape_of(count, D),
            shape_of(count, width),
            shape_of(count, width),
            shape_of(count, D, f32),
            shape_of(count, 128, f32),
            shape_of(count, D, f32),
            shape_of(count, 128, f32),
            shape_of(count, D, f32),
            shape_of(count, D),
        ],
        compiler_params=kernel_params(),
        cost_estimate=cost(5 * count * D * (2 * width + D), context, *weights),
    )(context, rows, *weights, *vectors)


def feed_back(layer, above, proj, qkv_weight, saved, weights, gains):
    count = above.shape[0]
    width = weights[1].shape[1]
    f32 = jnp.float32
    lead, lead_specs = [above], [row_spec(D)]
    if proj is not None:
        lead += [proj, qkv_weight]
        lead_specs += [part_spec(), whole_spec(qkv_weight.shape)]
    return pl.pallas_call(
        functools.partial(feed_back_kernel, layer, proj is not None),
        grid=(count // ROW_TILE,),
        in_specs=lead_specs
        + [row_spec(D), row_spec(128), row_spec(width), row_spec(D), row_spec(128)]
        + [whole_spec(weight.shape) for weight in weights]
        + [whole_spec(gain.shape) for gain in gains],
        out_specs=[
            row_spec(D),
            row_spec(width),
            row_spec(D),
            row_spec(D),
            row_spec(D),
            pl.BlockSpec((8, D), lambda i: (0, 0)),
            pl.BlockSpec((1, width), lambda i: (0, 0)),
        ],
        out_shape=[
            shape_of(count, D),
            shape_of(count, width),
            shape_of(count, D, f32),
            shape_of(count, D),
            shape_of(count, D),
            shape_of(8, D, f32),
            shape_of(1, width, f32),
        ],
        compiler_params=kernel_params(),
        cost_estimate=cost(5 * count * D * (2 * width + D), above, *weights),
    )(*lead, *saved, *weights, *gains)


def input_grad(above, proj, qkv_weight):
    count = above.shape[0]
    return pl.pallas_call(
        input_grad_kernel,
        grid=(count // ROW_TILE,),
        in_specs=[
            row_spec(D),
            part_spec(),
            whole_spec(qkv_weight.shape),
        ],
        out_specs=row_spec(D),
        out_shape=shape_of(count, D, jnp.float32),
        compiler_params=kernel_params(),
        cost_estimate=cost(2.4 * count * D * 3 * D, above, qkv_weight),
    )(above, proj, qkv_weight)


def prepare(segment, parent, clusters):
    trees = parent.shape[0]
    segment = segment.reshape(trees, 1, TREE_LEN)
    clusters = clusters.reshape(PAIRS, 2, trees, TREE_LEN).transpose(2, 0, 1, 3)
    return pl.pallas_call(
        prep_kernel,
        grid=(trees, PAIRS),
        in_specs=[
            pl.BlockSpec(memory_space=pltpu.SMEM),
            pl.BlockSpec((1, 1, TREE_LEN), lambda tree, pair: (tree, 0, 0)),
            slot_spec(),
        ],
        out_specs=[slot_spec(), head_spec()],
        out_shape=[
            jax.ShapeDtypeStruct((trees, PAIRS, 2, TREE_LEN), jnp.int32),
            jax.ShapeDtypeStruct((trees, HEADS, TREE_LEN, LANES), jnp.bfloat16),
        ],
        compiler_params=kernel_params(),
        cost_estimate=pl.CostEstimate(
            flops=trees * 20_000_000_000, bytes_accessed=trees * 4_000_000, transcendentals=0
        ),
    )(parent, segment, clusters)


def weight_grad_kernel(split_y, at_ref, left_ref, right_ref, *refs):
    product = contract_first(
        left_ref[...].reshape(left_ref.shape[-2:]), right_ref[...].reshape(right_ref.shape[-2:])
    )
    if split_y is None:
        (out_ref,) = refs
        out_ref[...] = product.astype(jnp.bfloat16).reshape(out_ref.shape)
        return
    near_ref, (send_ref, keep_ref, sum_ref) = refs[0], refs[-3:]
    total = product + near_ref[...].astype(jnp.float32).reshape(product.shape)
    sum_ref[...] = total.astype(jnp.bfloat16).reshape(sum_ref.shape)
    if split_y:
        send_ref[0] = sum_ref[:, :, 1 - at_ref[2]]
        keep_ref[0] = sum_ref[:, :, at_ref[2]]
    else:
        send_ref[...] = sum_ref[:, 1 - at_ref[1]]
        keep_ref[...] = sum_ref[:, at_ref[1]]


class Grad:
    def __init__(self, number, left, right, tiles, half):
        self.number = number
        self.left, self.right = left, right
        self.tiles, self.half = tiles, half
        self.depth = left.shape[1]
        self.parts = 1 if self.depth > D else tiles
        self.rows = self.depth // (CHIPS_Z * CHIPS_X)

    def product(self, at, other, split_y=None, near=None, start=0, total=0, before=()):
        flip = 1 if other else 0
        left, right = self.left, self.right
        count = left.shape[0]
        tall = self.depth > D
        core = lambda at: lax.rem(at[3] + flip, CORES)
        in_specs = [
            pl.BlockSpec((count, D), (lambda i, at: (0, i)) if tall else (lambda i, at: (0, 0)))
        ]
        if right.ndim == 3:
            in_specs.append(pl.BlockSpec((1, count, self.half), lambda i, at: (i, 0, core(at))))
        elif tall:
            in_specs.append(pl.BlockSpec((count, self.half), lambda i, at: (0, core(at))))
        else:
            in_specs.append(
                pl.BlockSpec((count, self.half), lambda i, at: (0, core(at) * self.tiles + i))
            )
        zs = D // (self.rows * CHIPS_X)
        place = (lambda i: (0, i)) if tall else (lambda i: (i, 0))
        whole = (self.parts, CHIPS_Z, CHIPS_X, self.rows, self.half)
        block = (1, zs, CHIPS_X, self.rows, self.half)
        full = pl.BlockSpec(block, lambda i, at: (*place(i), 0, 0, 0))
        args, scratch = [left, right], []
        if split_y is None:
            out_specs, shapes = full, jax.ShapeDtypeStruct(whole, jnp.bfloat16)
        else:
            in_specs.append(full)
            args.append(near)
            in_specs += [pl.BlockSpec(memory_space=pl.ANY)] * len(before)
            args += before
            if split_y:
                short = self.rows // CHIPS_Y
                kept = (CHIPS_X, short, self.half)
                scratch = [pltpu.VMEM((zs, CHIPS_X, CHIPS_Y, short, self.half), jnp.bfloat16)]
                spec = pl.BlockSpec((1, zs, *kept), lambda i, at: (*place(i), 0, 0, 0))
                shape = (self.parts, CHIPS_Z, *kept)
            else:
                scratch = [pltpu.VMEM((zs, CHIPS_X, self.rows, self.half), jnp.bfloat16)]
                first = start // self.rows
                index = (lambda i, at: (i, first, 0)) if tall else (lambda i, at: (0, first + i, 0))
                spec = pl.BlockSpec((zs, self.rows, self.half), index)
                shape = (CHIPS_Z, total, self.half)
            out_specs, shapes = [spec] * 2, [jax.ShapeDtypeStruct(shape, jnp.bfloat16)] * 2
        return pl.pallas_call(
            functools.partial(weight_grad_kernel, split_y),
            grid_spec=pltpu.PrefetchScalarGridSpec(
                num_scalar_prefetch=1,
                grid=(self.tiles,),
                in_specs=in_specs,
                out_specs=out_specs,
                scratch_shapes=scratch,
            ),
            out_shape=shapes,
            input_output_aliases={4 + place: place for place in range(len(before))},
            compiler_params=kernel_params(),
            cost_estimate=cost(4 * count * D * self.tiles * self.half, left, right),
        )(at, *args)


class Place:
    def __init__(self):
        rep = lax.axis_index("rep")
        shard = lax.axis_index("shard")
        self.y, self.core = rep // CORES, rep % CORES
        self.z, self.x = shard // CHIPS_X, shard % CHIPS_X
        self.at = jnp.stack([self.z, self.x, self.y, self.core]).astype(jnp.int32)


def hop(value, dz=0, dx=0, dy=0, dc=0):
    pairs = []
    for y in range(CHIPS_Y):
        for c in range(CORES):
            for z in range(CHIPS_Z):
                for x in range(CHIPS_X):
                    source = ((y * CORES + c) * CHIPS_Z + z) * CHIPS_X + x
                    y2, c2 = (y + dy) % CHIPS_Y, (c + dc) % CORES
                    z2, x2 = (z + dz) % CHIPS_Z, (x + dx) % CHIPS_X
                    pairs.append((source, ((y2 * CORES + c2) * CHIPS_Z + z2) * CHIPS_X + x2))
    return lax.ppermute(value, AXES, pairs)


def spread_vectors(found, sizes):
    found = found[:, :, 0, :LAYERS].reshape(-1, LAYERS, found.shape[-1]).transpose(1, 0, 2)
    out, at = [], 0
    for size in sizes:
        out.append(found[:, :, at : at + size].reshape(LAYERS, -1).astype(jnp.float32))
        at += size
    return out


def cut_sums(place, groups):
    at = place.at
    arrived = []
    for grads, _ in groups:
        arrived.append([hop(grad.product(at, True), dc=1) for grad in grads])
    found = []
    for (grads, y_first), near in zip(groups, arrived):
        total = sum(grad.parts * grad.rows for grad in grads)
        start, pair = 0, ()
        for grad, item in zip(grads, near):
            if y_first:
                pair = grad.product(at, False, True, item)
            else:
                pair = grad.product(at, False, False, item, start, total, tuple(pair))
            start += grad.parts * grad.rows
        found.append(tuple(pair))
    return found


def prep_steps(ins, outs):
    trees, pairs = ins[2].shape[:2]
    for tree in range(trees):
        for pair in range(pairs):
            prep_pair(*ins, *outs, tree, tree, pair)
            yield


def gather_kernel(plan, work, work_ins, work_outs, *refs):
    count = len(plan)
    own_ins, ins, refs = refs[:work_ins], refs[work_ins : work_ins + count], refs[work_ins + count :]
    own_outs, outs = refs[:work_outs], refs[work_outs : work_outs + count]
    sems, local_sem = refs[work_outs + count : -1], refs[-1]
    todo = work(own_ins, own_outs)
    rep, shard = lax.axis_index("rep"), lax.axis_index("shard")
    y, core = lax.div(rep, CORES), lax.rem(rep, CORES)
    z, x = lax.div(shard, CHIPS_X), lax.rem(shard, CHIPS_X)

    def device(dz=0, dx=0, dy=0, dc=0):
        to_y, to_core = lax.rem(y + dy, CHIPS_Y), lax.rem(core + dc, CORES)
        to_z, to_x = lax.rem(z + dz, CHIPS_Z), lax.rem(x + dx, CHIPS_X)
        return (to_y * CORES + to_core, to_z * CHIPS_X + to_x)

    mates = [dict(dx=1), dict(dy=1), dict(dc=1)] + [dict(dz=k) for k in range(1, CHIPS_Z)]
    barrier = pltpu.get_barrier_semaphore()
    for mate in mates:
        pl.semaphore_signal(
            barrier, inc=1, device_id=device(**mate), device_id_type=pl.DeviceIdType.MESH
        )
    sent = []

    def send(source, target, m, number, **step):
        copy = pltpu.make_async_remote_copy(
            src_ref=source,
            dst_ref=target,
            send_sem=sems[m].at[0, number],
            recv_sem=sems[m].at[1, number],
            device_id=device(**step),
            device_id_type=pl.DeviceIdType.MESH,
        )
        copy.start()
        sent.append(copy)
        return copy

    def part(m, at_z, at_x, at_y, at_core):
        out, (layer, split_y, by_core) = outs[m], plan[m]
        columns = slice(None)
        if by_core:
            half = out.shape[-1] // CORES
            columns = pl.ds(pl.multiple_of(at_core * half, 128), half)
        at_z = slice(None) if at_z is None else at_z
        at_x = slice(None) if at_x is None else at_x
        return out.at[at_z, at_x, at_y if split_y else 0, :, columns]

    locals_ = []
    for m, (layer, split_y, by_core) in enumerate(plan):
        rows = outs[m].shape[3]
        source = ins[m] if layer is None else ins[m].at[layer]
        if by_core:
            half = outs[m].shape[-1] // CORES
            first = pl.multiple_of(y * rows, 16) if split_y else 0
            source = source.at[pl.ds(first, rows), pl.ds(pl.multiple_of(core * half, 128), half)]
        copy = pltpu.make_async_copy(source, part(m, z, x, y, core), local_sem.at[m])
        copy.start()
        locals_.append(copy)
    pl.semaphore_wait(barrier, len(mates))
    along_z, along_x, over_y, last = {}, {}, {}, []

    def spread(m, at_z, at_x):
        piece = part(m, at_z, at_x, y, core)
        if at_x is x:
            along_x[m].append(send(piece, piece, m, 3 + len(along_x[m]), dx=1))
        if plan[m][1]:
            over_y[m].append(send(piece, piece, m, 7 + len(over_y[m]), dy=1))

    def behind(k):
        return lax.rem(z + CHIPS_Z - k, CHIPS_Z)

    def after_x(m):
        for k in range(CHIPS_Z):
            if k % 2:
                next(todo, None)
            along_x[m][k].wait_recv()
            spread(m, behind(k), 1 - x)
        if plan[m][2]:
            piece = part(m, None, None, y, core)
            last.append(send(piece, piece, m, 15, dc=1))

    def after_y(m):
        if over_y[m]:
            for copy in over_y[m]:
                copy.wait_recv()
            piece = part(m, None, None, 1 - y, core)
            last.append(send(piece, piece, m, 16, dc=1))

    order = sorted(range(count), key=lambda m: (not plan[m][1], -outs[m].shape[-1]))

    def set_out(m):
        locals_[m].wait()
        mine = part(m, z, x, y, core)
        along_z[m] = [send(mine, mine, m, k - 1, dz=k) for k in range(1, CHIPS_Z)]
        along_x[m], over_y[m] = [], []
        spread(m, z, x)

    for m in order[:2]:
        set_out(m)
    for place, m in enumerate(order):
        for k in range(1, CHIPS_Z):
            next(todo, None)
            along_z[m][k - 1].wait_recv()
            spread(m, behind(k), x)
        if place + 2 < count:
            set_out(order[place + 2])
        if place:
            after_x(order[place - 1])
    after_x(order[-1])
    for m in order:
        after_y(m)
        next(todo, None)
    for _ in todo:
        pass
    for copy in last:
        copy.wait_recv()
    for copy in sent:
        copy.wait_send()


def gather(weights, wanted, work, work_args, work_shapes, number):
    low = jnp.bfloat16
    args, plan, shapes = [], [], []
    for which, layer, split_y in wanted:
        args.append(weights[which])
        plan.append((layer, split_y, layer is not None))
        rows, columns = weights[which].shape[-2:]
        split = CHIPS_Y if split_y else 1
        shapes.append((CHIPS_Z, CHIPS_X, split, rows // split, columns))
    whole = pl.BlockSpec(memory_space=pltpu.VMEM)
    small = pl.BlockSpec(memory_space=pltpu.SMEM)
    found = pl.pallas_call(
        functools.partial(gather_kernel, plan, work, len(work_args), len(work_shapes)),
        in_specs=[small if arg.shape[-1] == SEGMENTS else whole for arg in work_args]
        + [pl.BlockSpec(memory_space=pl.ANY)] * len(args),
        out_specs=[whole] * (len(work_shapes) + len(args)),
        out_shape=work_shapes + [jax.ShapeDtypeStruct(shape, low) for shape in shapes],
        scratch_shapes=[pltpu.SemaphoreType.DMA((2, 17))] * len(args)
        + [pltpu.SemaphoreType.DMA((len(args),))],
        compiler_params=pltpu.CompilerParams(
            vmem_limit_bytes=KERNEL_VMEM, collective_id=number, has_side_effects=True
        ),
        cost_estimate=pl.CostEstimate(flops=0, bytes_accessed=200_000_000, transcendentals=0),
    )(*work_args, *args)
    results, arrays = list(found[: len(work_shapes)]), found[len(work_shapes) :]
    for item, array in zip(wanted, arrays):
        results.append(array if item[1] is None else array.reshape(-1, array.shape[-1]))
    return results


def pack_sums(out_ref, ins):
    rows = 8 * LAYERS
    width = out_ref.shape[1]
    for layer in range(LAYERS):
        sums_ref, ffin_ref, _ = ins[3 * layer : 3 * layer + 3]
        out_ref[8 * layer : 8 * layer + 8] = sums_ref[...]
        for at in range(0, ffin_ref.shape[1], width):
            out_ref[rows : rows + 1] = ffin_ref[:, at : at + width]
            rows += 1
    for layer in range(LAYERS):
        ref = ins[3 * layer + 2]
        for pair in range(ref.shape[1]):
            value = ref[0, pair]
            for tree in range(1, ref.shape[0]):
                value = value + ref[tree, pair]
            out_ref[rows : rows + 8, pair * LANES : (pair + 1) * LANES] = value
        rows += 8


def sum_rows(ffin_width):
    return LAYERS * (16 + ffin_width // D)


def reduce_kernel(flats, count, vectors, work, work_ins, work_outs, *refs):
    take = iter(refs)

    def some(number):
        return [next(take) for _ in range(number)]

    own_ins = some(work_ins)
    a_ins = [some(2) for _ in range(flats)]
    b_ins = [some(2) for _ in range(count)]
    vec_ins = some(vectors)
    own_outs = some(work_outs)
    a_outs = [some(2) for _ in range(flats)]
    b_outs = some(count)
    vec_outs = some(1 if vectors else 0)
    a_scratch = [some(6) for _ in range(flats)]
    b_scratch = [some(6) for _ in range(count)]
    v_send, v_land = some(2) if vectors else (None, None)
    a_sems, b_sems = some(flats), some(count)
    v_sems = next(take) if vectors else None
    todo = work(own_ins, own_outs)
    rep, shard = lax.axis_index("rep"), lax.axis_index("shard")
    y, core = lax.div(rep, CORES), lax.rem(rep, CORES)
    z, x = lax.div(shard, CHIPS_X), lax.rem(shard, CHIPS_X)

    def device(dz=0, dx=0, dy=0, dc=0):
        to_y, to_core = lax.rem(y + dy, CHIPS_Y), lax.rem(core + dc, CORES)
        to_z, to_x = lax.rem(z + dz, CHIPS_Z), lax.rem(x + dx, CHIPS_X)
        return (to_y * CORES + to_core, to_z * CHIPS_X + to_x)

    flip_z = 1 + 2 * lax.rem(z, 2)
    mates = [dict(dx=1), dict(dy=1), dict(dc=1), dict(dy=1, dc=1)]
    mates += [dict(dz=k) for k in range(1, CHIPS_Z)]
    barrier = pltpu.get_barrier_semaphore()
    for mate in mates:
        pl.semaphore_signal(
            barrier, inc=1, device_id=device(**mate), device_id_type=pl.DeviceIdType.MESH
        )
    pl.semaphore_wait(barrier, len(mates))
    sent = []

    def send(source, target, sems, number, **step):
        copy = pltpu.make_async_remote_copy(
            src_ref=source,
            dst_ref=target,
            send_sem=sems.at[0, number],
            recv_sem=sems.at[1, number],
            device_id=device(**step),
            device_id_type=pl.DeviceIdType.MESH,
        )
        copy.start()
        sent.append(copy)
        return copy

    def wide(value):
        return value.astype(jnp.float32)

    order = (2, 1, 3, 0)
    ahead = [lax.rem(z + k, CHIPS_Z) for k in order]
    v_copies = []
    if vectors:
        pack_sums(v_send.at[0], vec_ins)
        v_copies.append(send(v_send.at[0], v_land.at[0], v_sems, 0, dc=1))
    a_x, b_y = [[] for _ in range(flats)], [[] for _ in range(count)]

    def set_out(j):
        to = ahead[j]
        for i, (first, _) in enumerate(a_ins):
            a_x[i].append(send(first.at[to], a_scratch[i][0].at[j], a_sems[i], j, dx=1))
        for i, (first, _) in enumerate(b_ins):
            b_y[i].append(send(first.at[:, to], b_scratch[i][0].at[j], b_sems[i], j, dy=1))

    set_out(0)
    set_out(1)
    steps = (dict(dc=1), dict(dy=1), dict(dx=1), dict(dz=2), dict(dz=flip_z))

    def add_vectors(s):
        if not vectors:
            return
        v_copies[s].wait_recv()
        total = v_send[s] + v_land[s]
        if s + 1 == len(steps):
            vec_outs[0][...] = total
        else:
            v_send[s + 1] = total
            v_copies.append(
                send(v_send.at[s + 1], v_land.at[s + 1], v_sems, s + 1, **steps[s + 1])
            )

    a_z, b_x, b_z = ([[] for _ in range(number)] for number in (flats, count, count))

    def b_along_z(i, j):
        k, keep = order[j], b_ins[i][1]
        over, _, x_land, z_send, z_land, _ = b_scratch[i]
        b_x[i][j].wait_recv()
        if k:
            total = wide(keep[:, ahead[j], x]) + wide(over[j, :, x]) + wide(x_land[j])
            z_send[k - 1] = total.astype(jnp.bfloat16)
            b_z[i].append(send(z_send.at[k - 1], z_land.at[k - 1], b_sems[i], 7 + k, dz=k))

    def b_along_x(i, j):
        keep, (over, x_send, x_land, *_) = b_ins[i][1], b_scratch[i]
        b_y[i][j].wait_recv()
        total = wide(keep[:, ahead[j], 1 - x]) + wide(over[j, :, 1 - x])
        x_send[j] = total.astype(jnp.bfloat16)
        b_x[i].append(send(x_send.at[j], x_land.at[j], b_sems[i], 4 + j, dx=1))

    for j, k in enumerate(order):
        next(todo, None)
        for i, (_, keep) in enumerate(a_ins):
            across, z_send, z_land, *_ = a_scratch[i]
            a_x[i][j].wait_recv()
            if k:
                total = wide(keep[ahead[j]]) + wide(across[j])
                z_send[k - 1] = total.astype(jnp.bfloat16)
                a_z[i].append(
                    send(z_send.at[k - 1], z_land.at[k - 1], a_sems[i], 3 + k, dz=k)
                )
        next(todo, None)
        for i in range(count):
            b_along_x(i, j)
        if j + 2 < CHIPS_Z:
            set_out(j + 2)
        if j:
            for i in range(count):
                b_along_z(i, j - 1)
        next(todo, None)
        add_vectors(j)
    for i in range(count):
        b_along_z(i, CHIPS_Z - 1)
    add_vectors(4)
    for _ in todo:
        pass
    over_y, ends = [], []
    for i, (_, keep) in enumerate(a_ins):
        across, _, z_land, y_send, y_land, _ = a_scratch[i]
        for copy in a_z[i]:
            copy.wait_recv()
        total = wide(keep[z]) + wide(across[CHIPS_Z - 1])
        for k in range(CHIPS_Z - 1):
            total = total + wide(z_land[k])
        y_send[...] = total.astype(jnp.bfloat16)
        over_y.append(send(y_send, y_land, a_sems[i], 7, dy=1))
    for i, (_, keep) in enumerate(b_ins):
        over, _, x_land, _, z_land, end_land = b_scratch[i]
        for copy in b_z[i]:
            copy.wait_recv()
        total = wide(keep[:, z, x]) + wide(over[3, :, x]) + wide(x_land[3])
        for k in range(CHIPS_Z - 1):
            total = total + wide(z_land[k])
        b_outs[i][0] = total.astype(jnp.bfloat16)
        for number, step in enumerate((dict(dy=1), dict(dc=1), dict(dy=1, dc=1))):
            ends.append(
                send(b_outs[i].at[0], end_land.at[number], b_sems[i], 11 + number, **step)
            )
    for i, (own, _) in enumerate(a_outs):
        *_, y_send, y_land, c_land = a_scratch[i]
        over_y[i].wait_recv()
        own[...] = (wide(y_send[...]) + wide(y_land[...])).astype(jnp.bfloat16)
        ends.append(send(own, c_land, a_sems[i], 8, dc=1))
    for copy in ends:
        copy.wait_recv()
    for i in range(count):
        b_outs[i][1:4] = b_scratch[i][5][...]
    for i, (_, other) in enumerate(a_outs):
        other[...] = a_scratch[i][5][...]
    for copy in sent:
        copy.wait_send()


def no_work(ins, outs):
    return iter(())


def reduce_sums(flats, pairs, sums, number, work=no_work, work_args=(), work_shapes=()):
    low = jnp.bfloat16
    whole = pl.BlockSpec(memory_space=pltpu.VMEM)
    far = pl.BlockSpec(memory_space=pl.ANY)
    args, specs = list(work_args), [whole] * len(work_args)
    outs, scratch = [], []
    for first, keep in flats:
        piece = keep.shape[1:]
        args += [first, keep]
        specs += [far, whole]
        outs += [piece, piece]
        scratch += [(CHIPS_Z, *piece), (CHIPS_Z - 1, *piece), (CHIPS_Z - 1, *piece)]
        scratch += [piece] * 3
    for first, keep in pairs:
        parts, _, _, rows, half = keep.shape
        block = (parts, rows, half)
        args += [first, keep]
        specs += [far, whole]
        outs.append((CORES * CHIPS_Y, *block))
        scratch += [
            (CHIPS_Z, parts, CHIPS_X, rows, half),
            (CHIPS_Z, *block),
            (CHIPS_Z, *block),
            (CHIPS_Z - 1, *block),
            (CHIPS_Z - 1, *block),
            (CORES * CHIPS_Y - 1, *block),
        ]
    args += sums
    specs += [whole] * len(sums)
    shapes = list(work_shapes) + [jax.ShapeDtypeStruct(shape, low) for shape in outs]
    scratch = [pltpu.VMEM(shape, low) for shape in scratch]
    if sums:
        vec = (sum_rows(sums[1].shape[1]), D)
        shapes.append(jax.ShapeDtypeStruct(vec, jnp.float32))
        scratch += [pltpu.VMEM((5, *vec), jnp.float32)] * 2
    scratch += [pltpu.SemaphoreType.DMA((2, 9))] * len(flats)
    scratch += [pltpu.SemaphoreType.DMA((2, 14))] * len(pairs)
    if sums:
        scratch.append(pltpu.SemaphoreType.DMA((2, 5)))
    return pl.pallas_call(
        functools.partial(
            reduce_kernel, len(flats), len(pairs), len(sums), work, len(work_args), len(work_shapes)
        ),
        in_specs=specs,
        out_specs=[whole] * len(shapes),
        out_shape=shapes,
        scratch_shapes=scratch,
        compiler_params=pltpu.CompilerParams(
            vmem_limit_bytes=KERNEL_VMEM, collective_id=number, has_side_effects=True
        ),
        cost_estimate=pl.CostEstimate(flops=0, bytes_accessed=200_000_000, transcendentals=0),
    )(*args)


def join_kernel(plan, count, at_ref, *refs):
    for ref, out, layer, outer, parts, dc, dy, start, rows in plan:
        ref, out_ref = refs[ref], refs[count + out]
        half = ref.shape[1]
        core = lax.rem(at_ref[3] + dc, CORES)
        row = 0
        if dy is not None:
            row = pl.multiple_of(lax.rem(at_ref[2] + dy, CHIPS_Y) * rows, 16)
        for part in range(parts):
            column = part * CORES + core if outer else core * parts + part
            column = pl.multiple_of(column * half, 128)
            value = ref[start + part * rows : start + (part + 1) * rows]
            out_ref[layer, pl.ds(row, rows), pl.ds(column, half)] = value.astype(jnp.float32)


def join(at, done, shapes):
    arrays, plan = [], []
    for out, (number, (tall, wide)) in enumerate(shapes.items()):
        for layer in range(LAYERS):
            pieces, start, rows = done[layer][number]
            for place, piece in enumerate(pieces):
                known = [other is piece for other in arrays]
                if not any(known):
                    arrays.append(piece)
                    known.append(True)
                parts = wide // (CORES * piece.shape[1])
                dy, dc = (place % CHIPS_Y, place // CHIPS_Y) if len(pieces) > CORES else (None, place)
                plan.append((known.index(True), out, layer, number == 0, parts, dc, dy, start, rows))
    zeros = lambda i, at: (0, 0)
    outs = [(LAYERS, *shape) for shape in shapes.values()]
    return pl.pallas_call(
        functools.partial(join_kernel, plan, len(arrays)),
        grid_spec=pltpu.PrefetchScalarGridSpec(
            num_scalar_prefetch=1,
            grid=(1,),
            in_specs=[pl.BlockSpec(array.shape, zeros) for array in arrays],
            out_specs=[pl.BlockSpec(out, lambda i, at: (0, 0, 0)) for out in outs],
        ),
        out_shape=[jax.ShapeDtypeStruct(out, jnp.float32) for out in outs],
        compiler_params=kernel_params(),
        cost_estimate=pl.CostEstimate(flops=0, bytes_accessed=4_000_000, transcendentals=0),
    )(at, *arrays)


def local(
    fast,
    inputs,
    cotangent,
    segment,
    parent,
    clusters,
    *weights,
):
    pieces = {}
    if fast:
        place = Place()
        at = place.at
        shards = dict(enumerate(weights))
        shards["vectors"] = jnp.pad(
            jnp.concatenate([weights[member] for member in VECTORS], axis=1),
            ((0, 16 - LAYERS), (0, 0)),
        )
        trees = parent.shape[0]
        slots, bias, found, qkv = gather(
            shards,
            (("vectors", None, False), (0, 0, True)),
            prep_steps,
            (
                parent,
                segment.reshape(trees, 1, TREE_LEN),
                clusters.reshape(PAIRS, 2, trees, TREE_LEN).transpose(2, 0, 1, 3),
            ),
            [
                jax.ShapeDtypeStruct((trees, PAIRS, 2, TREE_LEN), jnp.int32),
                jax.ShapeDtypeStruct((trees, HEADS, TREE_LEN, LANES), jnp.bfloat16),
            ],
            1,
        )
        vectors = spread_vectors(found, [weights[number].shape[1] for number in VECTORS])
        whole = {(0, 0): qkv}

        def attend_layer(layer, projected):
            last = layer + 1 == LAYERS
            wanted = [(6, layer, True), (8, layer, not last), (2, layer, last)]
            if not last:
                wanted.insert(2, (0, layer + 1, False))
            results = gather(
                shards, wanted, attend_steps, (projected, slots, bias), attend_shapes(trees), 2 + layer
            )
            for (number, at_layer, _), array in zip(wanted, results[4:]):
                whole[at_layer, number] = array
            return results[:4]

        def get(layer, number):
            return whole[layer, number]

        def attend_back_layer(layer, grad_context, heads, groups, waiting):
            flat, pair = cut_sums(place, groups)
            proj, head_sums, *ends = reduce_sums(
                [flat],
                [pair, *waiting],
                [],
                2 + LAYERS + layer,
                attend_back_steps,
                (slots, grad_context, *heads),
                attend_back_shapes(trees),
            )
            pieces[layer, "flat"] = ends[:2]
            pieces[layer, 6] = ends[2]
            if waiting:
                pieces[layer + 1, 0] = ends[3]
            return proj, head_sums

    else:
        slots, bias = prepare(segment, parent, clusters)
        vectors = [
            lax.all_gather(weights[number], "shard", axis=1, tiled=True).astype(jnp.float32)
            for number in VECTORS
        ]

        def attend_layer(layer, projected):
            return attend(projected, slots, bias)

        def get(layer, number):
            return lax.all_gather(weights[number][layer], "shard", axis=0, tiled=True)

        def own_sum(left, right):
            if right.ndim == 3:
                right = right.transpose(1, 0, 2).reshape(right.shape[1], -1)
            total = contract_first(left, right)
            total = lax.psum_scatter(total, "shard", scatter_dimension=0, tiled=True)
            return lax.psum(total.astype(jnp.bfloat16), "rep").astype(jnp.float32)

        def attend_back_layer(layer, grad_context, heads, groups, waiting):
            for grads, _ in groups:
                for grad in grads:
                    pieces[layer, grad.number] = own_sum(grad.left, grad.right)
            return attend_back(grad_context, slots, heads)

    vector = dict(zip(VECTORS, vectors))
    hidden, hidden_low = inputs, inputs
    saved = []
    for layer in range(LAYERS):
        pull = functools.partial(get, layer)
        projected = project(layer, hidden_low, pull(0), vector[1])
        context, *heads = attend_layer(layer, projected)
        entered = hidden_low
        middle, act, slope, *norms, hidden, hidden_low = feed(
            layer,
            context,
            hidden,
            [pull(2), pull(6), pull(8)],
            [vector[number] for number in (3, 4, 5, 7, 9, 10, 11)],
        )
        saved.append((entered, heads, context, middle, act, slope, norms))
    result = hidden_low
    above, proj = cotangent, None
    sums, waiting = [None] * LAYERS, []
    for layer in reversed(range(LAYERS)):
        entered, heads, context, middle, act, slope, norms = saved[layer]
        pull = functools.partial(get, layer)
        down, grad_pre, grad_attn, attn_low, grad_context, row_sums, ffin_sum = feed_back(
            layer,
            above,
            proj,
            None if proj is None else get(layer + 1, 0),
            [norms[2], norms[3], slope, norms[0], norms[1]],
            [pull(2), pull(6), pull(8)],
            [vector[4], vector[10]],
        )
        wide = grad_pre.shape[1] // CORES
        groups = (
            (
                (
                    Grad(8, act, down, act.shape[1] // D, UNIT),
                    Grad(2, context, attn_low, 1, UNIT),
                ),
                False,
            ),
            ((Grad(6, middle, grad_pre, wide // D, D),), True),
        )
        proj, head_sums = attend_back_layer(layer, grad_context, heads, groups, waiting)
        sums[layer] = [row_sums, ffin_sum, head_sums]
        above = grad_attn
        last = Grad(0, entered, proj, 3, UNIT)
        if not fast:
            pieces[layer, 0] = own_sum(last.left, last.right)
        elif layer:
            waiting = cut_sums(place, [((last,), True)])
    grad_input = input_grad(above, proj, get(0, 0))
    sums = [item for layer in sums for item in layer]
    if fast:
        (pair,) = cut_sums(place, [((last,), True)])
        pair, grad_input = lax.optimization_barrier((pair, grad_input))
        pieces[0, 0], total = reduce_sums([], [pair], sums, 0)
    else:
        norms, wide, heads = [], [], []
        for row_sums, ffin_sum, head_sums in (sums[:3], sums[3:]):
            norms.append(row_sums)
            wide.append(ffin_sum.reshape(-1, D))
            heads.append(head_sums.sum(0).transpose(1, 0, 2).reshape(8, D))
        total = lax.psum(jnp.concatenate(norms + wide + heads), AXES)
    count = lax.axis_size("shard")
    shard = lax.axis_index("shard")
    ffin_rows = sums[1].shape[1] // D

    def share(rows):
        stacked = jnp.stack([total[row].reshape(-1) for row in rows])
        width = stacked.shape[1] // count
        return lax.dynamic_slice_in_dim(stacked, shard * width, width, axis=1)

    starts = [0, 8, 16, 16 + ffin_rows]
    heads_at = [16 + 2 * ffin_rows, 24 + 2 * ffin_rows]
    grads = {
        1: share([slice(at, at + 3, 2) for at in heads_at]),
        7: share([slice(at, at + ffin_rows) for at in starts[2:]]),
    }
    for number, row in ((10, 0), (11, 1), (9, 2), (4, 3), (5, 4), (3, 5)):
        grads[number] = share([row, 8 + row])
    if fast:
        rows = {number: weights[number].shape[1] for number in MATRICES}
        parts = {number: weights[number].shape[2] // (CORES * UNIT) for number in MATRICES}
        known = [{} for _ in range(LAYERS)]
        for layer in range(LAYERS):
            start = 0
            for number in (8, 2):
                known[layer][number] = (pieces[layer, "flat"], start, rows[number])
                start += rows[number] * parts[number]
            for number in (6, 0):
                end = pieces[layer, number]
                end = end.reshape(end.shape[0], -1, end.shape[-1])
                known[layer][number] = (list(end), 0, rows[number] // CHIPS_Y)
        for numbers in (MATRICES,):
            shapes = {number: weights[number].shape[1:] for number in numbers}
            grads.update(zip(numbers, join(place.at, known, shapes)))
    else:
        for number in MATRICES:
            grads[number] = jnp.stack([pieces[layer, number] for layer in range(LAYERS)])
    return (result, grad_input, *[grads[number] for number in range(12)])


def solution(mesh):
    in_specs = (
        P(("rep", "shard"), None),
        P(("rep", "shard"), None),
        P(("rep", "shard")),
        P(("rep", "shard"), None),
        P(None, ("rep", "shard")),
        P(None, "shard", None),
        P(None, "shard"),
        P(None, "shard", None),
        P(None, "shard"),
        P(None, "shard"),
        P(None, "shard"),
        P(None, "shard", None),
        P(None, "shard"),
        P(None, "shard", None),
        P(None, "shard"),
        P(None, "shard"),
        P(None, "shard"),
    )
    out_specs = (
        P(("rep", "shard"), None),
        P(("rep", "shard"), None),
        P(None, "shard", None),
        P(None, "shard"),
        P(None, "shard", None),
        P(None, "shard"),
        P(None, "shard"),
        P(None, "shard"),
        P(None, "shard", None),
        P(None, "shard"),
        P(None, "shard", None),
        P(None, "shard"),
        P(None, "shard"),
        P(None, "shard"),
    )
    fast = mesh.shape["rep"] == CHIPS_Y * CORES and mesh.shape["shard"] == CHIPS_Z * CHIPS_X
    return jax.shard_map(
        functools.partial(local, fast),
        mesh=mesh,
        in_specs=in_specs,
        out_specs=out_specs,
        check_vma=False,
    )
```

```python
import functools

import jax
import jax.numpy as jnp
from jax import lax
from jax.experimental import pallas as pl
from jax.experimental.pallas import tpu as pltpu
from jax.sharding import PartitionSpec as P

D = 768
HEADS = 12
HEAD_DIM = 64
LAYERS = 2
CLUSTER = 128
TREE_LEN = 1024
SEGMENTS = 13
PAIRS = HEADS // 2
LANES = 2 * HEAD_DIM
KERNEL_VMEM = 60 * 2**20
ROW_TILE = 256
FEED_TILE = 768
DEPTH_TILE = 384
INV_ROOT = (2.0 * 3.141592653589793) ** -0.5
MATRICES = (0, 2, 6, 8)
VECTORS = (1, 3, 4, 5, 7, 9, 10, 11)
UNIT = 384
AXES = ("rep", "shard")
CHIPS_Z, CHIPS_X, CHIPS_Y, CORES = 4, 2, 2, 2
norm_eps = 1e-06


def one_hot_rows(slot_row):
    length = slot_row.shape[-1]
    rows = lax.broadcasted_iota(jnp.int32, (length, length), 0)
    return jnp.where(rows == slot_row, 1.0, 0.0).astype(jnp.bfloat16)


def first_lanes(length):
    return lax.broadcasted_iota(jnp.int32, (length, LANES), 1) < HEAD_DIM


def contract_last(left_side, right_side):
    return lax.dot_general(
        left_side, right_side, (((1,), (1,)), ((), ())), preferred_element_type=jnp.float32
    )


def contract_first(left_side, right_side):
    return lax.dot_general(
        left_side, right_side, (((0,), (0,)), ((), ())), preferred_element_type=jnp.float32
    )


def cluster_blocks(values):
    return [values[at : at + CLUSTER] for at in range(0, values.shape[0], CLUSTER)]


def attend_pair(slots, query, key, value, bias, store):
    low = first_lanes(TREE_LEN)
    query = query * jnp.bfloat16(HEAD_DIM**-0.5)
    packed = (
        jnp.where(low, query, pltpu.roll(key, HEAD_DIM, 1)),
        jnp.where(low, pltpu.roll(query, HEAD_DIM, 1), key),
    )
    context = []
    for head in range(2):
        table = one_hot_rows(slots[head : head + 1])
        joined = jnp.concatenate([packed[head], value], axis=1)
        found = jnp.dot(table, joined, preferred_element_type=jnp.float32).astype(jnp.bfloat16)
        both, values = found[:, :LANES], found[:, LANES:]
        store("both", head, both)
        store("values", head, values)
        queries = jnp.where(low, both, jnp.bfloat16(0))
        keys = pltpu.roll(both, HEAD_DIM, 1)
        scores = jnp.concatenate(
            [contract_last(q, k) for q, k in zip(cluster_blocks(queries), cluster_blocks(keys))],
            axis=0,
        )
        scores = scores + bias[head].astype(jnp.float32)
        numerator = jnp.exp(scores - jnp.max(scores, axis=1, keepdims=True))
        total = jnp.sum(numerator, axis=1, keepdims=True)
        soft = (numerator * (1.0 / total)).astype(jnp.bfloat16)
        store("soft", head, soft)
        out = jnp.concatenate(
            [
                jnp.dot(p, v, preferred_element_type=jnp.float32)
                for p, v in zip(cluster_blocks(soft), cluster_blocks(values))
            ],
            axis=0,
        ).astype(jnp.bfloat16)
        context.append(contract_first(table, out))
        if head == 0:
            yield
    store("context", None, jnp.where(low, context[0], context[1]).astype(jnp.bfloat16))


def attend_kernel(slot_ref, query_ref, key_ref, value_ref, bias_ref, ctx_ref, qk_ref, val_ref, p_ref):
    refs = {"both": qk_ref, "values": val_ref, "soft": p_ref}

    def store(name, head, value):
        if head is None:
            ctx_ref[...] = value
        else:
            refs[name][0, head] = value

    for _ in attend_pair(
        slot_ref[0, 0], query_ref[...], key_ref[...], value_ref[...], bias_ref[0], store
    ):
        pass


def attend_steps(ins, outs):
    projected_ref, slot_ref, bias_ref = ins
    ctx_ref, qk_ref, val_ref, p_ref = outs
    refs = {"both": qk_ref, "values": val_ref, "soft": p_ref}
    for tree in range(slot_ref.shape[0]):
        rows = slice(tree * TREE_LEN, (tree + 1) * TREE_LEN)
        for pair in range(PAIRS):
            lanes = [slice((part * PAIRS + pair) * LANES, (part * PAIRS + pair + 1) * LANES) for part in range(3)]
            heads = slice(2 * pair, 2 * pair + 2)

            def store(name, head, value):
                if head is None:
                    ctx_ref[rows, lanes[0]] = value
                else:
                    refs[name][tree, 2 * pair + head] = value

            yield from attend_pair(
                slot_ref[tree, pair],
                *[projected_ref[rows, part] for part in lanes],
                bias_ref[tree, heads],
                store,
            )
            yield


def attend_back_pair(slots, grads, both_of, values_of, soft_of, store):
    low = first_lanes(TREE_LEN)
    placed = []
    for head in range(2):
        table = one_hot_rows(slots[head : head + 1])
        found = jnp.dot(table, grads, preferred_element_type=jnp.float32)
        found = jnp.where(low == (head == 0), found, 0.0).astype(jnp.bfloat16)
        both, values, soft = both_of(head), values_of(head), soft_of(head)
        grad_soft = jnp.concatenate(
            [contract_last(g, v) for g, v in zip(cluster_blocks(found), cluster_blocks(values))],
            axis=0,
        )
        grad_value = jnp.concatenate(
            [contract_first(p, g) for p, g in zip(cluster_blocks(soft), cluster_blocks(found))],
            axis=0,
        ).astype(jnp.bfloat16)
        weights = soft.astype(jnp.float32)
        delta = jnp.sum(weights * grad_soft, axis=1, keepdims=True)
        grad_scores = (weights * (grad_soft - delta)).astype(jnp.bfloat16)
        pairs = list(zip(cluster_blocks(grad_scores), cluster_blocks(both)))
        by_key = jnp.concatenate([contract_first(s, b) for s, b in pairs], axis=0)
        by_query = jnp.concatenate(
            [jnp.dot(s, b, preferred_element_type=jnp.float32) for s, b in pairs], axis=0
        )
        mixed = jnp.where(low, by_key, by_query * HEAD_DIM**-0.5).astype(jnp.bfloat16)
        joined = jnp.concatenate([mixed, grad_value], axis=1)
        placed.append(contract_first(table, joined))
        if head == 0:
            yield
    first, second = placed
    queries = jnp.where(low, pltpu.roll(first[:, :LANES], HEAD_DIM, 1), second[:, :LANES])
    keys = jnp.where(low, first[:, :LANES], pltpu.roll(second[:, :LANES], HEAD_DIM, 1))
    values = jnp.where(low, first[:, LANES:], second[:, LANES:])
    sums = []
    for part, grad in enumerate((queries, keys, values)):
        rounded = grad.astype(jnp.bfloat16)
        store(part, rounded)
        sums.append(rows_sum(rounded.astype(jnp.float32)))
    store(None, jnp.concatenate(sums + [jnp.zeros((5, LANES), jnp.float32)], axis=0))


def attend_back_kernel(slot_ref, grad_ref, qk_ref, val_ref, p_ref, out_ref, sums_ref):
    def store(part, value):
        if part is None:
            sums_ref[0, 0] = value
        else:
            out_ref[part] = value

    refs = [lambda head, ref=ref: ref[0, head] for ref in (qk_ref, val_ref, p_ref)]
    for _ in attend_back_pair(slot_ref[0, 0], grad_ref[...], *refs, store):
        pass


def attend_back_steps(ins, outs):
    slot_ref, grad_ref, *kept = ins
    out_ref, sums_ref = outs
    for tree in range(slot_ref.shape[0]):
        rows = slice(tree * TREE_LEN, (tree + 1) * TREE_LEN)
        for pair in range(PAIRS):
            lanes = slice(pair * LANES, (pair + 1) * LANES)

            def store(part, value):
                if part is None:
                    sums_ref[tree, pair] = value
                else:
                    out_ref[part, rows, lanes] = value

            refs = [lambda head, ref=ref: ref[tree, 2 * pair + head] for ref in kept]
            yield from attend_back_pair(slot_ref[tree, pair], grad_ref[rows, lanes], *refs, store)
            yield


def slot_spec(start=0):
    return pl.BlockSpec((1, 1, 2, TREE_LEN), lambda tree, pair: (tree, start + pair, 0, 0))


def head_spec(start=0):
    return pl.BlockSpec((1, 2, TREE_LEN, LANES), lambda tree, pair: (tree, start + pair, 0, 0))


def column_spec(offset):
    return pl.BlockSpec((TREE_LEN, LANES), lambda tree, pair: (tree, offset + pair))


def kernel_params():
    return pltpu.CompilerParams(vmem_limit_bytes=KERNEL_VMEM)


def attend_shapes(trees):
    stored = jax.ShapeDtypeStruct((trees, HEADS, TREE_LEN, LANES), jnp.bfloat16)
    return [jax.ShapeDtypeStruct((trees * TREE_LEN, D), jnp.bfloat16), stored, stored, stored]


def attend(projected, slots, bias):
    trees = slots.shape[0]
    return pl.pallas_call(
        attend_kernel,
        grid=(trees, PAIRS),
        in_specs=[
            slot_spec(),
            column_spec(0),
            column_spec(PAIRS),
            column_spec(2 * PAIRS),
            head_spec(),
        ],
        out_specs=[column_spec(0), head_spec(), head_spec(), head_spec()],
        out_shape=attend_shapes(trees),
        compiler_params=kernel_params(),
        cost_estimate=pl.CostEstimate(
            flops=trees * 30_000_000_000, bytes_accessed=trees * 20_000_000, transcendentals=0
        ),
    )(slots, projected, projected, projected, bias)


def attend_back_shapes(trees):
    return [
        jax.ShapeDtypeStruct((3, trees * TREE_LEN, D), jnp.bfloat16),
        jax.ShapeDtypeStruct((trees, PAIRS, 8, LANES), jnp.float32),
    ]


def attend_back(grad_context, slots, kept):
    trees = slots.shape[0]
    return pl.pallas_call(
        attend_back_kernel,
        grid=(trees, PAIRS),
        in_specs=[slot_spec(), column_spec(0), head_spec(), head_spec(), head_spec()],
        out_specs=[
            pl.BlockSpec((3, TREE_LEN, LANES), lambda tree, pair: (0, tree, pair)),
            pl.BlockSpec((1, 1, 8, LANES), lambda tree, pair: (tree, pair, 0, 0)),
        ],
        out_shape=attend_back_shapes(trees),
        compiler_params=kernel_params(),
        cost_estimate=pl.CostEstimate(
            flops=trees * 35_000_000_000, bytes_accessed=trees * 20_000_000, transcendentals=0
        ),
    )(slots, grad_context, *kept)


def erf_parts(values):
    size = jnp.abs(values)
    turn = 1.0 / (1.0 + (0.3275911 * 0.5**0.5) * size)
    bell = jnp.exp(-0.5 * values * values)
    series = 1.061405429 * 0.5
    for factor in (-1.453152027, 1.421413741, -0.284496736, 0.254829592):
        series = series * turn + factor * 0.5
    tail = series * turn * bell
    return jnp.where(values < 0.0, tail, 1.0 - tail), bell


def norm_parts(values):
    centred = values - jnp.mean(values, axis=-1, keepdims=True)
    scale = lax.rsqrt(jnp.mean(centred * centred, axis=-1, keepdims=True) + norm_eps)
    return centred * scale, scale


def norm_back(grad, normal, scale, gain):
    inner = grad * gain
    mean = jnp.mean(inner, axis=-1, keepdims=True)
    along = jnp.mean(inner * normal, axis=-1, keepdims=True)
    return scale * (inner - mean - normal * along)


def spread(column):
    return jnp.broadcast_to(column, (column.shape[0], 128))


def rows_sum(values):
    return jnp.sum(values, axis=0, keepdims=True)


def project_kernel(layer, rows_ref, weight_ref, bias_ref, out_ref):
    product = jnp.dot(rows_ref[...], weight_ref[...], preferred_element_type=jnp.float32)
    bias = bias_ref[layer : layer + 1]
    out_ref[:, :D] = (product[:, :D] + bias[:, :D]).astype(jnp.bfloat16)
    out_ref[:, D : 2 * D] = product[:, D : 2 * D].astype(jnp.bfloat16)
    out_ref[:, 2 * D :] = (product[:, 2 * D :] + bias[:, D:]).astype(jnp.bfloat16)


def feed_kernel(
    layer,
    context_ref,
    rows_ref,
    out_weight_ref,
    ffin_weight_ref,
    ffout_weight_ref,
    out_bias_ref,
    attn_gain_ref,
    attn_shift_ref,
    ffin_bias_ref,
    ffout_bias_ref,
    ffn_gain_ref,
    ffn_shift_ref,
    hidden_ref,
    act_ref,
    slope_ref,
    attn_normal_ref,
    attn_scale_ref,
    ffn_normal_ref,
    ffn_scale_ref,
    result_ref,
    result_low_ref,
):
    here = slice(layer, layer + 1)
    product = jnp.dot(context_ref[...], out_weight_ref[...], preferred_element_type=jnp.float32)
    attn_sum = rows_ref[...].astype(jnp.float32) + product + out_bias_ref[here]
    normal, scale = norm_parts(attn_sum)
    attn_normal_ref[...] = normal
    attn_scale_ref[...] = spread(scale)
    hidden = normal * attn_gain_ref[here] + attn_shift_ref[here]
    hidden_low = hidden.astype(jnp.bfloat16)
    hidden_ref[...] = hidden_low
    total = hidden + ffout_bias_ref[here]
    width = ffin_weight_ref.shape[1]
    for at in range(0, width, FEED_TILE):
        part = slice(at, at + FEED_TILE)
        pre = (
            jnp.dot(hidden_low, ffin_weight_ref[:, part], preferred_element_type=jnp.float32)
            + ffin_bias_ref[here, part]
        )
        below, bell = erf_parts(pre)
        act = (pre * below).astype(jnp.bfloat16)
        act_ref[:, part] = act
        slope_ref[:, part] = (below + pre * bell * INV_ROOT).astype(jnp.bfloat16)
        total = total + jnp.dot(
            act, ffout_weight_ref[part, :], preferred_element_type=jnp.float32
        )
    normal, scale = norm_parts(total)
    ffn_normal_ref[...] = normal
    ffn_scale_ref[...] = spread(scale)
    result = normal * ffn_gain_ref[here] + ffn_shift_ref[here]
    result_ref[...] = result
    result_low_ref[...] = result.astype(jnp.bfloat16)


def add_projected(grad, proj_ref, weight_ref):
    for part in range(3):
        grad = grad + contract_last(proj_ref[part], weight_ref[:, part * D : (part + 1) * D])
    return grad


def feed_back_kernel(layer, with_proj, *refs):
    here = slice(layer, layer + 1)
    if with_proj:
        above_ref, proj_ref, qkv_weight_ref, *refs = refs
        grad = add_projected(above_ref[...], proj_ref, qkv_weight_ref)
    else:
        above_ref, *refs = refs
        grad = above_ref[...].astype(jnp.float32)
    (
        ffn_normal_ref,
        ffn_scale_ref,
        slope_ref,
        attn_normal_ref,
        attn_scale_ref,
        out_weight_ref,
        ffin_weight_ref,
        ffout_weight_ref,
        attn_gain_ref,
        ffn_gain_ref,
        down_ref,
        pre_ref,
        attn_ref,
        attn_low_ref,
        context_ref,
        sums_ref,
        ffin_sum_ref,
    ) = refs

    @pl.when(pl.program_id(0) == 0)
    def _():
        sums_ref[...] = jnp.zeros_like(sums_ref)
        ffin_sum_ref[...] = jnp.zeros_like(ffin_sum_ref)

    normal = ffn_normal_ref[...]
    sums_ref[0:1] += rows_sum(grad * normal)
    sums_ref[1:2] += rows_sum(grad)
    grad_sum = norm_back(grad, normal, ffn_scale_ref[:, 0:1], ffn_gain_ref[here])
    down = grad_sum.astype(jnp.bfloat16)
    down_ref[...] = down
    sums_ref[2:3] += rows_sum(down.astype(jnp.float32))
    total = grad_sum
    width = ffin_weight_ref.shape[1]
    for at in range(0, width, FEED_TILE):
        part = slice(at, at + FEED_TILE)
        grad_act = contract_last(down, ffout_weight_ref[part, :])
        pre = (grad_act * slope_ref[:, part].astype(jnp.float32)).astype(jnp.bfloat16)
        pre_ref[:, part] = pre
        ffin_sum_ref[:, part] += rows_sum(pre.astype(jnp.float32))
        total = total + contract_last(pre, ffin_weight_ref[:, part])
    normal = attn_normal_ref[...]
    sums_ref[3:4] += rows_sum(total * normal)
    sums_ref[4:5] += rows_sum(total)
    attn = norm_back(total, normal, attn_scale_ref[:, 0:1], attn_gain_ref[here])
    attn_ref[...] = attn
    low = attn.astype(jnp.bfloat16)
    attn_low_ref[...] = low
    sums_ref[5:6] += rows_sum(low.astype(jnp.float32))
    context_ref[...] = contract_last(low, out_weight_ref[...]).astype(jnp.bfloat16)


def input_grad_kernel(above_ref, proj_ref, weight_ref, out_ref):
    out_ref[...] = add_projected(above_ref[...], proj_ref, weight_ref)


def prep_pair(parent_ref, segment_ref, cluster_ref, slot_ref, bias_ref, row, tree, pair):
    segs = segment_ref[tree]
    length = segs.shape[1]

    def parent_of(values):
        found = jnp.zeros_like(values)
        for number in range(SEGMENTS):
            found = jnp.where(values == number, parent_ref[row, number], found)
        return found

    parents = parent_of(segs)
    grands = parent_of(parents)
    ids = jnp.concatenate([segs, parents, grands, jnp.zeros((5, length), jnp.int32)], axis=0)
    ids = jnp.concatenate([ids, jnp.zeros((8, length), jnp.int32)], axis=0)
    ids = ids.astype(jnp.float32).astype(jnp.bfloat16)
    count = length // CLUSTER
    order = lax.broadcasted_iota(jnp.int32, (count, length), 0)
    lanes = lax.broadcasted_iota(jnp.int32, (count, length), 1)
    for head in range(2):
        member = order == cluster_ref[tree, pair, head : head + 1, :]
        ranks = member.astype(jnp.int32)
        step = 1
        while step < length:
            ranks = ranks + jnp.where(lanes >= step, pltpu.roll(ranks, step, 1), 0)
            step *= 2
        slot = jnp.sum(
            jnp.where(member, ranks - 1 + CLUSTER * order, 0), axis=0, keepdims=True
        )
        slot_ref[tree, pair, head : head + 1, :] = slot
        table = one_hot_rows(slot)
        rows = contract_last(ids, table)
        columns = jnp.concatenate([rows] * (128 // rows.shape[0]), axis=0).T
        for at in range(0, length, CLUSTER):
            here = rows[0:1, at : at + CLUSTER]
            block = columns[at : at + CLUSTER]
            allowed = (
                (here == block[:, 0:1]) | (here == block[:, 1:2]) | (here == block[:, 2:3])
            )
            bias_ref[tree, 2 * pair + head, at : at + CLUSTER, :] = jnp.where(allowed, 0.0, -1e30).astype(
                jnp.bfloat16
            )


def prep_kernel(*refs):
    prep_pair(*refs, pl.program_id(0), 0, 0)


def row_spec(width, rows=ROW_TILE):
    return pl.BlockSpec((rows, width), lambda i: (i, 0))


def whole_spec(shape):
    return pl.BlockSpec(
        shape, lambda i: (0,) * len(shape), pipeline_mode=pl.Buffered(1)
    )


def part_spec(rows=ROW_TILE):
    return pl.BlockSpec((3, rows, D), lambda i: (0, i, 0))


def cost(flops, *arrays):
    moved = sum(array.size * array.dtype.itemsize for array in arrays)
    return pl.CostEstimate(flops=int(flops), bytes_accessed=moved, transcendentals=0)


def shape_of(rows, width, kind=jnp.bfloat16):
    return jax.ShapeDtypeStruct((rows, width), kind)


def project(layer, rows, weight, bias):
    count, width = rows.shape[0], weight.shape[1]
    return pl.pallas_call(
        functools.partial(project_kernel, layer),
        grid=(count // ROW_TILE,),
        in_specs=[row_spec(D), whole_spec(weight.shape), whole_spec(bias.shape)],
        out_specs=row_spec(width),
        out_shape=shape_of(count, width),
        compiler_params=kernel_params(),
        cost_estimate=cost(2.4 * count * D * width, rows, weight),
    )(rows, weight, bias)


def feed(layer, context, rows, weights, vectors):
    count = context.shape[0]
    width = weights[1].shape[1]
    f32 = jnp.float32
    return pl.pallas_call(
        functools.partial(feed_kernel, layer),
        grid=(count // ROW_TILE,),
        in_specs=[row_spec(D), row_spec(D)]
        + [whole_spec(weight.shape) for weight in weights]
        + [whole_spec(vector.shape) for vector in vectors],
        out_specs=[
            row_spec(D),
            row_spec(width),
            row_spec(width),
            row_spec(D),
            row_spec(128),
            row_spec(D),
            row_spec(128),
            row_spec(D),
            row_spec(D),
        ],
        out_shape=[
            shape_of(count, D),
            shape_of(count, width),
            shape_of(count, width),
            shape_of(count, D, f32),
            shape_of(count, 128, f32),
            shape_of(count, D, f32),
            shape_of(count, 128, f32),
            shape_of(count, D, f32),
            shape_of(count, D),
        ],
        compiler_params=kernel_params(),
        cost_estimate=cost(5 * count * D * (2 * width + D), context, *weights),
    )(context, rows, *weights, *vectors)


def feed_back(layer, above, proj, qkv_weight, saved, weights, gains):
    count = above.shape[0]
    width = weights[1].shape[1]
    f32 = jnp.float32
    lead, lead_specs = [above], [row_spec(D)]
    if proj is not None:
        lead += [proj, qkv_weight]
        lead_specs += [part_spec(), whole_spec(qkv_weight.shape)]
    return pl.pallas_call(
        functools.partial(feed_back_kernel, layer, proj is not None),
        grid=(count // ROW_TILE,),
        in_specs=lead_specs
        + [row_spec(D), row_spec(128), row_spec(width), row_spec(D), row_spec(128)]
        + [whole_spec(weight.shape) for weight in weights]
        + [whole_spec(gain.shape) for gain in gains],
        out_specs=[
            row_spec(D),
            row_spec(width),
            row_spec(D),
            row_spec(D),
            row_spec(D),
            pl.BlockSpec((8, D), lambda i: (0, 0)),
            pl.BlockSpec((1, width), lambda i: (0, 0)),
        ],
        out_shape=[
            shape_of(count, D),
            shape_of(count, width),
            shape_of(count, D, f32),
            shape_of(count, D),
            shape_of(count, D),
            shape_of(8, D, f32),
            shape_of(1, width, f32),
        ],
        compiler_params=kernel_params(),
        cost_estimate=cost(5 * count * D * (2 * width + D), above, *weights),
    )(*lead, *saved, *weights, *gains)


def input_grad(above, proj, qkv_weight):
    count = above.shape[0]
    return pl.pallas_call(
        input_grad_kernel,
        grid=(count // ROW_TILE,),
        in_specs=[
            row_spec(D),
            part_spec(),
            whole_spec(qkv_weight.shape),
        ],
        out_specs=row_spec(D),
        out_shape=shape_of(count, D, jnp.float32),
        compiler_params=kernel_params(),
        cost_estimate=cost(2.4 * count * D * 3 * D, above, qkv_weight),
    )(above, proj, qkv_weight)


def prepare(segment, parent, clusters):
    trees = parent.shape[0]
    segment = segment.reshape(trees, 1, TREE_LEN)
    clusters = clusters.reshape(PAIRS, 2, trees, TREE_LEN).transpose(2, 0, 1, 3)
    return pl.pallas_call(
        prep_kernel,
        grid=(trees, PAIRS),
        in_specs=[
            pl.BlockSpec(memory_space=pltpu.SMEM),
            pl.BlockSpec((1, 1, TREE_LEN), lambda tree, pair: (tree, 0, 0)),
            slot_spec(),
        ],
        out_specs=[slot_spec(), head_spec()],
        out_shape=[
            jax.ShapeDtypeStruct((trees, PAIRS, 2, TREE_LEN), jnp.int32),
            jax.ShapeDtypeStruct((trees, HEADS, TREE_LEN, LANES), jnp.bfloat16),
        ],
        compiler_params=kernel_params(),
        cost_estimate=pl.CostEstimate(
            flops=trees * 20_000_000_000, bytes_accessed=trees * 4_000_000, transcendentals=0
        ),
    )(parent, segment, clusters)


def weight_grad_kernel(split_y, at_ref, left_ref, right_ref, *refs):
    product = contract_first(
        left_ref[...].reshape(left_ref.shape[-2:]), right_ref[...].reshape(right_ref.shape[-2:])
    )
    if split_y is None:
        (out_ref,) = refs
        out_ref[...] = product.astype(jnp.bfloat16).reshape(out_ref.shape)
        return
    near_ref, (send_ref, keep_ref, sum_ref) = refs[0], refs[-3:]
    total = product + near_ref[...].astype(jnp.float32).reshape(product.shape)
    sum_ref[...] = total.astype(jnp.bfloat16).reshape(sum_ref.shape)
    if split_y:
        send_ref[0] = sum_ref[:, :, 1 - at_ref[2]]
        keep_ref[0] = sum_ref[:, :, at_ref[2]]
    else:
        send_ref[...] = sum_ref[:, 1 - at_ref[1]]
        keep_ref[...] = sum_ref[:, at_ref[1]]


class Grad:
    def __init__(self, number, left, right, tiles, half):
        self.number = number
        self.left, self.right = left, right
        self.tiles, self.half = tiles, half
        self.depth = left.shape[1]
        self.parts = 1 if self.depth > D else tiles
        self.rows = self.depth // (CHIPS_Z * CHIPS_X)

    def product(self, at, other, split_y=None, near=None, start=0, total=0, before=()):
        flip = 1 if other else 0
        left, right = self.left, self.right
        count = left.shape[0]
        tall = self.depth > D
        core = lambda at: lax.rem(at[3] + flip, CORES)
        in_specs = [
            pl.BlockSpec((count, D), (lambda i, at: (0, i)) if tall else (lambda i, at: (0, 0)))
        ]
        if right.ndim == 3:
            in_specs.append(pl.BlockSpec((1, count, self.half), lambda i, at: (i, 0, core(at))))
        elif tall:
            in_specs.append(pl.BlockSpec((count, self.half), lambda i, at: (0, core(at))))
        else:
            in_specs.append(
                pl.BlockSpec((count, self.half), lambda i, at: (0, core(at) * self.tiles + i))
            )
        zs = D // (self.rows * CHIPS_X)
        place = (lambda i: (0, i)) if tall else (lambda i: (i, 0))
        whole = (self.parts, CHIPS_Z, CHIPS_X, self.rows, self.half)
        block = (1, zs, CHIPS_X, self.rows, self.half)
        full = pl.BlockSpec(block, lambda i, at: (*place(i), 0, 0, 0))
        args, scratch = [left, right], []
        if split_y is None:
            out_specs, shapes = full, jax.ShapeDtypeStruct(whole, jnp.bfloat16)
        else:
            in_specs.append(full)
            args.append(near)
            in_specs += [pl.BlockSpec(memory_space=pl.ANY)] * len(before)
            args += before
            if split_y:
                short = self.rows // CHIPS_Y
                kept = (CHIPS_X, short, self.half)
                scratch = [pltpu.VMEM((zs, CHIPS_X, CHIPS_Y, short, self.half), jnp.bfloat16)]
                spec = pl.BlockSpec((1, zs, *kept), lambda i, at: (*place(i), 0, 0, 0))
                shape = (self.parts, CHIPS_Z, *kept)
            else:
                scratch = [pltpu.VMEM((zs, CHIPS_X, self.rows, self.half), jnp.bfloat16)]
                first = start // self.rows
                index = (lambda i, at: (i, first, 0)) if tall else (lambda i, at: (0, first + i, 0))
                spec = pl.BlockSpec((zs, self.rows, self.half), index)
                shape = (CHIPS_Z, total, self.half)
            out_specs, shapes = [spec] * 2, [jax.ShapeDtypeStruct(shape, jnp.bfloat16)] * 2
        return pl.pallas_call(
            functools.partial(weight_grad_kernel, split_y),
            grid_spec=pltpu.PrefetchScalarGridSpec(
                num_scalar_prefetch=1,
                grid=(self.tiles,),
                in_specs=in_specs,
                out_specs=out_specs,
                scratch_shapes=scratch,
            ),
            out_shape=shapes,
            input_output_aliases={4 + place: place for place in range(len(before))},
            compiler_params=kernel_params(),
            cost_estimate=cost(4 * count * D * self.tiles * self.half, left, right),
        )(at, *args)


class Place:
    def __init__(self):
        rep = lax.axis_index("rep")
        shard = lax.axis_index("shard")
        self.y, self.core = rep // CORES, rep % CORES
        self.z, self.x = shard // CHIPS_X, shard % CHIPS_X
        self.at = jnp.stack([self.z, self.x, self.y, self.core]).astype(jnp.int32)


def hop(value, dz=0, dx=0, dy=0, dc=0):
    pairs = []
    for y in range(CHIPS_Y):
        for c in range(CORES):
            for z in range(CHIPS_Z):
                for x in range(CHIPS_X):
                    source = ((y * CORES + c) * CHIPS_Z + z) * CHIPS_X + x
                    y2, c2 = (y + dy) % CHIPS_Y, (c + dc) % CORES
                    z2, x2 = (z + dz) % CHIPS_Z, (x + dx) % CHIPS_X
                    pairs.append((source, ((y2 * CORES + c2) * CHIPS_Z + z2) * CHIPS_X + x2))
    return lax.ppermute(value, AXES, pairs)


def cut_sums(place, groups):
    at = place.at
    arrived = []
    for grads, _ in groups:
        arrived.append([hop(grad.product(at, True), dc=1) for grad in grads])
    found = []
    for (grads, y_first), near in zip(groups, arrived):
        total = sum(grad.parts * grad.rows for grad in grads)
        start, pair = 0, ()
        for grad, item in zip(grads, near):
            if y_first:
                pair = grad.product(at, False, True, item)
            else:
                pair = grad.product(at, False, False, item, start, total, tuple(pair))
            start += grad.parts * grad.rows
        found.append(tuple(pair))
    return found


def prep_steps(ins, outs):
    trees, pairs = ins[2].shape[:2]
    for tree in range(trees):
        for pair in range(pairs):
            prep_pair(*ins, *outs[:2], tree, tree, pair)
            yield


def gather_kernel(plan, arrays, ending, work, work_ins, work_outs, *refs):
    count = len(plan)
    own_ins, ins, refs = refs[:work_ins], refs[work_ins : work_ins + arrays], refs[work_ins + arrays :]
    own_outs, outs = refs[:work_outs], refs[work_outs : work_outs + arrays]
    sems, local_sem = refs[work_outs + arrays : -1], refs[-1]
    todo = work(own_ins, own_outs)
    rep, shard = lax.axis_index("rep"), lax.axis_index("shard")
    y, core = lax.div(rep, CORES), lax.rem(rep, CORES)
    z, x = lax.div(shard, CHIPS_X), lax.rem(shard, CHIPS_X)

    def device(dz=0, dx=0, dy=0, dc=0):
        to_y, to_core = lax.rem(y + dy, CHIPS_Y), lax.rem(core + dc, CORES)
        to_z, to_x = lax.rem(z + dz, CHIPS_Z), lax.rem(x + dx, CHIPS_X)
        return (to_y * CORES + to_core, to_z * CHIPS_X + to_x)

    mates = [dict(dx=1), dict(dy=1), dict(dc=1)] + [dict(dz=k) for k in range(1, CHIPS_Z)]
    barrier = pltpu.get_barrier_semaphore()
    for mate in mates:
        pl.semaphore_signal(
            barrier, inc=1, device_id=device(**mate), device_id_type=pl.DeviceIdType.MESH
        )
    sent = []

    def send(source, target, m, number, **step):
        copy = pltpu.make_async_remote_copy(
            src_ref=source,
            dst_ref=target,
            send_sem=sems[m].at[0, number],
            recv_sem=sems[m].at[1, number],
            device_id=device(**step),
            device_id_type=pl.DeviceIdType.MESH,
        )
        copy.start()
        sent.append(copy)
        return copy

    def part(m, at_z, at_x, at_y, at_core):
        which, _, split_y, by_core, row, rows, column, columns = plan[m]
        out = outs[which]
        at_columns = slice(None)
        if by_core:
            first = at_core * (out.shape[-1] // CORES) + column
            at_columns = pl.ds(pl.multiple_of(first, 128), columns)
        at_z = slice(None) if at_z is None else at_z
        at_x = slice(None) if at_x is None else at_x
        return out.at[at_z, at_x, at_y if split_y else 0, pl.ds(row, rows), at_columns]

    locals_ = []
    for m, (which, layer, split_y, by_core, row, rows, column, columns) in enumerate(plan):
        source = ins[which] if layer is None else ins[which].at[layer]
        if by_core:
            first = row
            if split_y:
                first = pl.multiple_of(y * outs[which].shape[3] + row, 16)
            start = core * (outs[which].shape[-1] // CORES) + column
            source = source.at[pl.ds(first, rows), pl.ds(pl.multiple_of(start, 128), columns)]
        copy = pltpu.make_async_copy(source, part(m, z, x, y, core), local_sem.at[m])
        copy.start()
        locals_.append(copy)
    pl.semaphore_wait(barrier, len(mates))
    along_z, along_x, over_y, last = {}, {}, {}, []

    def spread(m, at_z, at_x):
        piece = part(m, at_z, at_x, y, core)
        if at_x is x:
            along_x[m].append(send(piece, piece, m, 3 + len(along_x[m]), dx=1))
        if plan[m][2]:
            over_y[m].append(send(piece, piece, m, 7 + len(over_y[m]), dy=1))

    def behind(k):
        return lax.rem(z + CHIPS_Z - k, CHIPS_Z)

    def after_x(m):
        for k in range(CHIPS_Z):
            if k == 1:
                next(todo, None)
            along_x[m][k].wait_recv()
            spread(m, behind(k), 1 - x)
        if plan[m][3]:
            piece = part(m, None, None, y, core)
            last.append(send(piece, piece, m, 15, dc=1))

    def after_y(m):
        if over_y[m]:
            for copy in over_y[m]:
                copy.wait_recv()
            piece = part(m, None, None, 1 - y, core)
            last.append(send(piece, piece, m, 16, dc=1))

    order = range(count)

    def set_out(m):
        locals_[m].wait()
        mine = part(m, z, x, y, core)
        along_z[m] = [send(mine, mine, m, k - 1, dz=k) for k in range(1, CHIPS_Z)]
        along_x[m], over_y[m] = [], []
        spread(m, z, x)

    for m in order[:2]:
        set_out(m)
    for place, m in enumerate(order):
        for k in range(1, CHIPS_Z):
            if k != 2:
                next(todo, None)
            along_z[m][k - 1].wait_recv()
            spread(m, behind(k), x)
        if place + 2 < count:
            set_out(order[place + 2])
        if place:
            after_x(order[place - 1])
    after_x(order[-1])
    ending(own_outs, outs)
    for m in order:
        after_y(m)
        next(todo, None)
    for _ in todo:
        pass
    for copy in last:
        copy.wait_recv()
    for copy in sent:
        copy.wait_send()


def no_ending(own_outs, outs):
    pass


def spread_vectors(sizes, own_outs, outs):
    found = outs[0]
    for shard in range(CHIPS_Z * CHIPS_X):
        rows = found[shard // CHIPS_X, shard % CHIPS_X, 0].astype(jnp.float32)
        at = 0
        for out_ref, size in zip(own_outs[-len(sizes) :], sizes):
            out_ref[:, shard * size : (shard + 1) * size] = rows[:LAYERS, at : at + size]
            at += size


def gather(weights, wanted, work, work_args, work_shapes, number, ending=no_ending):
    low = jnp.bfloat16
    args, plan, shapes = [], [], []
    for which, layer, split_y, tall, wide in wanted:
        rows, columns = weights[which].shape[-2:]
        split = CHIPS_Y if split_y else 1
        rows //= split
        half = columns if layer is None else columns // CORES
        for piece in range(tall * wide):
            row, column = divmod(piece, wide)
            plan.append(
                (
                    len(args),
                    layer,
                    split_y,
                    layer is not None,
                    row * (rows // tall),
                    rows // tall,
                    column * (half // wide),
                    half // wide,
                )
            )
        args.append(weights[which])
        shapes.append((CHIPS_Z, CHIPS_X, split, rows, columns))
    whole = pl.BlockSpec(memory_space=pltpu.VMEM)
    small = pl.BlockSpec(memory_space=pltpu.SMEM)
    found = pl.pallas_call(
        functools.partial(
            gather_kernel, plan, len(args), ending, work, len(work_args), len(work_shapes)
        ),
        in_specs=[small if arg.shape[-1] == SEGMENTS else whole for arg in work_args]
        + [pl.BlockSpec(memory_space=pl.ANY)] * len(args),
        out_specs=[whole] * (len(work_shapes) + len(args)),
        out_shape=work_shapes + [jax.ShapeDtypeStruct(shape, low) for shape in shapes],
        scratch_shapes=[pltpu.SemaphoreType.DMA((2, 17))] * len(plan)
        + [pltpu.SemaphoreType.DMA((len(plan),))],
        compiler_params=pltpu.CompilerParams(
            vmem_limit_bytes=KERNEL_VMEM, collective_id=number, has_side_effects=True
        ),
        cost_estimate=pl.CostEstimate(flops=0, bytes_accessed=200_000_000, transcendentals=0),
    )(*work_args, *args)
    results, arrays = list(found[: len(work_shapes)]), found[len(work_shapes) :]
    for item, array in zip(wanted, arrays):
        results.append(array if item[1] is None else array.reshape(-1, array.shape[-1]))
    return results


def pack_sums(out_ref, ins):
    rows = 8 * LAYERS
    width = out_ref.shape[1]
    for layer in range(LAYERS):
        sums_ref, ffin_ref, _ = ins[3 * layer : 3 * layer + 3]
        out_ref[8 * layer : 8 * layer + 8] = sums_ref[...]
        for at in range(0, ffin_ref.shape[1], width):
            out_ref[rows : rows + 1] = ffin_ref[:, at : at + width]
            rows += 1
    for layer in range(LAYERS):
        ref = ins[3 * layer + 2]
        for pair in range(ref.shape[1]):
            value = ref[0, pair]
            for tree in range(1, ref.shape[0]):
                value = value + ref[tree, pair]
            out_ref[rows : rows + 8, pair * LANES : (pair + 1) * LANES] = value
        rows += 8


def sum_rows(ffin_width):
    return LAYERS * (16 + ffin_width // D)


def reduce_kernel(flats, count, vectors, work, work_ins, work_outs, *refs):
    take = iter(refs)

    def some(number):
        return [next(take) for _ in range(number)]

    own_ins = some(work_ins)
    a_ins = [some(2) for _ in range(flats)]
    b_ins = [some(2) for _ in range(count)]
    vec_ins = some(vectors)
    own_outs = some(work_outs)
    a_outs = [some(2) for _ in range(flats)]
    b_outs = some(count)
    vec_outs = some(1 if vectors else 0)
    a_scratch = [some(6) for _ in range(flats)]
    b_scratch = [some(6) for _ in range(count)]
    v_send, v_land = some(2) if vectors else (None, None)
    a_sems, b_sems = some(flats), some(count)
    v_sems = next(take) if vectors else None
    todo = work(own_ins, own_outs)
    rep, shard = lax.axis_index("rep"), lax.axis_index("shard")
    y, core = lax.div(rep, CORES), lax.rem(rep, CORES)
    z, x = lax.div(shard, CHIPS_X), lax.rem(shard, CHIPS_X)

    def device(dz=0, dx=0, dy=0, dc=0):
        to_y, to_core = lax.rem(y + dy, CHIPS_Y), lax.rem(core + dc, CORES)
        to_z, to_x = lax.rem(z + dz, CHIPS_Z), lax.rem(x + dx, CHIPS_X)
        return (to_y * CORES + to_core, to_z * CHIPS_X + to_x)

    flip_z = 1 + 2 * lax.rem(z, 2)
    mates = [dict(dx=1), dict(dy=1), dict(dc=1), dict(dy=1, dc=1)]
    mates += [dict(dz=k) for k in range(1, CHIPS_Z)]
    barrier = pltpu.get_barrier_semaphore()
    for mate in mates:
        pl.semaphore_signal(
            barrier, inc=1, device_id=device(**mate), device_id_type=pl.DeviceIdType.MESH
        )
    pl.semaphore_wait(barrier, len(mates))
    sent = []

    def send(source, target, sems, number, **step):
        copy = pltpu.make_async_remote_copy(
            src_ref=source,
            dst_ref=target,
            send_sem=sems.at[0, number],
            recv_sem=sems.at[1, number],
            device_id=device(**step),
            device_id_type=pl.DeviceIdType.MESH,
        )
        copy.start()
        sent.append(copy)
        return copy

    def wide(value):
        return value.astype(jnp.float32)

    order = (2, 1, 3, 0)
    ahead = [lax.rem(z + k, CHIPS_Z) for k in order]
    v_copies = []
    if vectors:
        pack_sums(v_send.at[0], vec_ins)
        v_copies.append(send(v_send.at[0], v_land.at[0], v_sems, 0, dc=1))
    a_x, b_y = [[] for _ in range(flats)], [[] for _ in range(count)]

    def set_out(j):
        to = ahead[j]
        for i, (first, _) in enumerate(a_ins):
            a_x[i].append(send(first.at[to], a_scratch[i][0].at[j], a_sems[i], j, dx=1))
        for i, (first, _) in enumerate(b_ins):
            b_y[i].append(send(first.at[:, to], b_scratch[i][0].at[j], b_sems[i], j, dy=1))

    set_out(0)
    set_out(1)
    steps = (dict(dc=1), dict(dy=1), dict(dx=1), dict(dz=2), dict(dz=flip_z))

    def add_vectors(s):
        if not vectors:
            return
        v_copies[s].wait_recv()
        total = v_send[s] + v_land[s]
        if s + 1 == len(steps):
            vec_outs[0][...] = total
        else:
            v_send[s + 1] = total
            v_copies.append(
                send(v_send.at[s + 1], v_land.at[s + 1], v_sems, s + 1, **steps[s + 1])
            )

    a_z, b_x, b_z = ([[] for _ in range(number)] for number in (flats, count, count))

    def b_along_z(i, j):
        k, keep = order[j], b_ins[i][1]
        over, _, x_land, z_send, z_land, _ = b_scratch[i]
        b_x[i][j].wait_recv()
        if k:
            total = wide(keep[:, ahead[j], x]) + wide(over[j, :, x]) + wide(x_land[j])
            z_send[k - 1] = total.astype(jnp.bfloat16)
            b_z[i].append(send(z_send.at[k - 1], z_land.at[k - 1], b_sems[i], 7 + k, dz=k))

    def b_along_x(i, j):
        keep, (over, x_send, x_land, *_) = b_ins[i][1], b_scratch[i]
        b_y[i][j].wait_recv()
        total = wide(keep[:, ahead[j], 1 - x]) + wide(over[j, :, 1 - x])
        x_send[j] = total.astype(jnp.bfloat16)
        b_x[i].append(send(x_send.at[j], x_land.at[j], b_sems[i], 4 + j, dx=1))

    for j, k in enumerate(order):
        next(todo, None)
        for i, (_, keep) in enumerate(a_ins):
            across, z_send, z_land, *_ = a_scratch[i]
            a_x[i][j].wait_recv()
            if k:
                total = wide(keep[ahead[j]]) + wide(across[j])
                z_send[k - 1] = total.astype(jnp.bfloat16)
                a_z[i].append(
                    send(z_send.at[k - 1], z_land.at[k - 1], a_sems[i], 3 + k, dz=k)
                )
        next(todo, None)
        for i in range(count):
            b_along_x(i, j)
        if j + 2 < CHIPS_Z:
            set_out(j + 2)
        if j:
            for i in range(count):
                b_along_z(i, j - 1)
        next(todo, None)
        add_vectors(j)
    for i in range(count):
        b_along_z(i, CHIPS_Z - 1)
    add_vectors(4)
    for _ in todo:
        pass
    over_y, ends = [], []
    for i, (_, keep) in enumerate(a_ins):
        across, _, z_land, y_send, y_land, _ = a_scratch[i]
        for copy in a_z[i]:
            copy.wait_recv()
        total = wide(keep[z]) + wide(across[CHIPS_Z - 1])
        for k in range(CHIPS_Z - 1):
            total = total + wide(z_land[k])
        y_send[...] = total.astype(jnp.bfloat16)
        over_y.append(send(y_send, y_land, a_sems[i], 7, dy=1))
    for i, (_, keep) in enumerate(b_ins):
        over, _, x_land, _, z_land, end_land = b_scratch[i]
        for copy in b_z[i]:
            copy.wait_recv()
        total = wide(keep[:, z, x]) + wide(over[3, :, x]) + wide(x_land[3])
        for k in range(CHIPS_Z - 1):
            total = total + wide(z_land[k])
        b_outs[i][0] = total.astype(jnp.bfloat16)
        for number, step in enumerate((dict(dy=1), dict(dc=1), dict(dy=1, dc=1))):
            ends.append(
                send(b_outs[i].at[0], end_land.at[number], b_sems[i], 11 + number, **step)
            )
    for i, (own, _) in enumerate(a_outs):
        *_, y_send, y_land, c_land = a_scratch[i]
        over_y[i].wait_recv()
        own[...] = (wide(y_send[...]) + wide(y_land[...])).astype(jnp.bfloat16)
        ends.append(send(own, c_land, a_sems[i], 8, dc=1))
    for copy in ends:
        copy.wait_recv()
    for i in range(count):
        b_outs[i][1:4] = b_scratch[i][5][...]
    for i, (_, other) in enumerate(a_outs):
        other[...] = a_scratch[i][5][...]
    for copy in sent:
        copy.wait_send()


def no_work(ins, outs):
    return iter(())


def reduce_sums(flats, pairs, sums, number, work=no_work, work_args=(), work_shapes=()):
    low = jnp.bfloat16
    whole = pl.BlockSpec(memory_space=pltpu.VMEM)
    far = pl.BlockSpec(memory_space=pl.ANY)
    args, specs = list(work_args), [whole] * len(work_args)
    outs, scratch = [], []
    for first, keep in flats:
        piece = keep.shape[1:]
        args += [first, keep]
        specs += [far, whole]
        outs += [piece, piece]
        scratch += [(CHIPS_Z, *piece), (CHIPS_Z - 1, *piece), (CHIPS_Z - 1, *piece)]
        scratch += [piece] * 3
    for first, keep in pairs:
        parts, _, _, rows, half = keep.shape
        block = (parts, rows, half)
        args += [first, keep]
        specs += [far, whole]
        outs.append((CORES * CHIPS_Y, *block))
        scratch += [
            (CHIPS_Z, parts, CHIPS_X, rows, half),
            (CHIPS_Z, *block),
            (CHIPS_Z, *block),
            (CHIPS_Z - 1, *block),
            (CHIPS_Z - 1, *block),
            (CORES * CHIPS_Y - 1, *block),
        ]
    args += sums
    specs += [whole] * len(sums)
    shapes = list(work_shapes) + [jax.ShapeDtypeStruct(shape, low) for shape in outs]
    scratch = [pltpu.VMEM(shape, low) for shape in scratch]
    if sums:
        vec = (sum_rows(sums[1].shape[1]), D)
        shapes.append(jax.ShapeDtypeStruct(vec, jnp.float32))
        scratch += [pltpu.VMEM((5, *vec), jnp.float32)] * 2
    scratch += [pltpu.SemaphoreType.DMA((2, 9))] * len(flats)
    scratch += [pltpu.SemaphoreType.DMA((2, 14))] * len(pairs)
    if sums:
        scratch.append(pltpu.SemaphoreType.DMA((2, 5)))
    return pl.pallas_call(
        functools.partial(
            reduce_kernel, len(flats), len(pairs), len(sums), work, len(work_args), len(work_shapes)
        ),
        in_specs=specs,
        out_specs=[whole] * len(shapes),
        out_shape=shapes,
        scratch_shapes=scratch,
        compiler_params=pltpu.CompilerParams(
            vmem_limit_bytes=KERNEL_VMEM, collective_id=number, has_side_effects=True
        ),
        cost_estimate=pl.CostEstimate(flops=0, bytes_accessed=200_000_000, transcendentals=0),
    )(*args)


def join_kernel(plan, count, at_ref, *refs):
    for ref, out, layer, outer, parts, dc, dy, start, rows in plan:
        ref, out_ref = refs[ref], refs[count + out]
        half = ref.shape[1]
        core = lax.rem(at_ref[3] + dc, CORES)
        row = 0
        if dy is not None:
            row = pl.multiple_of(lax.rem(at_ref[2] + dy, CHIPS_Y) * rows, 16)
        for part in range(parts):
            column = part * CORES + core if outer else core * parts + part
            column = pl.multiple_of(column * half, 128)
            value = ref[start + part * rows : start + (part + 1) * rows]
            out_ref[layer, pl.ds(row, rows), pl.ds(column, half)] = value.astype(jnp.float32)


def join(at, done, shapes):
    arrays, plan = [], []
    for out, (number, (tall, wide)) in enumerate(shapes.items()):
        for layer in range(LAYERS):
            pieces, start, rows = done[layer][number]
            for place, piece in enumerate(pieces):
                known = [other is piece for other in arrays]
                if not any(known):
                    arrays.append(piece)
                    known.append(True)
                parts = wide // (CORES * piece.shape[1])
                dy, dc = (place % CHIPS_Y, place // CHIPS_Y) if len(pieces) > CORES else (None, place)
                plan.append((known.index(True), out, layer, number == 0, parts, dc, dy, start, rows))
    zeros = lambda i, at: (0, 0)
    outs = [(LAYERS, *shape) for shape in shapes.values()]
    return pl.pallas_call(
        functools.partial(join_kernel, plan, len(arrays)),
        grid_spec=pltpu.PrefetchScalarGridSpec(
            num_scalar_prefetch=1,
            grid=(1,),
            in_specs=[pl.BlockSpec(array.shape, zeros) for array in arrays],
            out_specs=[pl.BlockSpec(out, lambda i, at: (0, 0, 0)) for out in outs],
        ),
        out_shape=[jax.ShapeDtypeStruct(out, jnp.float32) for out in outs],
        compiler_params=kernel_params(),
        cost_estimate=pl.CostEstimate(flops=0, bytes_accessed=4_000_000, transcendentals=0),
    )(at, *arrays)


def local(
    fast,
    inputs,
    cotangent,
    segment,
    parent,
    clusters,
    *weights,
):
    pieces = {}
    if fast:
        place = Place()
        at = place.at
        shards = dict(enumerate(weights))
        shards["vectors"] = jnp.pad(
            jnp.concatenate([weights[member] for member in VECTORS], axis=1),
            ((0, 16 - LAYERS), (0, 0)),
        )
        trees = parent.shape[0]
        sizes = [weights[number].shape[1] for number in VECTORS]
        slots, bias, *vectors, _, qkv = gather(
            shards,
            (("vectors", None, False, 1, 1), (0, 0, True, 1, 3)),
            prep_steps,
            (
                parent,
                segment.reshape(trees, 1, TREE_LEN),
                clusters.reshape(PAIRS, 2, trees, TREE_LEN).transpose(2, 0, 1, 3),
            ),
            [
                jax.ShapeDtypeStruct((trees, PAIRS, 2, TREE_LEN), jnp.int32),
                jax.ShapeDtypeStruct((trees, HEADS, TREE_LEN, LANES), jnp.bfloat16),
                *[
                    jax.ShapeDtypeStruct((LAYERS, CHIPS_Z * CHIPS_X * size), jnp.float32)
                    for size in sizes
                ],
            ],
            1,
            functools.partial(spread_vectors, sizes),
        )
        whole = {(0, 0): qkv}

        def attend_layer(layer, projected):
            last = layer + 1 == LAYERS
            if last:
                wanted = [(8, layer, False, 4, 1), (6, layer, True, 1, 2), (2, layer, True, 1, 1)]
            else:
                wanted = [(6, layer, True, 1, 2), (8, layer, True, 2, 1)]
                wanted += [(0, layer + 1, False, 1, 3), (2, layer, False, 1, 1)]
            results = gather(
                shards, wanted, attend_steps, (projected, slots, bias), attend_shapes(trees), 2 + layer
            )
            for (number, at_layer, *_), array in zip(wanted, results[4:]):
                whole[at_layer, number] = array
            return results[:4]

        def get(layer, number):
            return whole[layer, number]

        def attend_back_layer(layer, grad_context, heads, groups, waiting):
            flat, pair = cut_sums(place, groups)
            proj, head_sums, *ends = reduce_sums(
                [flat],
                [pair, *waiting],
                [],
                2 + LAYERS + layer,
                attend_back_steps,
                (slots, grad_context, *heads),
                attend_back_shapes(trees),
            )
            pieces[layer, "flat"] = ends[:2]
            pieces[layer, 6] = ends[2]
            if waiting:
                pieces[layer + 1, 0] = ends[3]
            return proj, head_sums

    else:
        slots, bias = prepare(segment, parent, clusters)
        vectors = [
            lax.all_gather(weights[number], "shard", axis=1, tiled=True).astype(jnp.float32)
            for number in VECTORS
        ]

        def attend_layer(layer, projected):
            return attend(projected, slots, bias)

        def get(layer, number):
            return lax.all_gather(weights[number][layer], "shard", axis=0, tiled=True)

        def own_sum(left, right):
            if right.ndim == 3:
                right = right.transpose(1, 0, 2).reshape(right.shape[1], -1)
            total = contract_first(left, right)
            total = lax.psum_scatter(total, "shard", scatter_dimension=0, tiled=True)
            return lax.psum(total.astype(jnp.bfloat16), "rep").astype(jnp.float32)

        def attend_back_layer(layer, grad_context, heads, groups, waiting):
            for grads, _ in groups:
                for grad in grads:
                    pieces[layer, grad.number] = own_sum(grad.left, grad.right)
            return attend_back(grad_context, slots, heads)

    vector = dict(zip(VECTORS, vectors))
    hidden, hidden_low = inputs, inputs
    saved = []
    for layer in range(LAYERS):
        pull = functools.partial(get, layer)
        projected = project(layer, hidden_low, pull(0), vector[1])
        context, *heads = attend_layer(layer, projected)
        entered = hidden_low
        middle, act, slope, *norms, hidden, hidden_low = feed(
            layer,
            context,
            hidden,
            [pull(2), pull(6), pull(8)],
            [vector[number] for number in (3, 4, 5, 7, 9, 10, 11)],
        )
        saved.append((entered, heads, context, middle, act, slope, norms))
    result = hidden_low
    above, proj = cotangent, None
    sums, waiting = [None] * LAYERS, []
    for layer in reversed(range(LAYERS)):
        entered, heads, context, middle, act, slope, norms = saved[layer]
        pull = functools.partial(get, layer)
        down, grad_pre, grad_attn, attn_low, grad_context, row_sums, ffin_sum = feed_back(
            layer,
            above,
            proj,
            None if proj is None else get(layer + 1, 0),
            [norms[2], norms[3], slope, norms[0], norms[1]],
            [pull(2), pull(6), pull(8)],
            [vector[4], vector[10]],
        )
        wide = grad_pre.shape[1] // CORES
        groups = (
            (
                (
                    Grad(8, act, down, act.shape[1] // D, UNIT),
                    Grad(2, context, attn_low, 1, UNIT),
                ),
                False,
            ),
            ((Grad(6, middle, grad_pre, wide // D, D),), True),
        )
        proj, head_sums = attend_back_layer(layer, grad_context, heads, groups, waiting)
        sums[layer] = [row_sums, ffin_sum, head_sums]
        above = grad_attn
        last = Grad(0, entered, proj, 3, UNIT)
        if not fast:
            pieces[layer, 0] = own_sum(last.left, last.right)
        elif layer:
            waiting = cut_sums(place, [((last,), True)])
    grad_input = input_grad(above, proj, get(0, 0))
    sums = [item for layer in sums for item in layer]
    if fast:
        (pair,) = cut_sums(place, [((last,), True)])
        pair, grad_input = lax.optimization_barrier((pair, grad_input))
        pieces[0, 0], total = reduce_sums([], [pair], sums, 0)
    else:
        norms, wide, heads = [], [], []
        for row_sums, ffin_sum, head_sums in (sums[:3], sums[3:]):
            norms.append(row_sums)
            wide.append(ffin_sum.reshape(-1, D))
            heads.append(head_sums.sum(0).transpose(1, 0, 2).reshape(8, D))
        total = lax.psum(jnp.concatenate(norms + wide + heads), AXES)
    count = lax.axis_size("shard")
    shard = lax.axis_index("shard")
    ffin_rows = sums[1].shape[1] // D

    def share(rows):
        stacked = jnp.stack([total[row].reshape(-1) for row in rows])
        width = stacked.shape[1] // count
        return lax.dynamic_slice_in_dim(stacked, shard * width, width, axis=1)

    starts = [0, 8, 16, 16 + ffin_rows]
    heads_at = [16 + 2 * ffin_rows, 24 + 2 * ffin_rows]
    grads = {
        1: share([slice(at, at + 3, 2) for at in heads_at]),
        7: share([slice(at, at + ffin_rows) for at in starts[2:]]),
    }
    for number, row in ((10, 0), (11, 1), (9, 2), (4, 3), (5, 4), (3, 5)):
        grads[number] = share([row, 8 + row])
    if fast:
        rows = {number: weights[number].shape[1] for number in MATRICES}
        parts = {number: weights[number].shape[2] // (CORES * UNIT) for number in MATRICES}
        known = [{} for _ in range(LAYERS)]
        for layer in range(LAYERS):
            start = 0
            for number in (8, 2):
                known[layer][number] = (pieces[layer, "flat"], start, rows[number])
                start += rows[number] * parts[number]
            for number in (6, 0):
                end = pieces[layer, number]
                end = end.reshape(end.shape[0], -1, end.shape[-1])
                known[layer][number] = (list(end), 0, rows[number] // CHIPS_Y)
        for numbers in (MATRICES,):
            shapes = {number: weights[number].shape[1:] for number in numbers}
            grads.update(zip(numbers, join(place.at, known, shapes)))
    else:
        for number in MATRICES:
            grads[number] = jnp.stack([pieces[layer, number] for layer in range(LAYERS)])
    return (result, grad_input, *[grads[number] for number in range(12)])


def solution(mesh):
    in_specs = (
        P(("rep", "shard"), None),
        P(("rep", "shard"), None),
        P(("rep", "shard")),
        P(("rep", "shard"), None),
        P(None, ("rep", "shard")),
        P(None, "shard", None),
        P(None, "shard"),
        P(None, "shard", None),
        P(None, "shard"),
        P(None, "shard"),
        P(None, "shard"),
        P(None, "shard", None),
        P(None, "shard"),
        P(None, "shard", None),
        P(None, "shard"),
        P(None, "shard"),
        P(None, "shard"),
    )
    out_specs = (
        P(("rep", "shard"), None),
        P(("rep", "shard"), None),
        P(None, "shard", None),
        P(None, "shard"),
        P(None, "shard", None),
        P(None, "shard"),
        P(None, "shard"),
        P(None, "shard"),
        P(None, "shard", None),
        P(None, "shard"),
        P(None, "shard", None),
        P(None, "shard"),
        P(None, "shard"),
        P(None, "shard"),
    )
    fast = mesh.shape["rep"] == CHIPS_Y * CORES and mesh.shape["shard"] == CHIPS_Z * CHIPS_X
    return jax.shard_map(
        functools.partial(local, fast),
        mesh=mesh,
        in_specs=in_specs,
        out_specs=out_specs,
        check_vma=False,
    )
```

```python
import functools

import jax
import jax.numpy as jnp
from jax import lax
from jax.experimental import pallas as pl
from jax.experimental.pallas import tpu as pltpu
from jax.sharding import PartitionSpec as P

D = 768
HEADS = 12
HEAD_DIM = 64
LAYERS = 2
CLUSTER = 128
TREE_LEN = 1024
SEGMENTS = 13
PAIRS = HEADS // 2
LANES = 2 * HEAD_DIM
KERNEL_VMEM = 60 * 2**20
ROW_TILE = 256
FEED_TILE = 768
DEPTH_TILE = 384
INV_ROOT = (2.0 * 3.141592653589793) ** -0.5
MATRICES = (0, 2, 6, 8)
VECTORS = (1, 3, 4, 5, 7, 9, 10, 11)
UNIT = 384
AXES = ("rep", "shard")
CHIPS_Z, CHIPS_X, CHIPS_Y, CORES = 4, 2, 2, 2
norm_eps = 1e-06


def one_hot_rows(slot_row):
    length = slot_row.shape[-1]
    rows = lax.broadcasted_iota(jnp.int32, (length, length), 0)
    return jnp.where(rows == slot_row, 1.0, 0.0).astype(jnp.bfloat16)


def first_lanes(length):
    return lax.broadcasted_iota(jnp.int32, (length, LANES), 1) < HEAD_DIM


def contract_last(left_side, right_side):
    return lax.dot_general(
        left_side, right_side, (((1,), (1,)), ((), ())), preferred_element_type=jnp.float32
    )


def contract_first(left_side, right_side):
    return lax.dot_general(
        left_side, right_side, (((0,), (0,)), ((), ())), preferred_element_type=jnp.float32
    )


def cluster_blocks(values):
    return [values[at : at + CLUSTER] for at in range(0, values.shape[0], CLUSTER)]


def attend_pair(slots, query, key, value, bias, store):
    low = first_lanes(TREE_LEN)
    query = query * jnp.bfloat16(HEAD_DIM**-0.5)
    packed = (
        jnp.where(low, query, pltpu.roll(key, HEAD_DIM, 1)),
        jnp.where(low, pltpu.roll(query, HEAD_DIM, 1), key),
    )
    context = []
    for head in range(2):
        table = one_hot_rows(slots[head : head + 1])
        joined = jnp.concatenate([packed[head], value], axis=1)
        found = jnp.dot(table, joined, preferred_element_type=jnp.float32).astype(jnp.bfloat16)
        both, values = found[:, :LANES], found[:, LANES:]
        store("both", head, both)
        store("values", head, values)
        queries = jnp.where(low, both, jnp.bfloat16(0))
        keys = pltpu.roll(both, HEAD_DIM, 1)
        scores = jnp.concatenate(
            [contract_last(q, k) for q, k in zip(cluster_blocks(queries), cluster_blocks(keys))],
            axis=0,
        )
        scores = scores + bias[head].astype(jnp.float32)
        numerator = jnp.exp(scores - jnp.max(scores, axis=1, keepdims=True))
        total = jnp.sum(numerator, axis=1, keepdims=True)
        soft = (numerator * (1.0 / total)).astype(jnp.bfloat16)
        store("soft", head, soft)
        out = jnp.concatenate(
            [
                jnp.dot(p, v, preferred_element_type=jnp.float32)
                for p, v in zip(cluster_blocks(soft), cluster_blocks(values))
            ],
            axis=0,
        ).astype(jnp.bfloat16)
        context.append(contract_first(table, out))
        if head == 0:
            yield
    store("context", None, jnp.where(low, context[0], context[1]).astype(jnp.bfloat16))


def attend_kernel(slot_ref, query_ref, key_ref, value_ref, bias_ref, ctx_ref, qk_ref, val_ref, p_ref):
    refs = {"both": qk_ref, "values": val_ref, "soft": p_ref}

    def store(name, head, value):
        if head is None:
            ctx_ref[...] = value
        else:
            refs[name][0, head] = value

    for _ in attend_pair(
        slot_ref[0, 0], query_ref[...], key_ref[...], value_ref[...], bias_ref[0], store
    ):
        pass


def attend_steps(ins, outs):
    projected_ref, slot_ref, bias_ref = ins
    ctx_ref, qk_ref, val_ref, p_ref = outs
    refs = {"both": qk_ref, "values": val_ref, "soft": p_ref}
    for tree in range(slot_ref.shape[0]):
        rows = slice(tree * TREE_LEN, (tree + 1) * TREE_LEN)
        for pair in range(PAIRS):
            lanes = [slice((part * PAIRS + pair) * LANES, (part * PAIRS + pair + 1) * LANES) for part in range(3)]
            heads = slice(2 * pair, 2 * pair + 2)

            def store(name, head, value):
                if head is None:
                    ctx_ref[rows, lanes[0]] = value
                else:
                    refs[name][tree, 2 * pair + head] = value

            yield from attend_pair(
                slot_ref[tree, pair],
                *[projected_ref[rows, part] for part in lanes],
                bias_ref[tree, heads],
                store,
            )
            yield


def attend_back_pair(slots, grads, both_of, values_of, soft_of, store):
    low = first_lanes(TREE_LEN)
    placed = []
    for head in range(2):
        table = one_hot_rows(slots[head : head + 1])
        found = jnp.dot(table, grads, preferred_element_type=jnp.float32)
        found = jnp.where(low == (head == 0), found, 0.0).astype(jnp.bfloat16)
        both, values, soft = both_of(head), values_of(head), soft_of(head)
        grad_soft = jnp.concatenate(
            [contract_last(g, v) for g, v in zip(cluster_blocks(found), cluster_blocks(values))],
            axis=0,
        )
        grad_value = jnp.concatenate(
            [contract_first(p, g) for p, g in zip(cluster_blocks(soft), cluster_blocks(found))],
            axis=0,
        ).astype(jnp.bfloat16)
        weights = soft.astype(jnp.float32)
        delta = jnp.sum(weights * grad_soft, axis=1, keepdims=True)
        grad_scores = (weights * (grad_soft - delta)).astype(jnp.bfloat16)
        pairs = list(zip(cluster_blocks(grad_scores), cluster_blocks(both)))
        by_key = jnp.concatenate([contract_first(s, b) for s, b in pairs], axis=0)
        by_query = jnp.concatenate(
            [jnp.dot(s, b, preferred_element_type=jnp.float32) for s, b in pairs], axis=0
        )
        mixed = jnp.where(low, by_key, by_query * HEAD_DIM**-0.5).astype(jnp.bfloat16)
        joined = jnp.concatenate([mixed, grad_value], axis=1)
        placed.append(contract_first(table, joined))
        if head == 0:
            yield
    first, second = placed
    queries = jnp.where(low, pltpu.roll(first[:, :LANES], HEAD_DIM, 1), second[:, :LANES])
    keys = jnp.where(low, first[:, :LANES], pltpu.roll(second[:, :LANES], HEAD_DIM, 1))
    values = jnp.where(low, first[:, LANES:], second[:, LANES:])
    sums = []
    for part, grad in enumerate((queries, keys, values)):
        rounded = grad.astype(jnp.bfloat16)
        store(part, rounded)
        sums.append(rows_sum(rounded.astype(jnp.float32)))
    store(None, jnp.concatenate(sums + [jnp.zeros((5, LANES), jnp.float32)], axis=0))


def attend_back_kernel(slot_ref, grad_ref, qk_ref, val_ref, p_ref, out_ref, sums_ref):
    def store(part, value):
        if part is None:
            sums_ref[0, 0] = value
        else:
            out_ref[part] = value

    refs = [lambda head, ref=ref: ref[0, head] for ref in (qk_ref, val_ref, p_ref)]
    for _ in attend_back_pair(slot_ref[0, 0], grad_ref[...], *refs, store):
        pass


def attend_back_steps(ins, outs):
    slot_ref, grad_ref, *kept = ins
    out_ref, sums_ref = outs
    for tree in range(slot_ref.shape[0]):
        rows = slice(tree * TREE_LEN, (tree + 1) * TREE_LEN)
        for pair in range(PAIRS):
            lanes = slice(pair * LANES, (pair + 1) * LANES)

            def store(part, value):
                if part is None:
                    sums_ref[tree, pair] = value
                else:
                    out_ref[part, rows, lanes] = value

            refs = [lambda head, ref=ref: ref[tree, 2 * pair + head] for ref in kept]
            yield from attend_back_pair(slot_ref[tree, pair], grad_ref[rows, lanes], *refs, store)
            yield


def slot_spec(start=0):
    return pl.BlockSpec((1, 1, 2, TREE_LEN), lambda tree, pair: (tree, start + pair, 0, 0))


def head_spec(start=0):
    return pl.BlockSpec((1, 2, TREE_LEN, LANES), lambda tree, pair: (tree, start + pair, 0, 0))


def column_spec(offset):
    return pl.BlockSpec((TREE_LEN, LANES), lambda tree, pair: (tree, offset + pair))


def kernel_params():
    return pltpu.CompilerParams(vmem_limit_bytes=KERNEL_VMEM)


def attend_shapes(trees):
    stored = jax.ShapeDtypeStruct((trees, HEADS, TREE_LEN, LANES), jnp.bfloat16)
    return [jax.ShapeDtypeStruct((trees * TREE_LEN, D), jnp.bfloat16), stored, stored, stored]


def attend(projected, slots, bias):
    trees = slots.shape[0]
    return pl.pallas_call(
        attend_kernel,
        grid=(trees, PAIRS),
        in_specs=[
            slot_spec(),
            column_spec(0),
            column_spec(PAIRS),
            column_spec(2 * PAIRS),
            head_spec(),
        ],
        out_specs=[column_spec(0), head_spec(), head_spec(), head_spec()],
        out_shape=attend_shapes(trees),
        compiler_params=kernel_params(),
        cost_estimate=pl.CostEstimate(
            flops=trees * 30_000_000_000, bytes_accessed=trees * 20_000_000, transcendentals=0
        ),
    )(slots, projected, projected, projected, bias)


def attend_back_shapes(trees):
    return [
        jax.ShapeDtypeStruct((3, trees * TREE_LEN, D), jnp.bfloat16),
        jax.ShapeDtypeStruct((trees, PAIRS, 8, LANES), jnp.float32),
    ]


def attend_back(grad_context, slots, kept):
    trees = slots.shape[0]
    return pl.pallas_call(
        attend_back_kernel,
        grid=(trees, PAIRS),
        in_specs=[slot_spec(), column_spec(0), head_spec(), head_spec(), head_spec()],
        out_specs=[
            pl.BlockSpec((3, TREE_LEN, LANES), lambda tree, pair: (0, tree, pair)),
            pl.BlockSpec((1, 1, 8, LANES), lambda tree, pair: (tree, pair, 0, 0)),
        ],
        out_shape=attend_back_shapes(trees),
        compiler_params=kernel_params(),
        cost_estimate=pl.CostEstimate(
            flops=trees * 35_000_000_000, bytes_accessed=trees * 20_000_000, transcendentals=0
        ),
    )(slots, grad_context, *kept)


def erf_parts(values):
    size = jnp.abs(values)
    turn = 1.0 / (1.0 + (0.3275911 * 0.5**0.5) * size)
    bell = jnp.exp(-0.5 * values * values)
    series = 1.061405429 * 0.5
    for factor in (-1.453152027, 1.421413741, -0.284496736, 0.254829592):
        series = series * turn + factor * 0.5
    tail = series * turn * bell
    return jnp.where(values < 0.0, tail, 1.0 - tail), bell


def norm_parts(values):
    centred = values - jnp.mean(values, axis=-1, keepdims=True)
    scale = lax.rsqrt(jnp.mean(centred * centred, axis=-1, keepdims=True) + norm_eps)
    return centred * scale, scale


def norm_back(grad, normal, scale, gain):
    inner = grad * gain
    mean = jnp.mean(inner, axis=-1, keepdims=True)
    along = jnp.mean(inner * normal, axis=-1, keepdims=True)
    return scale * (inner - mean - normal * along)


def spread(column):
    return jnp.broadcast_to(column, (column.shape[0], 128))


def rows_sum(values):
    return jnp.sum(values, axis=0, keepdims=True)


def project_kernel(layer, rows_ref, weight_ref, bias_ref, out_ref):
    product = jnp.dot(rows_ref[...], weight_ref[...], preferred_element_type=jnp.float32)
    bias = bias_ref[layer : layer + 1]
    out_ref[:, :D] = (product[:, :D] + bias[:, :D]).astype(jnp.bfloat16)
    out_ref[:, D : 2 * D] = product[:, D : 2 * D].astype(jnp.bfloat16)
    out_ref[:, 2 * D :] = (product[:, 2 * D :] + bias[:, D:]).astype(jnp.bfloat16)


def feed_kernel(
    layer,
    context_ref,
    rows_ref,
    out_weight_ref,
    ffin_weight_ref,
    ffout_weight_ref,
    out_bias_ref,
    attn_gain_ref,
    attn_shift_ref,
    ffin_bias_ref,
    ffout_bias_ref,
    ffn_gain_ref,
    ffn_shift_ref,
    hidden_ref,
    act_ref,
    slope_ref,
    attn_normal_ref,
    attn_scale_ref,
    ffn_normal_ref,
    ffn_scale_ref,
    result_ref,
    result_low_ref,
):
    here = slice(layer, layer + 1)
    product = jnp.dot(context_ref[...], out_weight_ref[...], preferred_element_type=jnp.float32)
    attn_sum = rows_ref[...].astype(jnp.float32) + product + out_bias_ref[here]
    normal, scale = norm_parts(attn_sum)
    attn_normal_ref[...] = normal
    attn_scale_ref[...] = spread(scale)
    hidden = normal * attn_gain_ref[here] + attn_shift_ref[here]
    hidden_low = hidden.astype(jnp.bfloat16)
    hidden_ref[...] = hidden_low
    total = hidden + ffout_bias_ref[here]
    width = ffin_weight_ref.shape[1]
    for at in range(0, width, FEED_TILE):
        part = slice(at, at + FEED_TILE)
        pre = (
            jnp.dot(hidden_low, ffin_weight_ref[:, part], preferred_element_type=jnp.float32)
            + ffin_bias_ref[here, part]
        )
        below, bell = erf_parts(pre)
        act = (pre * below).astype(jnp.bfloat16)
        act_ref[:, part] = act
        slope_ref[:, part] = (below + pre * bell * INV_ROOT).astype(jnp.bfloat16)
        total = total + jnp.dot(
            act, ffout_weight_ref[part, :], preferred_element_type=jnp.float32
        )
    normal, scale = norm_parts(total)
    ffn_normal_ref[...] = normal
    ffn_scale_ref[...] = spread(scale)
    result = normal * ffn_gain_ref[here] + ffn_shift_ref[here]
    result_ref[...] = result
    result_low_ref[...] = result.astype(jnp.bfloat16)


def add_projected(grad, proj_ref, weight_ref):
    for part in range(3):
        grad = grad + contract_last(proj_ref[part], weight_ref[:, part * D : (part + 1) * D])
    return grad


def feed_back_kernel(layer, with_proj, *refs):
    here = slice(layer, layer + 1)
    if with_proj:
        above_ref, proj_ref, qkv_weight_ref, *refs = refs
        grad = add_projected(above_ref[...], proj_ref, qkv_weight_ref)
    else:
        above_ref, *refs = refs
        grad = above_ref[...].astype(jnp.float32)
    (
        ffn_normal_ref,
        ffn_scale_ref,
        slope_ref,
        attn_normal_ref,
        attn_scale_ref,
        out_weight_ref,
        ffin_weight_ref,
        ffout_weight_ref,
        attn_gain_ref,
        ffn_gain_ref,
        down_ref,
        pre_ref,
        attn_ref,
        attn_low_ref,
        context_ref,
        sums_ref,
        ffin_sum_ref,
    ) = refs

    @pl.when(pl.program_id(0) == 0)
    def _():
        sums_ref[...] = jnp.zeros_like(sums_ref)
        ffin_sum_ref[...] = jnp.zeros_like(ffin_sum_ref)

    normal = ffn_normal_ref[...]
    sums_ref[0:1] += rows_sum(grad * normal)
    sums_ref[1:2] += rows_sum(grad)
    grad_sum = norm_back(grad, normal, ffn_scale_ref[:, 0:1], ffn_gain_ref[here])
    down = grad_sum.astype(jnp.bfloat16)
    down_ref[...] = down
    sums_ref[2:3] += rows_sum(down.astype(jnp.float32))
    total = grad_sum
    width = ffin_weight_ref.shape[1]
    for at in range(0, width, FEED_TILE):
        part = slice(at, at + FEED_TILE)
        grad_act = contract_last(down, ffout_weight_ref[part, :])
        pre = (grad_act * slope_ref[:, part].astype(jnp.float32)).astype(jnp.bfloat16)
        pre_ref[:, part] = pre
        ffin_sum_ref[:, part] += rows_sum(pre.astype(jnp.float32))
        total = total + contract_last(pre, ffin_weight_ref[:, part])
    normal = attn_normal_ref[...]
    sums_ref[3:4] += rows_sum(total * normal)
    sums_ref[4:5] += rows_sum(total)
    attn = norm_back(total, normal, attn_scale_ref[:, 0:1], attn_gain_ref[here])
    attn_ref[...] = attn
    low = attn.astype(jnp.bfloat16)
    attn_low_ref[...] = low
    sums_ref[5:6] += rows_sum(low.astype(jnp.float32))
    context_ref[...] = contract_last(low, out_weight_ref[...]).astype(jnp.bfloat16)


def input_grad_kernel(above_ref, proj_ref, weight_ref, out_ref):
    out_ref[...] = add_projected(above_ref[...], proj_ref, weight_ref)


def prep_pair(parent_ref, segment_ref, cluster_ref, slot_ref, bias_ref, row, tree, pair):
    segs = segment_ref[tree]
    length = segs.shape[1]

    def parent_of(values):
        found = jnp.zeros_like(values)
        for number in range(SEGMENTS):
            found = jnp.where(values == number, parent_ref[row, number], found)
        return found

    parents = parent_of(segs)
    grands = parent_of(parents)
    ids = jnp.concatenate([segs, parents, grands, jnp.zeros((5, length), jnp.int32)], axis=0)
    ids = jnp.concatenate([ids, jnp.zeros((8, length), jnp.int32)], axis=0)
    ids = ids.astype(jnp.float32).astype(jnp.bfloat16)
    count = length // CLUSTER
    order = lax.broadcasted_iota(jnp.int32, (count, length), 0)
    lanes = lax.broadcasted_iota(jnp.int32, (count, length), 1)
    for head in range(2):
        member = order == cluster_ref[tree, pair, head : head + 1, :]
        ranks = member.astype(jnp.int32)
        step = 1
        while step < length:
            ranks = ranks + jnp.where(lanes >= step, pltpu.roll(ranks, step, 1), 0)
            step *= 2
        slot = jnp.sum(
            jnp.where(member, ranks - 1 + CLUSTER * order, 0), axis=0, keepdims=True
        )
        slot_ref[tree, pair, head : head + 1, :] = slot
        table = one_hot_rows(slot)
        rows = contract_last(ids, table)
        columns = jnp.concatenate([rows] * (128 // rows.shape[0]), axis=0).T
        for at in range(0, length, CLUSTER):
            here = rows[0:1, at : at + CLUSTER]
            block = columns[at : at + CLUSTER]
            allowed = (
                (here == block[:, 0:1]) | (here == block[:, 1:2]) | (here == block[:, 2:3])
            )
            bias_ref[tree, 2 * pair + head, at : at + CLUSTER, :] = jnp.where(allowed, 0.0, -1e30).astype(
                jnp.bfloat16
            )


def prep_kernel(*refs):
    prep_pair(*refs, pl.program_id(0), 0, 0)


def row_spec(width, rows=ROW_TILE):
    return pl.BlockSpec((rows, width), lambda i: (i, 0))


def whole_spec(shape):
    return pl.BlockSpec(
        shape, lambda i: (0,) * len(shape), pipeline_mode=pl.Buffered(1)
    )


def part_spec(rows=ROW_TILE):
    return pl.BlockSpec((3, rows, D), lambda i: (0, i, 0))


def cost(flops, *arrays):
    moved = sum(array.size * array.dtype.itemsize for array in arrays)
    return pl.CostEstimate(flops=int(flops), bytes_accessed=moved, transcendentals=0)


def shape_of(rows, width, kind=jnp.bfloat16):
    return jax.ShapeDtypeStruct((rows, width), kind)


def project(layer, rows, weight, bias):
    count, width = rows.shape[0], weight.shape[1]
    return pl.pallas_call(
        functools.partial(project_kernel, layer),
        grid=(count // ROW_TILE,),
        in_specs=[row_spec(D), whole_spec(weight.shape), whole_spec(bias.shape)],
        out_specs=row_spec(width),
        out_shape=shape_of(count, width),
        compiler_params=kernel_params(),
        cost_estimate=cost(2.4 * count * D * width, rows, weight),
    )(rows, weight, bias)


def feed(layer, context, rows, weights, vectors):
    count = context.shape[0]
    width = weights[1].shape[1]
    f32 = jnp.float32
    return pl.pallas_call(
        functools.partial(feed_kernel, layer),
        grid=(count // ROW_TILE,),
        in_specs=[row_spec(D), row_spec(D)]
        + [whole_spec(weight.shape) for weight in weights]
        + [whole_spec(vector.shape) for vector in vectors],
        out_specs=[
            row_spec(D),
            row_spec(width),
            row_spec(width),
            row_spec(D),
            row_spec(128),
            row_spec(D),
            row_spec(128),
            row_spec(D),
            row_spec(D),
        ],
        out_shape=[
            shape_of(count, D),
            shape_of(count, width),
            shape_of(count, width),
            shape_of(count, D, f32),
            shape_of(count, 128, f32),
            shape_of(count, D, f32),
            shape_of(count, 128, f32),
            shape_of(count, D, f32),
            shape_of(count, D),
        ],
        compiler_params=kernel_params(),
        cost_estimate=cost(5 * count * D * (2 * width + D), context, *weights),
    )(context, rows, *weights, *vectors)


def feed_back(layer, above, proj, qkv_weight, saved, weights, gains):
    count = above.shape[0]
    width = weights[1].shape[1]
    f32 = jnp.float32
    lead, lead_specs = [above], [row_spec(D)]
    if proj is not None:
        lead += [proj, qkv_weight]
        lead_specs += [part_spec(), whole_spec(qkv_weight.shape)]
    return pl.pallas_call(
        functools.partial(feed_back_kernel, layer, proj is not None),
        grid=(count // ROW_TILE,),
        in_specs=lead_specs
        + [row_spec(D), row_spec(128), row_spec(width), row_spec(D), row_spec(128)]
        + [whole_spec(weight.shape) for weight in weights]
        + [whole_spec(gain.shape) for gain in gains],
        out_specs=[
            row_spec(D),
            row_spec(width),
            row_spec(D),
            row_spec(D),
            row_spec(D),
            pl.BlockSpec((8, D), lambda i: (0, 0)),
            pl.BlockSpec((1, width), lambda i: (0, 0)),
        ],
        out_shape=[
            shape_of(count, D),
            shape_of(count, width),
            shape_of(count, D, f32),
            shape_of(count, D),
            shape_of(count, D),
            shape_of(8, D, f32),
            shape_of(1, width, f32),
        ],
        compiler_params=kernel_params(),
        cost_estimate=cost(5 * count * D * (2 * width + D), above, *weights),
    )(*lead, *saved, *weights, *gains)


def input_grad(above, proj, qkv_weight):
    count = above.shape[0]
    return pl.pallas_call(
        input_grad_kernel,
        grid=(count // ROW_TILE,),
        in_specs=[
            row_spec(D),
            part_spec(),
            whole_spec(qkv_weight.shape),
        ],
        out_specs=row_spec(D),
        out_shape=shape_of(count, D, jnp.float32),
        compiler_params=kernel_params(),
        cost_estimate=cost(2.4 * count * D * 3 * D, above, qkv_weight),
    )(above, proj, qkv_weight)


def prepare(segment, parent, clusters):
    trees = parent.shape[0]
    segment = segment.reshape(trees, 1, TREE_LEN)
    clusters = clusters.reshape(PAIRS, 2, trees, TREE_LEN).transpose(2, 0, 1, 3)
    return pl.pallas_call(
        prep_kernel,
        grid=(trees, PAIRS),
        in_specs=[
            pl.BlockSpec(memory_space=pltpu.SMEM),
            pl.BlockSpec((1, 1, TREE_LEN), lambda tree, pair: (tree, 0, 0)),
            slot_spec(),
        ],
        out_specs=[slot_spec(), head_spec()],
        out_shape=[
            jax.ShapeDtypeStruct((trees, PAIRS, 2, TREE_LEN), jnp.int32),
            jax.ShapeDtypeStruct((trees, HEADS, TREE_LEN, LANES), jnp.bfloat16),
        ],
        compiler_params=kernel_params(),
        cost_estimate=pl.CostEstimate(
            flops=trees * 20_000_000_000, bytes_accessed=trees * 4_000_000, transcendentals=0
        ),
    )(parent, segment, clusters)


def weight_grad_kernel(split_y, at_ref, left_ref, right_ref, *refs):
    product = contract_first(
        left_ref[...].reshape(left_ref.shape[-2:]), right_ref[...].reshape(right_ref.shape[-2:])
    )
    if split_y is None:
        (out_ref,) = refs
        out_ref[...] = product.astype(jnp.bfloat16).reshape(out_ref.shape)
        return
    near_ref, (send_ref, keep_ref, sum_ref) = refs[0], refs[-3:]
    total = product + near_ref[...].astype(jnp.float32).reshape(product.shape)
    sum_ref[...] = total.astype(jnp.bfloat16).reshape(sum_ref.shape)
    if split_y:
        send_ref[0] = sum_ref[:, :, 1 - at_ref[2]]
        keep_ref[0] = sum_ref[:, :, at_ref[2]]
    else:
        send_ref[...] = sum_ref[:, 1 - at_ref[1]]
        keep_ref[...] = sum_ref[:, at_ref[1]]


class Grad:
    def __init__(self, number, left, right, tiles, half):
        self.number = number
        self.left, self.right = left, right
        self.tiles, self.half = tiles, half
        self.depth = left.shape[1]
        self.parts = 1 if self.depth > D else tiles
        self.rows = self.depth // (CHIPS_Z * CHIPS_X)

    def product(self, at, other, split_y=None, near=None, start=0, total=0, before=()):
        flip = 1 if other else 0
        left, right = self.left, self.right
        count = left.shape[0]
        tall = self.depth > D
        core = lambda at: lax.rem(at[3] + flip, CORES)
        in_specs = [
            pl.BlockSpec((count, D), (lambda i, at: (0, i)) if tall else (lambda i, at: (0, 0)))
        ]
        if right.ndim == 3:
            in_specs.append(pl.BlockSpec((1, count, self.half), lambda i, at: (i, 0, core(at))))
        elif tall:
            in_specs.append(pl.BlockSpec((count, self.half), lambda i, at: (0, core(at))))
        else:
            in_specs.append(
                pl.BlockSpec((count, self.half), lambda i, at: (0, core(at) * self.tiles + i))
            )
        zs = D // (self.rows * CHIPS_X)
        place = (lambda i: (0, i)) if tall else (lambda i: (i, 0))
        whole = (self.parts, CHIPS_Z, CHIPS_X, self.rows, self.half)
        block = (1, zs, CHIPS_X, self.rows, self.half)
        full = pl.BlockSpec(block, lambda i, at: (*place(i), 0, 0, 0))
        args, scratch = [left, right], []
        if split_y is None:
            out_specs, shapes = full, jax.ShapeDtypeStruct(whole, jnp.bfloat16)
        else:
            in_specs.append(full)
            args.append(near)
            in_specs += [pl.BlockSpec(memory_space=pl.ANY)] * len(before)
            args += before
            if split_y:
                short = self.rows // CHIPS_Y
                kept = (CHIPS_X, short, self.half)
                scratch = [pltpu.VMEM((zs, CHIPS_X, CHIPS_Y, short, self.half), jnp.bfloat16)]
                spec = pl.BlockSpec((1, zs, *kept), lambda i, at: (*place(i), 0, 0, 0))
                shape = (self.parts, CHIPS_Z, *kept)
            else:
                scratch = [pltpu.VMEM((zs, CHIPS_X, self.rows, self.half), jnp.bfloat16)]
                first = start // self.rows
                index = (lambda i, at: (i, first, 0)) if tall else (lambda i, at: (0, first + i, 0))
                spec = pl.BlockSpec((zs, self.rows, self.half), index)
                shape = (CHIPS_Z, total, self.half)
            out_specs, shapes = [spec] * 2, [jax.ShapeDtypeStruct(shape, jnp.bfloat16)] * 2
        return pl.pallas_call(
            functools.partial(weight_grad_kernel, split_y),
            grid_spec=pltpu.PrefetchScalarGridSpec(
                num_scalar_prefetch=1,
                grid=(self.tiles,),
                in_specs=in_specs,
                out_specs=out_specs,
                scratch_shapes=scratch,
            ),
            out_shape=shapes,
            input_output_aliases={4 + place: place for place in range(len(before))},
            compiler_params=kernel_params(),
            cost_estimate=cost(4 * count * D * self.tiles * self.half, left, right),
        )(at, *args)


class Place:
    def __init__(self):
        rep = lax.axis_index("rep")
        shard = lax.axis_index("shard")
        self.y, self.core = rep // CORES, rep % CORES
        self.z, self.x = shard // CHIPS_X, shard % CHIPS_X
        self.at = jnp.stack([self.z, self.x, self.y, self.core]).astype(jnp.int32)


def hop(value, dz=0, dx=0, dy=0, dc=0):
    pairs = []
    for y in range(CHIPS_Y):
        for c in range(CORES):
            for z in range(CHIPS_Z):
                for x in range(CHIPS_X):
                    source = ((y * CORES + c) * CHIPS_Z + z) * CHIPS_X + x
                    y2, c2 = (y + dy) % CHIPS_Y, (c + dc) % CORES
                    z2, x2 = (z + dz) % CHIPS_Z, (x + dx) % CHIPS_X
                    pairs.append((source, ((y2 * CORES + c2) * CHIPS_Z + z2) * CHIPS_X + x2))
    return lax.ppermute(value, AXES, pairs)


def cut_sums(place, groups):
    at = place.at
    arrived = []
    for grads, _ in groups:
        arrived.append([hop(grad.product(at, True), dc=1) for grad in grads])
    found = []
    for (grads, y_first), near in zip(groups, arrived):
        total = sum(grad.parts * grad.rows for grad in grads)
        start, pair = 0, ()
        for grad, item in zip(grads, near):
            if y_first:
                pair = grad.product(at, False, True, item)
            else:
                pair = grad.product(at, False, False, item, start, total, tuple(pair))
            start += grad.parts * grad.rows
        found.append(tuple(pair))
    return found


def prep_steps(ins, outs):
    trees, pairs = ins[2].shape[:2]
    for tree in range(trees):
        for pair in range(pairs):
            prep_pair(*ins, *outs[:2], tree, tree, pair)
            yield


def gather_kernel(plan, arrays, ending, work, work_ins, work_outs, *refs):
    count = len(plan)
    own_ins, ins, refs = refs[:work_ins], refs[work_ins : work_ins + arrays], refs[work_ins + arrays :]
    own_outs, outs = refs[:work_outs], refs[work_outs : work_outs + arrays]
    sems, local_sem = refs[work_outs + arrays : -1], refs[-1]
    todo = work(own_ins, own_outs)
    rep, shard = lax.axis_index("rep"), lax.axis_index("shard")
    y, core = lax.div(rep, CORES), lax.rem(rep, CORES)
    z, x = lax.div(shard, CHIPS_X), lax.rem(shard, CHIPS_X)

    def device(dz=0, dx=0, dy=0, dc=0):
        to_y, to_core = lax.rem(y + dy, CHIPS_Y), lax.rem(core + dc, CORES)
        to_z, to_x = lax.rem(z + dz, CHIPS_Z), lax.rem(x + dx, CHIPS_X)
        return (to_y * CORES + to_core, to_z * CHIPS_X + to_x)

    mates = [dict(dx=1), dict(dy=1), dict(dc=1)] + [dict(dz=k) for k in range(1, CHIPS_Z)]
    barrier = pltpu.get_barrier_semaphore()
    for mate in mates:
        pl.semaphore_signal(
            barrier, inc=1, device_id=device(**mate), device_id_type=pl.DeviceIdType.MESH
        )
    sent = []

    def send(source, target, m, number, **step):
        copy = pltpu.make_async_remote_copy(
            src_ref=source,
            dst_ref=target,
            send_sem=sems[m].at[0, number],
            recv_sem=sems[m].at[1, number],
            device_id=device(**step),
            device_id_type=pl.DeviceIdType.MESH,
        )
        copy.start()
        sent.append(copy)
        return copy

    def part(m, at_z, at_x, at_y, at_core):
        which, _, split_y, by_core, row, rows, column, columns = plan[m]
        out = outs[which]
        at_columns = slice(None)
        if by_core:
            first = at_core * (out.shape[-1] // CORES) + column
            at_columns = pl.ds(pl.multiple_of(first, 128), columns)
        at_z = slice(None) if at_z is None else at_z
        at_x = slice(None) if at_x is None else at_x
        return out.at[at_z, at_x, at_y if split_y else 0, pl.ds(row, rows), at_columns]

    locals_ = []
    for m, (which, layer, split_y, by_core, row, rows, column, columns) in enumerate(plan):
        source = ins[which] if layer is None else ins[which].at[layer]
        if by_core:
            first = row
            if split_y:
                first = pl.multiple_of(y * outs[which].shape[3] + row, 16)
            start = core * (outs[which].shape[-1] // CORES) + column
            source = source.at[pl.ds(first, rows), pl.ds(pl.multiple_of(start, 128), columns)]
        copy = pltpu.make_async_copy(source, part(m, z, x, y, core), local_sem.at[m])
        copy.start()
        locals_.append(copy)
    pl.semaphore_wait(barrier, len(mates))
    along_z, along_x, over_y, last = {}, {}, {}, []

    def spread(m, at_z, at_x):
        piece = part(m, at_z, at_x, y, core)
        if at_x is x:
            along_x[m].append(send(piece, piece, m, 3 + len(along_x[m]), dx=1))
        if plan[m][2]:
            over_y[m].append(send(piece, piece, m, 7 + len(over_y[m]), dy=1))

    def behind(k):
        return lax.rem(z + CHIPS_Z - k, CHIPS_Z)

    def after_x(m):
        for k in range(CHIPS_Z):
            if k % 2:
                next(todo, None)
            along_x[m][k].wait_recv()
            spread(m, behind(k), 1 - x)
        if plan[m][3]:
            piece = part(m, None, None, y, core)
            last.append(send(piece, piece, m, 15, dc=1))

    def after_y(m):
        if over_y[m]:
            for copy in over_y[m]:
                copy.wait_recv()
            piece = part(m, None, None, 1 - y, core)
            last.append(send(piece, piece, m, 16, dc=1))

    order = range(count)

    def set_out(m):
        locals_[m].wait()
        mine = part(m, z, x, y, core)
        along_z[m] = [send(mine, mine, m, k - 1, dz=k) for k in range(1, CHIPS_Z)]
        along_x[m], over_y[m] = [], []
        spread(m, z, x)

    for m in order[:2]:
        set_out(m)
    for place, m in enumerate(order):
        for k in range(1, CHIPS_Z):
            next(todo, None)
            along_z[m][k - 1].wait_recv()
            spread(m, behind(k), x)
        if place + 2 < count:
            set_out(order[place + 2])
        if place:
            after_x(order[place - 1])
    after_x(order[-1])
    ending(own_outs, outs)
    for m in order:
        after_y(m)
        next(todo, None)
    for _ in todo:
        pass
    for copy in last:
        copy.wait_recv()
    for copy in sent:
        copy.wait_send()


def no_ending(own_outs, outs):
    pass


def spread_vectors(sizes, own_outs, outs):
    found = outs[-1]
    for shard in range(CHIPS_Z * CHIPS_X):
        rows = found[shard // CHIPS_X, shard % CHIPS_X, 0].astype(jnp.float32)
        at = 0
        for out_ref, size in zip(own_outs[-len(sizes) :], sizes):
            out_ref[:, shard * size : (shard + 1) * size] = rows[:LAYERS, at : at + size]
            at += size


def gather(weights, wanted, work, work_args, work_shapes, number, ending=no_ending):
    low = jnp.bfloat16
    args, plan, shapes = [], [], []
    for which, layer, split_y, tall, wide in wanted:
        rows, columns = weights[which].shape[-2:]
        split = CHIPS_Y if split_y else 1
        rows //= split
        half = columns if layer is None else columns // CORES
        for piece in range(tall * wide):
            row, column = divmod(piece, wide)
            plan.append(
                (
                    len(args),
                    layer,
                    split_y,
                    layer is not None,
                    row * (rows // tall),
                    rows // tall,
                    column * (half // wide),
                    half // wide,
                )
            )
        args.append(weights[which])
        shapes.append((CHIPS_Z, CHIPS_X, split, rows, columns))
    whole = pl.BlockSpec(memory_space=pltpu.VMEM)
    small = pl.BlockSpec(memory_space=pltpu.SMEM)
    found = pl.pallas_call(
        functools.partial(
            gather_kernel, plan, len(args), ending, work, len(work_args), len(work_shapes)
        ),
        in_specs=[small if arg.shape[-1] == SEGMENTS else whole for arg in work_args]
        + [pl.BlockSpec(memory_space=pl.ANY)] * len(args),
        out_specs=[whole] * (len(work_shapes) + len(args)),
        out_shape=work_shapes + [jax.ShapeDtypeStruct(shape, low) for shape in shapes],
        scratch_shapes=[pltpu.SemaphoreType.DMA((2, 17))] * len(plan)
        + [pltpu.SemaphoreType.DMA((len(plan),))],
        compiler_params=pltpu.CompilerParams(
            vmem_limit_bytes=KERNEL_VMEM, collective_id=number, has_side_effects=True
        ),
        cost_estimate=pl.CostEstimate(flops=0, bytes_accessed=200_000_000, transcendentals=0),
    )(*work_args, *args)
    results, arrays = list(found[: len(work_shapes)]), found[len(work_shapes) :]
    for item, array in zip(wanted, arrays):
        results.append(array if item[1] is None else array.reshape(-1, array.shape[-1]))
    return results


def pack_sums(out_ref, ins):
    rows = 8 * LAYERS
    width = out_ref.shape[1]
    for layer in range(LAYERS):
        sums_ref, ffin_ref, _ = ins[3 * layer : 3 * layer + 3]
        out_ref[8 * layer : 8 * layer + 8] = sums_ref[...]
        for at in range(0, ffin_ref.shape[1], width):
            out_ref[rows : rows + 1] = ffin_ref[:, at : at + width]
            rows += 1
    for layer in range(LAYERS):
        ref = ins[3 * layer + 2]
        for pair in range(ref.shape[1]):
            value = ref[0, pair]
            for tree in range(1, ref.shape[0]):
                value = value + ref[tree, pair]
            out_ref[rows : rows + 8, pair * LANES : (pair + 1) * LANES] = value
        rows += 8


def sum_rows(ffin_width):
    return LAYERS * (16 + ffin_width // D)


def reduce_kernel(flats, count, vectors, work, work_ins, work_outs, *refs):
    take = iter(refs)

    def some(number):
        return [next(take) for _ in range(number)]

    own_ins = some(work_ins)
    a_ins = [some(2) for _ in range(flats)]
    b_ins = [some(2) for _ in range(count)]
    vec_ins = some(vectors)
    own_outs = some(work_outs)
    a_outs = [some(2) for _ in range(flats)]
    b_outs = some(count)
    vec_outs = some(1 if vectors else 0)
    a_scratch = [some(6) for _ in range(flats)]
    b_scratch = [some(6) for _ in range(count)]
    v_send, v_land = some(2) if vectors else (None, None)
    a_sems, b_sems = some(flats), some(count)
    v_sems = next(take) if vectors else None
    todo = work(own_ins, own_outs)
    rep, shard = lax.axis_index("rep"), lax.axis_index("shard")
    y, core = lax.div(rep, CORES), lax.rem(rep, CORES)
    z, x = lax.div(shard, CHIPS_X), lax.rem(shard, CHIPS_X)

    def device(dz=0, dx=0, dy=0, dc=0):
        to_y, to_core = lax.rem(y + dy, CHIPS_Y), lax.rem(core + dc, CORES)
        to_z, to_x = lax.rem(z + dz, CHIPS_Z), lax.rem(x + dx, CHIPS_X)
        return (to_y * CORES + to_core, to_z * CHIPS_X + to_x)

    flip_z = 1 + 2 * lax.rem(z, 2)
    mates = [dict(dx=1), dict(dy=1), dict(dc=1), dict(dy=1, dc=1)]
    mates += [dict(dz=k) for k in range(1, CHIPS_Z)]
    barrier = pltpu.get_barrier_semaphore()
    for mate in mates:
        pl.semaphore_signal(
            barrier, inc=1, device_id=device(**mate), device_id_type=pl.DeviceIdType.MESH
        )
    pl.semaphore_wait(barrier, len(mates))
    sent = []

    def send(source, target, sems, number, **step):
        copy = pltpu.make_async_remote_copy(
            src_ref=source,
            dst_ref=target,
            send_sem=sems.at[0, number],
            recv_sem=sems.at[1, number],
            device_id=device(**step),
            device_id_type=pl.DeviceIdType.MESH,
        )
        copy.start()
        sent.append(copy)
        return copy

    def wide(value):
        return value.astype(jnp.float32)

    order = (2, 1, 3, 0)
    ahead = [lax.rem(z + k, CHIPS_Z) for k in order]
    v_copies = []
    if vectors:
        pack_sums(v_send.at[0], vec_ins)
        v_copies.append(send(v_send.at[0], v_land.at[0], v_sems, 0, dc=1))
    a_x, b_y = [[] for _ in range(flats)], [[] for _ in range(count)]

    def set_out(j):
        to = ahead[j]
        for i, (first, _) in enumerate(a_ins):
            a_x[i].append(send(first.at[to], a_scratch[i][0].at[j], a_sems[i], j, dx=1))
        for i, (first, _) in enumerate(b_ins):
            b_y[i].append(send(first.at[:, to], b_scratch[i][0].at[j], b_sems[i], j, dy=1))

    set_out(0)
    set_out(1)
    steps = (dict(dc=1), dict(dy=1), dict(dx=1), dict(dz=2), dict(dz=flip_z))

    def add_vectors(s):
        if not vectors:
            return
        v_copies[s].wait_recv()
        total = v_send[s] + v_land[s]
        if s + 1 == len(steps):
            vec_outs[0][...] = total
        else:
            v_send[s + 1] = total
            v_copies.append(
                send(v_send.at[s + 1], v_land.at[s + 1], v_sems, s + 1, **steps[s + 1])
            )

    a_z, b_x, b_z = ([[] for _ in range(number)] for number in (flats, count, count))

    def b_along_z(i, j):
        k, keep = order[j], b_ins[i][1]
        over, _, x_land, z_send, z_land, _ = b_scratch[i]
        b_x[i][j].wait_recv()
        if k:
            total = wide(keep[:, ahead[j], x]) + wide(over[j, :, x]) + wide(x_land[j])
            z_send[k - 1] = total.astype(jnp.bfloat16)
            b_z[i].append(send(z_send.at[k - 1], z_land.at[k - 1], b_sems[i], 7 + k, dz=k))

    def b_along_x(i, j):
        keep, (over, x_send, x_land, *_) = b_ins[i][1], b_scratch[i]
        b_y[i][j].wait_recv()
        total = wide(keep[:, ahead[j], 1 - x]) + wide(over[j, :, 1 - x])
        x_send[j] = total.astype(jnp.bfloat16)
        b_x[i].append(send(x_send.at[j], x_land.at[j], b_sems[i], 4 + j, dx=1))

    for j, k in enumerate(order):
        next(todo, None)
        for i, (_, keep) in enumerate(a_ins):
            across, z_send, z_land, *_ = a_scratch[i]
            a_x[i][j].wait_recv()
            if k:
                total = wide(keep[ahead[j]]) + wide(across[j])
                z_send[k - 1] = total.astype(jnp.bfloat16)
                a_z[i].append(
                    send(z_send.at[k - 1], z_land.at[k - 1], a_sems[i], 3 + k, dz=k)
                )
        next(todo, None)
        for i in range(count):
            b_along_x(i, j)
        if j + 2 < CHIPS_Z:
            set_out(j + 2)
        if j:
            for i in range(count):
                b_along_z(i, j - 1)
        next(todo, None)
        add_vectors(j)
    for i in range(count):
        b_along_z(i, CHIPS_Z - 1)
    add_vectors(4)
    for _ in todo:
        pass
    over_y, ends = [], []
    for i, (_, keep) in enumerate(a_ins):
        across, _, z_land, y_send, y_land, _ = a_scratch[i]
        for copy in a_z[i]:
            copy.wait_recv()
        total = wide(keep[z]) + wide(across[CHIPS_Z - 1])
        for k in range(CHIPS_Z - 1):
            total = total + wide(z_land[k])
        y_send[...] = total.astype(jnp.bfloat16)
        over_y.append(send(y_send, y_land, a_sems[i], 7, dy=1))
    for i, (_, keep) in enumerate(b_ins):
        over, _, x_land, _, z_land, end_land = b_scratch[i]
        for copy in b_z[i]:
            copy.wait_recv()
        total = wide(keep[:, z, x]) + wide(over[3, :, x]) + wide(x_land[3])
        for k in range(CHIPS_Z - 1):
            total = total + wide(z_land[k])
        b_outs[i][0] = total.astype(jnp.bfloat16)
        for number, step in enumerate((dict(dy=1), dict(dc=1), dict(dy=1, dc=1))):
            ends.append(
                send(b_outs[i].at[0], end_land.at[number], b_sems[i], 11 + number, **step)
            )
    for i, (own, _) in enumerate(a_outs):
        *_, y_send, y_land, c_land = a_scratch[i]
        over_y[i].wait_recv()
        own[...] = (wide(y_send[...]) + wide(y_land[...])).astype(jnp.bfloat16)
        ends.append(send(own, c_land, a_sems[i], 8, dc=1))
    for copy in ends:
        copy.wait_recv()
    for i in range(count):
        b_outs[i][1:4] = b_scratch[i][5][...]
    for i, (_, other) in enumerate(a_outs):
        other[...] = a_scratch[i][5][...]
    for copy in sent:
        copy.wait_send()


def no_work(ins, outs):
    return iter(())


def reduce_sums(flats, pairs, sums, number, work=no_work, work_args=(), work_shapes=()):
    low = jnp.bfloat16
    whole = pl.BlockSpec(memory_space=pltpu.VMEM)
    far = pl.BlockSpec(memory_space=pl.ANY)
    args, specs = list(work_args), [whole] * len(work_args)
    outs, scratch = [], []
    for first, keep in flats:
        piece = keep.shape[1:]
        args += [first, keep]
        specs += [far, whole]
        outs += [piece, piece]
        scratch += [(CHIPS_Z, *piece), (CHIPS_Z - 1, *piece), (CHIPS_Z - 1, *piece)]
        scratch += [piece] * 3
    for first, keep in pairs:
        parts, _, _, rows, half = keep.shape
        block = (parts, rows, half)
        args += [first, keep]
        specs += [far, whole]
        outs.append((CORES * CHIPS_Y, *block))
        scratch += [
            (CHIPS_Z, parts, CHIPS_X, rows, half),
            (CHIPS_Z, *block),
            (CHIPS_Z, *block),
            (CHIPS_Z - 1, *block),
            (CHIPS_Z - 1, *block),
            (CORES * CHIPS_Y - 1, *block),
        ]
    args += sums
    specs += [whole] * len(sums)
    shapes = list(work_shapes) + [jax.ShapeDtypeStruct(shape, low) for shape in outs]
    scratch = [pltpu.VMEM(shape, low) for shape in scratch]
    if sums:
        vec = (sum_rows(sums[1].shape[1]), D)
        shapes.append(jax.ShapeDtypeStruct(vec, jnp.float32))
        scratch += [pltpu.VMEM((5, *vec), jnp.float32)] * 2
    scratch += [pltpu.SemaphoreType.DMA((2, 9))] * len(flats)
    scratch += [pltpu.SemaphoreType.DMA((2, 14))] * len(pairs)
    if sums:
        scratch.append(pltpu.SemaphoreType.DMA((2, 5)))
    return pl.pallas_call(
        functools.partial(
            reduce_kernel, len(flats), len(pairs), len(sums), work, len(work_args), len(work_shapes)
        ),
        in_specs=specs,
        out_specs=[whole] * len(shapes),
        out_shape=shapes,
        scratch_shapes=scratch,
        compiler_params=pltpu.CompilerParams(
            vmem_limit_bytes=KERNEL_VMEM, collective_id=number, has_side_effects=True
        ),
        cost_estimate=pl.CostEstimate(flops=0, bytes_accessed=200_000_000, transcendentals=0),
    )(*args)


def join_kernel(plan, count, at_ref, *refs):
    for ref, out, layer, outer, parts, dc, dy, start, rows in plan:
        ref, out_ref = refs[ref], refs[count + out]
        half = ref.shape[1]
        core = lax.rem(at_ref[3] + dc, CORES)
        row = 0
        if dy is not None:
            row = pl.multiple_of(lax.rem(at_ref[2] + dy, CHIPS_Y) * rows, 16)
        for part in range(parts):
            column = part * CORES + core if outer else core * parts + part
            column = pl.multiple_of(column * half, 128)
            value = ref[start + part * rows : start + (part + 1) * rows]
            out_ref[layer, pl.ds(row, rows), pl.ds(column, half)] = value.astype(jnp.float32)


def join(at, done, shapes):
    arrays, plan = [], []
    for out, (number, (tall, wide)) in enumerate(shapes.items()):
        for layer in range(LAYERS):
            pieces, start, rows = done[layer][number]
            for place, piece in enumerate(pieces):
                known = [other is piece for other in arrays]
                if not any(known):
                    arrays.append(piece)
                    known.append(True)
                parts = wide // (CORES * piece.shape[1])
                dy, dc = (place % CHIPS_Y, place // CHIPS_Y) if len(pieces) > CORES else (None, place)
                plan.append((known.index(True), out, layer, number == 0, parts, dc, dy, start, rows))
    zeros = lambda i, at: (0, 0)
    outs = [(LAYERS, *shape) for shape in shapes.values()]
    return pl.pallas_call(
        functools.partial(join_kernel, plan, len(arrays)),
        grid_spec=pltpu.PrefetchScalarGridSpec(
            num_scalar_prefetch=1,
            grid=(1,),
            in_specs=[pl.BlockSpec(array.shape, zeros) for array in arrays],
            out_specs=[pl.BlockSpec(out, lambda i, at: (0, 0, 0)) for out in outs],
        ),
        out_shape=[jax.ShapeDtypeStruct(out, jnp.float32) for out in outs],
        compiler_params=kernel_params(),
        cost_estimate=pl.CostEstimate(flops=0, bytes_accessed=4_000_000, transcendentals=0),
    )(at, *arrays)


def local(
    fast,
    inputs,
    cotangent,
    segment,
    parent,
    clusters,
    *weights,
):
    pieces = {}
    if fast:
        place = Place()
        at = place.at
        shards = dict(enumerate(weights))
        shards["vectors"] = jnp.pad(
            jnp.concatenate([weights[member] for member in VECTORS], axis=1),
            ((0, 16 - LAYERS), (0, 0)),
        )
        trees = parent.shape[0]
        sizes = [weights[number].shape[1] for number in VECTORS]
        slots, bias, *vectors, qkv, _ = gather(
            shards,
            ((0, 0, True, 1, 1), ("vectors", None, False, 1, 1)),
            prep_steps,
            (
                parent,
                segment.reshape(trees, 1, TREE_LEN),
                clusters.reshape(PAIRS, 2, trees, TREE_LEN).transpose(2, 0, 1, 3),
            ),
            [
                jax.ShapeDtypeStruct((trees, PAIRS, 2, TREE_LEN), jnp.int32),
                jax.ShapeDtypeStruct((trees, HEADS, TREE_LEN, LANES), jnp.bfloat16),
                *[
                    jax.ShapeDtypeStruct((LAYERS, CHIPS_Z * CHIPS_X * size), jnp.float32)
                    for size in sizes
                ],
            ],
            1,
            functools.partial(spread_vectors, sizes),
        )
        whole = {(0, 0): qkv}

        def attend_layer(layer, projected):
            last = layer + 1 == LAYERS
            if last:
                wanted = [(6, layer, True, 1, 1), (2, layer, True, 1, 1), (8, layer, False, 1, 1)]
            else:
                wanted = [(6, layer, True, 1, 1), (8, layer, True, 1, 1)]
                wanted += [(0, layer + 1, False, 1, 1), (2, layer, False, 1, 1)]
            results = gather(
                shards, wanted, attend_steps, (projected, slots, bias), attend_shapes(trees), 2 + layer
            )
            for (number, at_layer, *_), array in zip(wanted, results[4:]):
                whole[at_layer, number] = array
            return results[:4]

        def get(layer, number):
            return whole[layer, number]

        def attend_back_layer(layer, grad_context, heads, groups, waiting):
            flat, pair = cut_sums(place, groups)
            proj, head_sums, *ends = reduce_sums(
                [flat],
                [pair, *waiting],
                [],
                2 + LAYERS + layer,
                attend_back_steps,
                (slots, grad_context, *heads),
                attend_back_shapes(trees),
            )
            pieces[layer, "flat"] = ends[:2]
            pieces[layer, 6] = ends[2]
            if waiting:
                pieces[layer + 1, 0] = ends[3]
            return proj, head_sums

    else:
        slots, bias = prepare(segment, parent, clusters)
        vectors = [
            lax.all_gather(weights[number], "shard", axis=1, tiled=True).astype(jnp.float32)
            for number in VECTORS
        ]

        def attend_layer(layer, projected):
            return attend(projected, slots, bias)

        def get(layer, number):
            return lax.all_gather(weights[number][layer], "shard", axis=0, tiled=True)

        def own_sum(left, right):
            if right.ndim == 3:
                right = right.transpose(1, 0, 2).reshape(right.shape[1], -1)
            total = contract_first(left, right)
            total = lax.psum_scatter(total, "shard", scatter_dimension=0, tiled=True)
            return lax.psum(total.astype(jnp.bfloat16), "rep").astype(jnp.float32)

        def attend_back_layer(layer, grad_context, heads, groups, waiting):
            for grads, _ in groups:
                for grad in grads:
                    pieces[layer, grad.number] = own_sum(grad.left, grad.right)
            return attend_back(grad_context, slots, heads)

    vector = dict(zip(VECTORS, vectors))
    hidden, hidden_low = inputs, inputs
    saved = []
    for layer in range(LAYERS):
        pull = functools.partial(get, layer)
        projected = project(layer, hidden_low, pull(0), vector[1])
        context, *heads = attend_layer(layer, projected)
        entered = hidden_low
        middle, act, slope, *norms, hidden, hidden_low = feed(
            layer,
            context,
            hidden,
            [pull(2), pull(6), pull(8)],
            [vector[number] for number in (3, 4, 5, 7, 9, 10, 11)],
        )
        saved.append((entered, heads, context, middle, act, slope, norms))
    result = hidden_low
    above, proj = cotangent, None
    sums, waiting = [None] * LAYERS, []
    for layer in reversed(range(LAYERS)):
        entered, heads, context, middle, act, slope, norms = saved[layer]
        pull = functools.partial(get, layer)
        down, grad_pre, grad_attn, attn_low, grad_context, row_sums, ffin_sum = feed_back(
            layer,
            above,
            proj,
            None if proj is None else get(layer + 1, 0),
            [norms[2], norms[3], slope, norms[0], norms[1]],
            [pull(2), pull(6), pull(8)],
            [vector[4], vector[10]],
        )
        wide = grad_pre.shape[1] // CORES
        groups = (
            (
                (
                    Grad(8, act, down, act.shape[1] // D, UNIT),
                    Grad(2, context, attn_low, 1, UNIT),
                ),
                False,
            ),
            ((Grad(6, middle, grad_pre, wide // D, D),), True),
        )
        proj, head_sums = attend_back_layer(layer, grad_context, heads, groups, waiting)
        sums[layer] = [row_sums, ffin_sum, head_sums]
        above = grad_attn
        last = Grad(0, entered, proj, 3, UNIT)
        if not fast:
            pieces[layer, 0] = own_sum(last.left, last.right)
        elif layer:
            waiting = cut_sums(place, [((last,), True)])
    grad_input = input_grad(above, proj, get(0, 0))
    sums = [item for layer in sums for item in layer]
    if fast:
        (pair,) = cut_sums(place, [((last,), True)])
        pair, grad_input = lax.optimization_barrier((pair, grad_input))
        pieces[0, 0], total = reduce_sums([], [pair], sums, 0)
    else:
        norms, wide, heads = [], [], []
        for row_sums, ffin_sum, head_sums in (sums[:3], sums[3:]):
            norms.append(row_sums)
            wide.append(ffin_sum.reshape(-1, D))
            heads.append(head_sums.sum(0).transpose(1, 0, 2).reshape(8, D))
        total = lax.psum(jnp.concatenate(norms + wide + heads), AXES)
    count = lax.axis_size("shard")
    shard = lax.axis_index("shard")
    ffin_rows = sums[1].shape[1] // D

    def share(rows):
        stacked = jnp.stack([total[row].reshape(-1) for row in rows])
        width = stacked.shape[1] // count
        return lax.dynamic_slice_in_dim(stacked, shard * width, width, axis=1)

    starts = [0, 8, 16, 16 + ffin_rows]
    heads_at = [16 + 2 * ffin_rows, 24 + 2 * ffin_rows]
    grads = {
        1: share([slice(at, at + 3, 2) for at in heads_at]),
        7: share([slice(at, at + ffin_rows) for at in starts[2:]]),
    }
    for number, row in ((10, 0), (11, 1), (9, 2), (4, 3), (5, 4), (3, 5)):
        grads[number] = share([row, 8 + row])
    if fast:
        rows = {number: weights[number].shape[1] for number in MATRICES}
        parts = {number: weights[number].shape[2] // (CORES * UNIT) for number in MATRICES}
        known = [{} for _ in range(LAYERS)]
        for layer in range(LAYERS):
            start = 0
            for number in (8, 2):
                known[layer][number] = (pieces[layer, "flat"], start, rows[number])
                start += rows[number] * parts[number]
            for number in (6, 0):
                end = pieces[layer, number]
                end = end.reshape(end.shape[0], -1, end.shape[-1])
                known[layer][number] = (list(end), 0, rows[number] // CHIPS_Y)
        for numbers in (MATRICES,):
            shapes = {number: weights[number].shape[1:] for number in numbers}
            grads.update(zip(numbers, join(place.at, known, shapes)))
    else:
        for number in MATRICES:
            grads[number] = jnp.stack([pieces[layer, number] for layer in range(LAYERS)])
    return (result, grad_input, *[grads[number] for number in range(12)])


def solution(mesh):
    in_specs = (
        P(("rep", "shard"), None),
        P(("rep", "shard"), None),
        P(("rep", "shard")),
        P(("rep", "shard"), None),
        P(None, ("rep", "shard")),
        P(None, "shard", None),
        P(None, "shard"),
        P(None, "shard", None),
        P(None, "shard"),
        P(None, "shard"),
        P(None, "shard"),
        P(None, "shard", None),
        P(None, "shard"),
        P(None, "shard", None),
        P(None, "shard"),
        P(None, "shard"),
        P(None, "shard"),
    )
    out_specs = (
        P(("rep", "shard"), None),
        P(("rep", "shard"), None),
        P(None, "shard", None),
        P(None, "shard"),
        P(None, "shard", None),
        P(None, "shard"),
        P(None, "shard"),
        P(None, "shard"),
        P(None, "shard", None),
        P(None, "shard"),
        P(None, "shard", None),
        P(None, "shard"),
        P(None, "shard"),
        P(None, "shard"),
    )
    fast = mesh.shape["rep"] == CHIPS_Y * CORES and mesh.shape["shard"] == CHIPS_Z * CHIPS_X
    return jax.shard_map(
        functools.partial(local, fast),
        mesh=mesh,
        in_specs=in_specs,
        out_specs=out_specs,
        check_vma=False,
    )
```

```python
import functools

import jax
import jax.numpy as jnp
from jax import lax
from jax.experimental import pallas as pl
from jax.experimental.pallas import tpu as pltpu
from jax.sharding import PartitionSpec as P

D = 768
HEADS = 12
HEAD_DIM = 64
LAYERS = 2
CLUSTER = 128
TREE_LEN = 1024
SEGMENTS = 13
PAIRS = HEADS // 2
LANES = 2 * HEAD_DIM
KERNEL_VMEM = 60 * 2**20
ROW_TILE = 256
FEED_TILE = 768
DEPTH_TILE = 384
INV_ROOT = (2.0 * 3.141592653589793) ** -0.5
MATRICES = (0, 2, 6, 8)
VECTORS = (1, 3, 4, 5, 7, 9, 10, 11)
UNIT = 384
AXES = ("rep", "shard")
CHIPS_Z, CHIPS_X, CHIPS_Y, CORES = 4, 2, 2, 2
norm_eps = 1e-06


def one_hot_rows(slot_row):
    length = slot_row.shape[-1]
    rows = lax.broadcasted_iota(jnp.int32, (length, length), 0)
    return jnp.where(rows == slot_row, 1.0, 0.0).astype(jnp.bfloat16)


def first_lanes(length):
    return lax.broadcasted_iota(jnp.int32, (length, LANES), 1) < HEAD_DIM


def contract_last(left_side, right_side):
    return lax.dot_general(
        left_side, right_side, (((1,), (1,)), ((), ())), preferred_element_type=jnp.float32
    )


def contract_first(left_side, right_side):
    return lax.dot_general(
        left_side, right_side, (((0,), (0,)), ((), ())), preferred_element_type=jnp.float32
    )


def cluster_blocks(values):
    return [values[at : at + CLUSTER] for at in range(0, values.shape[0], CLUSTER)]


def attend_pair(slots, query, key, value, bias, store):
    low = first_lanes(TREE_LEN)
    query = query * jnp.bfloat16(HEAD_DIM**-0.5)
    packed = (
        jnp.where(low, query, pltpu.roll(key, HEAD_DIM, 1)),
        jnp.where(low, pltpu.roll(query, HEAD_DIM, 1), key),
    )
    context = []
    for head in range(2):
        table = one_hot_rows(slots[head : head + 1])
        joined = jnp.concatenate([packed[head], value], axis=1)
        found = jnp.dot(table, joined, preferred_element_type=jnp.float32).astype(jnp.bfloat16)
        both, values = found[:, :LANES], found[:, LANES:]
        store("both", head, both)
        store("values", head, values)
        queries = jnp.where(low, both, jnp.bfloat16(0))
        keys = pltpu.roll(both, HEAD_DIM, 1)
        scores = jnp.concatenate(
            [contract_last(q, k) for q, k in zip(cluster_blocks(queries), cluster_blocks(keys))],
            axis=0,
        )
        scores = scores + bias[head].astype(jnp.float32)
        numerator = jnp.exp(scores - jnp.max(scores, axis=1, keepdims=True))
        total = jnp.sum(numerator, axis=1, keepdims=True)
        soft = (numerator * (1.0 / total)).astype(jnp.bfloat16)
        store("soft", head, soft)
        out = jnp.concatenate(
            [
                jnp.dot(p, v, preferred_element_type=jnp.float32)
                for p, v in zip(cluster_blocks(soft), cluster_blocks(values))
            ],
            axis=0,
        ).astype(jnp.bfloat16)
        context.append(contract_first(table, out))
        if head == 0:
            yield
    store("context", None, jnp.where(low, context[0], context[1]).astype(jnp.bfloat16))


def attend_kernel(slot_ref, query_ref, key_ref, value_ref, bias_ref, ctx_ref, qk_ref, val_ref, p_ref):
    refs = {"both": qk_ref, "values": val_ref, "soft": p_ref}

    def store(name, head, value):
        if head is None:
            ctx_ref[...] = value
        else:
            refs[name][0, head] = value

    for _ in attend_pair(
        slot_ref[0, 0], query_ref[...], key_ref[...], value_ref[...], bias_ref[0], store
    ):
        pass


def attend_steps(ins, outs):
    projected_ref, slot_ref, bias_ref = ins
    ctx_ref, qk_ref, val_ref, p_ref = outs
    refs = {"both": qk_ref, "values": val_ref, "soft": p_ref}
    for tree in range(slot_ref.shape[0]):
        rows = slice(tree * TREE_LEN, (tree + 1) * TREE_LEN)
        for pair in range(PAIRS):
            lanes = [slice((part * PAIRS + pair) * LANES, (part * PAIRS + pair + 1) * LANES) for part in range(3)]
            heads = slice(2 * pair, 2 * pair + 2)

            def store(name, head, value):
                if head is None:
                    ctx_ref[rows, lanes[0]] = value
                else:
                    refs[name][tree, 2 * pair + head] = value

            yield from attend_pair(
                slot_ref[tree, pair],
                *[projected_ref[rows, part] for part in lanes],
                bias_ref[tree, heads],
                store,
            )
            yield


def attend_back_pair(slots, grads, both_of, values_of, soft_of, store):
    low = first_lanes(TREE_LEN)
    placed = []
    for head in range(2):
        table = one_hot_rows(slots[head : head + 1])
        found = jnp.dot(table, grads, preferred_element_type=jnp.float32)
        found = jnp.where(low == (head == 0), found, 0.0).astype(jnp.bfloat16)
        both, values, soft = both_of(head), values_of(head), soft_of(head)
        grad_soft = jnp.concatenate(
            [contract_last(g, v) for g, v in zip(cluster_blocks(found), cluster_blocks(values))],
            axis=0,
        )
        grad_value = jnp.concatenate(
            [contract_first(p, g) for p, g in zip(cluster_blocks(soft), cluster_blocks(found))],
            axis=0,
        ).astype(jnp.bfloat16)
        weights = soft.astype(jnp.float32)
        delta = jnp.sum(weights * grad_soft, axis=1, keepdims=True)
        grad_scores = (weights * (grad_soft - delta)).astype(jnp.bfloat16)
        pairs = list(zip(cluster_blocks(grad_scores), cluster_blocks(both)))
        by_key = jnp.concatenate([contract_first(s, b) for s, b in pairs], axis=0)
        by_query = jnp.concatenate(
            [jnp.dot(s, b, preferred_element_type=jnp.float32) for s, b in pairs], axis=0
        )
        mixed = jnp.where(low, by_key, by_query * HEAD_DIM**-0.5).astype(jnp.bfloat16)
        joined = jnp.concatenate([mixed, grad_value], axis=1)
        placed.append(contract_first(table, joined))
        if head == 0:
            yield
    first, second = placed
    queries = jnp.where(low, pltpu.roll(first[:, :LANES], HEAD_DIM, 1), second[:, :LANES])
    keys = jnp.where(low, first[:, :LANES], pltpu.roll(second[:, :LANES], HEAD_DIM, 1))
    values = jnp.where(low, first[:, LANES:], second[:, LANES:])
    sums = []
    for part, grad in enumerate((queries, keys, values)):
        rounded = grad.astype(jnp.bfloat16)
        store(part, rounded)
        sums.append(rows_sum(rounded.astype(jnp.float32)))
    store(None, jnp.concatenate(sums + [jnp.zeros((5, LANES), jnp.float32)], axis=0))


def attend_back_kernel(slot_ref, grad_ref, qk_ref, val_ref, p_ref, out_ref, sums_ref):
    def store(part, value):
        if part is None:
            sums_ref[0, 0] = value
        else:
            out_ref[part] = value

    refs = [lambda head, ref=ref: ref[0, head] for ref in (qk_ref, val_ref, p_ref)]
    for _ in attend_back_pair(slot_ref[0, 0], grad_ref[...], *refs, store):
        pass


def attend_back_steps(ins, outs):
    slot_ref, grad_ref, *kept = ins
    out_ref, sums_ref = outs
    for tree in range(slot_ref.shape[0]):
        rows = slice(tree * TREE_LEN, (tree + 1) * TREE_LEN)
        for pair in range(PAIRS):
            lanes = slice(pair * LANES, (pair + 1) * LANES)

            def store(part, value):
                if part is None:
                    sums_ref[tree, pair] = value
                else:
                    out_ref[part, rows, lanes] = value

            refs = [lambda head, ref=ref: ref[tree, 2 * pair + head] for ref in kept]
            yield from attend_back_pair(slot_ref[tree, pair], grad_ref[rows, lanes], *refs, store)
            yield


def slot_spec(start=0):
    return pl.BlockSpec((1, 1, 2, TREE_LEN), lambda tree, pair: (tree, start + pair, 0, 0))


def head_spec(start=0):
    return pl.BlockSpec((1, 2, TREE_LEN, LANES), lambda tree, pair: (tree, start + pair, 0, 0))


def column_spec(offset):
    return pl.BlockSpec((TREE_LEN, LANES), lambda tree, pair: (tree, offset + pair))


def kernel_params():
    return pltpu.CompilerParams(vmem_limit_bytes=KERNEL_VMEM)


def attend_shapes(trees):
    stored = jax.ShapeDtypeStruct((trees, HEADS, TREE_LEN, LANES), jnp.bfloat16)
    return [jax.ShapeDtypeStruct((trees * TREE_LEN, D), jnp.bfloat16), stored, stored, stored]


def attend(projected, slots, bias):
    trees = slots.shape[0]
    return pl.pallas_call(
        attend_kernel,
        grid=(trees, PAIRS),
        in_specs=[
            slot_spec(),
            column_spec(0),
            column_spec(PAIRS),
            column_spec(2 * PAIRS),
            head_spec(),
        ],
        out_specs=[column_spec(0), head_spec(), head_spec(), head_spec()],
        out_shape=attend_shapes(trees),
        compiler_params=kernel_params(),
        cost_estimate=pl.CostEstimate(
            flops=trees * 30_000_000_000, bytes_accessed=trees * 20_000_000, transcendentals=0
        ),
    )(slots, projected, projected, projected, bias)


def attend_back_shapes(trees):
    return [
        jax.ShapeDtypeStruct((3, trees * TREE_LEN, D), jnp.bfloat16),
        jax.ShapeDtypeStruct((trees, PAIRS, 8, LANES), jnp.float32),
    ]


def attend_back(grad_context, slots, kept):
    trees = slots.shape[0]
    return pl.pallas_call(
        attend_back_kernel,
        grid=(trees, PAIRS),
        in_specs=[slot_spec(), column_spec(0), head_spec(), head_spec(), head_spec()],
        out_specs=[
            pl.BlockSpec((3, TREE_LEN, LANES), lambda tree, pair: (0, tree, pair)),
            pl.BlockSpec((1, 1, 8, LANES), lambda tree, pair: (tree, pair, 0, 0)),
        ],
        out_shape=attend_back_shapes(trees),
        compiler_params=kernel_params(),
        cost_estimate=pl.CostEstimate(
            flops=trees * 35_000_000_000, bytes_accessed=trees * 20_000_000, transcendentals=0
        ),
    )(slots, grad_context, *kept)


def erf_parts(values):
    size = jnp.abs(values)
    turn = 1.0 / (1.0 + (0.3275911 * 0.5**0.5) * size)
    bell = jnp.exp(-0.5 * values * values)
    series = 1.061405429 * 0.5
    for factor in (-1.453152027, 1.421413741, -0.284496736, 0.254829592):
        series = series * turn + factor * 0.5
    tail = series * turn * bell
    return jnp.where(values < 0.0, tail, 1.0 - tail), bell


def norm_parts(values):
    centred = values - jnp.mean(values, axis=-1, keepdims=True)
    scale = lax.rsqrt(jnp.mean(centred * centred, axis=-1, keepdims=True) + norm_eps)
    return centred * scale, scale


def norm_back(grad, normal, scale, gain):
    inner = grad * gain
    mean = jnp.mean(inner, axis=-1, keepdims=True)
    along = jnp.mean(inner * normal, axis=-1, keepdims=True)
    return scale * (inner - mean - normal * along)


def spread(column):
    return jnp.broadcast_to(column, (column.shape[0], 128))


def rows_sum(values):
    return jnp.sum(values, axis=0, keepdims=True)


def project_kernel(layer, rows_ref, weight_ref, bias_ref, out_ref):
    product = jnp.dot(rows_ref[...], weight_ref[...], preferred_element_type=jnp.float32)
    bias = bias_ref[layer : layer + 1]
    out_ref[:, :D] = (product[:, :D] + bias[:, :D]).astype(jnp.bfloat16)
    out_ref[:, D : 2 * D] = product[:, D : 2 * D].astype(jnp.bfloat16)
    out_ref[:, 2 * D :] = (product[:, 2 * D :] + bias[:, D:]).astype(jnp.bfloat16)


def feed_kernel(
    layer,
    context_ref,
    rows_ref,
    out_weight_ref,
    ffin_weight_ref,
    ffout_weight_ref,
    out_bias_ref,
    attn_gain_ref,
    attn_shift_ref,
    ffin_bias_ref,
    ffout_bias_ref,
    ffn_gain_ref,
    ffn_shift_ref,
    hidden_ref,
    act_ref,
    slope_ref,
    attn_normal_ref,
    attn_scale_ref,
    ffn_normal_ref,
    ffn_scale_ref,
    result_ref,
    result_low_ref,
):
    here = slice(layer, layer + 1)
    product = jnp.dot(context_ref[...], out_weight_ref[...], preferred_element_type=jnp.float32)
    attn_sum = rows_ref[...].astype(jnp.float32) + product + out_bias_ref[here]
    normal, scale = norm_parts(attn_sum)
    attn_normal_ref[...] = normal
    attn_scale_ref[...] = spread(scale)
    hidden = normal * attn_gain_ref[here] + attn_shift_ref[here]
    hidden_low = hidden.astype(jnp.bfloat16)
    hidden_ref[...] = hidden_low
    total = hidden + ffout_bias_ref[here]
    width = ffin_weight_ref.shape[1]
    for at in range(0, width, FEED_TILE):
        part = slice(at, at + FEED_TILE)
        pre = (
            jnp.dot(hidden_low, ffin_weight_ref[:, part], preferred_element_type=jnp.float32)
            + ffin_bias_ref[here, part]
        )
        below, bell = erf_parts(pre)
        act = (pre * below).astype(jnp.bfloat16)
        act_ref[:, part] = act
        slope_ref[:, part] = (below + pre * bell * INV_ROOT).astype(jnp.bfloat16)
        total = total + jnp.dot(
            act, ffout_weight_ref[part, :], preferred_element_type=jnp.float32
        )
    normal, scale = norm_parts(total)
    ffn_normal_ref[...] = normal
    ffn_scale_ref[...] = spread(scale)
    result = normal * ffn_gain_ref[here] + ffn_shift_ref[here]
    result_ref[...] = result
    result_low_ref[...] = result.astype(jnp.bfloat16)


def add_projected(grad, proj_ref, weight_ref):
    for part in range(3):
        grad = grad + contract_last(proj_ref[part], weight_ref[:, part * D : (part + 1) * D])
    return grad


def feed_back_kernel(layer, with_proj, *refs):
    here = slice(layer, layer + 1)
    if with_proj:
        above_ref, proj_ref, qkv_weight_ref, *refs = refs
        grad = add_projected(above_ref[...], proj_ref, qkv_weight_ref)
    else:
        above_ref, *refs = refs
        grad = above_ref[...].astype(jnp.float32)
    (
        ffn_normal_ref,
        ffn_scale_ref,
        slope_ref,
        attn_normal_ref,
        attn_scale_ref,
        out_weight_ref,
        ffin_weight_ref,
        ffout_weight_ref,
        attn_gain_ref,
        ffn_gain_ref,
        down_ref,
        pre_ref,
        attn_ref,
        attn_low_ref,
        context_ref,
        sums_ref,
        ffin_sum_ref,
    ) = refs

    @pl.when(pl.program_id(0) == 0)
    def _():
        sums_ref[...] = jnp.zeros_like(sums_ref)
        ffin_sum_ref[...] = jnp.zeros_like(ffin_sum_ref)

    normal = ffn_normal_ref[...]
    sums_ref[0:1] += rows_sum(grad * normal)
    sums_ref[1:2] += rows_sum(grad)
    grad_sum = norm_back(grad, normal, ffn_scale_ref[:, 0:1], ffn_gain_ref[here])
    down = grad_sum.astype(jnp.bfloat16)
    down_ref[...] = down
    sums_ref[2:3] += rows_sum(down.astype(jnp.float32))
    total = grad_sum
    width = ffin_weight_ref.shape[1]
    for at in range(0, width, FEED_TILE):
        part = slice(at, at + FEED_TILE)
        grad_act = contract_last(down, ffout_weight_ref[part, :])
        pre = (grad_act * slope_ref[:, part].astype(jnp.float32)).astype(jnp.bfloat16)
        pre_ref[:, part] = pre
        ffin_sum_ref[:, part] += rows_sum(pre.astype(jnp.float32))
        total = total + contract_last(pre, ffin_weight_ref[:, part])
    normal = attn_normal_ref[...]
    sums_ref[3:4] += rows_sum(total * normal)
    sums_ref[4:5] += rows_sum(total)
    attn = norm_back(total, normal, attn_scale_ref[:, 0:1], attn_gain_ref[here])
    attn_ref[...] = attn
    low = attn.astype(jnp.bfloat16)
    attn_low_ref[...] = low
    sums_ref[5:6] += rows_sum(low.astype(jnp.float32))
    context_ref[...] = contract_last(low, out_weight_ref[...]).astype(jnp.bfloat16)


def input_grad_kernel(above_ref, proj_ref, weight_ref, out_ref):
    out_ref[...] = add_projected(above_ref[...], proj_ref, weight_ref)


def prep_pair(parent_ref, segment_ref, cluster_ref, slot_ref, bias_ref, row, tree, pair):
    segs = segment_ref[tree]
    length = segs.shape[1]

    def parent_of(values):
        found = jnp.zeros_like(values)
        for number in range(SEGMENTS):
            found = jnp.where(values == number, parent_ref[row, number], found)
        return found

    parents = parent_of(segs)
    grands = parent_of(parents)
    ids = jnp.concatenate([segs, parents, grands, jnp.zeros((5, length), jnp.int32)], axis=0)
    ids = jnp.concatenate([ids, jnp.zeros((8, length), jnp.int32)], axis=0)
    ids = ids.astype(jnp.float32).astype(jnp.bfloat16)
    count = length // CLUSTER
    order = lax.broadcasted_iota(jnp.int32, (count, length), 0)
    lanes = lax.broadcasted_iota(jnp.int32, (count, length), 1)
    for head in range(2):
        member = order == cluster_ref[tree, pair, head : head + 1, :]
        ranks = member.astype(jnp.int32)
        step = 1
        while step < length:
            ranks = ranks + jnp.where(lanes >= step, pltpu.roll(ranks, step, 1), 0)
            step *= 2
        slot = jnp.sum(
            jnp.where(member, ranks - 1 + CLUSTER * order, 0), axis=0, keepdims=True
        )
        slot_ref[tree, pair, head : head + 1, :] = slot
        table = one_hot_rows(slot)
        rows = contract_last(ids, table)
        columns = jnp.concatenate([rows] * (128 // rows.shape[0]), axis=0).T
        for at in range(0, length, CLUSTER):
            here = rows[0:1, at : at + CLUSTER]
            block = columns[at : at + CLUSTER]
            allowed = (
                (here == block[:, 0:1]) | (here == block[:, 1:2]) | (here == block[:, 2:3])
            )
            bias_ref[tree, 2 * pair + head, at : at + CLUSTER, :] = jnp.where(allowed, 0.0, -1e30).astype(
                jnp.bfloat16
            )


def prep_kernel(*refs):
    prep_pair(*refs, pl.program_id(0), 0, 0)


def row_spec(width, rows=ROW_TILE):
    return pl.BlockSpec((rows, width), lambda i: (i, 0))


def whole_spec(shape):
    return pl.BlockSpec(
        shape, lambda i: (0,) * len(shape), pipeline_mode=pl.Buffered(1)
    )


def part_spec(rows=ROW_TILE):
    return pl.BlockSpec((3, rows, D), lambda i: (0, i, 0))


def cost(flops, *arrays):
    moved = sum(array.size * array.dtype.itemsize for array in arrays)
    return pl.CostEstimate(flops=int(flops), bytes_accessed=moved, transcendentals=0)


def shape_of(rows, width, kind=jnp.bfloat16):
    return jax.ShapeDtypeStruct((rows, width), kind)


def project(layer, rows, weight, bias):
    count, width = rows.shape[0], weight.shape[1]
    return pl.pallas_call(
        functools.partial(project_kernel, layer),
        grid=(count // ROW_TILE,),
        in_specs=[row_spec(D), whole_spec(weight.shape), whole_spec(bias.shape)],
        out_specs=row_spec(width),
        out_shape=shape_of(count, width),
        compiler_params=kernel_params(),
        cost_estimate=cost(2.4 * count * D * width, rows, weight),
    )(rows, weight, bias)


def feed(layer, context, rows, weights, vectors):
    count = context.shape[0]
    width = weights[1].shape[1]
    f32 = jnp.float32
    return pl.pallas_call(
        functools.partial(feed_kernel, layer),
        grid=(count // ROW_TILE,),
        in_specs=[row_spec(D), row_spec(D)]
        + [whole_spec(weight.shape) for weight in weights]
        + [whole_spec(vector.shape) for vector in vectors],
        out_specs=[
            row_spec(D),
            row_spec(width),
            row_spec(width),
            row_spec(D),
            row_spec(128),
            row_spec(D),
            row_spec(128),
            row_spec(D),
            row_spec(D),
        ],
        out_shape=[
            shape_of(count, D),
            shape_of(count, width),
            shape_of(count, width),
            shape_of(count, D, f32),
            shape_of(count, 128, f32),
            shape_of(count, D, f32),
            shape_of(count, 128, f32),
            shape_of(count, D, f32),
            shape_of(count, D),
        ],
        compiler_params=kernel_params(),
        cost_estimate=cost(5 * count * D * (2 * width + D), context, *weights),
    )(context, rows, *weights, *vectors)


def feed_back(layer, above, proj, qkv_weight, saved, weights, gains):
    count = above.shape[0]
    width = weights[1].shape[1]
    f32 = jnp.float32
    lead, lead_specs = [above], [row_spec(D)]
    if proj is not None:
        lead += [proj, qkv_weight]
        lead_specs += [part_spec(), whole_spec(qkv_weight.shape)]
    return pl.pallas_call(
        functools.partial(feed_back_kernel, layer, proj is not None),
        grid=(count // ROW_TILE,),
        in_specs=lead_specs
        + [row_spec(D), row_spec(128), row_spec(width), row_spec(D), row_spec(128)]
        + [whole_spec(weight.shape) for weight in weights]
        + [whole_spec(gain.shape) for gain in gains],
        out_specs=[
            row_spec(D),
            row_spec(width),
            row_spec(D),
            row_spec(D),
            row_spec(D),
            pl.BlockSpec((8, D), lambda i: (0, 0)),
            pl.BlockSpec((1, width), lambda i: (0, 0)),
        ],
        out_shape=[
            shape_of(count, D),
            shape_of(count, width),
            shape_of(count, D, f32),
            shape_of(count, D),
            shape_of(count, D),
            shape_of(8, D, f32),
            shape_of(1, width, f32),
        ],
        compiler_params=kernel_params(),
        cost_estimate=cost(5 * count * D * (2 * width + D), above, *weights),
    )(*lead, *saved, *weights, *gains)


def input_grad(above, proj, qkv_weight):
    count = above.shape[0]
    return pl.pallas_call(
        input_grad_kernel,
        grid=(count // ROW_TILE,),
        in_specs=[
            row_spec(D),
            part_spec(),
            whole_spec(qkv_weight.shape),
        ],
        out_specs=row_spec(D),
        out_shape=shape_of(count, D, jnp.float32),
        compiler_params=kernel_params(),
        cost_estimate=cost(2.4 * count * D * 3 * D, above, qkv_weight),
    )(above, proj, qkv_weight)


def prepare(segment, parent, clusters):
    trees = parent.shape[0]
    segment = segment.reshape(trees, 1, TREE_LEN)
    clusters = clusters.reshape(PAIRS, 2, trees, TREE_LEN).transpose(2, 0, 1, 3)
    return pl.pallas_call(
        prep_kernel,
        grid=(trees, PAIRS),
        in_specs=[
            pl.BlockSpec(memory_space=pltpu.SMEM),
            pl.BlockSpec((1, 1, TREE_LEN), lambda tree, pair: (tree, 0, 0)),
            slot_spec(),
        ],
        out_specs=[slot_spec(), head_spec()],
        out_shape=[
            jax.ShapeDtypeStruct((trees, PAIRS, 2, TREE_LEN), jnp.int32),
            jax.ShapeDtypeStruct((trees, HEADS, TREE_LEN, LANES), jnp.bfloat16),
        ],
        compiler_params=kernel_params(),
        cost_estimate=pl.CostEstimate(
            flops=trees * 20_000_000_000, bytes_accessed=trees * 4_000_000, transcendentals=0
        ),
    )(parent, segment, clusters)


def weight_grad_kernel(split_y, at_ref, left_ref, right_ref, *refs):
    product = contract_first(
        left_ref[...].reshape(left_ref.shape[-2:]), right_ref[...].reshape(right_ref.shape[-2:])
    )
    if split_y is None:
        (out_ref,) = refs
        out_ref[...] = product.astype(jnp.bfloat16).reshape(out_ref.shape)
        return
    near_ref, (send_ref, keep_ref, sum_ref) = refs[0], refs[-3:]
    total = product + near_ref[...].astype(jnp.float32).reshape(product.shape)
    sum_ref[...] = total.astype(jnp.bfloat16).reshape(sum_ref.shape)
    if split_y:
        send_ref[0] = sum_ref[:, :, 1 - at_ref[2]]
        keep_ref[0] = sum_ref[:, :, at_ref[2]]
    else:
        send_ref[...] = sum_ref[:, 1 - at_ref[1]]
        keep_ref[...] = sum_ref[:, at_ref[1]]


class Grad:
    def __init__(self, number, left, right, tiles, half):
        self.number = number
        self.left, self.right = left, right
        self.tiles, self.half = tiles, half
        self.depth = left.shape[1]
        self.parts = 1 if self.depth > D else tiles
        self.rows = self.depth // (CHIPS_Z * CHIPS_X)

    def product(self, at, other, split_y=None, near=None, start=0, total=0, before=()):
        flip = 1 if other else 0
        left, right = self.left, self.right
        count = left.shape[0]
        tall = self.depth > D
        core = lambda at: lax.rem(at[3] + flip, CORES)
        in_specs = [
            pl.BlockSpec((count, D), (lambda i, at: (0, i)) if tall else (lambda i, at: (0, 0)))
        ]
        if right.ndim == 3:
            in_specs.append(pl.BlockSpec((1, count, self.half), lambda i, at: (i, 0, core(at))))
        elif tall:
            in_specs.append(pl.BlockSpec((count, self.half), lambda i, at: (0, core(at))))
        else:
            in_specs.append(
                pl.BlockSpec((count, self.half), lambda i, at: (0, core(at) * self.tiles + i))
            )
        zs = D // (self.rows * CHIPS_X)
        place = (lambda i: (0, i)) if tall else (lambda i: (i, 0))
        whole = (self.parts, CHIPS_Z, CHIPS_X, self.rows, self.half)
        block = (1, zs, CHIPS_X, self.rows, self.half)
        full = pl.BlockSpec(block, lambda i, at: (*place(i), 0, 0, 0))
        args, scratch = [left, right], []
        if split_y is None:
            out_specs, shapes = full, jax.ShapeDtypeStruct(whole, jnp.bfloat16)
        else:
            in_specs.append(full)
            args.append(near)
            in_specs += [pl.BlockSpec(memory_space=pl.ANY)] * len(before)
            args += before
            if split_y:
                short = self.rows // CHIPS_Y
                kept = (CHIPS_X, short, self.half)
                scratch = [pltpu.VMEM((zs, CHIPS_X, CHIPS_Y, short, self.half), jnp.bfloat16)]
                spec = pl.BlockSpec((1, zs, *kept), lambda i, at: (*place(i), 0, 0, 0))
                shape = (self.parts, CHIPS_Z, *kept)
            else:
                scratch = [pltpu.VMEM((zs, CHIPS_X, self.rows, self.half), jnp.bfloat16)]
                first = start // self.rows
                index = (lambda i, at: (i, first, 0)) if tall else (lambda i, at: (0, first + i, 0))
                spec = pl.BlockSpec((zs, self.rows, self.half), index)
                shape = (CHIPS_Z, total, self.half)
            out_specs, shapes = [spec] * 2, [jax.ShapeDtypeStruct(shape, jnp.bfloat16)] * 2
        return pl.pallas_call(
            functools.partial(weight_grad_kernel, split_y),
            grid_spec=pltpu.PrefetchScalarGridSpec(
                num_scalar_prefetch=1,
                grid=(self.tiles,),
                in_specs=in_specs,
                out_specs=out_specs,
                scratch_shapes=scratch,
            ),
            out_shape=shapes,
            input_output_aliases={4 + place: place for place in range(len(before))},
            compiler_params=kernel_params(),
            cost_estimate=cost(4 * count * D * self.tiles * self.half, left, right),
        )(at, *args)


class Place:
    def __init__(self):
        rep = lax.axis_index("rep")
        shard = lax.axis_index("shard")
        self.y, self.core = rep // CORES, rep % CORES
        self.z, self.x = shard // CHIPS_X, shard % CHIPS_X
        self.at = jnp.stack([self.z, self.x, self.y, self.core]).astype(jnp.int32)


def hop(value, dz=0, dx=0, dy=0, dc=0):
    pairs = []
    for y in range(CHIPS_Y):
        for c in range(CORES):
            for z in range(CHIPS_Z):
                for x in range(CHIPS_X):
                    source = ((y * CORES + c) * CHIPS_Z + z) * CHIPS_X + x
                    y2, c2 = (y + dy) % CHIPS_Y, (c + dc) % CORES
                    z2, x2 = (z + dz) % CHIPS_Z, (x + dx) % CHIPS_X
                    pairs.append((source, ((y2 * CORES + c2) * CHIPS_Z + z2) * CHIPS_X + x2))
    return lax.ppermute(value, AXES, pairs)


def cut_sums(place, groups):
    at = place.at
    arrived = []
    for grads, _ in groups:
        arrived.append([hop(grad.product(at, True), dc=1) for grad in grads])
    found = []
    for (grads, y_first), near in zip(groups, arrived):
        total = sum(grad.parts * grad.rows for grad in grads)
        start, pair = 0, ()
        for grad, item in zip(grads, near):
            if y_first:
                pair = grad.product(at, False, True, item)
            else:
                pair = grad.product(at, False, False, item, start, total, tuple(pair))
            start += grad.parts * grad.rows
        found.append(tuple(pair))
    return found


def prep_steps(ins, outs):
    trees, pairs = ins[2].shape[:2]
    for tree in range(trees):
        for pair in range(pairs):
            prep_pair(*ins, *outs[:2], tree, tree, pair)
            yield


def gather_kernel(plan, arrays, ending, work, work_ins, work_outs, *refs):
    count = len(plan)
    own_ins, ins, refs = refs[:work_ins], refs[work_ins : work_ins + arrays], refs[work_ins + arrays :]
    own_outs, outs = refs[:work_outs], refs[work_outs : work_outs + arrays]
    sems, local_sem = refs[work_outs + arrays : -1], refs[-1]
    todo = work(own_ins, own_outs)
    rep, shard = lax.axis_index("rep"), lax.axis_index("shard")
    y, core = lax.div(rep, CORES), lax.rem(rep, CORES)
    z, x = lax.div(shard, CHIPS_X), lax.rem(shard, CHIPS_X)

    def device(dz=0, dx=0, dy=0, dc=0):
        to_y, to_core = lax.rem(y + dy, CHIPS_Y), lax.rem(core + dc, CORES)
        to_z, to_x = lax.rem(z + dz, CHIPS_Z), lax.rem(x + dx, CHIPS_X)
        return (to_y * CORES + to_core, to_z * CHIPS_X + to_x)

    mates = [dict(dx=1), dict(dy=1), dict(dc=1)] + [dict(dz=k) for k in range(1, CHIPS_Z)]
    barrier = pltpu.get_barrier_semaphore()
    for mate in mates:
        pl.semaphore_signal(
            barrier, inc=1, device_id=device(**mate), device_id_type=pl.DeviceIdType.MESH
        )
    sent = []

    def send(source, target, m, number, **step):
        copy = pltpu.make_async_remote_copy(
            src_ref=source,
            dst_ref=target,
            send_sem=sems[m].at[0, number],
            recv_sem=sems[m].at[1, number],
            device_id=device(**step),
            device_id_type=pl.DeviceIdType.MESH,
        )
        copy.start()
        sent.append(copy)
        return copy

    def part(m, at_z, at_x, at_y, at_core):
        which, _, split_y, by_core, row, rows, column, columns = plan[m]
        out = outs[which]
        at_columns = slice(None)
        if by_core:
            first = at_core * (out.shape[-1] // CORES) + column
            at_columns = pl.ds(pl.multiple_of(first, 128), columns)
        at_z = slice(None) if at_z is None else at_z
        at_x = slice(None) if at_x is None else at_x
        return out.at[at_z, at_x, at_y if split_y else 0, pl.ds(row, rows), at_columns]

    locals_ = []
    for m, (which, layer, split_y, by_core, row, rows, column, columns) in enumerate(plan):
        source = ins[which] if layer is None else ins[which].at[layer]
        if by_core:
            first = row
            if split_y:
                first = pl.multiple_of(y * outs[which].shape[3] + row, 16)
            start = core * (outs[which].shape[-1] // CORES) + column
            source = source.at[pl.ds(first, rows), pl.ds(pl.multiple_of(start, 128), columns)]
        copy = pltpu.make_async_copy(source, part(m, z, x, y, core), local_sem.at[m])
        copy.start()
        locals_.append(copy)
    pl.semaphore_wait(barrier, len(mates))
    along_z, along_x, over_y, last = {}, {}, {}, []

    def spread(m, at_z, at_x):
        piece = part(m, at_z, at_x, y, core)
        if at_x is x:
            along_x[m].append(send(piece, piece, m, 3 + len(along_x[m]), dx=1))
        if plan[m][2]:
            over_y[m].append(send(piece, piece, m, 7 + len(over_y[m]), dy=1))

    def behind(k):
        return lax.rem(z + CHIPS_Z - k, CHIPS_Z)

    def after_x(m):
        for k in range(CHIPS_Z):
            if k % 2:
                next(todo, None)
            along_x[m][k].wait_recv()
            spread(m, behind(k), 1 - x)
        if not plan[m][3]:
            ending(own_outs, outs)
        else:
            piece = part(m, None, None, y, core)
            last.append(send(piece, piece, m, 15, dc=1))

    def after_y(m):
        if over_y[m]:
            for copy in over_y[m]:
                copy.wait_recv()
            piece = part(m, None, None, 1 - y, core)
            last.append(send(piece, piece, m, 16, dc=1))

    order = range(count)

    def set_out(m):
        locals_[m].wait()
        mine = part(m, z, x, y, core)
        along_z[m] = [send(mine, mine, m, k - 1, dz=k) for k in range(1, CHIPS_Z)]
        along_x[m], over_y[m] = [], []
        spread(m, z, x)

    for m in order[:2]:
        set_out(m)
    for place, m in enumerate(order):
        for k in range(1, CHIPS_Z):
            next(todo, None)
            along_z[m][k - 1].wait_recv()
            spread(m, behind(k), x)
        if place + 2 < count:
            set_out(order[place + 2])
        if place:
            after_x(order[place - 1])
    after_x(order[-1])
    for m in order:
        after_y(m)
        next(todo, None)
    for _ in todo:
        pass
    for copy in last:
        copy.wait_recv()
    for copy in sent:
        copy.wait_send()


def no_ending(own_outs, outs):
    pass


def spread_vectors(sizes, own_outs, outs):
    found = outs[0]
    for shard in range(CHIPS_Z * CHIPS_X):
        rows = found[shard // CHIPS_X, shard % CHIPS_X, 0].astype(jnp.float32)
        at = 0
        for out_ref, size in zip(own_outs[-len(sizes) :], sizes):
            out_ref[:, shard * size : (shard + 1) * size] = rows[:LAYERS, at : at + size]
            at += size


def gather(weights, wanted, work, work_args, work_shapes, number, ending=no_ending):
    low = jnp.bfloat16
    args, plan, shapes = [], [], []
    for which, layer, split_y, tall, wide in wanted:
        rows, columns = weights[which].shape[-2:]
        split = CHIPS_Y if split_y else 1
        rows //= split
        half = columns if layer is None else columns // CORES
        for piece in range(tall * wide):
            row, column = divmod(piece, wide)
            plan.append(
                (
                    len(args),
                    layer,
                    split_y,
                    layer is not None,
                    row * (rows // tall),
                    rows // tall,
                    column * (half // wide),
                    half // wide,
                )
            )
        args.append(weights[which])
        shapes.append((CHIPS_Z, CHIPS_X, split, rows, columns))
    whole = pl.BlockSpec(memory_space=pltpu.VMEM)
    small = pl.BlockSpec(memory_space=pltpu.SMEM)
    found = pl.pallas_call(
        functools.partial(
            gather_kernel, plan, len(args), ending, work, len(work_args), len(work_shapes)
        ),
        in_specs=[small if arg.shape[-1] == SEGMENTS else whole for arg in work_args]
        + [pl.BlockSpec(memory_space=pl.ANY)] * len(args),
        out_specs=[whole] * (len(work_shapes) + len(args)),
        out_shape=work_shapes + [jax.ShapeDtypeStruct(shape, low) for shape in shapes],
        scratch_shapes=[pltpu.SemaphoreType.DMA((2, 17))] * len(plan)
        + [pltpu.SemaphoreType.DMA((len(plan),))],
        compiler_params=pltpu.CompilerParams(
            vmem_limit_bytes=KERNEL_VMEM, collective_id=number, has_side_effects=True
        ),
        cost_estimate=pl.CostEstimate(flops=0, bytes_accessed=200_000_000, transcendentals=0),
    )(*work_args, *args)
    results, arrays = list(found[: len(work_shapes)]), found[len(work_shapes) :]
    for item, array in zip(wanted, arrays):
        results.append(array if item[1] is None else array.reshape(-1, array.shape[-1]))
    return results


def pack_sums(out_ref, ins):
    rows = 8 * LAYERS
    width = out_ref.shape[1]
    for layer in range(LAYERS):
        sums_ref, ffin_ref, _ = ins[3 * layer : 3 * layer + 3]
        out_ref[8 * layer : 8 * layer + 8] = sums_ref[...]
        for at in range(0, ffin_ref.shape[1], width):
            out_ref[rows : rows + 1] = ffin_ref[:, at : at + width]
            rows += 1
    for layer in range(LAYERS):
        ref = ins[3 * layer + 2]
        for pair in range(ref.shape[1]):
            value = ref[0, pair]
            for tree in range(1, ref.shape[0]):
                value = value + ref[tree, pair]
            out_ref[rows : rows + 8, pair * LANES : (pair + 1) * LANES] = value
        rows += 8


def sum_rows(ffin_width):
    return LAYERS * (16 + ffin_width // D)


def reduce_kernel(flats, count, vectors, work, work_ins, work_outs, *refs):
    take = iter(refs)

    def some(number):
        return [next(take) for _ in range(number)]

    own_ins = some(work_ins)
    a_ins = [some(2) for _ in range(flats)]
    b_ins = [some(2) for _ in range(count)]
    vec_ins = some(vectors)
    own_outs = some(work_outs)
    a_outs = [some(2) for _ in range(flats)]
    b_outs = some(count)
    vec_outs = some(1 if vectors else 0)
    a_scratch = [some(6) for _ in range(flats)]
    b_scratch = [some(6) for _ in range(count)]
    v_send, v_land = some(2) if vectors else (None, None)
    a_sems, b_sems = some(flats), some(count)
    v_sems = next(take) if vectors else None
    todo = work(own_ins, own_outs)
    rep, shard = lax.axis_index("rep"), lax.axis_index("shard")
    y, core = lax.div(rep, CORES), lax.rem(rep, CORES)
    z, x = lax.div(shard, CHIPS_X), lax.rem(shard, CHIPS_X)

    def device(dz=0, dx=0, dy=0, dc=0):
        to_y, to_core = lax.rem(y + dy, CHIPS_Y), lax.rem(core + dc, CORES)
        to_z, to_x = lax.rem(z + dz, CHIPS_Z), lax.rem(x + dx, CHIPS_X)
        return (to_y * CORES + to_core, to_z * CHIPS_X + to_x)

    flip_z = 1 + 2 * lax.rem(z, 2)
    mates = [dict(dx=1), dict(dy=1), dict(dc=1), dict(dy=1, dc=1)]
    mates += [dict(dz=k) for k in range(1, CHIPS_Z)]
    barrier = pltpu.get_barrier_semaphore()
    for mate in mates:
        pl.semaphore_signal(
            barrier, inc=1, device_id=device(**mate), device_id_type=pl.DeviceIdType.MESH
        )
    pl.semaphore_wait(barrier, len(mates))
    sent = []

    def send(source, target, sems, number, **step):
        copy = pltpu.make_async_remote_copy(
            src_ref=source,
            dst_ref=target,
            send_sem=sems.at[0, number],
            recv_sem=sems.at[1, number],
            device_id=device(**step),
            device_id_type=pl.DeviceIdType.MESH,
        )
        copy.start()
        sent.append(copy)
        return copy

    def wide(value):
        return value.astype(jnp.float32)

    order = (2, 1, 3, 0)
    ahead = [lax.rem(z + k, CHIPS_Z) for k in order]
    v_copies = []
    if vectors:
        pack_sums(v_send.at[0], vec_ins)
        v_copies.append(send(v_send.at[0], v_land.at[0], v_sems, 0, dc=1))
    a_x, b_y = [[] for _ in range(flats)], [[] for _ in range(count)]

    def set_out(j):
        to = ahead[j]
        for i, (first, _) in enumerate(a_ins):
            a_x[i].append(send(first.at[to], a_scratch[i][0].at[j], a_sems[i], j, dx=1))
        for i, (first, _) in enumerate(b_ins):
            b_y[i].append(send(first.at[:, to], b_scratch[i][0].at[j], b_sems[i], j, dy=1))

    set_out(0)
    set_out(1)
    steps = (dict(dc=1), dict(dy=1), dict(dx=1), dict(dz=2), dict(dz=flip_z))

    def add_vectors(s):
        if not vectors:
            return
        v_copies[s].wait_recv()
        total = v_send[s] + v_land[s]
        if s + 1 == len(steps):
            vec_outs[0][...] = total
        else:
            v_send[s + 1] = total
            v_copies.append(
                send(v_send.at[s + 1], v_land.at[s + 1], v_sems, s + 1, **steps[s + 1])
            )

    a_z, b_x, b_z = ([[] for _ in range(number)] for number in (flats, count, count))

    def b_along_z(i, j):
        k, keep = order[j], b_ins[i][1]
        over, _, x_land, z_send, z_land, _ = b_scratch[i]
        b_x[i][j].wait_recv()
        if k:
            total = wide(keep[:, ahead[j], x]) + wide(over[j, :, x]) + wide(x_land[j])
            z_send[k - 1] = total.astype(jnp.bfloat16)
            b_z[i].append(send(z_send.at[k - 1], z_land.at[k - 1], b_sems[i], 7 + k, dz=k))

    def b_along_x(i, j):
        keep, (over, x_send, x_land, *_) = b_ins[i][1], b_scratch[i]
        b_y[i][j].wait_recv()
        total = wide(keep[:, ahead[j], 1 - x]) + wide(over[j, :, 1 - x])
        x_send[j] = total.astype(jnp.bfloat16)
        b_x[i].append(send(x_send.at[j], x_land.at[j], b_sems[i], 4 + j, dx=1))

    for j, k in enumerate(order):
        next(todo, None)
        for i, (_, keep) in enumerate(a_ins):
            across, z_send, z_land, *_ = a_scratch[i]
            a_x[i][j].wait_recv()
            if k:
                total = wide(keep[ahead[j]]) + wide(across[j])
                z_send[k - 1] = total.astype(jnp.bfloat16)
                a_z[i].append(
                    send(z_send.at[k - 1], z_land.at[k - 1], a_sems[i], 3 + k, dz=k)
                )
        next(todo, None)
        for i in range(count):
            b_along_x(i, j)
        if j + 2 < CHIPS_Z:
            set_out(j + 2)
        if j:
            for i in range(count):
                b_along_z(i, j - 1)
        next(todo, None)
        add_vectors(j)
    for i in range(count):
        b_along_z(i, CHIPS_Z - 1)
    add_vectors(4)
    for _ in todo:
        pass
    over_y, ends = [], []
    for i, (_, keep) in enumerate(a_ins):
        across, _, z_land, y_send, y_land, _ = a_scratch[i]
        for copy in a_z[i]:
            copy.wait_recv()
        total = wide(keep[z]) + wide(across[CHIPS_Z - 1])
        for k in range(CHIPS_Z - 1):
            total = total + wide(z_land[k])
        y_send[...] = total.astype(jnp.bfloat16)
        over_y.append(send(y_send, y_land, a_sems[i], 7, dy=1))
    for i, (_, keep) in enumerate(b_ins):
        over, _, x_land, _, z_land, end_land = b_scratch[i]
        for copy in b_z[i]:
            copy.wait_recv()
        total = wide(keep[:, z, x]) + wide(over[3, :, x]) + wide(x_land[3])
        for k in range(CHIPS_Z - 1):
            total = total + wide(z_land[k])
        b_outs[i][0] = total.astype(jnp.bfloat16)
        for number, step in enumerate((dict(dy=1), dict(dc=1), dict(dy=1, dc=1))):
            ends.append(
                send(b_outs[i].at[0], end_land.at[number], b_sems[i], 11 + number, **step)
            )
    for i, (own, _) in enumerate(a_outs):
        *_, y_send, y_land, c_land = a_scratch[i]
        over_y[i].wait_recv()
        own[...] = (wide(y_send[...]) + wide(y_land[...])).astype(jnp.bfloat16)
        ends.append(send(own, c_land, a_sems[i], 8, dc=1))
    for copy in ends:
        copy.wait_recv()
    for i in range(count):
        b_outs[i][1:4] = b_scratch[i][5][...]
    for i, (_, other) in enumerate(a_outs):
        other[...] = a_scratch[i][5][...]
    for copy in sent:
        copy.wait_send()


def no_work(ins, outs):
    return iter(())


def reduce_sums(flats, pairs, sums, number, work=no_work, work_args=(), work_shapes=()):
    low = jnp.bfloat16
    whole = pl.BlockSpec(memory_space=pltpu.VMEM)
    far = pl.BlockSpec(memory_space=pl.ANY)
    args, specs = list(work_args), [whole] * len(work_args)
    outs, scratch = [], []
    for first, keep in flats:
        piece = keep.shape[1:]
        args += [first, keep]
        specs += [far, whole]
        outs += [piece, piece]
        scratch += [(CHIPS_Z, *piece), (CHIPS_Z - 1, *piece), (CHIPS_Z - 1, *piece)]
        scratch += [piece] * 3
    for first, keep in pairs:
        parts, _, _, rows, half = keep.shape
        block = (parts, rows, half)
        args += [first, keep]
        specs += [far, whole]
        outs.append((CORES * CHIPS_Y, *block))
        scratch += [
            (CHIPS_Z, parts, CHIPS_X, rows, half),
            (CHIPS_Z, *block),
            (CHIPS_Z, *block),
            (CHIPS_Z - 1, *block),
            (CHIPS_Z - 1, *block),
            (CORES * CHIPS_Y - 1, *block),
        ]
    args += sums
    specs += [whole] * len(sums)
    shapes = list(work_shapes) + [jax.ShapeDtypeStruct(shape, low) for shape in outs]
    scratch = [pltpu.VMEM(shape, low) for shape in scratch]
    if sums:
        vec = (sum_rows(sums[1].shape[1]), D)
        shapes.append(jax.ShapeDtypeStruct(vec, jnp.float32))
        scratch += [pltpu.VMEM((5, *vec), jnp.float32)] * 2
    scratch += [pltpu.SemaphoreType.DMA((2, 9))] * len(flats)
    scratch += [pltpu.SemaphoreType.DMA((2, 14))] * len(pairs)
    if sums:
        scratch.append(pltpu.SemaphoreType.DMA((2, 5)))
    return pl.pallas_call(
        functools.partial(
            reduce_kernel, len(flats), len(pairs), len(sums), work, len(work_args), len(work_shapes)
        ),
        in_specs=specs,
        out_specs=[whole] * len(shapes),
        out_shape=shapes,
        scratch_shapes=scratch,
        compiler_params=pltpu.CompilerParams(
            vmem_limit_bytes=KERNEL_VMEM, collective_id=number, has_side_effects=True
        ),
        cost_estimate=pl.CostEstimate(flops=0, bytes_accessed=200_000_000, transcendentals=0),
    )(*args)


def join_kernel(plan, count, at_ref, *refs):
    for ref, out, layer, outer, parts, dc, dy, start, rows in plan:
        ref, out_ref = refs[ref], refs[count + out]
        half = ref.shape[1]
        core = lax.rem(at_ref[3] + dc, CORES)
        row = 0
        if dy is not None:
            row = pl.multiple_of(lax.rem(at_ref[2] + dy, CHIPS_Y) * rows, 16)
        for part in range(parts):
            column = part * CORES + core if outer else core * parts + part
            column = pl.multiple_of(column * half, 128)
            value = ref[start + part * rows : start + (part + 1) * rows]
            out_ref[layer, pl.ds(row, rows), pl.ds(column, half)] = value.astype(jnp.float32)


def join(at, done, shapes):
    arrays, plan = [], []
    for out, (number, (tall, wide)) in enumerate(shapes.items()):
        for layer in range(LAYERS):
            pieces, start, rows = done[layer][number]
            for place, piece in enumerate(pieces):
                known = [other is piece for other in arrays]
                if not any(known):
                    arrays.append(piece)
                    known.append(True)
                parts = wide // (CORES * piece.shape[1])
                dy, dc = (place % CHIPS_Y, place // CHIPS_Y) if len(pieces) > CORES else (None, place)
                plan.append((known.index(True), out, layer, number == 0, parts, dc, dy, start, rows))
    zeros = lambda i, at: (0, 0)
    outs = [(LAYERS, *shape) for shape in shapes.values()]
    return pl.pallas_call(
        functools.partial(join_kernel, plan, len(arrays)),
        grid_spec=pltpu.PrefetchScalarGridSpec(
            num_scalar_prefetch=1,
            grid=(1,),
            in_specs=[pl.BlockSpec(array.shape, zeros) for array in arrays],
            out_specs=[pl.BlockSpec(out, lambda i, at: (0, 0, 0)) for out in outs],
        ),
        out_shape=[jax.ShapeDtypeStruct(out, jnp.float32) for out in outs],
        compiler_params=kernel_params(),
        cost_estimate=pl.CostEstimate(flops=0, bytes_accessed=4_000_000, transcendentals=0),
    )(at, *arrays)


def local(
    fast,
    inputs,
    cotangent,
    segment,
    parent,
    clusters,
    *weights,
):
    pieces = {}
    if fast:
        place = Place()
        at = place.at
        shards = dict(enumerate(weights))
        shards["vectors"] = jnp.pad(
            jnp.concatenate([weights[member] for member in VECTORS], axis=1),
            ((0, 16 - LAYERS), (0, 0)),
        )
        trees = parent.shape[0]
        sizes = [weights[number].shape[1] for number in VECTORS]
        slots, bias, *vectors, _, qkv = gather(
            shards,
            (("vectors", None, False, 1, 1), (0, 0, True, 1, 1)),
            prep_steps,
            (
                parent,
                segment.reshape(trees, 1, TREE_LEN),
                clusters.reshape(PAIRS, 2, trees, TREE_LEN).transpose(2, 0, 1, 3),
            ),
            [
                jax.ShapeDtypeStruct((trees, PAIRS, 2, TREE_LEN), jnp.int32),
                jax.ShapeDtypeStruct((trees, HEADS, TREE_LEN, LANES), jnp.bfloat16),
                *[
                    jax.ShapeDtypeStruct((LAYERS, CHIPS_Z * CHIPS_X * size), jnp.float32)
                    for size in sizes
                ],
            ],
            1,
            functools.partial(spread_vectors, sizes),
        )
        whole = {(0, 0): qkv}

        def attend_layer(layer, projected):
            last = layer + 1 == LAYERS
            if last:
                wanted = [(6, layer, True, 1, 1), (2, layer, True, 1, 1), (8, layer, False, 1, 1)]
            else:
                wanted = [(6, layer, True, 1, 1), (8, layer, True, 1, 1)]
                wanted += [(0, layer + 1, False, 1, 1), (2, layer, False, 1, 1)]
            results = gather(
                shards, wanted, attend_steps, (projected, slots, bias), attend_shapes(trees), 2 + layer
            )
            for (number, at_layer, *_), array in zip(wanted, results[4:]):
                whole[at_layer, number] = array
            return results[:4]

        def get(layer, number):
            return whole[layer, number]

        def attend_back_layer(layer, grad_context, heads, groups, waiting):
            flat, pair = cut_sums(place, groups)
            proj, head_sums, *ends = reduce_sums(
                [flat],
                [pair, *waiting],
                [],
                2 + LAYERS + layer,
                attend_back_steps,
                (slots, grad_context, *heads),
                attend_back_shapes(trees),
            )
            pieces[layer, "flat"] = ends[:2]
            pieces[layer, 6] = ends[2]
            if waiting:
                pieces[layer + 1, 0] = ends[3]
            return proj, head_sums

    else:
        slots, bias = prepare(segment, parent, clusters)
        vectors = [
            lax.all_gather(weights[number], "shard", axis=1, tiled=True).astype(jnp.float32)
            for number in VECTORS
        ]

        def attend_layer(layer, projected):
            return attend(projected, slots, bias)

        def get(layer, number):
            return lax.all_gather(weights[number][layer], "shard", axis=0, tiled=True)

        def own_sum(left, right):
            if right.ndim == 3:
                right = right.transpose(1, 0, 2).reshape(right.shape[1], -1)
            total = contract_first(left, right)
            total = lax.psum_scatter(total, "shard", scatter_dimension=0, tiled=True)
            return lax.psum(total.astype(jnp.bfloat16), "rep").astype(jnp.float32)

        def attend_back_layer(layer, grad_context, heads, groups, waiting):
            for grads, _ in groups:
                for grad in grads:
                    pieces[layer, grad.number] = own_sum(grad.left, grad.right)
            return attend_back(grad_context, slots, heads)

    vector = dict(zip(VECTORS, vectors))
    hidden, hidden_low = inputs, inputs
    saved = []
    for layer in range(LAYERS):
        pull = functools.partial(get, layer)
        projected = project(layer, hidden_low, pull(0), vector[1])
        context, *heads = attend_layer(layer, projected)
        entered = hidden_low
        middle, act, slope, *norms, hidden, hidden_low = feed(
            layer,
            context,
            hidden,
            [pull(2), pull(6), pull(8)],
            [vector[number] for number in (3, 4, 5, 7, 9, 10, 11)],
        )
        saved.append((entered, heads, context, middle, act, slope, norms))
    result = hidden_low
    above, proj = cotangent, None
    sums, waiting = [None] * LAYERS, []
    for layer in reversed(range(LAYERS)):
        entered, heads, context, middle, act, slope, norms = saved[layer]
        pull = functools.partial(get, layer)
        down, grad_pre, grad_attn, attn_low, grad_context, row_sums, ffin_sum = feed_back(
            layer,
            above,
            proj,
            None if proj is None else get(layer + 1, 0),
            [norms[2], norms[3], slope, norms[0], norms[1]],
            [pull(2), pull(6), pull(8)],
            [vector[4], vector[10]],
        )
        wide = grad_pre.shape[1] // CORES
        groups = (
            (
                (
                    Grad(8, act, down, act.shape[1] // D, UNIT),
                    Grad(2, context, attn_low, 1, UNIT),
                ),
                False,
            ),
            ((Grad(6, middle, grad_pre, wide // D, D),), True),
        )
        proj, head_sums = attend_back_layer(layer, grad_context, heads, groups, waiting)
        sums[layer] = [row_sums, ffin_sum, head_sums]
        above = grad_attn
        last = Grad(0, entered, proj, 3, UNIT)
        if not fast:
            pieces[layer, 0] = own_sum(last.left, last.right)
        elif layer:
            waiting = cut_sums(place, [((last,), True)])
    grad_input = input_grad(above, proj, get(0, 0))
    sums = [item for layer in sums for item in layer]
    if fast:
        (pair,) = cut_sums(place, [((last,), True)])
        pair, grad_input = lax.optimization_barrier((pair, grad_input))
        pieces[0, 0], total = reduce_sums([], [pair], sums, 0)
    else:
        norms, wide, heads = [], [], []
        for row_sums, ffin_sum, head_sums in (sums[:3], sums[3:]):
            norms.append(row_sums)
            wide.append(ffin_sum.reshape(-1, D))
            heads.append(head_sums.sum(0).transpose(1, 0, 2).reshape(8, D))
        total = lax.psum(jnp.concatenate(norms + wide + heads), AXES)
    count = lax.axis_size("shard")
    shard = lax.axis_index("shard")
    ffin_rows = sums[1].shape[1] // D

    def share(rows):
        stacked = jnp.stack([total[row].reshape(-1) for row in rows])
        width = stacked.shape[1] // count
        return lax.dynamic_slice_in_dim(stacked, shard * width, width, axis=1)

    starts = [0, 8, 16, 16 + ffin_rows]
    heads_at = [16 + 2 * ffin_rows, 24 + 2 * ffin_rows]
    grads = {
        1: share([slice(at, at + 3, 2) for at in heads_at]),
        7: share([slice(at, at + ffin_rows) for at in starts[2:]]),
    }
    for number, row in ((10, 0), (11, 1), (9, 2), (4, 3), (5, 4), (3, 5)):
        grads[number] = share([row, 8 + row])
    if fast:
        rows = {number: weights[number].shape[1] for number in MATRICES}
        parts = {number: weights[number].shape[2] // (CORES * UNIT) for number in MATRICES}
        known = [{} for _ in range(LAYERS)]
        for layer in range(LAYERS):
            start = 0
            for number in (8, 2):
                known[layer][number] = (pieces[layer, "flat"], start, rows[number])
                start += rows[number] * parts[number]
            for number in (6, 0):
                end = pieces[layer, number]
                end = end.reshape(end.shape[0], -1, end.shape[-1])
                known[layer][number] = (list(end), 0, rows[number] // CHIPS_Y)
        for numbers in (MATRICES,):
            shapes = {number: weights[number].shape[1:] for number in numbers}
            grads.update(zip(numbers, join(place.at, known, shapes)))
    else:
        for number in MATRICES:
            grads[number] = jnp.stack([pieces[layer, number] for layer in range(LAYERS)])
    return (result, grad_input, *[grads[number] for number in range(12)])


def solution(mesh):
    in_specs = (
        P(("rep", "shard"), None),
        P(("rep", "shard"), None),
        P(("rep", "shard")),
        P(("rep", "shard"), None),
        P(None, ("rep", "shard")),
        P(None, "shard", None),
        P(None, "shard"),
        P(None, "shard", None),
        P(None, "shard"),
        P(None, "shard"),
        P(None, "shard"),
        P(None, "shard", None),
        P(None, "shard"),
        P(None, "shard", None),
        P(None, "shard"),
        P(None, "shard"),
        P(None, "shard"),
    )
    out_specs = (
        P(("rep", "shard"), None),
        P(("rep", "shard"), None),
        P(None, "shard", None),
        P(None, "shard"),
        P(None, "shard", None),
        P(None, "shard"),
        P(None, "shard"),
        P(None, "shard"),
        P(None, "shard", None),
        P(None, "shard"),
        P(None, "shard", None),
        P(None, "shard"),
        P(None, "shard"),
        P(None, "shard"),
    )
    fast = mesh.shape["rep"] == CHIPS_Y * CORES and mesh.shape["shard"] == CHIPS_Z * CHIPS_X
    return jax.shard_map(
        functools.partial(local, fast),
        mesh=mesh,
        in_specs=in_specs,
        out_specs=out_specs,
        check_vma=False,
    )
```

```python
import functools

import jax
import jax.numpy as jnp
from jax import lax
from jax.experimental import pallas as pl
from jax.experimental.pallas import tpu as pltpu
from jax.sharding import PartitionSpec as P

D = 768
HEADS = 12
HEAD_DIM = 64
LAYERS = 2
CLUSTER = 128
TREE_LEN = 1024
SEGMENTS = 13
PAIRS = HEADS // 2
LANES = 2 * HEAD_DIM
KERNEL_VMEM = 60 * 2**20
ROW_TILE = 256
FEED_TILE = 768
DEPTH_TILE = 384
INV_ROOT = (2.0 * 3.141592653589793) ** -0.5
MATRICES = (0, 2, 6, 8)
VECTORS = (1, 3, 4, 5, 7, 9, 10, 11)
UNIT = 384
AXES = ("rep", "shard")
CHIPS_Z, CHIPS_X, CHIPS_Y, CORES = 4, 2, 2, 2
norm_eps = 1e-06


def one_hot_rows(slot_row):
    length = slot_row.shape[-1]
    rows = lax.broadcasted_iota(jnp.int32, (length, length), 0)
    return jnp.where(rows == slot_row, 1.0, 0.0).astype(jnp.bfloat16)


def first_lanes(length):
    return lax.broadcasted_iota(jnp.int32, (length, LANES), 1) < HEAD_DIM


def contract_last(left_side, right_side):
    return lax.dot_general(
        left_side, right_side, (((1,), (1,)), ((), ())), preferred_element_type=jnp.float32
    )


def contract_first(left_side, right_side):
    return lax.dot_general(
        left_side, right_side, (((0,), (0,)), ((), ())), preferred_element_type=jnp.float32
    )


def cluster_blocks(values):
    return [values[at : at + CLUSTER] for at in range(0, values.shape[0], CLUSTER)]


def attend_pair(slots, query, key, value, bias, store):
    low = first_lanes(TREE_LEN)
    query = query * jnp.bfloat16(HEAD_DIM**-0.5)
    packed = (
        jnp.where(low, query, pltpu.roll(key, HEAD_DIM, 1)),
        jnp.where(low, pltpu.roll(query, HEAD_DIM, 1), key),
    )
    context = []
    for head in range(2):
        table = one_hot_rows(slots[head : head + 1])
        joined = jnp.concatenate([packed[head], value], axis=1)
        found = jnp.dot(table, joined, preferred_element_type=jnp.float32).astype(jnp.bfloat16)
        both, values = found[:, :LANES], found[:, LANES:]
        store("both", head, both)
        store("values", head, values)
        queries = jnp.where(low, both, jnp.bfloat16(0))
        keys = pltpu.roll(both, HEAD_DIM, 1)
        scores = jnp.concatenate(
            [contract_last(q, k) for q, k in zip(cluster_blocks(queries), cluster_blocks(keys))],
            axis=0,
        )
        scores = scores + bias[head].astype(jnp.float32)
        numerator = jnp.exp(scores - jnp.max(scores, axis=1, keepdims=True))
        total = jnp.sum(numerator, axis=1, keepdims=True)
        soft = (numerator * (1.0 / total)).astype(jnp.bfloat16)
        store("soft", head, soft)
        out = jnp.concatenate(
            [
                jnp.dot(p, v, preferred_element_type=jnp.float32)
                for p, v in zip(cluster_blocks(soft), cluster_blocks(values))
            ],
            axis=0,
        ).astype(jnp.bfloat16)
        context.append(contract_first(table, out))
        if head == 0:
            yield
    store("context", None, jnp.where(low, context[0], context[1]).astype(jnp.bfloat16))


def attend_kernel(slot_ref, query_ref, key_ref, value_ref, bias_ref, ctx_ref, qk_ref, val_ref, p_ref):
    refs = {"both": qk_ref, "values": val_ref, "soft": p_ref}

    def store(name, head, value):
        if head is None:
            ctx_ref[...] = value
        else:
            refs[name][0, head] = value

    for _ in attend_pair(
        slot_ref[0, 0], query_ref[...], key_ref[...], value_ref[...], bias_ref[0], store
    ):
        pass


def attend_steps(ins, outs):
    projected_ref, slot_ref, bias_ref = ins
    ctx_ref, qk_ref, val_ref, p_ref = outs
    refs = {"both": qk_ref, "values": val_ref, "soft": p_ref}
    for tree in range(slot_ref.shape[0]):
        rows = slice(tree * TREE_LEN, (tree + 1) * TREE_LEN)
        for pair in range(PAIRS):
            lanes = [slice((part * PAIRS + pair) * LANES, (part * PAIRS + pair + 1) * LANES) for part in range(3)]
            heads = slice(2 * pair, 2 * pair + 2)

            def store(name, head, value):
                if head is None:
                    ctx_ref[rows, lanes[0]] = value
                else:
                    refs[name][tree, 2 * pair + head] = value

            yield from attend_pair(
                slot_ref[tree, pair],
                *[projected_ref[rows, part] for part in lanes],
                bias_ref[tree, heads],
                store,
            )
            yield


def attend_back_pair(slots, grads, both_of, values_of, soft_of, store):
    low = first_lanes(TREE_LEN)
    placed = []
    for head in range(2):
        table = one_hot_rows(slots[head : head + 1])
        found = jnp.dot(table, grads, preferred_element_type=jnp.float32)
        found = jnp.where(low == (head == 0), found, 0.0).astype(jnp.bfloat16)
        both, values, soft = both_of(head), values_of(head), soft_of(head)
        grad_soft = jnp.concatenate(
            [contract_last(g, v) for g, v in zip(cluster_blocks(found), cluster_blocks(values))],
            axis=0,
        )
        grad_value = jnp.concatenate(
            [contract_first(p, g) for p, g in zip(cluster_blocks(soft), cluster_blocks(found))],
            axis=0,
        ).astype(jnp.bfloat16)
        weights = soft.astype(jnp.float32)
        delta = jnp.sum(weights * grad_soft, axis=1, keepdims=True)
        grad_scores = (weights * (grad_soft - delta)).astype(jnp.bfloat16)
        pairs = list(zip(cluster_blocks(grad_scores), cluster_blocks(both)))
        by_key = jnp.concatenate([contract_first(s, b) for s, b in pairs], axis=0)
        by_query = jnp.concatenate(
            [jnp.dot(s, b, preferred_element_type=jnp.float32) for s, b in pairs], axis=0
        )
        mixed = jnp.where(low, by_key, by_query * HEAD_DIM**-0.5).astype(jnp.bfloat16)
        joined = jnp.concatenate([mixed, grad_value], axis=1)
        placed.append(contract_first(table, joined))
        if head == 0:
            yield
    first, second = placed
    queries = jnp.where(low, pltpu.roll(first[:, :LANES], HEAD_DIM, 1), second[:, :LANES])
    keys = jnp.where(low, first[:, :LANES], pltpu.roll(second[:, :LANES], HEAD_DIM, 1))
    values = jnp.where(low, first[:, LANES:], second[:, LANES:])
    sums = []
    for part, grad in enumerate((queries, keys, values)):
        rounded = grad.astype(jnp.bfloat16)
        store(part, rounded)
        sums.append(rows_sum(rounded.astype(jnp.float32)))
    store(None, jnp.concatenate(sums + [jnp.zeros((5, LANES), jnp.float32)], axis=0))


def attend_back_kernel(slot_ref, grad_ref, qk_ref, val_ref, p_ref, out_ref, sums_ref):
    def store(part, value):
        if part is None:
            sums_ref[0, 0] = value
        else:
            out_ref[part] = value

    refs = [lambda head, ref=ref: ref[0, head] for ref in (qk_ref, val_ref, p_ref)]
    for _ in attend_back_pair(slot_ref[0, 0], grad_ref[...], *refs, store):
        pass


def attend_back_steps(ins, outs):
    slot_ref, grad_ref, *kept = ins
    out_ref, sums_ref = outs
    for tree in range(slot_ref.shape[0]):
        rows = slice(tree * TREE_LEN, (tree + 1) * TREE_LEN)
        for pair in range(PAIRS):
            lanes = slice(pair * LANES, (pair + 1) * LANES)

            def store(part, value):
                if part is None:
                    sums_ref[tree, pair] = value
                else:
                    out_ref[part, rows, lanes] = value

            refs = [lambda head, ref=ref: ref[tree, 2 * pair + head] for ref in kept]
            yield from attend_back_pair(slot_ref[tree, pair], grad_ref[rows, lanes], *refs, store)
            yield


def slot_spec(start=0):
    return pl.BlockSpec((1, 1, 2, TREE_LEN), lambda tree, pair: (tree, start + pair, 0, 0))


def head_spec(start=0):
    return pl.BlockSpec((1, 2, TREE_LEN, LANES), lambda tree, pair: (tree, start + pair, 0, 0))


def column_spec(offset):
    return pl.BlockSpec((TREE_LEN, LANES), lambda tree, pair: (tree, offset + pair))


def kernel_params():
    return pltpu.CompilerParams(vmem_limit_bytes=KERNEL_VMEM)


def attend_shapes(trees):
    stored = jax.ShapeDtypeStruct((trees, HEADS, TREE_LEN, LANES), jnp.bfloat16)
    return [jax.ShapeDtypeStruct((trees * TREE_LEN, D), jnp.bfloat16), stored, stored, stored]


def attend(projected, slots, bias):
    trees = slots.shape[0]
    return pl.pallas_call(
        attend_kernel,
        grid=(trees, PAIRS),
        in_specs=[
            slot_spec(),
            column_spec(0),
            column_spec(PAIRS),
            column_spec(2 * PAIRS),
            head_spec(),
        ],
        out_specs=[column_spec(0), head_spec(), head_spec(), head_spec()],
        out_shape=attend_shapes(trees),
        compiler_params=kernel_params(),
        cost_estimate=pl.CostEstimate(
            flops=trees * 30_000_000_000, bytes_accessed=trees * 20_000_000, transcendentals=0
        ),
    )(slots, projected, projected, projected, bias)


def attend_back_shapes(trees):
    return [
        jax.ShapeDtypeStruct((3, trees * TREE_LEN, D), jnp.bfloat16),
        jax.ShapeDtypeStruct((trees, PAIRS, 8, LANES), jnp.float32),
    ]


def attend_back(grad_context, slots, kept):
    trees = slots.shape[0]
    return pl.pallas_call(
        attend_back_kernel,
        grid=(trees, PAIRS),
        in_specs=[slot_spec(), column_spec(0), head_spec(), head_spec(), head_spec()],
        out_specs=[
            pl.BlockSpec((3, TREE_LEN, LANES), lambda tree, pair: (0, tree, pair)),
            pl.BlockSpec((1, 1, 8, LANES), lambda tree, pair: (tree, pair, 0, 0)),
        ],
        out_shape=attend_back_shapes(trees),
        compiler_params=kernel_params(),
        cost_estimate=pl.CostEstimate(
            flops=trees * 35_000_000_000, bytes_accessed=trees * 20_000_000, transcendentals=0
        ),
    )(slots, grad_context, *kept)


def erf_parts(values):
    size = jnp.abs(values)
    turn = 1.0 / (1.0 + (0.3275911 * 0.5**0.5) * size)
    bell = jnp.exp(-0.5 * values * values)
    series = 1.061405429 * 0.5
    for factor in (-1.453152027, 1.421413741, -0.284496736, 0.254829592):
        series = series * turn + factor * 0.5
    tail = series * turn * bell
    return jnp.where(values < 0.0, tail, 1.0 - tail), bell


def norm_parts(values):
    centred = values - jnp.mean(values, axis=-1, keepdims=True)
    scale = lax.rsqrt(jnp.mean(centred * centred, axis=-1, keepdims=True) + norm_eps)
    return centred * scale, scale


def norm_back(grad, normal, scale, gain):
    inner = grad * gain
    mean = jnp.mean(inner, axis=-1, keepdims=True)
    along = jnp.mean(inner * normal, axis=-1, keepdims=True)
    return scale * (inner - mean - normal * along)


def spread(column):
    return jnp.broadcast_to(column, (column.shape[0], 128))


def rows_sum(values):
    return jnp.sum(values, axis=0, keepdims=True)


def project_kernel(layer, rows_ref, weight_ref, bias_ref, out_ref):
    product = jnp.dot(rows_ref[...], weight_ref[...], preferred_element_type=jnp.float32)
    bias = bias_ref[layer : layer + 1]
    out_ref[:, :D] = (product[:, :D] + bias[:, :D]).astype(jnp.bfloat16)
    out_ref[:, D : 2 * D] = product[:, D : 2 * D].astype(jnp.bfloat16)
    out_ref[:, 2 * D :] = (product[:, 2 * D :] + bias[:, D:]).astype(jnp.bfloat16)


def feed_kernel(
    layer,
    context_ref,
    rows_ref,
    out_weight_ref,
    ffin_weight_ref,
    ffout_weight_ref,
    out_bias_ref,
    attn_gain_ref,
    attn_shift_ref,
    ffin_bias_ref,
    ffout_bias_ref,
    ffn_gain_ref,
    ffn_shift_ref,
    hidden_ref,
    act_ref,
    slope_ref,
    attn_normal_ref,
    attn_scale_ref,
    ffn_normal_ref,
    ffn_scale_ref,
    result_ref,
    result_low_ref,
):
    here = slice(layer, layer + 1)
    product = jnp.dot(context_ref[...], out_weight_ref[...], preferred_element_type=jnp.float32)
    attn_sum = rows_ref[...].astype(jnp.float32) + product + out_bias_ref[here]
    normal, scale = norm_parts(attn_sum)
    attn_normal_ref[...] = normal
    attn_scale_ref[...] = spread(scale)
    hidden = normal * attn_gain_ref[here] + attn_shift_ref[here]
    hidden_low = hidden.astype(jnp.bfloat16)
    hidden_ref[...] = hidden_low
    total = hidden + ffout_bias_ref[here]
    width = ffin_weight_ref.shape[1]
    for at in range(0, width, FEED_TILE):
        part = slice(at, at + FEED_TILE)
        pre = (
            jnp.dot(hidden_low, ffin_weight_ref[:, part], preferred_element_type=jnp.float32)
            + ffin_bias_ref[here, part]
        )
        below, bell = erf_parts(pre)
        act = (pre * below).astype(jnp.bfloat16)
        act_ref[:, part] = act
        slope_ref[:, part] = (below + pre * bell * INV_ROOT).astype(jnp.bfloat16)
        total = total + jnp.dot(
            act, ffout_weight_ref[part, :], preferred_element_type=jnp.float32
        )
    normal, scale = norm_parts(total)
    ffn_normal_ref[...] = normal
    ffn_scale_ref[...] = spread(scale)
    result = normal * ffn_gain_ref[here] + ffn_shift_ref[here]
    result_ref[...] = result
    result_low_ref[...] = result.astype(jnp.bfloat16)


def add_projected(grad, proj_ref, weight_ref):
    for part in range(3):
        grad = grad + contract_last(proj_ref[part], weight_ref[:, part * D : (part + 1) * D])
    return grad


def feed_back_kernel(layer, with_proj, *refs):
    here = slice(layer, layer + 1)
    if with_proj:
        above_ref, proj_ref, qkv_weight_ref, *refs = refs
        grad = add_projected(above_ref[...], proj_ref, qkv_weight_ref)
    else:
        above_ref, *refs = refs
        grad = above_ref[...].astype(jnp.float32)
    (
        ffn_normal_ref,
        ffn_scale_ref,
        slope_ref,
        attn_normal_ref,
        attn_scale_ref,
        out_weight_ref,
        ffin_weight_ref,
        ffout_weight_ref,
        attn_gain_ref,
        ffn_gain_ref,
        down_ref,
        pre_ref,
        attn_ref,
        attn_low_ref,
        context_ref,
        sums_ref,
        ffin_sum_ref,
    ) = refs

    @pl.when(pl.program_id(0) == 0)
    def _():
        sums_ref[...] = jnp.zeros_like(sums_ref)
        ffin_sum_ref[...] = jnp.zeros_like(ffin_sum_ref)

    normal = ffn_normal_ref[...]
    sums_ref[0:1] += rows_sum(grad * normal)
    sums_ref[1:2] += rows_sum(grad)
    grad_sum = norm_back(grad, normal, ffn_scale_ref[:, 0:1], ffn_gain_ref[here])
    down = grad_sum.astype(jnp.bfloat16)
    down_ref[...] = down
    sums_ref[2:3] += rows_sum(down.astype(jnp.float32))
    total = grad_sum
    width = ffin_weight_ref.shape[1]
    for at in range(0, width, FEED_TILE):
        part = slice(at, at + FEED_TILE)
        grad_act = contract_last(down, ffout_weight_ref[part, :])
        pre = (grad_act * slope_ref[:, part].astype(jnp.float32)).astype(jnp.bfloat16)
        pre_ref[:, part] = pre
        ffin_sum_ref[:, part] += rows_sum(pre.astype(jnp.float32))
        total = total + contract_last(pre, ffin_weight_ref[:, part])
    normal = attn_normal_ref[...]
    sums_ref[3:4] += rows_sum(total * normal)
    sums_ref[4:5] += rows_sum(total)
    attn = norm_back(total, normal, attn_scale_ref[:, 0:1], attn_gain_ref[here])
    attn_ref[...] = attn
    low = attn.astype(jnp.bfloat16)
    attn_low_ref[...] = low
    sums_ref[5:6] += rows_sum(low.astype(jnp.float32))
    context_ref[...] = contract_last(low, out_weight_ref[...]).astype(jnp.bfloat16)


def input_grad_kernel(above_ref, proj_ref, weight_ref, out_ref):
    out_ref[...] = add_projected(above_ref[...], proj_ref, weight_ref)


def prep_pair(parent_ref, segment_ref, cluster_ref, slot_ref, bias_ref, row, tree, pair):
    segs = segment_ref[tree]
    length = segs.shape[1]

    def parent_of(values):
        found = jnp.zeros_like(values)
        for number in range(SEGMENTS):
            found = jnp.where(values == number, parent_ref[row, number], found)
        return found

    parents = parent_of(segs)
    grands = parent_of(parents)
    ids = jnp.concatenate([segs, parents, grands, jnp.zeros((5, length), jnp.int32)], axis=0)
    ids = jnp.concatenate([ids, jnp.zeros((8, length), jnp.int32)], axis=0)
    ids = ids.astype(jnp.float32).astype(jnp.bfloat16)
    count = length // CLUSTER
    order = lax.broadcasted_iota(jnp.int32, (count, length), 0)
    lanes = lax.broadcasted_iota(jnp.int32, (count, length), 1)
    for head in range(2):
        member = order == cluster_ref[tree, pair, head : head + 1, :]
        ranks = member.astype(jnp.int32)
        step = 1
        while step < length:
            ranks = ranks + jnp.where(lanes >= step, pltpu.roll(ranks, step, 1), 0)
            step *= 2
        slot = jnp.sum(
            jnp.where(member, ranks - 1 + CLUSTER * order, 0), axis=0, keepdims=True
        )
        slot_ref[tree, pair, head : head + 1, :] = slot
        table = one_hot_rows(slot)
        rows = contract_last(ids, table)
        columns = jnp.concatenate([rows] * (128 // rows.shape[0]), axis=0).T
        for at in range(0, length, CLUSTER):
            here = rows[0:1, at : at + CLUSTER]
            block = columns[at : at + CLUSTER]
            allowed = (
                (here == block[:, 0:1]) | (here == block[:, 1:2]) | (here == block[:, 2:3])
            )
            bias_ref[tree, 2 * pair + head, at : at + CLUSTER, :] = jnp.where(allowed, 0.0, -1e30).astype(
                jnp.bfloat16
            )


def prep_kernel(*refs):
    prep_pair(*refs, pl.program_id(0), 0, 0)


def row_spec(width, rows=ROW_TILE):
    return pl.BlockSpec((rows, width), lambda i: (i, 0))


def whole_spec(shape):
    return pl.BlockSpec(
        shape, lambda i: (0,) * len(shape), pipeline_mode=pl.Buffered(1)
    )


def part_spec(rows=ROW_TILE):
    return pl.BlockSpec((3, rows, D), lambda i: (0, i, 0))


def cost(flops, *arrays):
    moved = sum(array.size * array.dtype.itemsize for array in arrays)
    return pl.CostEstimate(flops=int(flops), bytes_accessed=moved, transcendentals=0)


def shape_of(rows, width, kind=jnp.bfloat16):
    return jax.ShapeDtypeStruct((rows, width), kind)


def project(layer, rows, weight, bias):
    count, width = rows.shape[0], weight.shape[1]
    return pl.pallas_call(
        functools.partial(project_kernel, layer),
        grid=(count // ROW_TILE,),
        in_specs=[row_spec(D), whole_spec(weight.shape), whole_spec(bias.shape)],
        out_specs=row_spec(width),
        out_shape=shape_of(count, width),
        compiler_params=kernel_params(),
        cost_estimate=cost(2.4 * count * D * width, rows, weight),
    )(rows, weight, bias)


def feed(layer, context, rows, weights, vectors):
    count = context.shape[0]
    width = weights[1].shape[1]
    f32 = jnp.float32
    return pl.pallas_call(
        functools.partial(feed_kernel, layer),
        grid=(count // ROW_TILE,),
        in_specs=[row_spec(D), row_spec(D)]
        + [whole_spec(weight.shape) for weight in weights]
        + [whole_spec(vector.shape) for vector in vectors],
        out_specs=[
            row_spec(D),
            row_spec(width),
            row_spec(width),
            row_spec(D),
            row_spec(128),
            row_spec(D),
            row_spec(128),
            row_spec(D),
            row_spec(D),
        ],
        out_shape=[
            shape_of(count, D),
            shape_of(count, width),
            shape_of(count, width),
            shape_of(count, D, f32),
            shape_of(count, 128, f32),
            shape_of(count, D, f32),
            shape_of(count, 128, f32),
            shape_of(count, D, f32),
            shape_of(count, D),
        ],
        compiler_params=kernel_params(),
        cost_estimate=cost(5 * count * D * (2 * width + D), context, *weights),
    )(context, rows, *weights, *vectors)


def feed_back(layer, above, proj, qkv_weight, saved, weights, gains):
    count = above.shape[0]
    width = weights[1].shape[1]
    f32 = jnp.float32
    lead, lead_specs = [above], [row_spec(D)]
    if proj is not None:
        lead += [proj, qkv_weight]
        lead_specs += [part_spec(), whole_spec(qkv_weight.shape)]
    return pl.pallas_call(
        functools.partial(feed_back_kernel, layer, proj is not None),
        grid=(count // ROW_TILE,),
        in_specs=lead_specs
        + [row_spec(D), row_spec(128), row_spec(width), row_spec(D), row_spec(128)]
        + [whole_spec(weight.shape) for weight in weights]
        + [whole_spec(gain.shape) for gain in gains],
        out_specs=[
            row_spec(D),
            row_spec(width),
            row_spec(D),
            row_spec(D),
            row_spec(D),
            pl.BlockSpec((8, D), lambda i: (0, 0)),
            pl.BlockSpec((1, width), lambda i: (0, 0)),
        ],
        out_shape=[
            shape_of(count, D),
            shape_of(count, width),
            shape_of(count, D, f32),
            shape_of(count, D),
            shape_of(count, D),
            shape_of(8, D, f32),
            shape_of(1, width, f32),
        ],
        compiler_params=kernel_params(),
        cost_estimate=cost(5 * count * D * (2 * width + D), above, *weights),
    )(*lead, *saved, *weights, *gains)


def input_grad(above, proj, qkv_weight):
    count = above.shape[0]
    return pl.pallas_call(
        input_grad_kernel,
        grid=(count // ROW_TILE,),
        in_specs=[
            row_spec(D),
            part_spec(),
            whole_spec(qkv_weight.shape),
        ],
        out_specs=row_spec(D),
        out_shape=shape_of(count, D, jnp.float32),
        compiler_params=kernel_params(),
        cost_estimate=cost(2.4 * count * D * 3 * D, above, qkv_weight),
    )(above, proj, qkv_weight)


def prepare(segment, parent, clusters):
    trees = parent.shape[0]
    segment = segment.reshape(trees, 1, TREE_LEN)
    clusters = clusters.reshape(PAIRS, 2, trees, TREE_LEN).transpose(2, 0, 1, 3)
    return pl.pallas_call(
        prep_kernel,
        grid=(trees, PAIRS),
        in_specs=[
            pl.BlockSpec(memory_space=pltpu.SMEM),
            pl.BlockSpec((1, 1, TREE_LEN), lambda tree, pair: (tree, 0, 0)),
            slot_spec(),
        ],
        out_specs=[slot_spec(), head_spec()],
        out_shape=[
            jax.ShapeDtypeStruct((trees, PAIRS, 2, TREE_LEN), jnp.int32),
            jax.ShapeDtypeStruct((trees, HEADS, TREE_LEN, LANES), jnp.bfloat16),
        ],
        compiler_params=kernel_params(),
        cost_estimate=pl.CostEstimate(
            flops=trees * 20_000_000_000, bytes_accessed=trees * 4_000_000, transcendentals=0
        ),
    )(parent, segment, clusters)


def weight_grad_kernel(split_y, at_ref, left_ref, right_ref, *refs):
    product = contract_first(
        left_ref[...].reshape(left_ref.shape[-2:]), right_ref[...].reshape(right_ref.shape[-2:])
    )
    if split_y is None:
        (out_ref,) = refs
        out_ref[...] = product.astype(jnp.bfloat16).reshape(out_ref.shape)
        return
    near_ref, (send_ref, keep_ref, sum_ref) = refs[0], refs[-3:]
    total = product + near_ref[...].astype(jnp.float32).reshape(product.shape)
    sum_ref[...] = total.astype(jnp.bfloat16).reshape(sum_ref.shape)
    if split_y:
        send_ref[0] = sum_ref[:, :, 1 - at_ref[2]]
        keep_ref[0] = sum_ref[:, :, at_ref[2]]
    else:
        send_ref[...] = sum_ref[:, 1 - at_ref[1]]
        keep_ref[...] = sum_ref[:, at_ref[1]]


class Grad:
    def __init__(self, number, left, right, tiles, half):
        self.number = number
        self.left, self.right = left, right
        self.tiles, self.half = tiles, half
        self.depth = left.shape[1]
        self.parts = 1 if self.depth > D else tiles
        self.rows = self.depth // (CHIPS_Z * CHIPS_X)

    def product(self, at, other, split_y=None, near=None, start=0, total=0, before=()):
        flip = 1 if other else 0
        left, right = self.left, self.right
        count = left.shape[0]
        tall = self.depth > D
        core = lambda at: lax.rem(at[3] + flip, CORES)
        in_specs = [
            pl.BlockSpec((count, D), (lambda i, at: (0, i)) if tall else (lambda i, at: (0, 0)))
        ]
        if right.ndim == 3:
            in_specs.append(pl.BlockSpec((1, count, self.half), lambda i, at: (i, 0, core(at))))
        elif tall:
            in_specs.append(pl.BlockSpec((count, self.half), lambda i, at: (0, core(at))))
        else:
            in_specs.append(
                pl.BlockSpec((count, self.half), lambda i, at: (0, core(at) * self.tiles + i))
            )
        zs = D // (self.rows * CHIPS_X)
        place = (lambda i: (0, i)) if tall else (lambda i: (i, 0))
        whole = (self.parts, CHIPS_Z, CHIPS_X, self.rows, self.half)
        block = (1, zs, CHIPS_X, self.rows, self.half)
        full = pl.BlockSpec(block, lambda i, at: (*place(i), 0, 0, 0))
        args, scratch = [left, right], []
        if split_y is None:
            out_specs, shapes = full, jax.ShapeDtypeStruct(whole, jnp.bfloat16)
        else:
            in_specs.append(full)
            args.append(near)
            in_specs += [pl.BlockSpec(memory_space=pl.ANY)] * len(before)
            args += before
            if split_y:
                short = self.rows // CHIPS_Y
                kept = (CHIPS_X, short, self.half)
                scratch = [pltpu.VMEM((zs, CHIPS_X, CHIPS_Y, short, self.half), jnp.bfloat16)]
                spec = pl.BlockSpec((1, zs, *kept), lambda i, at: (*place(i), 0, 0, 0))
                shape = (self.parts, CHIPS_Z, *kept)
            else:
                scratch = [pltpu.VMEM((zs, CHIPS_X, self.rows, self.half), jnp.bfloat16)]
                first = start // self.rows
                index = (lambda i, at: (i, first, 0)) if tall else (lambda i, at: (0, first + i, 0))
                spec = pl.BlockSpec((zs, self.rows, self.half), index)
                shape = (CHIPS_Z, total, self.half)
            out_specs, shapes = [spec] * 2, [jax.ShapeDtypeStruct(shape, jnp.bfloat16)] * 2
        return pl.pallas_call(
            functools.partial(weight_grad_kernel, split_y),
            grid_spec=pltpu.PrefetchScalarGridSpec(
                num_scalar_prefetch=1,
                grid=(self.tiles,),
                in_specs=in_specs,
                out_specs=out_specs,
                scratch_shapes=scratch,
            ),
            out_shape=shapes,
            input_output_aliases={4 + place: place for place in range(len(before))},
            compiler_params=kernel_params(),
            cost_estimate=cost(4 * count * D * self.tiles * self.half, left, right),
        )(at, *args)


class Place:
    def __init__(self):
        rep = lax.axis_index("rep")
        shard = lax.axis_index("shard")
        self.y, self.core = rep // CORES, rep % CORES
        self.z, self.x = shard // CHIPS_X, shard % CHIPS_X
        self.at = jnp.stack([self.z, self.x, self.y, self.core]).astype(jnp.int32)


def hop(value, dz=0, dx=0, dy=0, dc=0):
    pairs = []
    for y in range(CHIPS_Y):
        for c in range(CORES):
            for z in range(CHIPS_Z):
                for x in range(CHIPS_X):
                    source = ((y * CORES + c) * CHIPS_Z + z) * CHIPS_X + x
                    y2, c2 = (y + dy) % CHIPS_Y, (c + dc) % CORES
                    z2, x2 = (z + dz) % CHIPS_Z, (x + dx) % CHIPS_X
                    pairs.append((source, ((y2 * CORES + c2) * CHIPS_Z + z2) * CHIPS_X + x2))
    return lax.ppermute(value, AXES, pairs)


def cut_sums(place, groups):
    at = place.at
    arrived = []
    for grads, _ in groups:
        arrived.append([hop(grad.product(at, True), dc=1) for grad in grads])
    found = []
    for (grads, y_first), near in zip(groups, arrived):
        total = sum(grad.parts * grad.rows for grad in grads)
        start, pair = 0, ()
        for grad, item in zip(grads, near):
            if y_first:
                pair = grad.product(at, False, True, item)
            else:
                pair = grad.product(at, False, False, item, start, total, tuple(pair))
            start += grad.parts * grad.rows
        found.append(tuple(pair))
    return found


def prep_steps(ins, outs):
    trees, pairs = ins[2].shape[:2]
    for tree in range(trees):
        for pair in range(pairs):
            prep_pair(*ins, *outs[:2], tree, tree, pair)
            yield


def gather_kernel(plan, arrays, ending, work, work_ins, work_outs, *refs):
    count = len(plan)
    own_ins, ins, refs = refs[:work_ins], refs[work_ins : work_ins + arrays], refs[work_ins + arrays :]
    own_outs, outs = refs[:work_outs], refs[work_outs : work_outs + arrays]
    sems, local_sem = refs[work_outs + arrays : -1], refs[-1]
    todo = work(own_ins, own_outs)
    rep, shard = lax.axis_index("rep"), lax.axis_index("shard")
    y, core = lax.div(rep, CORES), lax.rem(rep, CORES)
    z, x = lax.div(shard, CHIPS_X), lax.rem(shard, CHIPS_X)

    def device(dz=0, dx=0, dy=0, dc=0):
        to_y, to_core = lax.rem(y + dy, CHIPS_Y), lax.rem(core + dc, CORES)
        to_z, to_x = lax.rem(z + dz, CHIPS_Z), lax.rem(x + dx, CHIPS_X)
        return (to_y * CORES + to_core, to_z * CHIPS_X + to_x)

    mates = [dict(dx=1), dict(dy=1), dict(dc=1)] + [dict(dz=k) for k in range(1, CHIPS_Z)]
    barrier = pltpu.get_barrier_semaphore()
    for mate in mates:
        pl.semaphore_signal(
            barrier, inc=1, device_id=device(**mate), device_id_type=pl.DeviceIdType.MESH
        )
    sent = []

    def send(source, target, m, number, **step):
        copy = pltpu.make_async_remote_copy(
            src_ref=source,
            dst_ref=target,
            send_sem=sems[m].at[0, number],
            recv_sem=sems[m].at[1, number],
            device_id=device(**step),
            device_id_type=pl.DeviceIdType.MESH,
        )
        copy.start()
        sent.append(copy)
        return copy

    def part(m, at_z, at_x, at_y, at_core):
        which, _, split_y, by_core, row, rows, column, columns = plan[m]
        out = outs[which]
        at_columns = slice(None)
        if by_core:
            first = at_core * (out.shape[-1] // CORES) + column
            at_columns = pl.ds(pl.multiple_of(first, 128), columns)
        at_z = slice(None) if at_z is None else at_z
        at_x = slice(None) if at_x is None else at_x
        return out.at[at_z, at_x, at_y if split_y else 0, pl.ds(row, rows), at_columns]

    locals_ = []
    for m, (which, layer, split_y, by_core, row, rows, column, columns) in enumerate(plan):
        source = ins[which] if layer is None else ins[which].at[layer]
        if by_core:
            first = row
            if split_y:
                first = pl.multiple_of(y * outs[which].shape[3] + row, 16)
            start = core * (outs[which].shape[-1] // CORES) + column
            source = source.at[pl.ds(first, rows), pl.ds(pl.multiple_of(start, 128), columns)]
        copy = pltpu.make_async_copy(source, part(m, z, x, y, core), local_sem.at[m])
        copy.start()
        locals_.append(copy)
    pl.semaphore_wait(barrier, len(mates))
    along_z, along_x, over_y, last = {}, {}, {}, []

    def spread(m, at_z, at_x):
        piece = part(m, at_z, at_x, y, core)
        if at_x is x:
            along_x[m].append(send(piece, piece, m, 3 + len(along_x[m]), dx=1))
        if plan[m][2]:
            over_y[m].append(send(piece, piece, m, 7 + len(over_y[m]), dy=1))

    def behind(k):
        return lax.rem(z + CHIPS_Z - k, CHIPS_Z)

    def after_x(m):
        for k in range(CHIPS_Z):
            if k % 2:
                next(todo, None)
            along_x[m][k].wait_recv()
            spread(m, behind(k), 1 - x)
        if not plan[m][3]:
            ending(own_outs, outs)
        else:
            piece = part(m, None, None, y, core)
            last.append(send(piece, piece, m, 15, dc=1))

    def after_y(m):
        if over_y[m]:
            for copy in over_y[m]:
                copy.wait_recv()
            piece = part(m, None, None, 1 - y, core)
            last.append(send(piece, piece, m, 16, dc=1))

    order = range(count)

    def set_out(m):
        locals_[m].wait()
        mine = part(m, z, x, y, core)
        along_z[m] = [send(mine, mine, m, k - 1, dz=k) for k in range(1, CHIPS_Z)]
        along_x[m], over_y[m] = [], []
        spread(m, z, x)

    for m in order[:2]:
        set_out(m)
    for place, m in enumerate(order):
        for k in range(1, CHIPS_Z):
            next(todo, None)
            along_z[m][k - 1].wait_recv()
            spread(m, behind(k), x)
        if place + 2 < count:
            set_out(order[place + 2])
        if place:
            after_x(order[place - 1])
    after_x(order[-1])
    for m in order:
        after_y(m)
        next(todo, None)
    for _ in todo:
        pass
    for copy in last:
        copy.wait_recv()
    for copy in sent:
        copy.wait_send()


def no_ending(own_outs, outs):
    pass


def spread_vectors(found, at, sizes, out_refs):
    for shard in range(CHIPS_Z * CHIPS_X):
        rows = found[shard // CHIPS_X, shard % CHIPS_X, 0].astype(jnp.float32)
        first = at
        for out_ref, size in zip(out_refs, sizes):
            out_ref[:, shard * size : (shard + 1) * size] = rows[:LAYERS, first : first + size]
            first += size


def attend_and_spread(sizes, ins, outs):
    yield from attend_steps(ins[:3], outs[:4])
    spread_vectors(ins[3], sizes[0], sizes[1:], outs[4:])


def gather(weights, wanted, work, work_args, work_shapes, number, ending=no_ending):
    low = jnp.bfloat16
    args, plan, shapes = [], [], []
    for which, layer, split_y, tall, wide in wanted:
        rows, columns = weights[which].shape[-2:]
        split = CHIPS_Y if split_y else 1
        rows //= split
        half = columns if layer is None else columns // CORES
        for piece in range(tall * wide):
            row, column = divmod(piece, wide)
            plan.append(
                (
                    len(args),
                    layer,
                    split_y,
                    layer is not None,
                    row * (rows // tall),
                    rows // tall,
                    column * (half // wide),
                    half // wide,
                )
            )
        args.append(weights[which])
        shapes.append((CHIPS_Z, CHIPS_X, split, rows, columns))
    whole = pl.BlockSpec(memory_space=pltpu.VMEM)
    small = pl.BlockSpec(memory_space=pltpu.SMEM)
    found = pl.pallas_call(
        functools.partial(
            gather_kernel, plan, len(args), ending, work, len(work_args), len(work_shapes)
        ),
        in_specs=[small if arg.shape[-1] == SEGMENTS else whole for arg in work_args]
        + [pl.BlockSpec(memory_space=pl.ANY)] * len(args),
        out_specs=[whole] * (len(work_shapes) + len(args)),
        out_shape=work_shapes + [jax.ShapeDtypeStruct(shape, low) for shape in shapes],
        scratch_shapes=[pltpu.SemaphoreType.DMA((2, 17))] * len(plan)
        + [pltpu.SemaphoreType.DMA((len(plan),))],
        compiler_params=pltpu.CompilerParams(
            vmem_limit_bytes=KERNEL_VMEM, collective_id=number, has_side_effects=True
        ),
        cost_estimate=pl.CostEstimate(flops=0, bytes_accessed=200_000_000, transcendentals=0),
    )(*work_args, *args)
    results, arrays = list(found[: len(work_shapes)]), found[len(work_shapes) :]
    for item, array in zip(wanted, arrays):
        results.append(array if item[1] is None else array.reshape(-1, array.shape[-1]))
    return results


def pack_sums(out_ref, ins):
    rows = 8 * LAYERS
    width = out_ref.shape[1]
    for layer in range(LAYERS):
        sums_ref, ffin_ref, _ = ins[3 * layer : 3 * layer + 3]
        out_ref[8 * layer : 8 * layer + 8] = sums_ref[...]
        for at in range(0, ffin_ref.shape[1], width):
            out_ref[rows : rows + 1] = ffin_ref[:, at : at + width]
            rows += 1
    for layer in range(LAYERS):
        ref = ins[3 * layer + 2]
        for pair in range(ref.shape[1]):
            value = ref[0, pair]
            for tree in range(1, ref.shape[0]):
                value = value + ref[tree, pair]
            out_ref[rows : rows + 8, pair * LANES : (pair + 1) * LANES] = value
        rows += 8


def sum_rows(ffin_width):
    return LAYERS * (16 + ffin_width // D)


def reduce_kernel(flats, count, vectors, work, work_ins, work_outs, *refs):
    take = iter(refs)

    def some(number):
        return [next(take) for _ in range(number)]

    own_ins = some(work_ins)
    a_ins = [some(2) for _ in range(flats)]
    b_ins = [some(2) for _ in range(count)]
    vec_ins = some(vectors)
    own_outs = some(work_outs)
    a_outs = [some(2) for _ in range(flats)]
    b_outs = some(count)
    vec_outs = some(1 if vectors else 0)
    a_scratch = [some(6) for _ in range(flats)]
    b_scratch = [some(6) for _ in range(count)]
    v_send, v_land = some(2) if vectors else (None, None)
    a_sems, b_sems = some(flats), some(count)
    v_sems = next(take) if vectors else None
    todo = work(own_ins, own_outs)
    rep, shard = lax.axis_index("rep"), lax.axis_index("shard")
    y, core = lax.div(rep, CORES), lax.rem(rep, CORES)
    z, x = lax.div(shard, CHIPS_X), lax.rem(shard, CHIPS_X)

    def device(dz=0, dx=0, dy=0, dc=0):
        to_y, to_core = lax.rem(y + dy, CHIPS_Y), lax.rem(core + dc, CORES)
        to_z, to_x = lax.rem(z + dz, CHIPS_Z), lax.rem(x + dx, CHIPS_X)
        return (to_y * CORES + to_core, to_z * CHIPS_X + to_x)

    flip_z = 1 + 2 * lax.rem(z, 2)
    mates = [dict(dx=1), dict(dy=1), dict(dc=1), dict(dy=1, dc=1)]
    mates += [dict(dz=k) for k in range(1, CHIPS_Z)]
    barrier = pltpu.get_barrier_semaphore()
    for mate in mates:
        pl.semaphore_signal(
            barrier, inc=1, device_id=device(**mate), device_id_type=pl.DeviceIdType.MESH
        )
    pl.semaphore_wait(barrier, len(mates))
    sent = []

    def send(source, target, sems, number, **step):
        copy = pltpu.make_async_remote_copy(
            src_ref=source,
            dst_ref=target,
            send_sem=sems.at[0, number],
            recv_sem=sems.at[1, number],
            device_id=device(**step),
            device_id_type=pl.DeviceIdType.MESH,
        )
        copy.start()
        sent.append(copy)
        return copy

    def wide(value):
        return value.astype(jnp.float32)

    order = (2, 1, 3, 0)
    ahead = [lax.rem(z + k, CHIPS_Z) for k in order]
    v_copies = []
    if vectors:
        pack_sums(v_send.at[0], vec_ins)
        v_copies.append(send(v_send.at[0], v_land.at[0], v_sems, 0, dc=1))
    a_x, b_y = [[] for _ in range(flats)], [[] for _ in range(count)]

    def set_out(j):
        to = ahead[j]
        for i, (first, _) in enumerate(a_ins):
            a_x[i].append(send(first.at[to], a_scratch[i][0].at[j], a_sems[i], j, dx=1))
        for i, (first, _) in enumerate(b_ins):
            b_y[i].append(send(first.at[:, to], b_scratch[i][0].at[j], b_sems[i], j, dy=1))

    set_out(0)
    set_out(1)
    steps = (dict(dc=1), dict(dy=1), dict(dx=1), dict(dz=2), dict(dz=flip_z))

    def add_vectors(s):
        if not vectors:
            return
        v_copies[s].wait_recv()
        total = v_send[s] + v_land[s]
        if s + 1 == len(steps):
            vec_outs[0][...] = total
        else:
            v_send[s + 1] = total
            v_copies.append(
                send(v_send.at[s + 1], v_land.at[s + 1], v_sems, s + 1, **steps[s + 1])
            )

    a_z, b_x, b_z = ([[] for _ in range(number)] for number in (flats, count, count))

    def b_along_z(i, j):
        k, keep = order[j], b_ins[i][1]
        over, _, x_land, z_send, z_land, _ = b_scratch[i]
        b_x[i][j].wait_recv()
        if k:
            total = wide(keep[:, ahead[j], x]) + wide(over[j, :, x]) + wide(x_land[j])
            z_send[k - 1] = total.astype(jnp.bfloat16)
            b_z[i].append(send(z_send.at[k - 1], z_land.at[k - 1], b_sems[i], 7 + k, dz=k))

    def b_along_x(i, j):
        keep, (over, x_send, x_land, *_) = b_ins[i][1], b_scratch[i]
        b_y[i][j].wait_recv()
        total = wide(keep[:, ahead[j], 1 - x]) + wide(over[j, :, 1 - x])
        x_send[j] = total.astype(jnp.bfloat16)
        b_x[i].append(send(x_send.at[j], x_land.at[j], b_sems[i], 4 + j, dx=1))

    for j, k in enumerate(order):
        next(todo, None)
        for i, (_, keep) in enumerate(a_ins):
            across, z_send, z_land, *_ = a_scratch[i]
            a_x[i][j].wait_recv()
            if k:
                total = wide(keep[ahead[j]]) + wide(across[j])
                z_send[k - 1] = total.astype(jnp.bfloat16)
                a_z[i].append(
                    send(z_send.at[k - 1], z_land.at[k - 1], a_sems[i], 3 + k, dz=k)
                )
        next(todo, None)
        for i in range(count):
            b_along_x(i, j)
        if j + 2 < CHIPS_Z:
            set_out(j + 2)
        if j:
            for i in range(count):
                b_along_z(i, j - 1)
        next(todo, None)
        add_vectors(j)
    for i in range(count):
        b_along_z(i, CHIPS_Z - 1)
    add_vectors(4)
    for _ in todo:
        pass
    over_y, ends = [], []
    for i, (_, keep) in enumerate(a_ins):
        across, _, z_land, y_send, y_land, _ = a_scratch[i]
        for copy in a_z[i]:
            copy.wait_recv()
        total = wide(keep[z]) + wide(across[CHIPS_Z - 1])
        for k in range(CHIPS_Z - 1):
            total = total + wide(z_land[k])
        y_send[...] = total.astype(jnp.bfloat16)
        over_y.append(send(y_send, y_land, a_sems[i], 7, dy=1))
    for i, (_, keep) in enumerate(b_ins):
        over, _, x_land, _, z_land, end_land = b_scratch[i]
        for copy in b_z[i]:
            copy.wait_recv()
        total = wide(keep[:, z, x]) + wide(over[3, :, x]) + wide(x_land[3])
        for k in range(CHIPS_Z - 1):
            total = total + wide(z_land[k])
        b_outs[i][0] = total.astype(jnp.bfloat16)
        for number, step in enumerate((dict(dy=1), dict(dc=1), dict(dy=1, dc=1))):
            ends.append(
                send(b_outs[i].at[0], end_land.at[number], b_sems[i], 11 + number, **step)
            )
    for i, (own, _) in enumerate(a_outs):
        *_, y_send, y_land, c_land = a_scratch[i]
        over_y[i].wait_recv()
        own[...] = (wide(y_send[...]) + wide(y_land[...])).astype(jnp.bfloat16)
        ends.append(send(own, c_land, a_sems[i], 8, dc=1))
    for copy in ends:
        copy.wait_recv()
    for i in range(count):
        b_outs[i][1:4] = b_scratch[i][5][...]
    for i, (_, other) in enumerate(a_outs):
        other[...] = a_scratch[i][5][...]
    for copy in sent:
        copy.wait_send()


def no_work(ins, outs):
    return iter(())


def reduce_sums(flats, pairs, sums, number, work=no_work, work_args=(), work_shapes=()):
    low = jnp.bfloat16
    whole = pl.BlockSpec(memory_space=pltpu.VMEM)
    far = pl.BlockSpec(memory_space=pl.ANY)
    args, specs = list(work_args), [whole] * len(work_args)
    outs, scratch = [], []
    for first, keep in flats:
        piece = keep.shape[1:]
        args += [first, keep]
        specs += [far, whole]
        outs += [piece, piece]
        scratch += [(CHIPS_Z, *piece), (CHIPS_Z - 1, *piece), (CHIPS_Z - 1, *piece)]
        scratch += [piece] * 3
    for first, keep in pairs:
        parts, _, _, rows, half = keep.shape
        block = (parts, rows, half)
        args += [first, keep]
        specs += [far, whole]
        outs.append((CORES * CHIPS_Y, *block))
        scratch += [
            (CHIPS_Z, parts, CHIPS_X, rows, half),
            (CHIPS_Z, *block),
            (CHIPS_Z, *block),
            (CHIPS_Z - 1, *block),
            (CHIPS_Z - 1, *block),
            (CORES * CHIPS_Y - 1, *block),
        ]
    args += sums
    specs += [whole] * len(sums)
    shapes = list(work_shapes) + [jax.ShapeDtypeStruct(shape, low) for shape in outs]
    scratch = [pltpu.VMEM(shape, low) for shape in scratch]
    if sums:
        vec = (sum_rows(sums[1].shape[1]), D)
        shapes.append(jax.ShapeDtypeStruct(vec, jnp.float32))
        scratch += [pltpu.VMEM((5, *vec), jnp.float32)] * 2
    scratch += [pltpu.SemaphoreType.DMA((2, 9))] * len(flats)
    scratch += [pltpu.SemaphoreType.DMA((2, 14))] * len(pairs)
    if sums:
        scratch.append(pltpu.SemaphoreType.DMA((2, 5)))
    return pl.pallas_call(
        functools.partial(
            reduce_kernel, len(flats), len(pairs), len(sums), work, len(work_args), len(work_shapes)
        ),
        in_specs=specs,
        out_specs=[whole] * len(shapes),
        out_shape=shapes,
        scratch_shapes=scratch,
        compiler_params=pltpu.CompilerParams(
            vmem_limit_bytes=KERNEL_VMEM, collective_id=number, has_side_effects=True
        ),
        cost_estimate=pl.CostEstimate(flops=0, bytes_accessed=200_000_000, transcendentals=0),
    )(*args)


def join_kernel(plan, count, at_ref, *refs):
    for ref, out, layer, outer, parts, dc, dy, start, rows in plan:
        ref, out_ref = refs[ref], refs[count + out]
        half = ref.shape[1]
        core = lax.rem(at_ref[3] + dc, CORES)
        row = 0
        if dy is not None:
            row = pl.multiple_of(lax.rem(at_ref[2] + dy, CHIPS_Y) * rows, 16)
        for part in range(parts):
            column = part * CORES + core if outer else core * parts + part
            column = pl.multiple_of(column * half, 128)
            value = ref[start + part * rows : start + (part + 1) * rows]
            out_ref[layer, pl.ds(row, rows), pl.ds(column, half)] = value.astype(jnp.float32)


def join(at, done, shapes):
    arrays, plan = [], []
    for out, (number, (tall, wide)) in enumerate(shapes.items()):
        for layer in range(LAYERS):
            pieces, start, rows = done[layer][number]
            for place, piece in enumerate(pieces):
                known = [other is piece for other in arrays]
                if not any(known):
                    arrays.append(piece)
                    known.append(True)
                parts = wide // (CORES * piece.shape[1])
                dy, dc = (place % CHIPS_Y, place // CHIPS_Y) if len(pieces) > CORES else (None, place)
                plan.append((known.index(True), out, layer, number == 0, parts, dc, dy, start, rows))
    zeros = lambda i, at: (0, 0)
    outs = [(LAYERS, *shape) for shape in shapes.values()]
    return pl.pallas_call(
        functools.partial(join_kernel, plan, len(arrays)),
        grid_spec=pltpu.PrefetchScalarGridSpec(
            num_scalar_prefetch=1,
            grid=(1,),
            in_specs=[pl.BlockSpec(array.shape, zeros) for array in arrays],
            out_specs=[pl.BlockSpec(out, lambda i, at: (0, 0, 0)) for out in outs],
        ),
        out_shape=[jax.ShapeDtypeStruct(out, jnp.float32) for out in outs],
        compiler_params=kernel_params(),
        cost_estimate=pl.CostEstimate(flops=0, bytes_accessed=4_000_000, transcendentals=0),
    )(at, *arrays)


def local(
    fast,
    inputs,
    cotangent,
    segment,
    parent,
    clusters,
    *weights,
):
    pieces = {}
    if fast:
        place = Place()
        at = place.at
        shards = dict(enumerate(weights))
        shards["vectors"] = jnp.pad(
            jnp.concatenate([weights[member] for member in VECTORS], axis=1),
            ((0, 16 - LAYERS), (0, 0)),
        )
        trees = parent.shape[0]
        sizes = [weights[number].shape[1] for number in VECTORS]
        slots, bias, *vectors, found, qkv = gather(
            shards,
            (("vectors", None, False, 1, 1), (0, 0, True, 1, 1)),
            prep_steps,
            (
                parent,
                segment.reshape(trees, 1, TREE_LEN),
                clusters.reshape(PAIRS, 2, trees, TREE_LEN).transpose(2, 0, 1, 3),
            ),
            [
                jax.ShapeDtypeStruct((trees, PAIRS, 2, TREE_LEN), jnp.int32),
                jax.ShapeDtypeStruct((trees, HEADS, TREE_LEN, LANES), jnp.bfloat16),
                *[
                    jax.ShapeDtypeStruct((LAYERS, CHIPS_Z * CHIPS_X * size), jnp.float32)
                    for size in sizes[:1]
                ],
            ],
            1,
            lambda own_outs, outs: spread_vectors(outs[0], 0, sizes[:1], own_outs[2:]),
        )
        whole = {(0, 0): qkv}

        def attend_layer(layer, projected):
            last = layer + 1 == LAYERS
            if last:
                wanted = [(6, layer, True, 1, 1), (2, layer, True, 1, 1), (8, layer, False, 1, 1)]
            else:
                wanted = [(6, layer, True, 1, 1), (8, layer, True, 1, 1)]
                wanted += [(0, layer + 1, False, 1, 1), (2, layer, False, 1, 1)]
            work, args, results_of = attend_steps, (projected, slots, bias), attend_shapes(trees)
            if layer == 0:
                work, args = functools.partial(attend_and_spread, sizes), (*args, found)
                results_of += [
                    jax.ShapeDtypeStruct((LAYERS, CHIPS_Z * CHIPS_X * size), jnp.float32)
                    for size in sizes[1:]
                ]
            results = gather(shards, wanted, work, args, results_of, 2 + layer)
            if layer == 0:
                vector.update(zip(VECTORS[1:], results[4:]))
            for (number, at_layer, *_), array in zip(wanted, results[len(results_of) :]):
                whole[at_layer, number] = array
            return results[:4]

        def get(layer, number):
            return whole[layer, number]

        def attend_back_layer(layer, grad_context, heads, groups, waiting):
            flat, pair = cut_sums(place, groups)
            proj, head_sums, *ends = reduce_sums(
                [flat],
                [pair, *waiting],
                [],
                2 + LAYERS + layer,
                attend_back_steps,
                (slots, grad_context, *heads),
                attend_back_shapes(trees),
            )
            pieces[layer, "flat"] = ends[:2]
            pieces[layer, 6] = ends[2]
            if waiting:
                pieces[layer + 1, 0] = ends[3]
            return proj, head_sums

    else:
        slots, bias = prepare(segment, parent, clusters)
        vectors = [
            lax.all_gather(weights[number], "shard", axis=1, tiled=True).astype(jnp.float32)
            for number in VECTORS
        ]

        def attend_layer(layer, projected):
            return attend(projected, slots, bias)

        def get(layer, number):
            return lax.all_gather(weights[number][layer], "shard", axis=0, tiled=True)

        def own_sum(left, right):
            if right.ndim == 3:
                right = right.transpose(1, 0, 2).reshape(right.shape[1], -1)
            total = contract_first(left, right)
            total = lax.psum_scatter(total, "shard", scatter_dimension=0, tiled=True)
            return lax.psum(total.astype(jnp.bfloat16), "rep").astype(jnp.float32)

        def attend_back_layer(layer, grad_context, heads, groups, waiting):
            for grads, _ in groups:
                for grad in grads:
                    pieces[layer, grad.number] = own_sum(grad.left, grad.right)
            return attend_back(grad_context, slots, heads)

    vector = dict(zip(VECTORS, vectors))
    hidden, hidden_low = inputs, inputs
    saved = []
    for layer in range(LAYERS):
        pull = functools.partial(get, layer)
        projected = project(layer, hidden_low, pull(0), vector[1])
        context, *heads = attend_layer(layer, projected)
        entered = hidden_low
        middle, act, slope, *norms, hidden, hidden_low = feed(
            layer,
            context,
            hidden,
            [pull(2), pull(6), pull(8)],
            [vector[number] for number in (3, 4, 5, 7, 9, 10, 11)],
        )
        saved.append((entered, heads, context, middle, act, slope, norms))
    result = hidden_low
    above, proj = cotangent, None
    sums, waiting = [None] * LAYERS, []
    for layer in reversed(range(LAYERS)):
        entered, heads, context, middle, act, slope, norms = saved[layer]
        pull = functools.partial(get, layer)
        down, grad_pre, grad_attn, attn_low, grad_context, row_sums, ffin_sum = feed_back(
            layer,
            above,
            proj,
            None if proj is None else get(layer + 1, 0),
            [norms[2], norms[3], slope, norms[0], norms[1]],
            [pull(2), pull(6), pull(8)],
            [vector[4], vector[10]],
        )
        wide = grad_pre.shape[1] // CORES
        groups = (
            (
                (
                    Grad(8, act, down, act.shape[1] // D, UNIT),
                    Grad(2, context, attn_low, 1, UNIT),
                ),
                False,
            ),
            ((Grad(6, middle, grad_pre, wide // D, D),), True),
        )
        proj, head_sums = attend_back_layer(layer, grad_context, heads, groups, waiting)
        sums[layer] = [row_sums, ffin_sum, head_sums]
        above = grad_attn
        last = Grad(0, entered, proj, 3, UNIT)
        if not fast:
            pieces[layer, 0] = own_sum(last.left, last.right)
        elif layer:
            waiting = cut_sums(place, [((last,), True)])
    grad_input = input_grad(above, proj, get(0, 0))
    sums = [item for layer in sums for item in layer]
    if fast:
        (pair,) = cut_sums(place, [((last,), True)])
        pair, grad_input = lax.optimization_barrier((pair, grad_input))
        pieces[0, 0], total = reduce_sums([], [pair], sums, 0)
    else:
        norms, wide, heads = [], [], []
        for row_sums, ffin_sum, head_sums in (sums[:3], sums[3:]):
            norms.append(row_sums)
            wide.append(ffin_sum.reshape(-1, D))
            heads.append(head_sums.sum(0).transpose(1, 0, 2).reshape(8, D))
        total = lax.psum(jnp.concatenate(norms + wide + heads), AXES)
    count = lax.axis_size("shard")
    shard = lax.axis_index("shard")
    ffin_rows = sums[1].shape[1] // D

    def share(rows):
        stacked = jnp.stack([total[row].reshape(-1) for row in rows])
        width = stacked.shape[1] // count
        return lax.dynamic_slice_in_dim(stacked, shard * width, width, axis=1)

    starts = [0, 8, 16, 16 + ffin_rows]
    heads_at = [16 + 2 * ffin_rows, 24 + 2 * ffin_rows]
    grads = {
        1: share([slice(at, at + 3, 2) for at in heads_at]),
        7: share([slice(at, at + ffin_rows) for at in starts[2:]]),
    }
    for number, row in ((10, 0), (11, 1), (9, 2), (4, 3), (5, 4), (3, 5)):
        grads[number] = share([row, 8 + row])
    if fast:
        rows = {number: weights[number].shape[1] for number in MATRICES}
        parts = {number: weights[number].shape[2] // (CORES * UNIT) for number in MATRICES}
        known = [{} for _ in range(LAYERS)]
        for layer in range(LAYERS):
            start = 0
            for number in (8, 2):
                known[layer][number] = (pieces[layer, "flat"], start, rows[number])
                start += rows[number] * parts[number]
            for number in (6, 0):
                end = pieces[layer, number]
                end = end.reshape(end.shape[0], -1, end.shape[-1])
                known[layer][number] = (list(end), 0, rows[number] // CHIPS_Y)
        for numbers in (MATRICES,):
            shapes = {number: weights[number].shape[1:] for number in numbers}
            grads.update(zip(numbers, join(place.at, known, shapes)))
    else:
        for number in MATRICES:
            grads[number] = jnp.stack([pieces[layer, number] for layer in range(LAYERS)])
    return (result, grad_input, *[grads[number] for number in range(12)])


def solution(mesh):
    in_specs = (
        P(("rep", "shard"), None),
        P(("rep", "shard"), None),
        P(("rep", "shard")),
        P(("rep", "shard"), None),
        P(None, ("rep", "shard")),
        P(None, "shard", None),
        P(None, "shard"),
        P(None, "shard", None),
        P(None, "shard"),
        P(None, "shard"),
        P(None, "shard"),
        P(None, "shard", None),
        P(None, "shard"),
        P(None, "shard", None),
        P(None, "shard"),
        P(None, "shard"),
        P(None, "shard"),
    )
    out_specs = (
        P(("rep", "shard"), None),
        P(("rep", "shard"), None),
        P(None, "shard", None),
        P(None, "shard"),
        P(None, "shard", None),
        P(None, "shard"),
        P(None, "shard"),
        P(None, "shard"),
        P(None, "shard", None),
        P(None, "shard"),
        P(None, "shard", None),
        P(None, "shard"),
        P(None, "shard"),
        P(None, "shard"),
    )
    fast = mesh.shape["rep"] == CHIPS_Y * CORES and mesh.shape["shard"] == CHIPS_Z * CHIPS_X
    return jax.shard_map(
        functools.partial(local, fast),
        mesh=mesh,
        in_specs=in_specs,
        out_specs=out_specs,
        check_vma=False,
    )
```
